32 devices in a mesh: dp: 8 (over z, x), tensor: 4 (over y, core).
Axes of the slice: x: 2, y: 2, z: 4, core: 2. Of those that a mesh axis runs over, the one named last changes fastest.
Arguments:
- tokens: bfloat16 [32768, 768], P('dp'), may hold values from -6 to 6
- lengths: int32 [64], P('dp'), may hold values from 40 to 512
- cotangent: bfloat16 [16384, 768], P('dp'), may hold values from -6 to 6
- query_weight: float32 [768, 768], P('dp', 'tensor'), may hold values from -0.21875 to 0.21875
- key_weight: float32 [768, 768], P('dp', 'tensor'), may hold values from -0.21875 to 0.21875
- value_weight: float32 [768, 768], P('dp', 'tensor'), may hold values from -0.21875 to 0.21875
- value_bias: float32 [768], P('tensor'), may hold values from -0.6 to 0.6
- output_weight: float32 [768, 768], P('tensor', 'dp'), may hold values from -1.75 to 1.75
- b_out: float32 [768], replicated, may hold values from -1.5 to 1.5
- rel_table: float32 [12, 1024], P('tensor'), may hold values from -4 to 4
- norm_gain: float32 [768], replicated, may hold values from 0.1 to 1.9
- norm_shift: float32 [768], replicated, may hold values from -1.5 to 1.5
- up_weight: float32 [768, 3072], P('dp', 'tensor'), may hold values from -0.21875 to 0.21875
- hidden_bias: float32 [3072], P('tensor'), may hold values from -1.5 to 1.5
- down_weight: float32 [3072, 768], P('tensor', 'dp'), may hold values from -0.109375 to 0.109375
- b_down: float32 [768], replicated, may hold values from -1.5 to 1.5
- final_gain: float32 [768], replicated, may hold values from 0.1 to 1.9
- final_shift: float32 [768], replicated, may hold values from -1.5 to 1.5
Outputs:
- output: bfloat16 [16384, 768], P('dp')
- tokens_grad: bfloat16 [32768, 768], P('dp')
- query_grad: float32 [768, 768], P('dp', 'tensor')
- key_grad: float32 [768, 768], P('dp', 'tensor')
- value_grad: float32 [768, 768], P('dp', 'tensor')
- vbias_grad: float32 [768], P('tensor')
- outw_grad: float32 [768, 768], P('tensor', 'dp')
- obias_grad: float32 [768], replicated
- table_grad: float32 [12, 1024], P('tensor')
- ngain_grad: float32 [768], replicated
- nshift_grad: float32 [768], replicated
- upw_grad: float32 [768, 3072], P('dp', 'tensor')
- ubias_grad: float32 [3072], P('tensor')
- downw_grad: float32 [3072, 768], P('tensor', 'dp')
- dbias_grad: float32 [768], replicated
- fgain_grad: float32 [768], replicated
- fshift_grad: float32 [768], replicated
The draws below stay inside these ranges and needn't reach their ends.
All inputs are finite; a program needn't handle non-finite values.
Results may differ from the reference program's by a relative error of at most 0.02.
Values may be sent and summed in bfloat16 or wider, within the bound.
A program may use at most 256 MiB of HBM per device.

```python
import jax
import jax.numpy as jnp
from jax import lax

D = 768
H = 12
DH = 64
FF = 3072
L = 512
MINLEN = 40
SEQ_DEV = 8
LQ = 256
REL = 1024
SEQS = 64
TOKENS = 32768
TOKENS_Q = 16384
N_TENSOR = 4


def touch_ends(values, stream_key, least, high):
    place = [jax.random.randint(jax.random.fold_in(stream_key, axis), (), 0, length) for axis, length in enumerate(values.shape)]
    main_axis = values.shape.index(max(values.shape))
    beside = place[:main_axis] + [(place[main_axis] + 1) % values.shape[main_axis]] + place[main_axis + 1:]
    return values.at[tuple(place)].set(least).at[tuple(beside)].set(high)


def steps_of(key, dims, shards, smallest, top_value):
    loudness = 1.0
    for position, shards_of in shards:
        draws = jax.random.uniform(jax.random.fold_in(jax.random.fold_in(key, 6), position), (shards_of,), jnp.float32, smallest / len(shards), top_value / len(shards))
        loudness = loudness * jnp.repeat(jnp.exp(draws), dims[position] // shards_of).reshape((-1,) + (1,) * (len(dims) - 1 - position))
    return loudness


def gaussian(own_key, shape, scale, bound, shards=(), kind=jnp.bfloat16):
    array = jax.random.normal(own_key, shape, jnp.float32) * scale
    if len(shards) > 0:
        array = steps_of(own_key, shape, shards, -0.22, 0.18) * array
    return jnp.clip(array, min=-bound, max=bound).astype(kind)


def setup_inputs(seed: int = 0) -> dict:
    seeds = jax.random.split(jax.random.key(seed), 19)
    return {
        "tokens": gaussian(seeds[0], (TOKENS, D), 1.0, 6.0, ((0, 8),)),
        "lengths": touch_ends(jax.random.randint(seeds[1], (SEQS,), MINLEN, L + 1), jax.random.fold_in(seeds[1], 1), MINLEN, L).astype(jnp.int32),
        "cotangent": gaussian(seeds[2], (TOKENS_Q, D), 1.0, 6.0, ((0, 8),)),
        "query_weight": gaussian(seeds[3], (D, H * DH), D ** -0.5, 0.21875, ((0, 8), (1, 4)), jnp.float32),
        "key_weight": gaussian(seeds[4], (D, H * DH), D ** -0.5, 0.21875, ((0, 8), (1, 4)), jnp.float32),
        "value_weight": gaussian(seeds[5], (D, H * DH), D ** -0.5, 0.21875, ((0, 8), (1, 4)), jnp.float32),
        "value_bias": gaussian(seeds[6], (H * DH,), 0.1, 0.6, ((0, 4),), jnp.float32),
        "output_weight": gaussian(seeds[7], (H * DH, D), (H * DH * 8 // L) ** -0.5, 1.75, ((0, 4), (1, 8)), jnp.float32),
        "b_out": gaussian(seeds[8], (D,), 0.3, 1.5, (), jnp.float32),
        "rel_table": gaussian(seeds[9], (H, REL), 1.0, 4.0, ((0, 4),), jnp.float32),
        "norm_gain": jnp.clip(1.0 + 0.18 * jax.random.normal(seeds[10], (D,), jnp.float32), 0.1, 1.9),
        "norm_shift": gaussian(seeds[11], (D,), 0.3, 1.5, (), jnp.float32),
        "up_weight": gaussian(seeds[12], (D, FF), D ** -0.5, 0.21875, ((0, 8), (1, 4)), jnp.float32),
        "hidden_bias": gaussian(seeds[13], (FF,), 0.3, 1.5, ((0, 4),), jnp.float32),
        "down_weight": gaussian(seeds[14], (FF, D), FF ** -0.5, 0.109375, ((0, 4), (1, 8)), jnp.float32),
        "b_down": gaussian(seeds[15], (D,), 0.3, 1.5, (), jnp.float32),
        "final_gain": jnp.clip(1.0 + 0.18 * jax.random.normal(seeds[16], (D,), jnp.float32), 0.1, 1.9),
        "final_shift": gaussian(seeds[17], (D,), 0.3, 1.5, (), jnp.float32),
    }


@jax.custom_vjp
def reduced_precision(v):
    return lax.optimization_barrier(v.astype(jnp.bfloat16)).astype(jnp.float32)

@jax.custom_vjp
def reduced_backward(v):
    return v

def low_keep(v):
    return (reduced_precision(v), None)

def low_pass(kept, grad):
    return (grad,)

def back_keep(v):
    return (v, None)

def back_low(kept, grad):
    return (reduced_precision(grad),)
reduced_precision.defvjp(low_keep, low_pass)
reduced_backward.defvjp(back_keep, back_low)
epsilon = 1e-06

def matrix_product(form, left, right):
    return jnp.einsum(form, left, right, precision=lax.Precision.HIGHEST)

def norm_rows(values, gain_vec, shift_vec):
    row_mean = lax.optimization_barrier(jnp.mean(values, axis=-1, keepdims=True))
    centred = values - row_mean
    row_var = lax.optimization_barrier(jnp.mean(centred * centred, axis=-1, keepdims=True))
    return centred * lax.rsqrt(row_var + epsilon) * gain_vec + shift_vec

def shifted_table(pos_table):
    starts = (L - 2 * jnp.arange(LQ)).astype(jnp.int32)

    def one_row(offset):
        return lax.dynamic_slice_in_dim(pos_table, offset, L, 1)
    return jnp.transpose(jax.vmap(one_row)(starts), (1, 0, 2))

def funnel_layer(weights, sequence_tokens, seq_lengths):
    query_weight, key_weight, value_weight, value_bias, output_weight, b_out, rel_table, norm_gain, norm_shift, up_weight, hidden_bias, down_weight, b_down, final_gain, final_shift = weights
    query_weight = reduced_precision(query_weight)
    key_weight = reduced_precision(key_weight)
    value_weight = reduced_precision(value_weight)
    output_weight = reduced_precision(output_weight)
    up_weight = reduced_precision(up_weight)
    down_weight = reduced_precision(down_weight)
    seq_count = sequence_tokens.shape[0]
    key_valid = jnp.arange(L).astype(jnp.int32)[None, :] < seq_lengths[:, None]
    query_valid = ((2 * jnp.arange(LQ)).astype(jnp.int32)[None, :] < seq_lengths[:, None]).astype(jnp.float32)
    pooled = lax.optimization_barrier(jnp.mean(sequence_tokens.reshape(seq_count, LQ, 2, D), axis=2))
    rel_bias = shifted_table(rel_table)
    group_heads = H // N_TENSOR
    group_cols = group_heads * DH
    group_units = FF // N_TENSOR
    score_scale = DH ** (-0.5)
    attention_mixed = jnp.zeros((seq_count, LQ, D), jnp.float32)
    for group_index in range(N_TENSOR):
        head_extent = slice(group_index * group_cols, (group_index + 1) * group_cols)
        token_local_rows = reduced_backward(sequence_tokens)
        pooled_local_rows = reduced_precision(lax.optimization_barrier(jnp.mean(token_local_rows.reshape(seq_count, LQ, 2, D), axis=2)))
        query_rows = reduced_backward(reduced_precision(matrix_product('sku,uz->skz', pooled_local_rows, query_weight[:, head_extent]) * score_scale))
        key_rows_reduced = reduced_backward(reduced_precision(matrix_product('yil,lj->yij', token_local_rows, key_weight[:, head_extent])))
        value_rows_reduced = reduced_backward(reduced_precision(matrix_product('yil,lj->yij', token_local_rows, value_weight[:, head_extent]) + value_bias[head_extent]))
        query_heads = query_rows.reshape(seq_count, LQ, group_heads, DH)
        key_heads = key_rows_reduced.reshape(seq_count, L, group_heads, DH)
        value_heads = value_rows_reduced.reshape(seq_count, L, group_heads, DH)
        group_bias = rel_bias[group_index * group_heads:(group_index + 1) * group_heads]
        scores = matrix_product('bqhe,bkhe->bhqk', query_heads, key_heads) + group_bias[None]
        scores = reduced_backward(scores)
        scores = jnp.where(key_valid[:, None, None, :], scores, -1e+30)
        attn_probs = jax.nn.softmax(scores, axis=-1)
        context_rows = matrix_product('bhqk,bkhe->bqhe', reduced_precision(attn_probs), value_heads).reshape(seq_count, LQ, group_cols)
        context_rows = reduced_backward(reduced_precision(context_rows))
        attention_mixed = attention_mixed + reduced_precision(matrix_product('atx,xo->ato', context_rows, output_weight[head_extent, :]))
    attention_mixed = reduced_backward(attention_mixed)
    hidden_in = pooled + attention_mixed + b_out
    normed = norm_rows(hidden_in, norm_gain, norm_shift)
    normalized_reduced = reduced_precision(normed)
    feedforward_result = jnp.zeros((seq_count, LQ, D), jnp.float32)
    for group_index in range(N_TENSOR):
        unit_extent = slice(group_index * group_units, (group_index + 1) * group_units)
        preactivation = reduced_backward(matrix_product('pjg,gy->pjy', reduced_backward(normalized_reduced), up_weight[:, unit_extent]) + hidden_bias[unit_extent])
        activation_output = reduced_precision(jax.nn.gelu(preactivation, approximate=False))
        feedforward_result = feedforward_result + reduced_precision(matrix_product('jtu,ul->jtl', activation_output, down_weight[unit_extent, :]))
    feedforward_result = reduced_backward(feedforward_result)
    summed = normed + feedforward_result + b_down
    return norm_rows(summed, final_gain, final_shift) * query_valid[..., None]

def reference(tokens, lengths, cotangent, query_weight, key_weight, value_weight, value_bias, output_weight, b_out, rel_table, norm_gain, norm_shift, up_weight, hidden_bias, down_weight, b_down, final_gain, final_shift):
    weights = tuple((param.astype(jnp.float32) for param in (query_weight, key_weight, value_weight, value_bias, output_weight, b_out, rel_table, norm_gain, norm_shift, up_weight, hidden_bias, down_weight, b_down, final_gain, final_shift)))
    steps_count = SEQS // SEQ_DEV
    block_tokens = tokens.astype(jnp.float32).reshape(steps_count, SEQ_DEV, L, D)
    block_cots = cotangent.astype(jnp.float32).reshape(steps_count, SEQ_DEV, LQ, D)
    block_lengths = lengths.reshape(steps_count, SEQ_DEV)

    def scan_step(totals, block_item):
        part_tokens, part_cots, part_lengths = block_item

        def forward(params, inputs):
            return funnel_layer(params, inputs, part_lengths)
        result, pull_back = jax.vjp(forward, weights, part_tokens)
        param_grads, input_grad = pull_back(part_cots)
        totals = jax.tree.map(lambda left, right: left + right, totals, param_grads)
        return (totals, (result.astype(jnp.bfloat16), input_grad.astype(jnp.bfloat16)))
    zero_grads = jax.tree.map(jnp.zeros_like, weights)
    totals, (outputs, input_grads) = lax.scan(scan_step, zero_grads, (block_tokens, block_cots, block_lengths))
    return (outputs.reshape(TOKENS_Q, D), input_grads.reshape(TOKENS, D), totals[0], totals[1], totals[2], totals[3], totals[4], totals[5], totals[6], totals[7], totals[8], totals[9], totals[10], totals[11], totals[12], totals[13], totals[14])
```

```python
import functools

import jax
import jax.numpy as jnp
from jax import lax
from jax.experimental import pallas as pl
from jax.experimental.pallas import tpu as pltpu
from jax.sharding import PartitionSpec as P

MESH = pl.DeviceIdType.MESH
F32 = jnp.float32
BF16 = jnp.bfloat16
EPS = 1e-06
VMEM_LIMIT = 58 * 2**20


def dot_nn(a, b):
    return lax.dot_general(a, b, (((1,), (0,)), ((), ())), preferred_element_type=F32)


def dot_nt(a, b):
    return lax.dot_general(a, b, (((1,), (1,)), ((), ())), preferred_element_type=F32)


def dot_tn(a, b):
    return lax.dot_general(a, b, (((0,), (0,)), ((), ())), preferred_element_type=F32)


def gather_kernel(
    n_hi, a_in, u_in, d_in, s_in, a_out, u_out, d_out, s_out, loc, zs, zr, ls, lr, fs, fr, cs, cr, ss, sr
):
    dp, t = lax.axis_index("dp"), lax.axis_index("tensor")
    hi, lo = dp // 2, lax.rem(dp, 2)
    core = lax.rem(t, 2)
    t_core = t + 1 - 2 * core
    t_y = lax.rem(t + 2, 4)
    t_d = lax.rem(t_core + 2, 4)
    dp_x = dp + 1 - 2 * lo

    def z_peer(s):
        return lax.rem(hi + s, n_hi) * 2 + lo

    def block(s, side):
        return lax.rem(hi - s + n_hi, n_hi) * 2 + side

    barrier = pltpu.get_barrier_semaphore()

    def greet(s, carry):
        pl.semaphore_signal(barrier, inc=1, device_id=(z_peer(s), t), device_id_type=MESH)
        return carry

    lax.fori_loop(1, n_hi, greet, 0)
    for peer in ((dp_x, t), (dp, t_y), (dp, t_core), (dp, t_d)):
        pl.semaphore_signal(barrier, inc=1, device_id=peer, device_id_type=MESH)
    pl.semaphore_wait(barrier, n_hi + 3)

    def remote(src, dst, send, recv, peer):
        return pltpu.make_async_remote_copy(
            src, dst, send, recv, device_id=peer, device_id_type=MESH
        )

    ins, outs = (a_in, u_in, d_in), (a_out, u_out, d_out)

    def small(i, peer):
        return remote(s_in, s_out.at[t], ss.at[i], sr.at[i], peer)

    small_peers = ((dp, t_core), (dp, t_y), (dp, t_d))
    small_local = pltpu.make_async_copy(s_in, s_out.at[t], loc.at[3])
    small_local.start()
    for i, peer in enumerate(small_peers):
        small(i, peer).start()

    def local(k):
        return pltpu.make_async_copy(ins[k], outs[k].at[t, dp], loc.at[k])

    def z_copy(k, s):
        return remote(ins[k], outs[k].at[t, dp], zs.at[k, s], zr.at[k, s], (z_peer(s), t))

    def line(k, s, way, src):
        b = block(s, lo)
        peer = (dp_x, t) if way == 0 else (dp, t_y)
        return remote(src, outs[k].at[t, b], ls.at[way, k, s], lr.at[way, k, s], peer)

    def fwd_x(k, s):
        where = outs[k].at[t_y, block(s, lo)]
        return remote(where, where, fs.at[k, s], fr.at[k, s], (dp_x, t))

    def fwd_y(k, s):
        where = outs[k].at[t, block(s, 1 - lo)]
        return remote(where, where, fs.at[k, s], fr.at[k, s], (dp, t_y))

    def to_core(k, s, which, src=None):
        tt = t if which < 2 else t_y
        side = lo if which % 2 == 0 else 1 - lo
        where = outs[k].at[tt, block(s, side)]
        return remote(
            where if src is None else src,
            where,
            cs.at[which, k, s],
            cr.at[which, k, s],
            (dp, t_core),
        )

    def start_z(k):
        local(k).start()

        def body(s, carry):
            z_copy(k, s).start()
            return carry

        lax.fori_loop(1, n_hi, body, 0)

    def first(k):
        line(k, 0, 0, ins[k]).start()
        line(k, 0, 1, ins[k]).start()
        to_core(k, 0, 0, ins[k]).start()

    def spread(k):
        def body(s, carry):
            z_copy(k, s).wait_recv()
            src = outs[k].at[t, block(s, lo)]
            line(k, s, 0, src).start()
            line(k, s, 1, src).start()
            to_core(k, s, 0).start()
            return carry

        lax.fori_loop(1, n_hi, body, 0)

    def forward(k):
        def body(s, carry):
            @pl.when(core == 0)
            def _():
                line(k, s, 0, ins[k]).wait_recv()
                fwd_y(k, s).start()
                to_core(k, s, 1).start()
                line(k, s, 1, ins[k]).wait_recv()
                to_core(k, s, 2).start()

            @pl.when(core == 1)
            def _():
                line(k, s, 1, ins[k]).wait_recv()
                fwd_x(k, s).start()
                to_core(k, s, 2).start()
                line(k, s, 0, ins[k]).wait_recv()
                to_core(k, s, 1).start()

            return carry

        lax.fori_loop(0, n_hi, body, 0)

    def last(k):
        def body(s, carry):
            fwd_y(k, s).wait_recv()
            to_core(k, s, 3).start()
            return carry

        lax.fori_loop(0, n_hi, body, 0)

    def finish(k):
        local(k).wait()

        def body(s, carry):
            line(k, s, 0, ins[k]).wait_send()
            line(k, s, 1, ins[k]).wait_send()
            fwd_y(k, s).wait_send()
            for which in range(4):
                to_core(k, s, which).wait_send()
                to_core(k, s, which).wait_recv()
            return carry

        lax.fori_loop(0, n_hi, body, 0)

        def zbody(s, carry):
            z_copy(k, s).wait_send()
            return carry

        lax.fori_loop(1, n_hi, zbody, 0)

    start_z(0)
    first(0)
    spread(0)
    start_z(1)
    first(1)
    forward(0)
    spread(1)
    start_z(2)
    first(2)
    last(0)
    forward(1)
    spread(2)
    last(1)
    forward(2)
    last(2)
    for k in range(3):
        finish(k)
    small_local.wait()
    for i, peer in enumerate(small_peers):
        small(i, peer).wait()


def gather_weights(a, u, d, small, n_dp):
    n_hi = n_dp // 2
    rows, width = a.shape
    whole = jax.ShapeDtypeStruct((4, n_dp, rows, width), BF16)
    dma = pltpu.SemaphoreType.DMA
    any_spec = pl.BlockSpec(memory_space=pl.ANY)
    a4, u4, d4, s4 = pl.pallas_call(
        functools.partial(gather_kernel, n_hi),
        out_shape=(whole, whole, whole, jax.ShapeDtypeStruct((4,) + small.shape, F32)),
        in_specs=[any_spec] * 4,
        out_specs=(any_spec,) * 4,
        scratch_shapes=[
            dma((4,)),
            dma((3, n_hi)),
            dma((3, n_hi)),
            dma((2, 3, n_hi)),
            dma((2, 3, n_hi)),
            dma((3, n_hi)),
            dma((3, n_hi)),
            dma((4, 3, n_hi)),
            dma((4, 3, n_hi)),
            dma((3,)),
            dma((3,)),
        ],
        compiler_params=pltpu.CompilerParams(collective_id=0, has_side_effects=True),
    )(a, u, d, small)
    flat = (4, n_dp * rows, width)
    return a4.reshape(flat), u4.reshape(flat), d4.reshape(flat), s4


def pool_matrix(pooled, length):
    i = lax.broadcasted_iota(jnp.int32, (pooled, length), 0)
    j = lax.broadcasted_iota(jnp.int32, (pooled, length), 1)
    return jnp.where(j // 2 == i, 0.5, 0.0).astype(BF16)


def lane_low(shape):
    return lax.broadcasted_iota(jnp.int32, shape, 1) < 64


def attention_kernel(
    n_seq, length, scal, x_ref, a_ref, s_ref, bo_ref, kv_ref, q_ref, p_ref, ctx_ref, hid_ref, pb_ref, bias
):
    half = length // 2
    step = pl.program_id(0)

    @pl.when(step == 0)
    def _():
        pool = pool_matrix(half, length)
        for b in range(n_seq):
            pooled = dot_nn(pool, x_ref[b * length : (b + 1) * length, :])
            hid_ref[b * half : (b + 1) * half, :] = pooled + bo_ref[...]
            pb_ref[b * half : (b + 1) * half, :] = pooled.astype(BF16)

    small = s_ref[0]
    for b in range(n_seq):
        rows = slice(b * length, (b + 1) * length)
        kv_ref[0, rows, :] = (dot_nn(x_ref[rows, :], a_ref[0, :, 0:384]) + small[3:4, 0:384]).astype(BF16)
        rows = slice(b * half, (b + 1) * half)
        q = dot_nn(pb_ref[rows, :], a_ref[0, :, 384:640]) * 0.125
        lanes = lax.broadcasted_iota(jnp.int32, q.shape, 1)
        q_ref[0, rows, :] = jnp.where(lanes < 192, q, 0.0).astype(BF16)
    for h in range(3):
        wide = jnp.broadcast_to(small[h : h + 1, :], (half, 2 * length))
        rolled = pltpu.roll(wide, length, 1, stride=2, stride_axis=0)
        bias[h] = rolled[:, :length].T
    low = lane_low((half, 128))
    keys = lax.broadcasted_iota(jnp.int32, (length, half), 0)

    def one_seq(b, carry):
        krows = pl.ds(pl.multiple_of(b * length, length), length)
        qrows = pl.ds(pl.multiple_of(b * half, half), half)
        valid = keys < scal[2 + b]
        q01 = q_ref[0, qrows, 0:128]
        zero = jnp.zeros_like(q01)
        heads = (
            (jnp.where(low, q01, zero), 0, 128),
            (jnp.where(low, zero, q01), 0, 128),
            (q_ref[0, qrows, 128:256], 256, 256),
        )
        contexts = []
        for h, (q, k_at, v_at) in enumerate(heads):
            s = dot_nt(kv_ref[0, krows, k_at : k_at + 128], q) + bias[h]
            s = jnp.where(valid, s, -1e30)
            e = jnp.exp(s - jnp.max(s, axis=0, keepdims=True))
            p = (e * (1.0 / jnp.sum(e, axis=0, keepdims=True))).astype(BF16)
            p_ref[0, b, h] = p
            contexts.append(dot_tn(kv_ref[0, krows, v_at : v_at + 128], p))
        c0, c1, c2 = contexts
        ctx01 = jnp.concatenate([c0[0:64], c1[64:128]], axis=0).T
        ctx2 = jnp.concatenate([jnp.zeros_like(c2[0:64]), c2[64:128]], axis=0).T
        ctx = jnp.concatenate([ctx2, ctx01], axis=1).astype(BF16)
        ctx_ref[0, qrows, :] = ctx
        hid_ref[qrows, :] += dot_nt(ctx, a_ref[0, :, 512:768])
        return carry

    lax.fori_loop(0, n_seq, one_seq, 0)


def attention_forward(scal, tokens, a4, s4, b_out, n_seq, length):
    half = length // 2
    width = tokens.shape[1]
    return pl.pallas_call(
        functools.partial(attention_kernel, n_seq, length),
        out_shape=(
            jax.ShapeDtypeStruct((4, n_seq * length, 384), BF16),
            jax.ShapeDtypeStruct((4, n_seq * half, 256), BF16),
            jax.ShapeDtypeStruct((4, n_seq, 3, length, half), BF16),
            jax.ShapeDtypeStruct((4, n_seq * half, 256), BF16),
            jax.ShapeDtypeStruct((n_seq * half, width), F32),
            jax.ShapeDtypeStruct((n_seq * half, width), BF16),
        ),
        grid_spec=pltpu.PrefetchScalarGridSpec(
            num_scalar_prefetch=1,
            grid=(4,),
            in_specs=[
                pl.BlockSpec((n_seq * length, width), lambda g, s: (s[0], 0)),
                pl.BlockSpec((1, width, 768), lambda g, s: (g, 0, 0)),
                pl.BlockSpec((1, 8, 1024), lambda g, s: (g, 0, 0)),
                pl.BlockSpec((1, width), lambda g, s: (0, 0)),
            ],
            out_specs=[
                pl.BlockSpec((1, n_seq * length, 384), lambda g, s: (g, 0, 0)),
                pl.BlockSpec((1, n_seq * half, 256), lambda g, s: (g, 0, 0)),
                pl.BlockSpec((1, n_seq, 3, length, half), lambda g, s: (g, 0, 0, 0, 0)),
                pl.BlockSpec((1, n_seq * half, 256), lambda g, s: (g, 0, 0)),
                pl.BlockSpec((n_seq * half, width), lambda g, s: (0, 0)),
                pl.BlockSpec((n_seq * half, width), lambda g, s: (0, 0)),
            ],
            scratch_shapes=[pltpu.VMEM((3, length, half), F32)],
        ),
        compiler_params=pltpu.CompilerParams(vmem_limit_bytes=VMEM_LIMIT),
        cost_estimate=pl.CostEstimate(flops=20 * 10**9, bytes_accessed=40 * 10**6, transcendentals=6 * 10**6),
    )(scal, tokens, a4, s4, b_out)


def row_mean(v):
    return jnp.mean(v, axis=-1, keepdims=True)


def ffn_kernel(
    n_seq, half, scal, hid_ref, cot_ref, u_ref, d_ref, s_ref, vec_ref,
    out_ref, ag_ref, gu_ref, gd_ref, gv_ref, nb_all, fg_all, act_all, pg_all, dg,
):
    b = pl.program_id(0)
    rows = pl.ds(pl.multiple_of(b * half, half), half)
    n_gain, n_shift, b_down, f_gain, f_shift = (vec_ref[i : i + 1, :] for i in range(5))

    @pl.when(b == 0)
    def _():
        gv_ref[...] = jnp.zeros_like(gv_ref)

    def add(i, v):
        gv_ref[i : i + 1, :] += jnp.sum(v, axis=0, keepdims=True)

    hid = hid_ref[...]
    centred = hid - row_mean(hid)
    inv1 = lax.rsqrt(row_mean(centred * centred) + EPS)
    unit1 = centred * inv1
    normed = unit1 * n_gain + n_shift
    nb = normed.astype(BF16)
    nb_all[rows, :] = nb
    summed = normed + b_down
    for t in range(4):
        pre = dot_nn(nb, u_ref[t]) + s_ref[t, 4:5, 0:768]
        cdf = 0.5 * (1.0 + lax.erf(pre * 0.7071067811865476))
        act = (pre * cdf).astype(BF16)
        dg[t] = cdf + pre * (0.3989422804014327 * jnp.exp(-0.5 * pre * pre))
        act_all[t, rows, :] = act
        summed = summed + dot_nt(act, d_ref[t])
    centred = summed - row_mean(summed)
    inv2 = lax.rsqrt(row_mean(centred * centred) + EPS)
    unit2 = centred * inv2
    valid = (2 * lax.broadcasted_iota(jnp.int32, (half, 1), 0) < scal[2 + b]).astype(F32)
    out_ref[...] = ((unit2 * f_gain + f_shift) * valid).astype(BF16)
    grad = cot_ref[...].astype(F32) * valid
    add(0, grad * unit2)
    add(1, grad)
    scaled = grad * f_gain
    grad_summed = inv2 * (scaled - row_mean(scaled) - unit2 * row_mean(scaled * unit2))
    add(2, grad_summed)
    fg = grad_summed.astype(BF16)
    fg_all[rows, :] = fg
    normed_grad = grad_summed
    for t in range(4):
        pg = (dot_nn(fg, d_ref[t]) * dg[t]).astype(BF16)
        pg_all[t, rows, :] = pg
        normed_grad = normed_grad + dot_nt(pg, u_ref[t])
    add(3, normed_grad * unit1)
    add(4, normed_grad)
    scaled = normed_grad * n_gain
    hidden_grad = inv1 * (scaled - row_mean(scaled) - unit1 * row_mean(scaled * unit1))
    add(5, hidden_grad)
    ag_ref[...] = hidden_grad.astype(BF16)

    @pl.when(b == n_seq - 1)
    def _():
        for i in range(2):
            t = 2 * scal[1] + i
            pg = pg_all[t]
            gu_ref[i] = dot_tn(nb_all[...], pg).astype(BF16)
            gd_ref[i] = dot_tn(fg_all[...], act_all[t]).astype(BF16)
            gv_ref[6 + i : 7 + i, :] = jnp.sum(pg.astype(F32), axis=0, keepdims=True)


def ffn(scal, hid, cotangent, u4, d4, s4, vectors, n_seq, half):
    width = hid.shape[1]
    once = pl.Buffered(1)
    return pl.pallas_call(
        functools.partial(ffn_kernel, n_seq, half),
        out_shape=(
            jax.ShapeDtypeStruct((n_seq * half, width), BF16),
            jax.ShapeDtypeStruct((n_seq * half, width), BF16),
            jax.ShapeDtypeStruct((2, width, 768), BF16),
            jax.ShapeDtypeStruct((2, width, 768), BF16),
            jax.ShapeDtypeStruct((8, width), F32),
        ),
        grid_spec=pltpu.PrefetchScalarGridSpec(
            num_scalar_prefetch=1,
            grid=(n_seq,),
            in_specs=[
                pl.BlockSpec((half, width), lambda b, s: (b, 0)),
                pl.BlockSpec((half, width), lambda b, s: (s[0] * n_seq + b, 0)),
                pl.BlockSpec((4, width, 768), lambda b, s: (0, 0, 0), pipeline_mode=once),
                pl.BlockSpec((4, width, 768), lambda b, s: (0, 0, 0), pipeline_mode=once),
                pl.BlockSpec((4, 8, 1024), lambda b, s: (0, 0, 0)),
                pl.BlockSpec((8, width), lambda b, s: (0, 0)),
            ],
            out_specs=[
                pl.BlockSpec((half, width), lambda b, s: (b, 0)),
                pl.BlockSpec((half, width), lambda b, s: (b, 0)),
                pl.BlockSpec((2, width, 768), lambda b, s: (0, 0, 0)),
                pl.BlockSpec((2, width, 768), lambda b, s: (0, 0, 0)),
                pl.BlockSpec((8, width), lambda b, s: (0, 0)),
            ],
            scratch_shapes=[
                pltpu.VMEM((n_seq * half, width), BF16),
                pltpu.VMEM((n_seq * half, width), BF16),
                pltpu.VMEM((4, n_seq * half, 768), BF16),
                pltpu.VMEM((4, n_seq * half, 768), BF16),
                pltpu.VMEM((4, half, 768), F32),
            ],
        ),
        compiler_params=pltpu.CompilerParams(vmem_limit_bytes=VMEM_LIMIT),
        cost_estimate=pl.CostEstimate(flops=24 * 10**9, bytes_accessed=30 * 10**6, transcendentals=6 * 10**6),
    )(scal, hid, cotangent, u4, d4, s4, vectors)


def backward_kernel(n_seq, length, own, scal, *refs):
    half = length // 2
    x_ref, a_ref, kv_ref, q_ref, p_ref, ctx_ref, ag_ref, pb_ref = refs[:8]
    refs = refs[8:]
    if own:
        tok_ref, pool_ref, ga_ref, tg_ref, vb_ref, kvd, qd_all, tacc = refs
    else:
        tok_in, pool_in, out_ref, tok_ref, pool_ref, kvd, qd_all = refs
    step = pl.program_id(0)

    @pl.when(step == 0)
    def _():
        if own:
            tok_ref[...] = jnp.zeros_like(tok_ref)
            pool_ref[...] = jnp.zeros_like(pool_ref)
        else:
            tok_ref[...] = tok_in[...]
            pool_ref[...] = pool_in[...]

    if own:
        tacc[...] = jnp.zeros_like(tacc)
    low = lane_low((half, 128))

    def one_seq(b, carry):
        krows = pl.ds(pl.multiple_of(b * length, length), length)
        qrows = pl.ds(pl.multiple_of(b * half, half), half)
        cg = dot_nn(ag_ref[qrows, :], a_ref[0, :, 512:768]).astype(BF16)
        q01 = q_ref[0, qrows, 0:128]
        q2 = q_ref[0, qrows, 128:256]
        cg2, cg01 = cg[:, 0:128], cg[:, 128:256]
        zero = jnp.zeros_like(q01)
        cg2 = jnp.where(low, zero, cg2)
        heads = (
            (jnp.where(low, q01, zero), jnp.where(low, cg01, zero), 0, 128),
            (jnp.where(low, zero, q01), jnp.where(low, zero, cg01), 0, 128),
            (q2, cg2, 256, 256),
        )
        kds, vds, qds = [], [], []
        for h, (q, g, k_at, v_at) in enumerate(heads):
            pb16 = p_ref[0, b, h]
            p = pb16.astype(F32)
            dp = dot_nt(kv_ref[0, krows, v_at : v_at + 128], g)
            row = jnp.sum(p * dp, axis=0, keepdims=True)
            sg = (p * (dp - row)).astype(BF16)
            if own:
                tacc[h] += sg.astype(F32)
            kds.append(dot_nn(sg, q))
            vds.append(dot_nn(pb16, g))
            qds.append(dot_tn(kv_ref[0, krows, k_at : k_at + 128], sg))
        kvd[krows, 0:128] = (kds[0] + kds[1]).astype(BF16)
        kvd[krows, 128:256] = (vds[0] + vds[1]).astype(BF16)
        kvd[krows, 256:384] = (kds[2] + vds[2]).astype(BF16)
        qd01 = jnp.concatenate([qds[0][0:64], qds[1][64:128]], axis=0).T
        qd2 = jnp.concatenate([qds[2][0:64], jnp.zeros_like(qds[2][0:64])], axis=0).T
        qd = jnp.concatenate([qd01, qd2], axis=1).astype(BF16)
        qd_all[qrows, :] = qd
        tok_ref[krows, :] += dot_nt(kvd[krows, :], a_ref[0, :, 0:384])
        pool_ref[qrows, :] += dot_nt(qd, a_ref[0, :, 384:640]) * 0.125
        return carry

    lax.fori_loop(0, n_seq, one_seq, 0)
    if own:
        ga_ref[0, :, 0:384] = dot_tn(x_ref[...], kvd[...]).astype(BF16)
        gq = dot_tn(pb_ref[...], qd_all[...]) * 0.125
        go = dot_tn(ag_ref[...], ctx_ref[0])
        ga_ref[0, :, 384:512] = gq[:, 0:128].astype(BF16)
        ga_ref[0, :, 512:640] = (gq[:, 128:256] + go[:, 0:128]).astype(BF16)
        ga_ref[0, :, 640:768] = go[:, 128:256].astype(BF16)
        vb_ref[0] = jnp.broadcast_to(jnp.sum(kvd[...].astype(F32), axis=0, keepdims=True), (8, 384))
        i = lax.broadcasted_iota(jnp.int32, (half, half), 0)
        flip = jnp.where(i + lax.broadcasted_iota(jnp.int32, (half, half), 1) == half - 1, 1.0, 0.0).astype(BF16)
        for h in range(3):
            high = tacc[h].astype(BF16)
            rest = (tacc[h] - high.astype(F32)).astype(BF16)
            turned = dot_nt(flip, high) + dot_nt(flip, rest)
            wide = jnp.concatenate([turned, jnp.zeros((half, length), F32)], axis=1)
            rolled = pltpu.roll(wide, 2, 1, stride=2, stride_axis=0)
            tg_ref[0, h : h + 1, :] = jnp.sum(rolled, axis=0, keepdims=True)
        tg_ref[0, 3:8, :] = jnp.zeros((5, 2 * length), F32)
    else:

        @pl.when(step == 1)
        def _():
            pool = pool_matrix(half, length)
            for b in range(n_seq):
                rows = slice(b * half, (b + 1) * half)
                total = (pool_ref[rows, :] + ag_ref[rows, :].astype(F32)).astype(BF16)
                rows = slice(b * length, (b + 1) * length)
                out_ref[rows, :] = (tok_ref[rows, :] + dot_tn(pool, total)).astype(BF16)


def attention_backward(own, scal, tokens, a4, kv, q, p, ctx, ag, pb, partial, n_seq, length):
    half = length // 2
    width = tokens.shape[1]
    once = pl.Buffered(1)
    n_tok, n_pool = n_seq * length, n_seq * half

    def group(g, s):
        return 2 * (s[1] if own else 1 - s[1]) + g

    def fixed(shape):
        return pl.BlockSpec(shape, lambda g, s: (0,) * len(shape), pipeline_mode=once)

    in_specs = [
        pl.BlockSpec((n_tok, width), lambda g, s: (s[0], 0), pipeline_mode=once),
        pl.BlockSpec((1, width, 768), lambda g, s: (group(g, s), 0, 0)),
        pl.BlockSpec((1, n_tok, 384), lambda g, s: (group(g, s), 0, 0)),
        pl.BlockSpec((1, n_pool, 256), lambda g, s: (group(g, s), 0, 0)),
        pl.BlockSpec((1, n_seq, 3, length, half), lambda g, s: (group(g, s), 0, 0, 0, 0)),
        pl.BlockSpec((1, n_pool, 256), lambda g, s: (group(g, s), 0, 0)),
        fixed((n_pool, width)),
        fixed((n_pool, width)),
    ]
    scratch = [pltpu.VMEM((n_tok, 384), BF16), pltpu.VMEM((n_pool, 256), BF16)]
    if own:
        out_shape = (
            jax.ShapeDtypeStruct((n_tok, width), F32),
            jax.ShapeDtypeStruct((n_pool, width), F32),
            jax.ShapeDtypeStruct((2, width, 768), BF16),
            jax.ShapeDtypeStruct((2, 8, 2 * length), F32),
            jax.ShapeDtypeStruct((2, 8, 384), F32),
        )
        out_specs = [
            fixed((n_tok, width)),
            fixed((n_pool, width)),
            pl.BlockSpec((1, width, 768), lambda g, s: (g, 0, 0)),
            pl.BlockSpec((1, 8, 2 * length), lambda g, s: (g, 0, 0)),
            pl.BlockSpec((1, 8, 384), lambda g, s: (g, 0, 0)),
        ]
        scratch.append(pltpu.VMEM((3, length, half), F32))
    else:
        in_specs += [fixed((n_tok, width)), fixed((n_pool, width))]
        out_shape = jax.ShapeDtypeStruct((n_tok, width), BF16)
        out_specs = fixed((n_tok, width))
        scratch = [pltpu.VMEM((n_tok, width), F32), pltpu.VMEM((n_pool, width), F32)] + scratch
    return pl.pallas_call(
        functools.partial(backward_kernel, n_seq, length, own),
        out_shape=out_shape,
        grid_spec=pltpu.PrefetchScalarGridSpec(
            num_scalar_prefetch=1, grid=(2,), in_specs=in_specs, out_specs=out_specs, scratch_shapes=scratch
        ),
        compiler_params=pltpu.CompilerParams(vmem_limit_bytes=VMEM_LIMIT),
        cost_estimate=pl.CostEstimate(flops=20 * 10**9, bytes_accessed=30 * 10**6, transcendentals=0),
    )(scal, tokens, a4, kv, q, p, ctx, ag, pb, *partial)


def swap(v, axis, bit, size):
    return lax.ppermute(v, axis, [(i, i ^ bit) for i in range(size)])


def reduce_groups(grads, n_dp):
    dp, t = lax.axis_index("dp"), lax.axis_index("tensor")
    core, hi, lo = t % 2, dp // 2, dp % 2
    n_hi = n_dp // 2
    mine = lax.dynamic_index_in_dim(grads, core, 0, keepdims=False)
    other = lax.dynamic_index_in_dim(grads, 1 - core, 0, keepdims=False)
    got = swap(other, "tensor", 1, 4)
    k, d, width = mine.shape
    total = (mine.astype(F32) + got.astype(F32)).astype(BF16).reshape(k, n_hi, 2, d // n_dp, width)
    keep = lax.dynamic_index_in_dim(total, lo, 2, keepdims=False)
    give = lax.dynamic_index_in_dim(total, 1 - lo, 2, keepdims=False)
    got = swap(give, "dp", 1, n_dp)
    total = (keep.astype(F32) + got.astype(F32)).astype(BF16)
    final = lax.dynamic_index_in_dim(total, hi, 1, keepdims=False).astype(F32)
    for s in range(1, n_hi):
        give = lax.dynamic_index_in_dim(total, (hi + s) % n_hi, 1, keepdims=False)
        got = lax.ppermute(give, "dp", [(i, (i + 2 * s) % n_dp) for i in range(n_dp)])
        final = final + got.astype(F32)
    return final


def reduce_small(v, n_dp):
    v = v + swap(v, "tensor", 1, 4)
    return lax.psum(v, "dp")


def shards(
    n_dp, tokens, lengths, cotangent, query_weight, key_weight, value_weight, value_bias, output_weight,
    b_out, rel_table, norm_gain, norm_shift, up_weight, hidden_bias, down_weight, b_down, final_gain, final_shift,
):
    seq_count = lengths.shape[0]
    length = tokens.shape[0] // seq_count
    half = length // 2
    n_seq = seq_count // 2
    t = lax.axis_index("tensor")
    core, y = t % 2, t // 2

    out_t = output_weight.T
    packed = jnp.concatenate(
        [
            key_weight[:, :128], value_weight[:, :128], key_weight[:, 128:], value_weight[:, 128:],
            query_weight, out_t[:, 128:], out_t[:, :128],
        ],
        axis=1,
    ).astype(BF16)
    zero = jnp.zeros((128,), F32)
    small = jnp.concatenate(
        [
            rel_table,
            jnp.concatenate([zero, value_bias[:128], zero[:64], value_bias[128:], jnp.zeros((640,), F32)])[None],
            jnp.pad(hidden_bias, (0, 256))[None],
            jnp.zeros((3, 1024), F32),
        ],
        axis=0,
    )
    a4, u4, d4, s4 = gather_weights(packed, up_weight.astype(BF16), down_weight.T.astype(BF16), small, n_dp)
    scal = jnp.concatenate([jnp.stack([core, y]), lax.dynamic_slice_in_dim(lengths, core * n_seq, n_seq)]).astype(jnp.int32)

    kv, q, p, ctx, hid, pb = attention_forward(scal, tokens, a4, s4, b_out[None], n_seq, length)
    zeros = jnp.zeros_like(norm_gain)
    vectors = jnp.stack([norm_gain, norm_shift, b_down, final_gain, final_shift, zeros, zeros, zeros])
    out_half, ag, gu, gd, gv = ffn(scal, hid, cotangent, u4, d4, s4, vectors, n_seq, half)
    tok, pool, ga, tg, vb = attention_backward(True, scal, tokens, a4, kv, q, p, ctx, ag, pb, (), n_seq, length)
    tok_half = attention_backward(False, scal, tokens, a4, kv, q, p, ctx, ag, pb, (tok, pool), n_seq, length)

    ffn_sum = reduce_groups(jnp.stack([gu, gd], axis=1), n_dp)
    a_sum = reduce_groups(ga[:, None], n_dp)[0]
    up_sum, down_sum = ffn_sum[0], ffn_sum[1].T
    key_sum = jnp.concatenate([a_sum[:, 0:128], a_sum[:, 256:320]], axis=1)
    value_sum = jnp.concatenate([a_sum[:, 128:256], a_sum[:, 320:384]], axis=1)
    query_sum = a_sum[:, 384:576]
    outw_sum = jnp.concatenate([a_sum[:, 640:768], a_sum[:, 576:640]], axis=1).T

    flat = jnp.concatenate([gv.reshape(-1), tg[:, :3].reshape(-1), vb[:, 0].reshape(-1)])
    flat = reduce_small(flat, n_dp)
    cut = gv.size
    gv = flat[:cut].reshape(gv.shape)
    tg_sum = lax.dynamic_index_in_dim(flat[cut : cut + 6 * 2 * length].reshape(2, 3, 2 * length), core, 0, keepdims=False)
    vb_sum = lax.dynamic_index_in_dim(flat[cut + 6 * 2 * length :].reshape(2, 384), core, 0, keepdims=False)
    vb_sum = jnp.concatenate([vb_sum[128:256], vb_sum[320:384]])
    ub_sum = lax.dynamic_index_in_dim(gv[6:8], core, 0, keepdims=False)

    def join(part):
        got = swap(part, "tensor", 1, 4)
        return jnp.where(core == 0, jnp.concatenate([part, got]), jnp.concatenate([got, part]))

    return (
        join(out_half), join(tok_half), query_sum, key_sum, value_sum, vb_sum, outw_sum, gv[5], tg_sum,
        gv[3], gv[4], up_sum, ub_sum, down_sum, gv[2], gv[0], gv[1],
    )


def solution(mesh):
    row, col, both, rep = P("dp", None), P("tensor", "dp"), P("dp", "tensor"), P()
    ten, table = P("tensor"), P("tensor", None)
    in_specs = (
        row, P("dp"), row, both, both, both, ten, col, rep, table, rep, rep, both, ten, col, rep, rep, rep,
    )
    out_specs = (
        row, row, both, both, both, ten, col, rep, table, rep, rep, both, ten, col, rep, rep, rep,
    )
    body = functools.partial(shards, mesh.shape["dp"])
    return jax.shard_map(body, mesh=mesh, in_specs=in_specs, out_specs=out_specs, check_vma=False)
```

```python
import functools

import jax
import jax.numpy as jnp
from jax import lax
from jax.experimental import pallas as pl
from jax.experimental.pallas import tpu as pltpu
from jax.sharding import PartitionSpec as P

MESH = pl.DeviceIdType.MESH
F32 = jnp.float32
BF16 = jnp.bfloat16
EPS = 1e-06
VMEM_LIMIT = 58 * 2**20


def dot_nn(a, b):
    return lax.dot_general(a, b, (((1,), (0,)), ((), ())), preferred_element_type=F32)


def dot_nt(a, b):
    return lax.dot_general(a, b, (((1,), (1,)), ((), ())), preferred_element_type=F32)


def dot_tn(a, b):
    return lax.dot_general(a, b, (((0,), (0,)), ((), ())), preferred_element_type=F32)


class Gather:
    def __init__(self, n_hi, ins, outs, s_in, s_out, sems):
        self.n_hi, self.ins, self.outs, self.s_in, self.s_out = n_hi, ins, outs, s_in, s_out
        self.loc, self.zs, self.zr, self.ls, self.lr, self.fs, self.fr, self.cs, self.cr, self.ss, self.sr = sems
        self.dp, self.t = lax.axis_index("dp"), lax.axis_index("tensor")
        self.hi, self.lo = self.dp // 2, lax.rem(self.dp, 2)
        self.core = lax.rem(self.t, 2)
        t_core = self.t + 1 - 2 * self.core
        self.to_x = (self.dp + 1 - 2 * self.lo, self.t)
        self.to_y = (self.dp, lax.rem(self.t + 2, 4))
        self.to_c = (self.dp, t_core)
        self.to_d = (self.dp, lax.rem(t_core + 2, 4))

    def z_peer(self, s):
        return (lax.rem(self.hi + s, self.n_hi) * 2 + self.lo, self.t)

    def block(self, s, side):
        return lax.rem(self.hi - s + self.n_hi, self.n_hi) * 2 + side

    def greet(self):
        barrier = pltpu.get_barrier_semaphore()

        def body(s, carry):
            pl.semaphore_signal(barrier, inc=1, device_id=self.z_peer(s), device_id_type=MESH)
            return carry

        lax.fori_loop(1, self.n_hi, body, 0)
        for peer in (self.to_x, self.to_y, self.to_c, self.to_d):
            pl.semaphore_signal(barrier, inc=1, device_id=peer, device_id_type=MESH)
        pl.semaphore_wait(barrier, self.n_hi + 3)

    def remote(self, src, dst, send, recv, peer):
        return pltpu.make_async_remote_copy(src, dst, send, recv, device_id=peer, device_id_type=MESH)

    def small(self):
        core = self.core
        return (
            pltpu.make_async_copy(self.s_in, self.s_out.at[core], self.loc.at[3]),
            self.remote(self.s_in, self.s_out.at[core], self.ss.at[0], self.sr.at[0], self.to_c),
            self.remote(self.s_in, self.s_out.at[2 + core], self.ss.at[1], self.sr.at[1], self.to_y),
            self.remote(self.s_in, self.s_out.at[2 + core], self.ss.at[2], self.sr.at[2], self.to_d),
        )

    def local(self, k):
        return pltpu.make_async_copy(self.ins[k], self.outs[k].at[self.core, self.dp], self.loc.at[k])

    def z_copy(self, k, s):
        return self.remote(
            self.ins[k], self.outs[k].at[self.core, self.dp], self.zs.at[k, s], self.zr.at[k, s], self.z_peer(s)
        )

    def line(self, k, s, way, own=False):
        out, b = self.outs[k], self.block(s, self.lo)
        src = self.ins[k] if own else out.at[self.core, b]
        dst = out.at[self.core if way == 0 else 2 + self.core, b]
        return self.remote(
            src, dst, self.ls.at[way, k, s], self.lr.at[way, k, s], self.to_x if way == 0 else self.to_y
        )

    def onward(self, k, s, way):
        out = self.outs[k]
        if way == 0:
            src = dst = out.at[2 + self.core, self.block(s, self.lo)]
        else:
            b = self.block(s, 1 - self.lo)
            src, dst = out.at[self.core, b], out.at[2 + self.core, b]
        return self.remote(src, dst, self.fs.at[k, s], self.fr.at[k, s], self.to_x if way == 0 else self.to_y)

    def to_core(self, k, s, which, own=False):
        out = self.outs[k]
        side = self.lo if which % 2 == 0 else 1 - self.lo
        where = out.at[self.core if which < 2 else 2 + self.core, self.block(s, side)]
        return self.remote(
            self.ins[k] if own else where, where, self.cs.at[which, k, s], self.cr.at[which, k, s], self.to_c
        )

    def each(self, first, body):
        def step(s, carry):
            body(s)
            return carry

        lax.fori_loop(first, self.n_hi, step, 0)

    def start(self, k):
        self.local(k).start()
        self.each(1, lambda s: self.z_copy(k, s).start())
        self.line(k, 0, 0, True).start()
        self.line(k, 0, 1, True).start()
        self.to_core(k, 0, 0, True).start()

    def spread(self, k):
        def body(s):
            self.z_copy(k, s).wait_recv()
            self.line(k, s, 0).start()
            self.line(k, s, 1).start()
            self.to_core(k, s, 0).start()

        self.each(1, body)

    def pass_on(self, k, order):
        def over_x(s):
            self.line(k, s, 0).wait_recv()
            self.onward(k, s, 1).start()
            self.to_core(k, s, 1).start()

        def over_y(s):
            self.line(k, s, 1).wait_recv()
            self.onward(k, s, 0).start()
            self.to_core(k, s, 2).start()

        if order == 0:
            self.each(0, over_x)
        elif order == 1:
            self.each(0, over_y)
        else:
            pl.when(self.core == 0)(lambda: self.each(0, over_x))
            pl.when(self.core == 1)(lambda: self.each(0, over_y))

    def complete(self, k, order):
        def late_y(s):
            self.line(k, s, 1).wait_recv()
            self.to_core(k, s, 2).start()

        def late_x(s):
            self.line(k, s, 0).wait_recv()
            self.to_core(k, s, 1).start()

        def diagonal(s):
            self.onward(k, s, 0).wait_recv()
            self.to_core(k, s, 3).start()

        if order == 0:
            self.each(0, late_y)
        elif order == 1:
            self.each(0, late_x)
        else:
            pl.when(self.core == 0)(lambda: self.each(0, late_y))
            pl.when(self.core == 1)(lambda: self.each(0, late_x))
        self.each(0, diagonal)

    def arrived(self, k, whiches):
        def body(s):
            for which in whiches:
                self.to_core(k, s, which).wait_recv()

        self.each(0, body)

    def sent(self, k):
        self.each(1, lambda s: self.z_copy(k, s).wait_send())

        def body(s):
            self.line(k, s, 0).wait_send()
            self.line(k, s, 1).wait_send()
            self.onward(k, s, 0).wait_send()
            for which in range(4):
                self.to_core(k, s, which).wait_send()

        self.each(0, body)


def gather_scratch(n_hi):
    dma = pltpu.SemaphoreType.DMA
    return [
        dma((4,)), dma((3, n_hi)), dma((3, n_hi)), dma((2, 3, n_hi)), dma((2, 3, n_hi)), dma((3, n_hi)),
        dma((3, n_hi)), dma((4, 3, n_hi)), dma((4, 3, n_hi)), dma((3,)), dma((3,)),
    ]


def pool_matrix(pooled, length):
    i = lax.broadcasted_iota(jnp.int32, (pooled, length), 0)
    j = lax.broadcasted_iota(jnp.int32, (pooled, length), 1)
    return jnp.where(j // 2 == i, 0.5, 0.0).astype(BF16)


def lane_low(shape):
    return lax.broadcasted_iota(jnp.int32, shape, 1) < 64


ORDERS = (0, 1, 2)


def attention_kernel(n_seq, length, n_dp, comm, *refs):
    half = length // 2
    group, b = pl.program_id(0), pl.program_id(1)
    step = group * n_seq + b
    core = lax.rem(lax.axis_index("tensor"), 2)
    len_ref, x_ref, bo_ref = refs[:3]
    refs = refs[3:]
    if comm:
        (kw, vw, qw, ow, uw, dw, tab, vbias, hbias) = refs[:9]
        kv_ref, q_ref, p_ref, ctx_ref, hid_ref, pb_ref, a_out, u_out, d_out, s_out = refs[9:19]
        bias, a_in, u_in, d_in, s_in, a_all, s_all, a_sem, s_sem = refs[19:28]
        net = Gather(n_dp // 2, (a_in, u_in, d_in), (a_all, u_out, d_out), s_in, s_all, refs[28:])

        def a_copy(g):
            return pltpu.make_async_copy(a_all.at[g], a_out.at[g], a_sem.at[g])

        s_copy = pltpu.make_async_copy(s_all, s_out, s_sem)

        @pl.when(step == 0)
        def _():
            k, v, o = kw[...], vw[...], ow[...].T
            parts = (k[:, :128], v[:, :128], k[:, 128:], v[:, 128:], qw[...], o[:, 128:], o[:, :128])
            a_in[...] = jnp.concatenate(parts, axis=1).astype(BF16)
            s_in[...] = jnp.zeros_like(s_in)
            s_in[0:3, :] = tab[...]
            s_in[3:4, 128:256] = vbias[:, 0:128]
            s_in[3:4, 320:384] = vbias[:, 128:192]
            s_in[4:5, 0 : hbias.shape[1]] = hbias[...]
            net.greet()
            for copy in net.small():
                copy.start()
            net.start(0)
            u_in[...] = uw[...].astype(BF16)
            d_in[...] = dw[...].T.astype(BF16)
            net.spread(0)
            net.start(1)
            net.pass_on(0, ORDERS[0])
            small = net.small()
            small[0].wait()
            for copy in small[1:]:
                copy.wait()
            s_copy.start()
            net.local(0).wait()
            net.arrived(0, (0, 1))

        def at(n, action):
            pl.when(step == n)(action)

        @pl.when(step == 2)
        def _():
            net.spread(1)
            net.start(2)

        pl.when(step == 5)(lambda: net.complete(0, ORDERS[0]))
        pl.when(step == 7)(lambda: net.spread(2))

        @pl.when(step == 8)
        def _():
            net.arrived(0, (2, 3))
            for g in range(4):
                a_copy(g).start()

        pl.when(step == 9)(lambda: net.pass_on(1, ORDERS[1]))
        pl.when(step == 11)(lambda: net.complete(1, ORDERS[1]))
        pl.when(step == 13)(lambda: net.pass_on(2, ORDERS[2]))

        def weights(lanes):
            return a_all[group, :, :, lanes].reshape(-1, lanes.stop - lanes.start)

        def small_row(i):
            return s_all[group, i : i + 1, :]
    else:
        a_ref, s_ref = refs[:2]
        kv_ref, q_ref, p_ref, ctx_ref, hid_ref, pb_ref, bias = refs[2:]

        def weights(lanes):
            return a_ref[0, :, lanes]

        def small_row(i):
            return s_ref[0, i : i + 1, :]

    krows = pl.ds(pl.multiple_of(b * length, length), length)
    qrows = pl.ds(pl.multiple_of(b * half, half), half)

    @pl.when(group == 0)
    def _():
        pooled = dot_nn(pool_matrix(half, length), x_ref[krows, :])
        hid_ref[qrows, :] = pooled + bo_ref[...]
        pb_ref[qrows, :] = pooled.astype(BF16)

    @pl.when(b == 0)
    def _():
        for h in range(3):
            wide = jnp.broadcast_to(small_row(h), (half, 2 * length))
            bias[h] = pltpu.roll(wide, length, 1, stride=2, stride_axis=0)[:, :length].T

    kv_ref[0] = (dot_nn(x_ref[krows, :], weights(slice(0, 384))) + small_row(3)[:, 0:384]).astype(BF16)
    q = dot_nn(pb_ref[qrows, :], weights(slice(384, 640))) * 0.125
    lanes = lax.broadcasted_iota(jnp.int32, q.shape, 1)
    q = jnp.where(lanes < 192, q, 0.0).astype(BF16)
    q_ref[0] = q
    low = lane_low((half, 128))
    valid = lax.broadcasted_iota(jnp.int32, (length, half), 0) < len_ref[core * n_seq + b]
    q01 = q[:, 0:128]
    zero = jnp.zeros_like(q01)
    heads = (
        (jnp.where(low, q01, zero), 0, 128),
        (jnp.where(low, zero, q01), 0, 128),
        (q[:, 128:256], 256, 256),
    )
    contexts = []
    for h, (qh, k_at, v_at) in enumerate(heads):
        s = dot_nt(kv_ref[0, :, k_at : k_at + 128], qh) + bias[h]
        s = jnp.where(valid, s, -1e30)
        e = jnp.exp(s - jnp.max(s, axis=0, keepdims=True))
        p = (e * (1.0 / jnp.sum(e, axis=0, keepdims=True))).astype(BF16)
        p_ref[0, 0, h] = p
        contexts.append(dot_tn(kv_ref[0, :, v_at : v_at + 128], p))
    c0, c1, c2 = contexts
    ctx01 = jnp.concatenate([c0[0:64], c1[64:128]], axis=0).T
    ctx2 = jnp.concatenate([jnp.zeros_like(c2[0:64]), c2[64:128]], axis=0).T
    ctx = jnp.concatenate([ctx2, ctx01], axis=1).astype(BF16)
    ctx_ref[0] = ctx
    hid_ref[qrows, :] += dot_nt(ctx, weights(slice(512, 768)))

    if comm:

        @pl.when(step == 4 * n_seq - 1)
        def _():
            net.complete(2, ORDERS[2])
            for k in range(3):
                net.sent(k)
            for k in (1, 2):
                net.local(k).wait()
                net.arrived(k, (0, 1, 2, 3))
            for g in range(4):
                a_copy(g).wait()
            s_copy.wait()


def my_core():
    return lax.rem(lax.axis_index("tensor"), 2)


def attention_forward(lengths, tokens, b_out, weights, n_dp, comm):
    n_seq = lengths.shape[0] // 2
    length = tokens.shape[0] // lengths.shape[0]
    half = length // 2
    width = tokens.shape[1]
    once = pl.Buffered(1)

    def fixed(shape):
        return pl.BlockSpec(shape, lambda g, b: (0,) * len(shape), pipeline_mode=once)

    in_specs = [
        pl.BlockSpec(memory_space=pltpu.SMEM),
        pl.BlockSpec((n_seq * length, width), lambda g, b: (my_core(), 0), pipeline_mode=once),
        fixed((1, width)),
    ]
    out_shape = [
        jax.ShapeDtypeStruct((4, n_seq * length, 384), BF16),
        jax.ShapeDtypeStruct((4, n_seq * half, 256), BF16),
        jax.ShapeDtypeStruct((4, n_seq, 3, length, half), BF16),
        jax.ShapeDtypeStruct((4, n_seq * half, 256), BF16),
        jax.ShapeDtypeStruct((n_seq * half, width), F32),
        jax.ShapeDtypeStruct((n_seq * half, width), BF16),
    ]
    out_specs = [
        pl.BlockSpec((1, length, 384), lambda g, b: (g, b, 0)),
        pl.BlockSpec((1, half, 256), lambda g, b: (g, b, 0)),
        pl.BlockSpec((1, 1, 3, length, half), lambda g, b: (g, b, 0, 0, 0)),
        pl.BlockSpec((1, half, 256), lambda g, b: (g, b, 0)),
        fixed((n_seq * half, width)),
        fixed((n_seq * half, width)),
    ]
    scratch = [pltpu.VMEM((3, length, half), F32)]
    params = {"vmem_limit_bytes": VMEM_LIMIT}
    if comm:
        rows = width // n_dp
        in_specs += [fixed(w.shape) for w in weights]
        whole = jax.ShapeDtypeStruct((4, n_dp, rows, width), BF16)
        small = jax.ShapeDtypeStruct((4, 8, 2 * length), F32)
        out_shape += [whole, whole, whole, small]
        out_specs += [pl.BlockSpec(memory_space=pl.ANY)] * 4
        scratch += [pltpu.VMEM((rows, width), BF16)] * 3
        scratch += [
            pltpu.VMEM((8, 2 * length), F32),
            pltpu.VMEM((4, n_dp, rows, width), BF16),
            pltpu.VMEM((4, 8, 2 * length), F32),
            pltpu.SemaphoreType.DMA((4,)),
            pltpu.SemaphoreType.DMA,
        ]
        scratch += gather_scratch(n_dp // 2)
        params.update(collective_id=0, has_side_effects=True)
    else:
        in_specs += [
            pl.BlockSpec((1, width, 768), lambda g, b: (g, 0, 0)),
            pl.BlockSpec((1, 8, 2 * length), lambda g, b: (g, 0, 0)),
        ]
    outs = pl.pallas_call(
        functools.partial(attention_kernel, n_seq, length, n_dp, comm),
        out_shape=out_shape,
        grid=(4, n_seq),
        in_specs=in_specs,
        out_specs=out_specs,
        scratch_shapes=scratch,
        compiler_params=pltpu.CompilerParams(**params),
        cost_estimate=pl.CostEstimate(flops=20 * 10**9, bytes_accessed=40 * 10**6, transcendentals=6 * 10**6),
    )(lengths, tokens, b_out, *weights)
    if comm:
        flat = (4, width, width)
        outs = list(outs)
        outs = outs[:6] + [w.reshape(flat) for w in outs[6:9]] + outs[9:]
    return outs


def row_mean(v):
    return jnp.mean(v, axis=-1, keepdims=True)


def ffn_kernel(
    n_seq, half, len_ref, hid_ref, cot_ref, u_ref, d_ref, s_ref, vec_ref,
    out_ref, ag_ref, gu_ref, gd_ref, gv_ref, nb_all, fg_all, act_all, pg_all, dg,
):
    b = pl.program_id(0)
    rows = pl.ds(pl.multiple_of(b * half, half), half)
    n_gain, n_shift, b_down, f_gain, f_shift = (vec_ref[i : i + 1, :] for i in range(5))

    @pl.when(b == 0)
    def _():
        gv_ref[...] = jnp.zeros_like(gv_ref)

    def add(i, v):
        gv_ref[i : i + 1, :] += jnp.sum(v, axis=0, keepdims=True)

    hid = hid_ref[...]
    centred = hid - row_mean(hid)
    inv1 = lax.rsqrt(row_mean(centred * centred) + EPS)
    unit1 = centred * inv1
    normed = unit1 * n_gain + n_shift
    nb = normed.astype(BF16)
    nb_all[rows, :] = nb
    summed = normed + b_down
    for t in range(4):
        pre = dot_nn(nb, u_ref[t]) + s_ref[t, 4:5, 0:768]
        cdf = 0.5 * (1.0 + lax.erf(pre * 0.7071067811865476))
        act = (pre * cdf).astype(BF16)
        dg[t] = cdf + pre * (0.3989422804014327 * jnp.exp(-0.5 * pre * pre))
        act_all[t, rows, :] = act
        summed = summed + dot_nt(act, d_ref[t])
    centred = summed - row_mean(summed)
    inv2 = lax.rsqrt(row_mean(centred * centred) + EPS)
    unit2 = centred * inv2
    valid = (2 * lax.broadcasted_iota(jnp.int32, (half, 1), 0) < len_ref[my_core() * n_seq + b]).astype(F32)
    out_ref[...] = ((unit2 * f_gain + f_shift) * valid).astype(BF16)
    grad = cot_ref[...].astype(F32) * valid
    add(0, grad * unit2)
    add(1, grad)
    scaled = grad * f_gain
    grad_summed = inv2 * (scaled - row_mean(scaled) - unit2 * row_mean(scaled * unit2))
    add(2, grad_summed)
    fg = grad_summed.astype(BF16)
    fg_all[rows, :] = fg
    normed_grad = grad_summed
    for t in range(4):
        pg = (dot_nn(fg, d_ref[t]) * dg[t]).astype(BF16)
        pg_all[t, rows, :] = pg
        normed_grad = normed_grad + dot_nt(pg, u_ref[t])
    add(3, normed_grad * unit1)
    add(4, normed_grad)
    scaled = normed_grad * n_gain
    hidden_grad = inv1 * (scaled - row_mean(scaled) - unit1 * row_mean(scaled * unit1))
    add(5, hidden_grad)
    ag_ref[...] = hidden_grad.astype(BF16)

    @pl.when(b == n_seq - 1)
    def _():
        for i in range(2):
            pg = pg_all[i]
            gu_ref[i] = dot_tn(nb_all[...], pg).astype(BF16)
            gd_ref[i] = dot_tn(fg_all[...], act_all[i]).astype(BF16)
            gv_ref[6 + i : 7 + i, :] = jnp.sum(pg.astype(F32), axis=0, keepdims=True)


def ffn(lengths, hid, cotangent, u4, d4, s4, vectors, n_seq, half):
    width = hid.shape[1]
    once = pl.Buffered(1)
    return pl.pallas_call(
        functools.partial(ffn_kernel, n_seq, half),
        out_shape=(
            jax.ShapeDtypeStruct((n_seq * half, width), BF16),
            jax.ShapeDtypeStruct((n_seq * half, width), BF16),
            jax.ShapeDtypeStruct((2, width, 768), BF16),
            jax.ShapeDtypeStruct((2, width, 768), BF16),
            jax.ShapeDtypeStruct((8, width), F32),
        ),
        grid=(n_seq,),
        in_specs=[
            pl.BlockSpec(memory_space=pltpu.SMEM),
            pl.BlockSpec((half, width), lambda b: (b, 0)),
            pl.BlockSpec((half, width), lambda b: (my_core() * n_seq + b, 0)),
            pl.BlockSpec((4, width, 768), lambda b: (0, 0, 0), pipeline_mode=once),
            pl.BlockSpec((4, width, 768), lambda b: (0, 0, 0), pipeline_mode=once),
            pl.BlockSpec(s4.shape, lambda b: (0, 0, 0), pipeline_mode=once),
            pl.BlockSpec(vectors.shape, lambda b: (0, 0), pipeline_mode=once),
        ],
        out_specs=[
            pl.BlockSpec((half, width), lambda b: (b, 0)),
            pl.BlockSpec((half, width), lambda b: (b, 0)),
            pl.BlockSpec((2, width, 768), lambda b: (0, 0, 0), pipeline_mode=once),
            pl.BlockSpec((2, width, 768), lambda b: (0, 0, 0), pipeline_mode=once),
            pl.BlockSpec((8, width), lambda b: (0, 0), pipeline_mode=once),
        ],
        scratch_shapes=[
            pltpu.VMEM((n_seq * half, width), BF16),
            pltpu.VMEM((n_seq * half, width), BF16),
            pltpu.VMEM((4, n_seq * half, 768), BF16),
            pltpu.VMEM((4, n_seq * half, 768), BF16),
            pltpu.VMEM((4, half, 768), F32),
        ],
        compiler_params=pltpu.CompilerParams(vmem_limit_bytes=VMEM_LIMIT),
        cost_estimate=pl.CostEstimate(flops=24 * 10**9, bytes_accessed=30 * 10**6, transcendentals=6 * 10**6),
    )(lengths, hid, cotangent, u4, d4, s4, vectors)


class Net:
    def __init__(self, n_hi):
        self.n_hi = n_hi
        self.dp, self.t = lax.axis_index("dp"), lax.axis_index("tensor")
        self.hi, self.lo = self.dp // 2, lax.rem(self.dp, 2)
        self.core = lax.rem(self.t, 2)
        self.to_x = (self.dp + 1 - 2 * self.lo, self.t)
        self.to_c = (self.dp, self.t + 1 - 2 * self.core)

    def place(self, s):
        return lax.rem(self.hi + s, self.n_hi)

    def z_peer(self, s):
        return (self.place(s) * 2 + self.lo, self.t)

    def greet(self):
        barrier = pltpu.get_barrier_semaphore()
        peers = [self.z_peer(s) for s in range(1, self.n_hi)] + [self.to_x, self.to_c]
        for peer in peers:
            pl.semaphore_signal(barrier, inc=1, device_id=peer, device_id_type=MESH)
        pl.semaphore_wait(barrier, len(peers))

    def remote(self, src, dst, send, recv, peer):
        return pltpu.make_async_remote_copy(src, dst, send, recv, device_id=peer, device_id_type=MESH)


class Scatter:
    def __init__(self, net, mine, other, bufs):
        self.net, self.mine, self.other = net, mine, other
        self.r1, self.t1, self.r2, self.t2, self.r3, self.sem, self.zs, self.zr = bufs

    @staticmethod
    def scratch(n_hi, rows, width, stages="cxz"):
        block = (rows, width)
        dma = pltpu.SemaphoreType.DMA
        both = (n_hi, 2) + block if "c" in stages else (8, 128)
        half = (n_hi,) + block
        return [
            pltpu.VMEM(both, BF16), pltpu.VMEM(both, BF16), pltpu.VMEM(half if "x" in stages else (8, 128), BF16),
            pltpu.VMEM(half, BF16), pltpu.VMEM(half if "z" in stages else (8, 128), BF16),
            dma((4,)), dma((n_hi,)), dma((n_hi,)),
        ]

    def over_core(self):
        return self.net.remote(self.other, self.r1, self.sem.at[0], self.sem.at[1], self.net.to_c)

    def over_x(self):
        return self.net.remote(
            self.t1.at[:, 1 - self.net.lo], self.r2, self.sem.at[2], self.sem.at[3], self.net.to_x
        )

    def over_z(self, s):
        return self.net.remote(
            self.t2.at[self.net.place(s)], self.r3.at[s], self.zs.at[s], self.zr.at[s], self.net.z_peer(s)
        )

    def core_to_x(self):
        self.over_core().wait_recv()
        self.t1[...] = self.mine + self.r1[...]
        self.over_x().start()

    def x_sum(self, out):
        self.over_x().wait_recv()
        out[...] = self.t1[:, self.net.lo] + self.r2[...]

    def start_z(self):
        for s in range(1, self.net.n_hi):
            self.over_z(s).start()

    def finish_z(self, out):
        total = self.t2[self.net.hi].astype(F32)
        for s in range(1, self.net.n_hi):
            self.over_z(s).wait_recv()
            total += self.r3[s].astype(F32)
        out[...] = total
        for s in range(1, self.net.n_hi):
            self.over_z(s).wait_send()

    def sent(self):
        self.over_core().wait_send()
        self.over_x().wait_send()


class SmallSum:
    def __init__(self, net, mine, other, bufs):
        self.net, self.mine, self.other = net, mine, other
        self.rc, self.v1, self.rx, self.v2, self.sem, self.zs, self.zr = bufs

    @staticmethod
    def scratch(n_hi, shape):
        dma = pltpu.SemaphoreType.DMA
        return [
            pltpu.VMEM(shape, F32), pltpu.VMEM(shape, F32), pltpu.VMEM(shape, F32), pltpu.VMEM((n_hi,) + shape, F32),
            dma((4,)), dma((n_hi,)), dma((n_hi,)),
        ]

    def over_core(self):
        return self.net.remote(self.other, self.rc, self.sem.at[0], self.sem.at[1], self.net.to_c)

    def over_x(self):
        return self.net.remote(self.v1, self.rx, self.sem.at[2], self.sem.at[3], self.net.to_x)

    def over_z(self, s):
        here = self.v2.at[self.net.hi]
        return self.net.remote(here, here, self.zs.at[s], self.zr.at[s], self.net.z_peer(s))

    def core_to_x(self):
        self.over_core().wait_recv()
        self.v1[...] = self.mine[...] + self.rc[...]
        self.over_x().start()

    def x_to_z(self):
        self.over_x().wait_recv()
        self.v2[self.net.hi] = self.v1[...] + self.rx[...]
        for s in range(1, self.net.n_hi):
            self.over_z(s).start()

    def finish(self, out):
        for s in range(1, self.net.n_hi):
            self.over_z(s).wait()
        out[...] = jnp.sum(self.v2[...], axis=0)
        self.over_core().wait_send()
        self.over_x().wait_send()


def backward_step(half, own, step_refs):
    kv_ref, q_ref, p_ref, ag, a_of, tacc, kvd, qd_ref = step_refs
    low = lane_low((half, 128))
    cg = dot_nn(ag, a_of(slice(512, 768))).astype(BF16)
    q01 = q_ref[0, :, 0:128]
    cg2, cg01 = cg[:, 0:128], cg[:, 128:256]
    zero = jnp.zeros_like(q01)
    heads = (
        (jnp.where(low, q01, zero), jnp.where(low, cg01, zero), 0, 128),
        (jnp.where(low, zero, q01), jnp.where(low, zero, cg01), 0, 128),
        (q_ref[0, :, 128:256], jnp.where(low, zero, cg2), 256, 256),
    )
    kds, vds, qds = [], [], []
    for h, (q, g, k_at, v_at) in enumerate(heads):
        pb16 = p_ref[0, 0, h]
        p = pb16.astype(F32)
        dp = dot_nt(kv_ref[0, :, v_at : v_at + 128], g)
        row = jnp.sum(p * dp, axis=0, keepdims=True)
        sg = (p * (dp - row)).astype(BF16)
        if own:
            tacc[h] += sg.astype(F32)
        kds.append(dot_nn(sg, q))
        vds.append(dot_nn(pb16, g))
        qds.append(dot_tn(kv_ref[0, :, k_at : k_at + 128], sg))
    kvd[:, 0:128] = (kds[0] + kds[1]).astype(BF16)
    kvd[:, 128:256] = (vds[0] + vds[1]).astype(BF16)
    kvd[:, 256:384] = (kds[2] + vds[2]).astype(BF16)
    qd01 = jnp.concatenate([qds[0][0:64], qds[1][64:128]], axis=0).T
    qd2 = jnp.concatenate([qds[2][0:64], jnp.zeros_like(qds[2][0:64])], axis=0).T
    qd = jnp.concatenate([qd01, qd2], axis=1).astype(BF16)
    qd_ref[...] = qd
    return dot_nt(kvd[...], a_of(slice(0, 384))), dot_nt(qd, a_of(slice(384, 640))) * 0.125


def own_kernel(n_seq, length, n_dp, comm, *refs):
    half = length // 2
    n_hi = n_dp // 2
    b, g = pl.program_id(0), pl.program_id(1)
    step = 2 * b + g
    x_ref, a_ref, kv_ref, q_ref, p_ref, ctx_ref, ag_ref, pb_ref = refs[:8]
    refs = refs[8:]
    if comm:
        gu_mine, gd_mine, gu_any, gd_any, gv_ref, half_any = refs[:6]
        tok_ref, pool_ref, ga_ref, sm_ref, up_out, gd_out, gv_out, out_any = refs[6:14]
        kvd, qd_all, tacc = refs[14:17]
        refs = refs[17:]
        net = Net(n_hi)
        other = 1 - net.core
        up = Scatter(net, gu_mine[0], gu_any.at[other], refs[0:8])
        down = Scatter(net, gd_mine[0], gd_any.at[other], refs[8:16])
        vec = SmallSum(net, gv_ref, gv_ref, refs[16:23])
        o_sem = refs[23]
        n_rows = n_seq * half
        there = out_any.at[pl.ds(pl.multiple_of(net.core * n_rows, n_rows), n_rows), :]
        o_local = pltpu.make_async_copy(half_any, there, o_sem.at[0])
        o_core = net.remote(half_any, there, o_sem.at[1], o_sem.at[2], net.to_c)

        @pl.when(step == 0)
        def _():
            net.greet()
            up.over_core().start()
            vec.over_core().start()
            down.over_core().start()
            o_core.start()
            o_local.start()

        @pl.when(step == 1)
        def _():
            up.core_to_x()
            vec.core_to_x()
            down.core_to_x()

        pl.when(step == 2)(vec.x_to_z)

        @pl.when(step == 5)
        def _():
            up.x_sum(up.t2)
            up.start_z()
    else:
        tok_ref, pool_ref, ga_ref, sm_ref, kvd, qd_all, tacc = refs

    @pl.when(b == 0)
    def _():
        tacc[g] = jnp.zeros_like(tacc[g])

    krows = pl.ds(pl.multiple_of(b * length, length), length)
    qrows = pl.ds(pl.multiple_of(b * half, half), half)
    tok, pool = backward_step(
        half,
        True,
        (kv_ref, q_ref, p_ref, ag_ref[qrows, :], lambda lanes: a_ref[g, :, lanes], tacc.at[g], kvd.at[g, krows],
         qd_all.at[g, qrows]),
    )

    @pl.when(g == 0)
    def _():
        tok_ref[...] = tok
        pool_ref[...] = pool

    @pl.when(g == 1)
    def _():
        tok_ref[...] += tok
        pool_ref[...] += pool

    @pl.when(b == n_seq - 1)
    def _():
        ga_ref[g, :, 0:384] = dot_tn(x_ref[...], kvd[g]).astype(BF16)
        gq = dot_tn(pb_ref[...], qd_all[g]) * 0.125
        go = dot_tn(ag_ref[...], ctx_ref[g])
        ga_ref[g, :, 384:512] = gq[:, 0:128].astype(BF16)
        ga_ref[g, :, 512:640] = (gq[:, 128:256] + go[:, 0:128]).astype(BF16)
        ga_ref[g, :, 640:768] = go[:, 128:256].astype(BF16)
        sm_ref[g, 3:8, :] = jnp.zeros((5, 2 * length), F32)
        sm_ref[g, 3:4, 0:384] = jnp.sum(kvd[g].astype(F32), axis=0, keepdims=True)
        i = lax.broadcasted_iota(jnp.int32, (half, half), 0)
        flip = jnp.where(i + lax.broadcasted_iota(jnp.int32, (half, half), 1) == half - 1, 1.0, 0.0).astype(BF16)
        for h in range(3):
            high = tacc[g, h].astype(BF16)
            rest = (tacc[g, h] - high.astype(F32)).astype(BF16)
            turned = dot_nt(flip, high) + dot_nt(flip, rest)
            wide = jnp.concatenate([turned, jnp.zeros((half, length), F32)], axis=1)
            rolled = pltpu.roll(wide, 2, 1, stride=2, stride_axis=0)
            sm_ref[g, h : h + 1, :] = jnp.sum(rolled, axis=0, keepdims=True)

    if comm:

        @pl.when(step == 2 * n_seq - 1)
        def _():
            down.x_sum(gd_out)
            vec.finish(gv_out)
            up.finish_z(up_out)
            up.sent()
            down.sent()
            o_local.wait()
            o_core.wait()


def rest_kernel(n_seq, length, n_dp, comm, *refs):
    half = length // 2
    n_hi = n_dp // 2
    b, g = pl.program_id(0), pl.program_id(1)
    step = 2 * b + g
    a_ref, kv_ref, q_ref, p_ref, ag_ref, tok_in, pool_in = refs[:7]
    refs = refs[7:]
    if comm:
        ga_mine, ga_any, gd_in, sm_mine, sm_any = refs[:5]
        tok_any, ga_out, down_out, sm_out = refs[5:9]
        kvd, qd, tok, pool, stage, t_sem = refs[9:15]
        refs = refs[15:]
        net = Net(n_hi)
        other = 1 - net.core
        att = Scatter(net, ga_mine[0], ga_any.at[other], refs[0:8])
        down = Scatter(net, None, None, refs[8:11] + (gd_in,) + refs[12:16])
        vec = SmallSum(net, sm_mine.at[0], sm_any.at[other], refs[16:23])

        def tok_copies(i):
            row = pl.multiple_of((net.core * n_seq + i) * length, length)
            there = tok_any.at[pl.ds(row, length), :]
            return (
                pltpu.make_async_copy(stage.at[i], there, t_sem.at[0, i]),
                net.remote(stage.at[i], there, t_sem.at[1, i], t_sem.at[2, i], net.to_c),
            )

        @pl.when(step == 0)
        def _():
            net.greet()
            att.over_core().start()
            vec.over_core().start()
            down.start_z()

        @pl.when(step == 1)
        def _():
            att.core_to_x()
            vec.core_to_x()

        pl.when(step == 2)(vec.x_to_z)

        @pl.when(step == 5)
        def _():
            att.x_sum(att.t2)
            att.start_z()
    else:
        tok_out, kvd, qd, tok, pool = refs

    tok_add, pool_add = backward_step(
        half, False, (kv_ref, q_ref, p_ref, ag_ref[...], lambda lanes: a_ref[g, :, lanes], None, kvd, qd)
    )

    @pl.when(g == 0)
    def _():
        tok[...] = tok_in[...] + tok_add
        pool[...] = pool_in[...] + pool_add

    @pl.when(g == 1)
    def _():
        total = (pool[...] + pool_add + ag_ref[...].astype(F32)).astype(BF16)
        final = (tok[...] + tok_add + dot_tn(pool_matrix(half, length), total)).astype(BF16)
        if comm:
            stage[b] = final
            for copy in tok_copies(b):
                copy.start()
        else:
            tok_out[...] = final

    if comm:

        @pl.when(step == 2 * n_seq - 1)
        def _():
            down.finish_z(down_out)
            vec.finish(sm_out)
            att.finish_z(ga_out)
            att.sent()
            for i in range(n_seq):
                for copy in tok_copies(i):
                    copy.wait()


def fixed(shape, first=None):
    def index(*grid):
        head = 0 if first is None else first()
        return (head,) + (0,) * (len(shape) - 1)

    return pl.BlockSpec(shape, index, pipeline_mode=pl.Buffered(1))


ANY = pl.BlockSpec(memory_space=pl.ANY)


def backward_specs(n_seq, length, width, own):
    half = length // 2
    at = 0 if own else 2
    return (
        fixed((2, width, 768), (lambda: 0) if own else (lambda: 1)),
        pl.BlockSpec((1, length, 384), lambda b, g: (at + g, b, 0)),
        pl.BlockSpec((1, half, 256), lambda b, g: (at + g, b, 0)),
        pl.BlockSpec((1, 1, 3, length, half), lambda b, g: (at + g, b, 0, 0, 0)),
    )


def backward_own(tokens, a4, kv, q, p, ctx, ag, pb, gu, gd, gv, out_half, n_seq, n_dp, comm):
    length = kv.shape[1] // n_seq
    half = length // 2
    width = tokens.shape[1]
    n_tok, n_pool = n_seq * length, n_seq * half
    a_spec, kv_spec, q_spec, p_spec = backward_specs(n_seq, length, width, True)
    in_specs = [
        fixed((n_tok, width), my_core), a_spec, kv_spec, q_spec, p_spec, fixed((2, n_pool, 256)),
        fixed((n_pool, width)), fixed((n_pool, width)),
    ]
    args = [tokens, a4, kv, q, p, ctx, ag, pb]
    out_shape = [
        jax.ShapeDtypeStruct((n_tok, width), F32),
        jax.ShapeDtypeStruct((n_pool, width), F32),
        jax.ShapeDtypeStruct((2, width, 768), BF16),
        jax.ShapeDtypeStruct((2, 8, 2 * length), F32),
    ]
    out_specs = [
        pl.BlockSpec((length, width), lambda b, g: (b, 0)),
        pl.BlockSpec((half, width), lambda b, g: (b, 0)),
        fixed((2, width, 768)),
        fixed((2, 8, 2 * length)),
    ]
    scratch = [
        pltpu.VMEM((2, n_tok, 384), BF16), pltpu.VMEM((2, n_pool, 256), BF16), pltpu.VMEM((2, 3, length, half), F32),
    ]
    params = {"vmem_limit_bytes": VMEM_LIMIT}
    if comm:
        n_hi, rows = n_dp // 2, width // n_dp
        split = (2, n_hi, 2, rows, width)
        gu, gd = gu.reshape(split), gd.reshape(split)
        in_specs += [fixed((1,) + split[1:], my_core)] * 2 + [ANY, ANY, fixed(gv.shape), ANY]
        args += [gu, gd, gu, gd, gv, out_half]
        out_shape += [
            jax.ShapeDtypeStruct((rows, width), F32),
            jax.ShapeDtypeStruct((n_hi, rows, width), BF16),
            jax.ShapeDtypeStruct(gv.shape, F32),
            jax.ShapeDtypeStruct((2 * n_pool, width), BF16),
        ]
        out_specs += [fixed((rows, width)), fixed((n_hi, rows, width)), fixed(gv.shape), ANY]
        scratch += Scatter.scratch(n_hi, rows, width) + Scatter.scratch(n_hi, rows, width, "cx")
        scratch += SmallSum.scratch(n_hi, gv.shape) + [pltpu.SemaphoreType.DMA((3,))]
        params.update(collective_id=1, has_side_effects=True)
    return pl.pallas_call(
        functools.partial(own_kernel, n_seq, length, n_dp, comm),
        out_shape=out_shape,
        grid=(n_seq, 2),
        in_specs=in_specs,
        out_specs=out_specs,
        scratch_shapes=scratch,
        compiler_params=pltpu.CompilerParams(**params),
        cost_estimate=pl.CostEstimate(flops=20 * 10**9, bytes_accessed=30 * 10**6, transcendentals=0),
    )(*args)


def backward_rest(a4, kv, q, p, ag, tok, pool, ga, gd, sm, n_seq, n_dp, comm):
    length = kv.shape[1] // n_seq
    half = length // 2
    width = ag.shape[1]
    n_tok = n_seq * length
    in_specs = list(backward_specs(n_seq, length, width, False)) + [
        pl.BlockSpec((half, width), lambda b, g: (b, 0)),
        pl.BlockSpec((length, width), lambda b, g: (b, 0)),
        pl.BlockSpec((half, width), lambda b, g: (b, 0)),
    ]
    args = [a4, kv, q, p, ag, tok, pool]
    scratch = [
        pltpu.VMEM((length, 384), BF16), pltpu.VMEM((half, 256), BF16), pltpu.VMEM((length, width), F32),
        pltpu.VMEM((half, width), F32),
    ]
    params = {"vmem_limit_bytes": VMEM_LIMIT}
    if comm:
        n_hi, rows = n_dp // 2, width // n_dp
        split = (2, n_hi, 2, rows, width)
        ga = ga.reshape(split)
        small = sm.shape[1:]
        in_specs += [
            fixed((1,) + split[1:], my_core), ANY, fixed((n_hi, rows, width)), fixed((1,) + small, my_core), ANY,
        ]
        args += [ga, ga, gd, sm, sm]
        out_shape = [
            jax.ShapeDtypeStruct((2 * n_tok, width), BF16),
            jax.ShapeDtypeStruct((rows, width), F32),
            jax.ShapeDtypeStruct((rows, width), F32),
            jax.ShapeDtypeStruct(small, F32),
        ]
        out_specs = [ANY, fixed((rows, width)), fixed((rows, width)), fixed(small)]
        scratch += [pltpu.VMEM((n_seq, length, width), BF16), pltpu.SemaphoreType.DMA((3, n_seq))]
        scratch += Scatter.scratch(n_hi, rows, width) + Scatter.scratch(n_hi, rows, width, "z")
        scratch += SmallSum.scratch(n_hi, small)
        params.update(collective_id=2, has_side_effects=True)
    else:
        out_shape = jax.ShapeDtypeStruct((n_tok, width), BF16)
        out_specs = pl.BlockSpec((length, width), lambda b, g: (b, 0))
    return pl.pallas_call(
        functools.partial(rest_kernel, n_seq, length, n_dp, comm),
        out_shape=out_shape,
        grid=(n_seq, 2),
        in_specs=in_specs,
        out_specs=out_specs,
        scratch_shapes=scratch,
        compiler_params=pltpu.CompilerParams(**params),
        cost_estimate=pl.CostEstimate(flops=20 * 10**9, bytes_accessed=30 * 10**6, transcendentals=0),
    )(*args)


def unpack(a_sum):
    key = jnp.concatenate([a_sum[:, 0:128], a_sum[:, 256:320]], axis=1)
    value = jnp.concatenate([a_sum[:, 128:256], a_sum[:, 320:384]], axis=1)
    out = jnp.concatenate([a_sum[:, 640:768], a_sum[:, 576:640]], axis=1).T
    return a_sum[:, 384:576], key, value, out


def gather_plain(weights, length):
    kw, vw, qw, ow, uw, dw, tab, vbias, hbias = weights
    ot = ow.T
    packed = jnp.concatenate([kw[:, :128], vw[:, :128], kw[:, 128:], vw[:, 128:], qw, ot[:, 128:], ot[:, :128]], axis=1)
    small = jnp.zeros((8, 2 * length), F32).at[0:3].set(tab).at[3, 128:256].set(vbias[0, :128])
    small = small.at[3, 320:384].set(vbias[0, 128:]).at[4, : hbias.shape[1]].set(hbias[0])
    first = 2 * (lax.axis_index("tensor") // 2)

    def groups(v):
        every = lax.all_gather(v, "tensor")
        return lax.dynamic_slice_in_dim(jnp.concatenate([every, every]), first, 4)

    wide = jnp.stack([packed, uw, dw.T], axis=1).astype(BF16)
    wide = groups(lax.all_gather(wide, "dp", axis=0, tiled=True))
    return wide[:, :, 0], wide[:, :, 1], wide[:, :, 2], groups(small)


def sum_plain(grads, n_dp):
    core = my_core()
    mine = lax.dynamic_index_in_dim(grads, core, 0, keepdims=False).astype(F32)
    other = lax.dynamic_index_in_dim(grads, 1 - core, 0, keepdims=False)
    total = mine + lax.ppermute(other, "tensor", [(i, i ^ 1) for i in range(4)]).astype(F32)
    return lax.psum_scatter(total, "dp", scatter_dimension=0, tiled=True)


def shards(
    n_dp, tokens, lengths, cotangent, query_weight, key_weight, value_weight, value_bias, output_weight,
    b_out, rel_table, norm_gain, norm_shift, up_weight, hidden_bias, down_weight, b_down, final_gain, final_shift,
):
    seq_count = lengths.shape[0]
    length = tokens.shape[0] // seq_count
    half = length // 2
    n_seq = seq_count // 2
    core = my_core()
    n_hi, rows = n_dp // 2, tokens.shape[1] // n_dp
    comm = rows % 16 == 0 and n_hi <= 4

    weights = (
        key_weight, value_weight, query_weight, output_weight, up_weight, down_weight, rel_table,
        value_bias[None], hidden_bias[None],
    )
    if not comm:
        weights = gather_plain(weights, length)
        a4, u4, d4, s4 = weights
        weights = (a4, s4)
    kv, q, p, ctx, hid, pb, *gathered = attention_forward(lengths, tokens, b_out[None], weights, n_dp, comm)
    if comm:
        a4, u4, d4, s4 = gathered
    vectors = jnp.stack([norm_gain, norm_shift, b_down, final_gain, final_shift])
    out_half, ag, gu, gd, gv = ffn(lengths, hid, cotangent, u4, d4, s4, vectors, n_seq, half)
    tok, pool, ga, sm, *sums = backward_own(tokens, a4, kv, q, p, ctx, ag, pb, gu, gd, gv, out_half, n_seq, n_dp, comm)
    if comm:
        up_sum, gd, gv, output = sums
        tokens_grad, a_sum, down_sum, sm = backward_rest(a4, kv, q, p, ag, tok, pool, ga, gd, sm, n_seq, n_dp, comm)
    else:
        tok_half = backward_rest(a4, kv, q, p, ag, tok, pool, ga, gd, sm, n_seq, n_dp, comm)
        up_sum, down_sum, a_sum = (sum_plain(v, n_dp) for v in (gu, gd, ga))
        sm, gv = lax.psum((sm, gv), "dp")

        def over_core(v):
            return lax.ppermute(v, "tensor", [(i, i ^ 1) for i in range(4)])

        gv = gv + over_core(gv)
        mine = lax.dynamic_index_in_dim(sm, core, 0, keepdims=False)
        sm = mine + over_core(lax.dynamic_index_in_dim(sm, 1 - core, 0, keepdims=False))

        def join(part):
            got = over_core(part)
            return jnp.where(core == 0, jnp.concatenate([part, got]), jnp.concatenate([got, part]))

        output, tokens_grad = join(out_half), join(tok_half)
    query_sum, key_sum, value_sum, outw_sum = unpack(a_sum)
    vbias_sum = jnp.concatenate([sm[3, 128:256], sm[3, 320:384]])
    ubias_sum = lax.dynamic_index_in_dim(gv[6:8], core, 0, keepdims=False)
    return (
        output, tokens_grad, query_sum, key_sum, value_sum, vbias_sum, outw_sum, gv[5], sm[0:3],
        gv[3], gv[4], up_sum, ubias_sum, down_sum.T, gv[2], gv[0], gv[1],
    )


def solution(mesh):
    row, col, both, rep = P("dp", None), P("tensor", "dp"), P("dp", "tensor"), P()
    ten, table = P("tensor"), P("tensor", None)
    in_specs = (
        row, P("dp"), row, both, both, both, ten, col, rep, table, rep, rep, both, ten, col, rep, rep, rep,
    )
    out_specs = (
        row, row, both, both, both, ten, col, rep, table, rep, rep, both, ten, col, rep, rep, rep,
    )
    body = functools.partial(shards, mesh.shape["dp"])
    return jax.shard_map(body, mesh=mesh, in_specs=in_specs, out_specs=out_specs, check_vma=False)
```

```python
import functools

import jax
import jax.numpy as jnp
from jax import lax
from jax.experimental import pallas as pl
from jax.experimental.pallas import tpu as pltpu
from jax.sharding import PartitionSpec as P

MESH = pl.DeviceIdType.MESH
F32 = jnp.float32
BF16 = jnp.bfloat16
EPS = 1e-06
VMEM_LIMIT = 58 * 2**20


def dot_nn(a, b):
    return lax.dot_general(a, b, (((1,), (0,)), ((), ())), preferred_element_type=F32)


def dot_nt(a, b):
    return lax.dot_general(a, b, (((1,), (1,)), ((), ())), preferred_element_type=F32)


def dot_tn(a, b):
    return lax.dot_general(a, b, (((0,), (0,)), ((), ())), preferred_element_type=F32)


class Gather:
    def __init__(self, n_hi, ins, outs, s_in, s_out, sems):
        self.n_hi, self.ins, self.outs, self.s_in, self.s_out = n_hi, ins, outs, s_in, s_out
        self.loc, self.zs, self.zr, self.ls, self.lr, self.fs, self.fr, self.cs, self.cr, self.ss, self.sr = sems
        self.dp, self.t = lax.axis_index("dp"), lax.axis_index("tensor")
        self.hi, self.lo = self.dp // 2, lax.rem(self.dp, 2)
        self.core = lax.rem(self.t, 2)
        t_core = self.t + 1 - 2 * self.core
        self.to_x = (self.dp + 1 - 2 * self.lo, self.t)
        self.to_y = (self.dp, lax.rem(self.t + 2, 4))
        self.to_c = (self.dp, t_core)
        self.to_d = (self.dp, lax.rem(t_core + 2, 4))

    def z_peer(self, s):
        return (lax.rem(self.hi + s, self.n_hi) * 2 + self.lo, self.t)

    def block(self, s, side):
        return lax.rem(self.hi - s + self.n_hi, self.n_hi) * 2 + side

    def greet(self):
        barrier = pltpu.get_barrier_semaphore()
        for s in range(1, self.n_hi):
            pl.semaphore_signal(barrier, inc=1, device_id=self.z_peer(s), device_id_type=MESH)
        for peer in (self.to_x, self.to_y, self.to_c, self.to_d):
            pl.semaphore_signal(barrier, inc=1, device_id=peer, device_id_type=MESH)
        pl.semaphore_wait(barrier, self.n_hi + 3)

    def remote(self, src, dst, send, recv, peer):
        return pltpu.make_async_remote_copy(src, dst, send, recv, device_id=peer, device_id_type=MESH)

    def small(self):
        core = self.core
        return (
            pltpu.make_async_copy(self.s_in, self.s_out.at[core], self.loc.at[3]),
            self.remote(self.s_in, self.s_out.at[core], self.ss.at[0], self.sr.at[0], self.to_c),
            self.remote(self.s_in, self.s_out.at[2 + core], self.ss.at[1], self.sr.at[1], self.to_y),
            self.remote(self.s_in, self.s_out.at[2 + core], self.ss.at[2], self.sr.at[2], self.to_d),
        )

    def local(self, k):
        return pltpu.make_async_copy(self.ins[k], self.outs[k].at[self.core, self.dp], self.loc.at[k])

    def z_copy(self, k, s):
        return self.remote(
            self.ins[k], self.outs[k].at[self.core, self.dp], self.zs.at[k, s], self.zr.at[k, s], self.z_peer(s)
        )

    def line(self, k, s, way, own=False):
        out, b = self.outs[k], self.block(s, self.lo)
        src = self.ins[k] if own else out.at[self.core, b]
        dst = out.at[self.core if way == 0 else 2 + self.core, b]
        return self.remote(
            src, dst, self.ls.at[way, k, s], self.lr.at[way, k, s], self.to_x if way == 0 else self.to_y
        )

    def onward(self, k, s, way):
        out = self.outs[k]
        if way == 0:
            src = dst = out.at[2 + self.core, self.block(s, self.lo)]
        else:
            b = self.block(s, 1 - self.lo)
            src, dst = out.at[self.core, b], out.at[2 + self.core, b]
        return self.remote(src, dst, self.fs.at[k, s], self.fr.at[k, s], self.to_x if way == 0 else self.to_y)

    def to_core(self, k, s, which, own=False):
        out = self.outs[k]
        side = self.lo if which % 2 == 0 else 1 - self.lo
        where = out.at[self.core if which < 2 else 2 + self.core, self.block(s, side)]
        return self.remote(
            self.ins[k] if own else where, where, self.cs.at[which, k, s], self.cr.at[which, k, s], self.to_c
        )

    def start(self, k):
        self.local(k).start()
        for s in range(1, self.n_hi):
            self.z_copy(k, s).start()
        self.line(k, 0, 0, True).start()
        self.line(k, 0, 1, True).start()
        self.to_core(k, 0, 0, True).start()

    def spread(self, k, s):
        self.z_copy(k, s).wait_recv()
        self.line(k, s, 0).start()
        self.line(k, s, 1).start()
        self.to_core(k, s, 0).start()

    def over_x(self, k, s):
        self.line(k, s, 0).wait_recv()
        self.onward(k, s, 1).start()
        self.to_core(k, s, 1).start()

    def over_y(self, k, s):
        self.line(k, s, 1).wait_recv()
        self.onward(k, s, 0).start()
        self.to_core(k, s, 2).start()

    def late_x(self, k, s):
        self.line(k, s, 0).wait_recv()
        self.to_core(k, s, 1).start()

    def late_y(self, k, s):
        self.line(k, s, 1).wait_recv()
        self.to_core(k, s, 2).start()

    def pass_on(self, k, s):
        if k == 2:
            pl.when(self.core == 0)(lambda: self.over_x(k, s))
            pl.when(self.core == 1)(lambda: self.over_y(k, s))
        else:
            (self.over_x, self.over_y)[k](k, s)

    def late(self, k):
        for s in range(self.n_hi):
            if k == 2:
                pl.when(self.core == 0)(lambda: self.late_y(k, s))
                pl.when(self.core == 1)(lambda: self.late_x(k, s))
            else:
                (self.late_y, self.late_x)[k](k, s)

    def diagonal(self, k, s):
        self.onward(k, s, 0).wait_recv()
        self.to_core(k, s, 3).start()

    def arrived(self, k, whiches):
        for s in range(self.n_hi):
            for which in whiches:
                self.to_core(k, s, which).wait_recv()

    def sent(self, k):
        for s in range(self.n_hi):
            if s > 0:
                self.z_copy(k, s).wait_send()
            self.line(k, s, 0).wait_send()
            self.line(k, s, 1).wait_send()
            self.onward(k, s, 0).wait_send()
            for which in range(4):
                self.to_core(k, s, which).wait_send()


def gather_scratch(n_hi):
    dma = pltpu.SemaphoreType.DMA
    return [
        dma((4,)), dma((3, n_hi)), dma((3, n_hi)), dma((2, 3, n_hi)), dma((2, 3, n_hi)), dma((3, n_hi)),
        dma((3, n_hi)), dma((4, 3, n_hi)), dma((4, 3, n_hi)), dma((3,)), dma((3,)),
    ]


def pool_matrix(pooled, length):
    i = lax.broadcasted_iota(jnp.int32, (pooled, length), 0)
    j = lax.broadcasted_iota(jnp.int32, (pooled, length), 1)
    return jnp.where(j // 2 == i, 0.5, 0.0).astype(BF16)


def lane_low(shape):
    return lax.broadcasted_iota(jnp.int32, shape, 1) < 64


def attention_kernel(n_seq, length, n_dp, comm, *refs):
    half = length // 2
    group, b = pl.program_id(0), pl.program_id(1)
    step = group * n_seq + b
    core = lax.rem(lax.axis_index("tensor"), 2)
    len_ref, x_any, bo_ref = refs[:3]
    refs = refs[3:]
    if comm:
        (kw, vw, qw, ow, uw, dw, tab, vbias, hbias) = refs[:9]
        kv_ref, q_ref, p_ref, ctx_ref, hid_ref, pb_ref, a_out, u_out, d_out, s_out = refs[9:19]
        bias, x_ref, x_sem, a_in, u_in, d_in, s_in, a_all, s_all, a_sem, s_sem = refs[19:30]
        net = Gather(n_dp // 2, (a_in, u_in, d_in), (a_all, u_out, d_out), s_in, s_all, refs[30:])
    else:
        a_ref, s_ref = refs[:2]
        kv_ref, q_ref, p_ref, ctx_ref, hid_ref, pb_ref, bias, x_ref, x_sem = refs[2:]
    n_tok = n_seq * length
    x_copy = pltpu.make_async_copy(x_any.at[pl.ds(pl.multiple_of(core * n_tok, n_tok), n_tok), :], x_ref, x_sem)

    def pool_rows():
        x_copy.wait()
        pool = pool_matrix(half, length)
        for i in range(n_seq):
            pooled = dot_nn(pool, x_ref[i * length : (i + 1) * length, :])
            hid_ref[i * half : (i + 1) * half, :] = pooled + bo_ref[...]
            pb_ref[i * half : (i + 1) * half, :] = pooled.astype(BF16)

    if comm:

        def a_copy(g):
            return pltpu.make_async_copy(a_all.at[g], a_out.at[g], a_sem.at[g])

        s_copy = pltpu.make_async_copy(s_all, s_out, s_sem)

        @pl.when(step == 0)
        def _():
            x_copy.start()
            k, v, o = kw[...], vw[...], ow[...].T
            parts = (k[:, :128], v[:, :128], k[:, 128:], v[:, 128:], qw[...], o[:, 128:], o[:, :128])
            a_in[...] = jnp.concatenate(parts, axis=1).astype(BF16)
            s_in[...] = jnp.zeros_like(s_in)
            s_in[0:3, :] = tab[...]
            s_in[3:4, 128:256] = vbias[:, 0:128]
            s_in[3:4, 320:384] = vbias[:, 128:192]
            s_in[4:5, 0 : hbias.shape[1]] = hbias[...]
            net.greet()
            for copy in net.small():
                copy.start()
            net.start(0)
            u_in[...] = uw[...].astype(BF16)
            d_in[...] = dw[...].T.astype(BF16)
            for s in range(1, n_dp // 2):
                net.spread(0, s)
                net.pass_on(0, s - 1)
            net.start(1)
            net.pass_on(0, n_dp // 2 - 1)
            pool_rows()
            small = net.small()
            small[0].wait()
            for copy in small[1:]:
                copy.wait()
            s_copy.start()
            net.local(0).wait()
            net.arrived(0, (0, 1))

        n_hi = n_dp // 2
        plan = {}

        def at(n, action, *args):
            plan.setdefault(min(n, 4 * n_seq - 1), []).append(functools.partial(action, *args))

        for s in range(1, n_hi):
            at(s, net.spread, 1, s)
        at(3, net.start, 2)
        at(4, net.late, 0)
        for s in range(n_hi):
            at(4, net.diagonal, 0, s)
        for s in range(1, n_hi):
            at((5, 7, 8)[s - 1], net.spread, 2, s)
        for s in range(n_hi):
            at((5, 6, 7, 9)[s], net.pass_on, 1, s)
        at(2 * n_seq, net.arrived, 0, (2, 3))
        for g in range(4):
            at(2 * n_seq, lambda i: a_copy(i).start(), g)
        at(9, net.late, 1)
        for s in range(n_hi):
            at(10 + s, net.pass_on, 2, s)
        for s in range(n_hi):
            at((11, 11, 12, 13)[s], net.diagonal, 1, s)
        at(14, net.late, 2)
        for n, actions in plan.items():

            @pl.when(step == n)
            def _():
                for action in actions:
                    action()

        def weights(lanes):
            return a_all[group, :, :, lanes].reshape(-1, lanes.stop - lanes.start)

        def small_row(i):
            return s_all[group, i : i + 1, :]
    else:

        @pl.when(step == 0)
        def _():
            x_copy.start()
            pool_rows()

        def weights(lanes):
            return a_ref[0, :, lanes]

        def small_row(i):
            return s_ref[0, i : i + 1, :]

    krows = pl.ds(pl.multiple_of(b * length, length), length)
    qrows = pl.ds(pl.multiple_of(b * half, half), half)

    @pl.when(b == 0)
    def _():
        for h in range(3):
            wide = jnp.broadcast_to(small_row(h), (half, 2 * length))
            bias[h] = pltpu.roll(wide, length, 1, stride=2, stride_axis=0)[:, :length].T

    kv_ref[0] = (dot_nn(x_ref[krows, :], weights(slice(0, 384))) + small_row(3)[:, 0:384]).astype(BF16)
    q = dot_nn(pb_ref[qrows, :], weights(slice(384, 640))) * 0.125
    lanes = lax.broadcasted_iota(jnp.int32, q.shape, 1)
    q = jnp.where(lanes < 192, q, 0.0).astype(BF16)
    q_ref[0] = q
    low = lane_low((half, 128))
    valid = lax.broadcasted_iota(jnp.int32, (length, half), 0) < len_ref[core * n_seq + b]
    q01 = q[:, 0:128]
    zero = jnp.zeros_like(q01)
    heads = (
        (jnp.where(low, q01, zero), 0, 128),
        (jnp.where(low, zero, q01), 0, 128),
        (q[:, 128:256], 256, 256),
    )
    contexts = []
    for h, (qh, k_at, v_at) in enumerate(heads):
        s = dot_nt(kv_ref[0, :, k_at : k_at + 128], qh) + bias[h]
        s = jnp.where(valid, s, -1e30)
        e = jnp.exp(s - jnp.max(s, axis=0, keepdims=True))
        p = (e * (1.0 / jnp.sum(e, axis=0, keepdims=True))).astype(BF16)
        p_ref[0, 0, h] = p
        contexts.append(dot_tn(kv_ref[0, :, v_at : v_at + 128], p))
    c0, c1, c2 = contexts
    ctx01 = jnp.concatenate([c0[0:64], c1[64:128]], axis=0).T
    ctx2 = jnp.concatenate([jnp.zeros_like(c2[0:64]), c2[64:128]], axis=0).T
    ctx = jnp.concatenate([ctx2, ctx01], axis=1).astype(BF16)
    ctx_ref[0] = ctx
    hid_ref[qrows, :] += dot_nt(ctx, weights(slice(512, 768)))

    if comm:

        @pl.when(step == 4 * n_seq - 1)
        def _():
            for s in range(n_hi):
                net.diagonal(2, s)
            for k in range(3):
                net.sent(k)
            for k in (1, 2):
                net.local(k).wait()
                net.arrived(k, (0, 1, 2, 3))
            for g in range(4):
                a_copy(g).wait()
            s_copy.wait()


def my_core():
    return lax.rem(lax.axis_index("tensor"), 2)


def attention_forward(lengths, tokens, b_out, weights, n_dp, comm):
    n_seq = lengths.shape[0] // 2
    length = tokens.shape[0] // lengths.shape[0]
    half = length // 2
    width = tokens.shape[1]
    once = pl.Buffered(1)

    def fixed(shape):
        return pl.BlockSpec(shape, lambda g, b: (0,) * len(shape), pipeline_mode=once)

    in_specs = [
        pl.BlockSpec(memory_space=pltpu.SMEM),
        pl.BlockSpec(memory_space=pl.ANY),
        fixed((1, width)),
    ]
    out_shape = [
        jax.ShapeDtypeStruct((4, n_seq * length, 384), BF16),
        jax.ShapeDtypeStruct((4, n_seq * half, 256), BF16),
        jax.ShapeDtypeStruct((4, n_seq, 3, length, half), BF16),
        jax.ShapeDtypeStruct((4, n_seq * half, 256), BF16),
        jax.ShapeDtypeStruct((n_seq * half, width), F32),
        jax.ShapeDtypeStruct((n_seq * half, width), BF16),
    ]
    out_specs = [
        pl.BlockSpec((1, length, 384), lambda g, b: (g, b, 0)),
        pl.BlockSpec((1, half, 256), lambda g, b: (g, b, 0)),
        pl.BlockSpec((1, 1, 3, length, half), lambda g, b: (g, b, 0, 0, 0)),
        pl.BlockSpec((1, half, 256), lambda g, b: (g, b, 0)),
        fixed((n_seq * half, width)),
        fixed((n_seq * half, width)),
    ]
    scratch = [
        pltpu.VMEM((3, length, half), F32), pltpu.VMEM((n_seq * length, width), BF16), pltpu.SemaphoreType.DMA,
    ]
    params = {"vmem_limit_bytes": VMEM_LIMIT}
    if comm:
        rows = width // n_dp
        in_specs += [fixed(w.shape) for w in weights]
        whole = jax.ShapeDtypeStruct((4, n_dp, rows, width), BF16)
        small = jax.ShapeDtypeStruct((4, 8, 2 * length), F32)
        out_shape += [whole, whole, whole, small]
        out_specs += [pl.BlockSpec(memory_space=pl.ANY)] * 4
        scratch += [pltpu.VMEM((rows, width), BF16)] * 3
        scratch += [
            pltpu.VMEM((8, 2 * length), F32),
            pltpu.VMEM((4, n_dp, rows, width), BF16),
            pltpu.VMEM((4, 8, 2 * length), F32),
            pltpu.SemaphoreType.DMA((4,)),
            pltpu.SemaphoreType.DMA,
        ]
        scratch += gather_scratch(n_dp // 2)
        params.update(collective_id=0, has_side_effects=True)
    else:
        in_specs += [
            pl.BlockSpec((1, width, 768), lambda g, b: (g, 0, 0)),
            pl.BlockSpec((1, 8, 2 * length), lambda g, b: (g, 0, 0)),
        ]
    outs = pl.pallas_call(
        functools.partial(attention_kernel, n_seq, length, n_dp, comm),
        out_shape=out_shape,
        grid=(4, n_seq),
        in_specs=in_specs,
        out_specs=out_specs,
        scratch_shapes=scratch,
        compiler_params=pltpu.CompilerParams(**params),
        cost_estimate=pl.CostEstimate(flops=20 * 10**9, bytes_accessed=40 * 10**6, transcendentals=6 * 10**6),
    )(lengths, tokens, b_out, *weights)
    if comm:
        flat = (4, width, width)
        outs = list(outs)
        outs = outs[:6] + [w.reshape(flat) for w in outs[6:9]] + outs[9:]
    return outs


def row_mean(v):
    return jnp.mean(v, axis=-1, keepdims=True)


def ffn_kernel(
    n_seq, half, len_ref, hid_ref, cot_ref, u_ref, d_ref, s_ref, vec_ref,
    out_ref, ag_ref, gu_ref, gd_ref, gv_ref, nb_all, fg_all, act_all, pg_all, dg,
):
    b = pl.program_id(0)
    rows = pl.ds(pl.multiple_of(b * half, half), half)
    n_gain, n_shift, b_down, f_gain, f_shift = (vec_ref[i : i + 1, :] for i in range(5))

    @pl.when(b == 0)
    def _():
        gv_ref[...] = jnp.zeros_like(gv_ref)

    def add(i, v):
        gv_ref[i : i + 1, :] += jnp.sum(v, axis=0, keepdims=True)

    hid = hid_ref[...]
    centred = hid - row_mean(hid)
    inv1 = lax.rsqrt(row_mean(centred * centred) + EPS)
    unit1 = centred * inv1
    normed = unit1 * n_gain + n_shift
    nb = normed.astype(BF16)
    nb_all[rows, :] = nb
    summed = normed + b_down
    for t in range(4):
        pre = dot_nn(nb, u_ref[t]) + s_ref[t, 4:5, 0:768]
        cdf = 0.5 * (1.0 + lax.erf(pre * 0.7071067811865476))
        act = (pre * cdf).astype(BF16)
        dg[t] = cdf + pre * (0.3989422804014327 * jnp.exp(-0.5 * pre * pre))
        act_all[t, rows, :] = act
        summed = summed + dot_nt(act, d_ref[t])
    centred = summed - row_mean(summed)
    inv2 = lax.rsqrt(row_mean(centred * centred) + EPS)
    unit2 = centred * inv2
    valid = (2 * lax.broadcasted_iota(jnp.int32, (half, 1), 0) < len_ref[my_core() * n_seq + b]).astype(F32)
    out_ref[...] = ((unit2 * f_gain + f_shift) * valid).astype(BF16)
    grad = cot_ref[...].astype(F32) * valid
    add(0, grad * unit2)
    add(1, grad)
    scaled = grad * f_gain
    grad_summed = inv2 * (scaled - row_mean(scaled) - unit2 * row_mean(scaled * unit2))
    add(2, grad_summed)
    fg = grad_summed.astype(BF16)
    fg_all[rows, :] = fg
    normed_grad = grad_summed
    for t in range(4):
        pg = (dot_nn(fg, d_ref[t]) * dg[t]).astype(BF16)
        pg_all[t, rows, :] = pg
        normed_grad = normed_grad + dot_nt(pg, u_ref[t])
    add(3, normed_grad * unit1)
    add(4, normed_grad)
    scaled = normed_grad * n_gain
    hidden_grad = inv1 * (scaled - row_mean(scaled) - unit1 * row_mean(scaled * unit1))
    add(5, hidden_grad)
    ag_ref[...] = hidden_grad.astype(BF16)

    @pl.when(b == n_seq - 1)
    def _():
        for i in range(2):
            pg = pg_all[i]
            gu_ref[i] = dot_tn(nb_all[...], pg).astype(BF16)
            gd_ref[i] = dot_tn(fg_all[...], act_all[i]).astype(BF16)
            gv_ref[6 + i : 7 + i, :] = jnp.sum(pg.astype(F32), axis=0, keepdims=True)


def ffn(lengths, hid, cotangent, u4, d4, s4, vectors, n_seq, half):
    width = hid.shape[1]
    once = pl.Buffered(1)
    return pl.pallas_call(
        functools.partial(ffn_kernel, n_seq, half),
        out_shape=(
            jax.ShapeDtypeStruct((n_seq * half, width), BF16),
            jax.ShapeDtypeStruct((n_seq * half, width), BF16),
            jax.ShapeDtypeStruct((2, width, 768), BF16),
            jax.ShapeDtypeStruct((2, width, 768), BF16),
            jax.ShapeDtypeStruct((8, width), F32),
        ),
        grid=(n_seq,),
        in_specs=[
            pl.BlockSpec(memory_space=pltpu.SMEM),
            pl.BlockSpec((half, width), lambda b: (b, 0)),
            pl.BlockSpec((half, width), lambda b: (my_core() * n_seq + b, 0)),
            pl.BlockSpec((4, width, 768), lambda b: (0, 0, 0), pipeline_mode=once),
            pl.BlockSpec((4, width, 768), lambda b: (0, 0, 0), pipeline_mode=once),
            pl.BlockSpec(s4.shape, lambda b: (0, 0, 0), pipeline_mode=once),
            pl.BlockSpec(vectors.shape, lambda b: (0, 0), pipeline_mode=once),
        ],
        out_specs=[
            pl.BlockSpec((half, width), lambda b: (b, 0)),
            pl.BlockSpec((half, width), lambda b: (b, 0)),
            pl.BlockSpec((2, width, 768), lambda b: (0, 0, 0), pipeline_mode=once),
            pl.BlockSpec((2, width, 768), lambda b: (0, 0, 0), pipeline_mode=once),
            pl.BlockSpec((8, width), lambda b: (0, 0), pipeline_mode=once),
        ],
        scratch_shapes=[
            pltpu.VMEM((n_seq * half, width), BF16),
            pltpu.VMEM((n_seq * half, width), BF16),
            pltpu.VMEM((4, n_seq * half, 768), BF16),
            pltpu.VMEM((4, n_seq * half, 768), BF16),
            pltpu.VMEM((4, half, 768), F32),
        ],
        compiler_params=pltpu.CompilerParams(vmem_limit_bytes=VMEM_LIMIT),
        cost_estimate=pl.CostEstimate(flops=24 * 10**9, bytes_accessed=30 * 10**6, transcendentals=6 * 10**6),
    )(lengths, hid, cotangent, u4, d4, s4, vectors)


class Net:
    def __init__(self, n_hi):
        self.n_hi = n_hi
        self.dp, self.t = lax.axis_index("dp"), lax.axis_index("tensor")
        self.hi, self.lo = self.dp // 2, lax.rem(self.dp, 2)
        self.core = lax.rem(self.t, 2)
        self.to_x = (self.dp + 1 - 2 * self.lo, self.t)
        self.to_c = (self.dp, self.t + 1 - 2 * self.core)

    def place(self, s):
        return lax.rem(self.hi + s, self.n_hi)

    def z_peer(self, s):
        return (self.place(s) * 2 + self.lo, self.t)

    def greet(self):
        barrier = pltpu.get_barrier_semaphore()
        peers = [self.z_peer(s) for s in range(1, self.n_hi)] + [self.to_x, self.to_c]
        for peer in peers:
            pl.semaphore_signal(barrier, inc=1, device_id=peer, device_id_type=MESH)
        pl.semaphore_wait(barrier, len(peers))

    def remote(self, src, dst, send, recv, peer):
        return pltpu.make_async_remote_copy(src, dst, send, recv, device_id=peer, device_id_type=MESH)


class Scatter:
    PARTS = 2

    def __init__(self, net, mine, other, bufs):
        self.net, self.mine, self.other = net, mine, other
        self.t1, self.t2, self.r3, self.sem, self.xs, self.xr, self.zs, self.zr = bufs
        self.rows = self.t2.shape[1] // self.PARTS

    @staticmethod
    def scratch(n_hi, rows, width):
        dma = pltpu.SemaphoreType.DMA
        both, half = pltpu.VMEM((n_hi, 2, rows, width), BF16), pltpu.VMEM((n_hi, rows, width), BF16)
        parts = Scatter.PARTS
        return [both, half, half, dma((2,)), dma((parts,)), dma((parts,)), dma((parts, n_hi)), dma((parts, n_hi))]

    def part(self, i):
        return pl.ds(i * self.rows, self.rows)

    def over_core(self):
        return self.net.remote(self.other, self.t1, self.sem.at[0], self.sem.at[1], self.net.to_c)

    def over_x(self, i):
        src = self.t1.at[:, 1 - self.net.lo, self.part(i)]
        return self.net.remote(src, self.t2.at[:, self.part(i)], self.xs.at[i], self.xr.at[i], self.net.to_x)

    def over_z(self, i, s):
        src = self.t2.at[self.net.place(s), self.part(i)]
        dst = self.r3.at[s, self.part(i)]
        return self.net.remote(src, dst, self.zs.at[i, s], self.zr.at[i, s], self.net.z_peer(s))

    def core_to_x(self):
        self.over_core().wait_recv()
        self.t1[...] += self.mine[...]
        for i in range(self.PARTS):
            self.over_x(i).start()

    def x_to_z(self, i):
        self.over_x(i).wait_recv()
        rows = self.part(i)
        self.t2[:, rows] += self.t1[:, self.net.lo, rows]
        for s in range(1, self.net.n_hi):
            self.over_z(i, s).start()

    def finish(self, out):
        for i in range(self.PARTS):
            rows = self.part(i)
            total = self.t2[self.net.hi, rows].astype(F32)
            for s in range(1, self.net.n_hi):
                self.over_z(i, s).wait_recv()
                total += self.r3[s, rows].astype(F32)
            out[rows, :] = total

    def sent(self):
        self.over_core().wait_send()
        for i in range(self.PARTS):
            self.over_x(i).wait_send()
            for s in range(1, self.net.n_hi):
                self.over_z(i, s).wait_send()


class SmallSum:
    def __init__(self, net, mine, other, bufs):
        self.net, self.mine, self.other = net, mine, other
        self.rc, self.v1, self.rx, self.v2, self.sem, self.zs, self.zr = bufs

    @staticmethod
    def scratch(n_hi, shape):
        dma = pltpu.SemaphoreType.DMA
        return [
            pltpu.VMEM(shape, F32), pltpu.VMEM(shape, F32), pltpu.VMEM(shape, F32), pltpu.VMEM((n_hi,) + shape, F32),
            dma((4,)), dma((n_hi,)), dma((n_hi,)),
        ]

    def over_core(self):
        return self.net.remote(self.other, self.rc, self.sem.at[0], self.sem.at[1], self.net.to_c)

    def over_x(self):
        return self.net.remote(self.v1, self.rx, self.sem.at[2], self.sem.at[3], self.net.to_x)

    def over_z(self, s):
        here = self.v2.at[self.net.hi]
        return self.net.remote(here, here, self.zs.at[s], self.zr.at[s], self.net.z_peer(s))

    def core_to_x(self):
        self.over_core().wait_recv()
        self.v1[...] = self.mine[...] + self.rc[...]
        self.over_x().start()

    def x_to_z(self):
        self.over_x().wait_recv()
        self.v2[self.net.hi] = self.v1[...] + self.rx[...]
        for s in range(1, self.net.n_hi):
            self.over_z(s).start()

    def finish(self, out):
        for s in range(1, self.net.n_hi):
            self.over_z(s).wait()
        out[...] = jnp.sum(self.v2[...], axis=0)
        self.over_core().wait_send()
        self.over_x().wait_send()

def backward_step(half, own, step_refs):
    kv_ref, q_ref, p_ref, ag, a_of, tacc, kvd, qd_ref = step_refs
    low = lane_low((half, 128))
    cg = dot_nn(ag, a_of(slice(512, 768))).astype(BF16)
    q01 = q_ref[0, :, 0:128]
    cg2, cg01 = cg[:, 0:128], cg[:, 128:256]
    zero = jnp.zeros_like(q01)
    heads = (
        (jnp.where(low, q01, zero), jnp.where(low, cg01, zero), 0, 128),
        (jnp.where(low, zero, q01), jnp.where(low, zero, cg01), 0, 128),
        (q_ref[0, :, 128:256], jnp.where(low, zero, cg2), 256, 256),
    )
    kds, vds, qds = [], [], []
    for h, (q, g, k_at, v_at) in enumerate(heads):
        pb16 = p_ref[0, 0, h]
        p = pb16.astype(F32)
        dp = dot_nt(kv_ref[0, :, v_at : v_at + 128], g)
        row = jnp.sum(p * dp, axis=0, keepdims=True)
        sg = (p * (dp - row)).astype(BF16)
        if own:
            tacc[h] += sg.astype(F32)
        kds.append(dot_nn(sg, q))
        vds.append(dot_nn(pb16, g))
        qds.append(dot_tn(kv_ref[0, :, k_at : k_at + 128], sg))
    kvd[:, 0:128] = (kds[0] + kds[1]).astype(BF16)
    kvd[:, 128:256] = (vds[0] + vds[1]).astype(BF16)
    kvd[:, 256:384] = (kds[2] + vds[2]).astype(BF16)
    qd01 = jnp.concatenate([qds[0][0:64], qds[1][64:128]], axis=0).T
    qd2 = jnp.concatenate([qds[2][0:64], jnp.zeros_like(qds[2][0:64])], axis=0).T
    qd = jnp.concatenate([qd01, qd2], axis=1).astype(BF16)
    qd_ref[...] = qd
    return dot_nt(kvd[...], a_of(slice(0, 384))), dot_nt(qd, a_of(slice(384, 640))) * 0.125


def backward_kernel(n_seq, length, n_dp, comm, *refs):
    half = length // 2
    n_hi = n_dp // 2
    step = pl.program_id(0)
    n_own = 2 * n_seq
    own = step < n_own
    b, g = lax.rem(step, n_own) // 2, 2 * (step // n_own) + lax.rem(step, 2)
    x_any, a_ref, kv_ref, q_ref, p_ref, ctx_any, ag_ref, pb_any = refs[:8]
    refs = refs[8:]
    if comm:
        gu_any, gd_any, gv_ref, half_ref = refs[:4]
        out_any, tok_any, up_out, down_out, a_out, gv_out, sm_out = refs[4:11]
        refs = refs[11:]
    else:
        tok_out, ga_ref, sm_ref = refs[:3]
        refs = refs[3:]
    kvd, qd_all, tacc, tok, pool, x_ref, ctx_ref, pb_ref, fetch = refs[:9]
    refs = refs[9:]
    core = my_core()
    n_tok = n_seq * length
    late = (
        pltpu.make_async_copy(x_any.at[pl.ds(pl.multiple_of(core * n_tok, n_tok), n_tok), :], x_ref, fetch.at[0]),
        pltpu.make_async_copy(ctx_any.at[0:2], ctx_ref, fetch.at[1]),
        pltpu.make_async_copy(pb_any, pb_ref, fetch.at[2]),
    )
    last = step == 2 * n_own - 1

    def at(n, *actions):
        @pl.when(step == n)
        def _():
            for action in actions:
                action()

    if comm:
        ga_ref, sm_ref, gu_mine, gd_mine, stage = refs[:5]
        net = Net(n_hi)
        other = 1 - core
        up = Scatter(net, gu_mine, gu_any.at[other], refs[5:13])
        down = Scatter(net, gd_mine, gd_any.at[other], refs[13:21])
        att = Scatter(net, ga_ref.at[core], ga_ref.at[other], refs[21:29])
        vec = SmallSum(net, gv_ref, gv_ref, refs[29:36])
        small = SmallSum(net, sm_ref.at[core], sm_ref.at[other], refs[36:43])
        o_sem, t_sem = refs[43:45]
        n_rows = n_seq * half
        there = out_any.at[pl.ds(pl.multiple_of(core * n_rows, n_rows), n_rows), :]
        o_copies = (
            pltpu.make_async_copy(half_ref, there, o_sem.at[0]),
            net.remote(half_ref, there, o_sem.at[1], o_sem.at[2], net.to_c),
        )
        mine = (
            pltpu.make_async_copy(gu_any.at[core], gu_mine, fetch.at[3]),
            pltpu.make_async_copy(gd_any.at[core], gd_mine, fetch.at[4]),
        )

        def tok_copies(i):
            row = pl.multiple_of((core * n_seq + i) * length, length)
            where = tok_any.at[pl.ds(row, length), :]
            return (
                pltpu.make_async_copy(stage.at[i], where, t_sem.at[0, i]),
                net.remote(stage.at[i], where, t_sem.at[1, i], t_sem.at[2, i], net.to_c),
            )

        @pl.when(step == 0)
        def _():
            for copy in mine:
                copy.start()
            net.greet()
            vec.over_core().start()
            up.over_core().start()
            down.over_core().start()
            for copy in o_copies:
                copy.start()

        at(1, vec.core_to_x)
        at(2, mine[0].wait, up.core_to_x, mine[1].wait, down.core_to_x)
        at(4, lambda: up.x_to_z(0))
        at(6, lambda: up.x_to_z(1), vec.x_to_z)
        at(7, lambda: down.x_to_z(0))
        at(8, att.over_core().start, small.over_core().start)
        at(9, small.core_to_x, lambda: down.x_to_z(1), att.core_to_x)
        at(13, lambda: att.x_to_z(0))
        at(15, small.x_to_z)
    @pl.when(step == 0)
    def _():
        for copy in late:
            copy.start()

    krows = pl.ds(pl.multiple_of(b * length, length), length)
    qrows = pl.ds(pl.multiple_of(b * half, half), half)

    def run(is_own):
        gg = lax.rem(g, 2) if is_own else 0
        kv_at, q_at = (kvd.at[gg, krows], qd_all.at[gg, qrows]) if is_own else (kvd.at[0, krows], qd_all.at[0, qrows])
        return backward_step(
            half,
            is_own,
            (kv_ref, q_ref, p_ref, ag_ref[qrows, :], lambda lanes: a_ref[g, :, lanes],
             tacc.at[gg] if is_own else None, kv_at, q_at),
        )

    @pl.when(own)
    def _():
        @pl.when(b == 0)
        def _():
            tacc[g] = jnp.zeros_like(tacc[g])

        tok_add, pool_add = run(True)

        @pl.when(g == 0)
        def _():
            tok[krows, :] = tok_add
            pool[qrows, :] = pool_add

        @pl.when(g == 1)
        def _():
            tok[krows, :] += tok_add
            pool[qrows, :] += pool_add

        @pl.when(step == n_own - 2)
        def _():
            for copy in late:
                copy.wait()

        @pl.when(b == n_seq - 1)
        def _():
            def store(lanes, v):
                v = v.astype(BF16)
                ga_ref[g, ..., lanes] = v.reshape(ga_ref.shape[1:-1] + v.shape[-1:])

            store(slice(0, 384), dot_tn(x_ref[...], kvd[g]))
            gq = dot_tn(pb_ref[...], qd_all[g]) * 0.125
            go = dot_tn(ag_ref[...], ctx_ref[g])
            store(slice(384, 512), gq[:, 0:128])
            store(slice(512, 640), gq[:, 128:256] + go[:, 0:128])
            store(slice(640, 768), go[:, 128:256])
            sm_ref[g, 3:8, :] = jnp.zeros((5, 2 * length), F32)
            sm_ref[g, 3:4, 0:384] = jnp.sum(kvd[g].astype(F32), axis=0, keepdims=True)
            i = lax.broadcasted_iota(jnp.int32, (half, half), 0)
            j = lax.broadcasted_iota(jnp.int32, (half, half), 1)
            flip = jnp.where(i + j == half - 1, 1.0, 0.0).astype(BF16)
            for h in range(3):
                high = tacc[g, h].astype(BF16)
                rest = (tacc[g, h] - high.astype(F32)).astype(BF16)
                turned = dot_nt(flip, high) + dot_nt(flip, rest)
                wide = jnp.concatenate([turned, jnp.zeros((half, length), F32)], axis=1)
                rolled = pltpu.roll(wide, 2, 1, stride=2, stride_axis=0)
                sm_ref[g, h : h + 1, :] = jnp.sum(rolled, axis=0, keepdims=True)

    @pl.when(jnp.logical_not(own))
    def _():
        tok_add, pool_add = run(False)

        @pl.when(g == 2)
        def _():
            tok[krows, :] += tok_add
            pool[qrows, :] += pool_add

        @pl.when(g == 3)
        def _():
            total = (pool[qrows, :] + pool_add + ag_ref[qrows, :].astype(F32)).astype(BF16)
            final = (tok[krows, :] + tok_add + dot_tn(pool_matrix(half, length), total)).astype(BF16)
            if comm:
                stage[b] = final
                for copy in tok_copies(b):
                    copy.start()
            else:
                tok_out[...] = final

    if comm:

        @pl.when(last)
        def _():
            vec.finish(gv_out)
            att.x_to_z(1)
            up.finish(up_out)
            down.finish(down_out)
            small.finish(sm_out)
            att.finish(a_out)
            for each in (up, down, att):
                each.sent()
            for copy in o_copies:
                copy.wait()
            for i in range(n_seq):
                for copy in tok_copies(i):
                    copy.wait()


def fixed(shape, first=None):
    def index(*grid):
        head = 0 if first is None else first()
        return (head,) + (0,) * (len(shape) - 1)

    return pl.BlockSpec(shape, index, pipeline_mode=pl.Buffered(1))


ANY = pl.BlockSpec(memory_space=pl.ANY)


def attention_backward(tokens, a4, kv, q, p, ctx, ag, pb, gu, gd, gv, out_half, n_seq, n_dp, comm):
    length = kv.shape[1] // n_seq
    half = length // 2
    width = tokens.shape[1]
    n_tok, n_pool = n_seq * length, n_seq * half
    n_own = 2 * n_seq
    n_hi, rows = n_dp // 2, width // n_dp

    def place(n):
        return 2 * (n // n_own) + lax.rem(n, 2), lax.rem(n, n_own) // 2

    in_specs = [
        ANY,
        fixed((4, width, 768)),
        pl.BlockSpec((1, length, 384), lambda n: place(n) + (0,)),
        pl.BlockSpec((1, half, 256), lambda n: place(n) + (0,)),
        pl.BlockSpec((1, 1, 3, length, half), lambda n: place(n) + (0, 0, 0)),
        ANY,
        fixed((n_pool, width)),
        ANY,
    ]
    args = [tokens, a4, kv, q, p, ctx, ag, pb]
    scratch = [
        pltpu.VMEM((2, n_tok, 384), BF16), pltpu.VMEM((2, n_pool, 256), BF16), pltpu.VMEM((2, 3, length, half), F32),
        pltpu.VMEM((n_tok, width), F32), pltpu.VMEM((n_pool, width), F32),
        pltpu.VMEM((n_tok, width), BF16), pltpu.VMEM((2, n_pool, 256), BF16), pltpu.VMEM((n_pool, width), BF16),
        pltpu.SemaphoreType.DMA((5,)),
    ]
    params = {"vmem_limit_bytes": VMEM_LIMIT}
    small = (8, 2 * length)
    if comm:
        split = (2, n_hi, 2, rows, width)
        in_specs += [ANY, ANY, fixed(gv.shape), fixed(out_half.shape)]
        args += [gu.reshape(split), gd.reshape(split), gv, out_half]
        shares = [jax.ShapeDtypeStruct((rows, width), F32)] * 3
        out_shape = [
            jax.ShapeDtypeStruct((2 * n_pool, width), BF16), jax.ShapeDtypeStruct((2 * n_tok, width), BF16), *shares,
            jax.ShapeDtypeStruct(gv.shape, F32), jax.ShapeDtypeStruct(small, F32),
        ]
        out_specs = [ANY, ANY] + [fixed((rows, width))] * 3 + [fixed(gv.shape), fixed(small)]
        scratch += [
            pltpu.VMEM(split, BF16), pltpu.VMEM((2,) + small, F32), pltpu.VMEM(split[1:], BF16),
            pltpu.VMEM(split[1:], BF16), pltpu.VMEM((n_seq, length, width), BF16),
        ]
        for _ in range(3):
            scratch += Scatter.scratch(n_hi, rows, width)
        scratch += SmallSum.scratch(n_hi, gv.shape) + SmallSum.scratch(n_hi, small)
        scratch += [pltpu.SemaphoreType.DMA((3,)), pltpu.SemaphoreType.DMA((3, n_seq))]
        params.update(collective_id=1, has_side_effects=True)
    else:
        out_shape = [
            jax.ShapeDtypeStruct((n_tok, width), BF16), jax.ShapeDtypeStruct((2, width, 768), BF16),
            jax.ShapeDtypeStruct((2,) + small, F32),
        ]
        out_specs = [
            pl.BlockSpec((length, width), lambda n: (jnp.maximum(n - n_own, 0) // 2, 0)), fixed((2, width, 768)),
            fixed((2,) + small),
        ]
    return pl.pallas_call(
        functools.partial(backward_kernel, n_seq, length, n_dp, comm),
        out_shape=out_shape,
        grid=(2 * n_own,),
        in_specs=in_specs,
        out_specs=out_specs,
        scratch_shapes=scratch,
        compiler_params=pltpu.CompilerParams(**params),
        cost_estimate=pl.CostEstimate(flops=40 * 10**9, bytes_accessed=30 * 10**6, transcendentals=0),
    )(*args)


def unpack(a_sum):
    key = jnp.concatenate([a_sum[:, 0:128], a_sum[:, 256:320]], axis=1)
    value = jnp.concatenate([a_sum[:, 128:256], a_sum[:, 320:384]], axis=1)
    out = jnp.concatenate([a_sum[:, 640:768], a_sum[:, 576:640]], axis=1).T
    return a_sum[:, 384:576], key, value, out


def gather_plain(weights, length):
    kw, vw, qw, ow, uw, dw, tab, vbias, hbias = weights
    ot = ow.T
    packed = jnp.concatenate([kw[:, :128], vw[:, :128], kw[:, 128:], vw[:, 128:], qw, ot[:, 128:], ot[:, :128]], axis=1)
    small = jnp.zeros((8, 2 * length), F32).at[0:3].set(tab).at[3, 128:256].set(vbias[0, :128])
    small = small.at[3, 320:384].set(vbias[0, 128:]).at[4, : hbias.shape[1]].set(hbias[0])
    first = 2 * (lax.axis_index("tensor") // 2)

    def groups(v):
        every = lax.all_gather(v, "tensor")
        return lax.dynamic_slice_in_dim(jnp.concatenate([every, every]), first, 4)

    wide = jnp.stack([packed, uw, dw.T], axis=1).astype(BF16)
    wide = groups(lax.all_gather(wide, "dp", axis=0, tiled=True))
    return wide[:, :, 0], wide[:, :, 1], wide[:, :, 2], groups(small)


def sum_plain(grads, n_dp):
    core = my_core()
    mine = lax.dynamic_index_in_dim(grads, core, 0, keepdims=False).astype(F32)
    other = lax.dynamic_index_in_dim(grads, 1 - core, 0, keepdims=False)
    total = mine + lax.ppermute(other, "tensor", [(i, i ^ 1) for i in range(4)]).astype(F32)
    return lax.psum_scatter(total, "dp", scatter_dimension=0, tiled=True)


def shards(
    n_dp, tokens, lengths, cotangent, query_weight, key_weight, value_weight, value_bias, output_weight,
    b_out, rel_table, norm_gain, norm_shift, up_weight, hidden_bias, down_weight, b_down, final_gain, final_shift,
):
    seq_count = lengths.shape[0]
    length = tokens.shape[0] // seq_count
    half = length // 2
    n_seq = seq_count // 2
    core = my_core()
    n_hi, rows = n_dp // 2, tokens.shape[1] // n_dp
    comm = rows % 16 == 0 and n_hi <= 4

    weights = (
        key_weight, value_weight, query_weight, output_weight, up_weight, down_weight, rel_table,
        value_bias[None], hidden_bias[None],
    )
    if not comm:
        weights = gather_plain(weights, length)
        a4, u4, d4, s4 = weights
        weights = (a4, s4)
    kv, q, p, ctx, hid, pb, *gathered = attention_forward(lengths, tokens, b_out[None], weights, n_dp, comm)
    if comm:
        a4, u4, d4, s4 = gathered
    vectors = jnp.stack([norm_gain, norm_shift, b_down, final_gain, final_shift])
    out_half, ag, gu, gd, gv = ffn(lengths, hid, cotangent, u4, d4, s4, vectors, n_seq, half)
    sums = attention_backward(tokens, a4, kv, q, p, ctx, ag, pb, gu, gd, gv, out_half, n_seq, n_dp, comm)
    if comm:
        output, tokens_grad, up_sum, down_sum, a_sum, gv, sm = sums
    else:
        tok_half, ga, sm = sums
        up_sum, down_sum, a_sum = (sum_plain(v, n_dp) for v in (gu, gd, ga))
        sm, gv = lax.psum((sm, gv), "dp")

        def over_core(v):
            return lax.ppermute(v, "tensor", [(i, i ^ 1) for i in range(4)])

        gv = gv + over_core(gv)
        mine = lax.dynamic_index_in_dim(sm, core, 0, keepdims=False)
        sm = mine + over_core(lax.dynamic_index_in_dim(sm, 1 - core, 0, keepdims=False))

        def join(part):
            got = over_core(part)
            return jnp.where(core == 0, jnp.concatenate([part, got]), jnp.concatenate([got, part]))

        output, tokens_grad = join(out_half), join(tok_half)
    query_sum, key_sum, value_sum, outw_sum = unpack(a_sum)
    vbias_sum = jnp.concatenate([sm[3, 128:256], sm[3, 320:384]])
    ubias_sum = lax.dynamic_index_in_dim(gv[6:8], core, 0, keepdims=False)
    return (
        output, tokens_grad, query_sum, key_sum, value_sum, vbias_sum, outw_sum, gv[5], sm[0:3],
        gv[3], gv[4], up_sum, ubias_sum, down_sum.T, gv[2], gv[0], gv[1],
    )


def solution(mesh):
    row, col, both, rep = P("dp", None), P("tensor", "dp"), P("dp", "tensor"), P()
    ten, table = P("tensor"), P("tensor", None)
    in_specs = (
        row, P("dp"), row, both, both, both, ten, col, rep, table, rep, rep, both, ten, col, rep, rep, rep,
    )
    out_specs = (
        row, row, both, both, both, ten, col, rep, table, rep, rep, both, ten, col, rep, rep, rep,
    )
    body = functools.partial(shards, mesh.shape["dp"])
    return jax.shard_map(body, mesh=mesh, in_specs=in_specs, out_specs=out_specs, check_vma=False)
```

```python
import functools

import jax
import jax.numpy as jnp
from jax import lax
from jax.experimental import pallas as pl
from jax.experimental.pallas import tpu as pltpu
from jax.sharding import PartitionSpec as P

MESH = pl.DeviceIdType.MESH
F32 = jnp.float32
BF16 = jnp.bfloat16
EPS = 1e-06
VMEM_LIMIT = 58 * 2**20


def dot_nn(a, b):
    return lax.dot_general(a, b, (((1,), (0,)), ((), ())), preferred_element_type=F32)


def dot_nt(a, b):
    return lax.dot_general(a, b, (((1,), (1,)), ((), ())), preferred_element_type=F32)


def dot_tn(a, b):
    return lax.dot_general(a, b, (((0,), (0,)), ((), ())), preferred_element_type=F32)


class Gather:
    def __init__(self, n_hi, ins, outs, s_in, s_out, sems):
        self.n_hi, self.ins, self.outs, self.s_in, self.s_out = n_hi, ins, outs, s_in, s_out
        self.loc, self.zs, self.zr, self.ls, self.lr, self.fs, self.fr, self.cs, self.cr, self.ss, self.sr = sems
        self.dp, self.t = lax.axis_index("dp"), lax.axis_index("tensor")
        self.hi, self.lo = self.dp // 2, lax.rem(self.dp, 2)
        self.core = lax.rem(self.t, 2)
        t_core = self.t + 1 - 2 * self.core
        self.to_x = (self.dp + 1 - 2 * self.lo, self.t)
        self.to_y = (self.dp, lax.rem(self.t + 2, 4))
        self.to_c = (self.dp, t_core)
        self.to_d = (self.dp, lax.rem(t_core + 2, 4))

    def block(self, s, side):
        return lax.rem(self.hi - s + self.n_hi, self.n_hi) * 2 + side

    def greet(self):
        barrier = pltpu.get_barrier_semaphore()
        for up, exists in ((0, self.hi < self.n_hi - 1), (1, self.hi > 0)):

            @pl.when(exists)
            def _():
                pl.semaphore_signal(barrier, inc=1, device_id=self.z_next(up), device_id_type=MESH)

        for peer in (self.to_x, self.to_y, self.to_c, self.to_d):
            pl.semaphore_signal(barrier, inc=1, device_id=peer, device_id_type=MESH)
        along_z = jnp.where(self.hi < self.n_hi - 1, 1, 0) + jnp.where(self.hi > 0, 1, 0)
        pl.semaphore_wait(barrier, 4 + along_z)

    def z_next(self, down):
        hi = jnp.maximum(self.hi - 1, 0) if down else jnp.minimum(self.hi + 1, self.n_hi - 1)
        return (hi * 2 + self.lo, self.t)

    def remote(self, src, dst, send, recv, peer):
        return pltpu.make_async_remote_copy(src, dst, send, recv, device_id=peer, device_id_type=MESH)

    def small(self):
        core = self.core
        return (
            pltpu.make_async_copy(self.s_in, self.s_out.at[core], self.loc.at[3]),
            self.remote(self.s_in, self.s_out.at[core], self.ss.at[0], self.sr.at[0], self.to_c),
            self.remote(self.s_in, self.s_out.at[2 + core], self.ss.at[1], self.sr.at[1], self.to_y),
            self.remote(self.s_in, self.s_out.at[2 + core], self.ss.at[2], self.sr.at[2], self.to_d),
        )

    def local(self, k):
        return pltpu.make_async_copy(self.ins[k], self.outs[k].at[self.core, self.dp], self.loc.at[k])

    def z_send(self, k, d, down):
        b = self.block(self.n_hi - d if down else d, self.lo)
        dst = self.outs[k].at[self.core, b]
        src = self.ins[k] if d == 0 else dst
        return self.remote(src, dst, self.zs.at[down, k, d], self.zr.at[down, k, d], self.z_next(down))

    def z_more(self, down):
        return self.hi > 0 if down else self.hi < self.n_hi - 1

    def z_came(self, d, down):
        return self.hi + d < self.n_hi if down else self.hi >= d

    def line(self, k, s, way, own=False):
        out, b = self.outs[k], self.block(s, self.lo)
        src = self.ins[k] if own else out.at[self.core, b]
        dst = out.at[self.core if way == 0 else 2 + self.core, b]
        return self.remote(
            src, dst, self.ls.at[way, k, s], self.lr.at[way, k, s], self.to_x if way == 0 else self.to_y
        )

    def onward(self, k, s, way):
        out = self.outs[k]
        if way == 0:
            src = dst = out.at[2 + self.core, self.block(s, self.lo)]
        else:
            b = self.block(s, 1 - self.lo)
            src, dst = out.at[self.core, b], out.at[2 + self.core, b]
        return self.remote(src, dst, self.fs.at[k, s], self.fr.at[k, s], self.to_x if way == 0 else self.to_y)

    def to_core(self, k, s, which, own=False):
        out = self.outs[k]
        side = self.lo if which % 2 == 0 else 1 - self.lo
        where = out.at[self.core if which < 2 else 2 + self.core, self.block(s, side)]
        return self.remote(
            self.ins[k] if own else where, where, self.cs.at[which, k, s], self.cr.at[which, k, s], self.to_c
        )

    def start(self, k):
        for down in range(2):
            pl.when(self.z_more(down))(lambda: self.z_send(k, 0, down).start())
        self.line(k, 0, 0, True).start()
        if k == 0:
            self.line(k, 0, 1, True).start()
        self.to_core(k, 0, 0, True).start()
        self.local(k).start()

    def lines_y(self, k):
        for s in range(self.n_hi):
            self.line(k, s, 1, s == 0).start()

    def near(self, d, action):
        if d == 0:
            action(0)
            return
        pl.when(self.z_came(d, 0))(lambda: action(d))
        pl.when(self.z_came(d, 1))(lambda: action(self.n_hi - d))

    def spread(self, k, d):
        for down in range(2):

            @pl.when(self.z_came(d, down))
            def _():
                self.z_send(k, d - 1, down).wait_recv()
                if d < self.n_hi - 1:
                    pl.when(self.z_more(down))(lambda: self.z_send(k, d, down).start())
                s = self.n_hi - d if down else d
                self.line(k, s, 0).start()
                if k == 0:
                    self.line(k, s, 1).start()
                self.to_core(k, s, 0).start()

    def over_x(self, k, s):
        self.line(k, s, 0).wait_recv()
        self.onward(k, s, 1).start()
        self.to_core(k, s, 1).start()

    def over_y(self, k, s):
        self.line(k, s, 1).wait_recv()
        self.onward(k, s, 0).start()
        self.to_core(k, s, 2).start()

    def late_x(self, k, s):
        self.line(k, s, 0).wait_recv()
        self.to_core(k, s, 1).start()

    def late_y(self, k, s):
        self.line(k, s, 1).wait_recv()
        self.to_core(k, s, 2).start()

    def pass_on(self, k, d, core=None):
        if k == 2:
            way = (self.over_x, self.over_y)[core]
            pl.when(self.core == core)(lambda: self.near(d, lambda s: way(k, s)))
        else:
            way = (self.over_x, self.over_y)[k]
            self.near(d, lambda s: way(k, s))

    def late(self, k):
        for s in range(self.n_hi):
            if k == 2:
                pl.when(self.core == 0)(lambda: self.late_y(k, s))
                pl.when(self.core == 1)(lambda: self.late_x(k, s))
            else:
                (self.late_y, self.late_x)[k](k, s)

    def diagonal(self, k, s):
        self.onward(k, s, 0).wait_recv()
        self.to_core(k, s, 3).start()

    def arrived(self, k, whiches):
        for s in range(self.n_hi):
            for which in whiches:
                self.to_core(k, s, which).wait_recv()

    def sent(self, k):
        for down in range(2):
            for d in range(self.n_hi - 1):
                came = self.z_more(down) if d == 0 else jnp.logical_and(self.z_more(down), self.z_came(d, down))
                pl.when(came)(lambda: self.z_send(k, d, down).wait_send())
        for s in range(self.n_hi):
            self.line(k, s, 0).wait_send()
            self.line(k, s, 1).wait_send()
            self.onward(k, s, 0).wait_send()
            for which in range(4):
                self.to_core(k, s, which).wait_send()


def gather_scratch(n_hi):
    dma = pltpu.SemaphoreType.DMA
    return [
        dma((4,)), dma((2, 3, n_hi)), dma((2, 3, n_hi)), dma((2, 3, n_hi)), dma((2, 3, n_hi)), dma((3, n_hi)),
        dma((3, n_hi)), dma((4, 3, n_hi)), dma((4, 3, n_hi)), dma((3,)), dma((3,)),
    ]


def pool_matrix(pooled, length):
    i = lax.broadcasted_iota(jnp.int32, (pooled, length), 0)
    j = lax.broadcasted_iota(jnp.int32, (pooled, length), 1)
    return jnp.where(j // 2 == i, 0.5, 0.0).astype(BF16)


def lane_low(shape):
    return lax.broadcasted_iota(jnp.int32, shape, 1) < 64


def attention_kernel(n_seq, length, n_dp, comm, *refs):
    half = length // 2
    group, b = pl.program_id(0), pl.program_id(1)
    step = group * n_seq + b
    core = lax.rem(lax.axis_index("tensor"), 2)
    len_ref, x_any, bo_ref = refs[:3]
    refs = refs[3:]
    if comm:
        (kw, vw, qw, ow, uw, dw, tab, vbias, hbias) = refs[:9]
        kv_ref, q_ref, p_ref, ctx_ref, hid_ref, pb_ref, a_out, u_out, d_out, s_out = refs[9:19]
        bias, x_ref, x_sem, a_in, u_in, d_in, s_in, a_all, s_all, a_sem, s_sem = refs[19:30]
        net = Gather(n_dp // 2, (a_in, u_in, d_in), (a_all, u_out, d_out), s_in, s_all, refs[30:])
    else:
        a_ref, s_ref = refs[:2]
        kv_ref, q_ref, p_ref, ctx_ref, hid_ref, pb_ref, bias, x_ref, x_sem = refs[2:]
    n_tok = n_seq * length
    x_copy = pltpu.make_async_copy(x_any.at[pl.ds(pl.multiple_of(core * n_tok, n_tok), n_tok), :], x_ref, x_sem)

    def pool_rows():
        x_copy.wait()
        pool = pool_matrix(half, length)
        for i in range(n_seq):
            pooled = dot_nn(pool, x_ref[i * length : (i + 1) * length, :])
            hid_ref[i * half : (i + 1) * half, :] = pooled + bo_ref[...].reshape(1, -1)
            pb_ref[i * half : (i + 1) * half, :] = pooled.astype(BF16)

    if comm:

        def a_copy(g):
            return pltpu.make_async_copy(a_all.at[g], a_out.at[g], a_sem.at[g])

        s_copy = pltpu.make_async_copy(s_all, s_out, s_sem)

        @pl.when(step == 0)
        def _():
            x_copy.start()
            k, v, o = kw[...], vw[...], ow[...].T
            parts = (k[:, :128], v[:, :128], k[:, 128:], v[:, 128:], qw[...], o[:, 128:], o[:, :128])
            a_in[...] = jnp.concatenate(parts, axis=1).astype(BF16)
            s_in[...] = jnp.zeros_like(s_in)
            s_in[0:3, :] = tab[...]
            vb = vbias[...].reshape(1, -1)
            s_in[3:4, 128:256] = vb[:, 0:128]
            s_in[3:4, 320:384] = vb[:, 128:192]
            s_in[4:5, 0 : hbias.shape[0]] = hbias[...].reshape(1, -1)
            net.greet()
            for copy in net.small():
                copy.start()
            net.start(0)
            u_in[...] = uw[...].astype(BF16)
            d_in[...] = dw[...].astype(BF16)
            for s in range(1, n_dp // 2):
                net.spread(0, s)
                net.pass_on(0, s - 1)
            net.start(1)
            net.pass_on(0, n_dp // 2 - 1)
            pool_rows()
            small = net.small()
            small[0].wait()
            for copy in small[1:]:
                copy.wait()
            s_copy.start()
            net.local(0).wait()
            net.arrived(0, (0, 1))

        n_hi = n_dp // 2
        plan = {}

        def at(n, action, *args):
            plan.setdefault(min(n, 4 * n_seq - 1), []).append(functools.partial(action, *args))

        for d in range(1, n_hi):
            at((1, 2, 3)[d - 1], net.spread, 1, d)
            at((5, 6, 7)[d - 1], net.spread, 2, d)
        at(3, net.start, 2)
        at(4, net.late, 0)
        for d in range(n_hi):
            at(4, net.diagonal, 0, d)
            at((6, 7, 8, 9)[d], net.pass_on, 1, d)
            at((10, 10, 11, 11)[d], net.pass_on, 2, d, 0)
            at((11, 12, 13, 14)[d], net.pass_on, 2, d, 1)
            at((11, 12, 13, 13)[d], lambda i: net.near(i, lambda s: net.diagonal(1, s)), d)
        at(3, net.lines_y, 1)
        at(2 * n_seq, net.arrived, 0, (2, 3))
        for g in range(4):
            at(2 * n_seq, lambda i: a_copy(i).start(), g)
        at(7, net.lines_y, 2)
        at(9, net.late, 1)
        at(14, net.late, 2)
        for n, actions in plan.items():

            @pl.when(step == n)
            def _():
                for action in actions:
                    action()

        def weights(lanes):
            return a_all[group, :, :, lanes].reshape(-1, lanes.stop - lanes.start)

        def small_row(i):
            return s_all[group, i : i + 1, :]
    else:

        @pl.when(step == 0)
        def _():
            x_copy.start()
            pool_rows()

        def weights(lanes):
            return a_ref[0, :, lanes]

        def small_row(i):
            return s_ref[0, i : i + 1, :]

    krows = pl.ds(pl.multiple_of(b * length, length), length)
    qrows = pl.ds(pl.multiple_of(b * half, half), half)

    @pl.when(b == 0)
    def _():
        for h in range(3):
            wide = jnp.broadcast_to(small_row(h), (half, 2 * length))
            bias[h] = pltpu.roll(wide, length, 1, stride=2, stride_axis=0)[:, :length].T

    kv_ref[0] = (dot_nn(x_ref[krows, :], weights(slice(0, 384))) + small_row(3)[:, 0:384]).astype(BF16)
    q = dot_nn(pb_ref[qrows, :], weights(slice(384, 640))) * 0.125
    lanes = lax.broadcasted_iota(jnp.int32, q.shape, 1)
    q = jnp.where(lanes < 192, q, 0.0).astype(BF16)
    q_ref[0] = q
    low = lane_low((half, 128))
    valid = lax.broadcasted_iota(jnp.int32, (length, half), 0) < len_ref[core * n_seq + b]
    q01 = q[:, 0:128]
    zero = jnp.zeros_like(q01)
    heads = (
        (jnp.where(low, q01, zero), 0, 128),
        (jnp.where(low, zero, q01), 0, 128),
        (q[:, 128:256], 256, 256),
    )
    contexts = []
    for h, (qh, k_at, v_at) in enumerate(heads):
        s = dot_nt(kv_ref[0, :, k_at : k_at + 128], qh) + bias[h]
        s = jnp.where(valid, s, -1e30)
        e = jnp.exp(s - jnp.max(s, axis=0, keepdims=True))
        p = (e * (1.0 / jnp.sum(e, axis=0, keepdims=True))).astype(BF16)
        p_ref[0, 0, h] = p
        contexts.append(dot_tn(kv_ref[0, :, v_at : v_at + 128], p))
    c0, c1, c2 = contexts
    ctx01 = jnp.concatenate([c0[0:64], c1[64:128]], axis=0).T
    ctx2 = jnp.concatenate([jnp.zeros_like(c2[0:64]), c2[64:128]], axis=0).T
    ctx = jnp.concatenate([ctx2, ctx01], axis=1).astype(BF16)
    ctx_ref[0] = ctx
    hid_ref[qrows, :] += dot_nt(ctx, weights(slice(512, 768)))

    if comm:

        @pl.when(step == 4 * n_seq - 1)
        def _():
            for s in range(n_hi):
                net.diagonal(2, s)
            for k in range(3):
                net.sent(k)
            for k in (1, 2):
                net.local(k).wait()
                net.arrived(k, (0, 1, 2, 3))
            for g in range(4):
                a_copy(g).wait()
            s_copy.wait()


def my_core():
    return lax.rem(lax.axis_index("tensor"), 2)


def attention_forward(lengths, tokens, b_out, weights, n_dp, comm):
    n_seq = lengths.shape[0] // 2
    length = tokens.shape[0] // lengths.shape[0]
    half = length // 2
    width = tokens.shape[1]
    once = pl.Buffered(1)

    def fixed(shape):
        return pl.BlockSpec(shape, lambda g, b: (0,) * len(shape), pipeline_mode=once)

    in_specs = [
        pl.BlockSpec(memory_space=pltpu.SMEM),
        pl.BlockSpec(memory_space=pl.ANY),
        fixed((width,)),
    ]
    out_shape = [
        jax.ShapeDtypeStruct((4, n_seq * length, 384), BF16),
        jax.ShapeDtypeStruct((4, n_seq * half, 256), BF16),
        jax.ShapeDtypeStruct((4, n_seq, 3, length, half), BF16),
        jax.ShapeDtypeStruct((4, n_seq * half, 256), BF16),
        jax.ShapeDtypeStruct((n_seq * half, width), F32),
        jax.ShapeDtypeStruct((n_seq * half, width), BF16),
    ]
    out_specs = [
        pl.BlockSpec((1, length, 384), lambda g, b: (g, b, 0)),
        pl.BlockSpec((1, half, 256), lambda g, b: (g, b, 0)),
        pl.BlockSpec((1, 1, 3, length, half), lambda g, b: (g, b, 0, 0, 0)),
        pl.BlockSpec((1, half, 256), lambda g, b: (g, b, 0)),
        fixed((n_seq * half, width)),
        fixed((n_seq * half, width)),
    ]
    scratch = [
        pltpu.VMEM((3, length, half), F32), pltpu.VMEM((n_seq * length, width), BF16), pltpu.SemaphoreType.DMA,
    ]
    params = {"vmem_limit_bytes": VMEM_LIMIT}
    if comm:
        rows = width // n_dp
        in_specs += [fixed(w.shape) for w in weights]
        whole = jax.ShapeDtypeStruct((4, n_dp, rows, width), BF16)
        small = jax.ShapeDtypeStruct((4, 8, 2 * length), F32)
        out_shape += [whole, whole, whole, small]
        out_specs += [pl.BlockSpec(memory_space=pl.ANY)] * 4
        scratch += [pltpu.VMEM((rows, width), BF16)] * 3
        scratch += [
            pltpu.VMEM((8, 2 * length), F32),
            pltpu.VMEM((4, n_dp, rows, width), BF16),
            pltpu.VMEM((4, 8, 2 * length), F32),
            pltpu.SemaphoreType.DMA((4,)),
            pltpu.SemaphoreType.DMA,
        ]
        scratch += gather_scratch(n_dp // 2)
        params.update(collective_id=0, has_side_effects=True)
    else:
        in_specs += [
            pl.BlockSpec((1, width, 768), lambda g, b: (g, 0, 0)),
            pl.BlockSpec((1, 8, 2 * length), lambda g, b: (g, 0, 0)),
        ]
    outs = pl.pallas_call(
        functools.partial(attention_kernel, n_seq, length, n_dp, comm),
        out_shape=out_shape,
        grid=(4, n_seq),
        in_specs=in_specs,
        out_specs=out_specs,
        scratch_shapes=scratch,
        compiler_params=pltpu.CompilerParams(**params),
        cost_estimate=pl.CostEstimate(flops=20 * 10**9, bytes_accessed=40 * 10**6, transcendentals=6 * 10**6),
    )(lengths, tokens, b_out, *weights)
    if comm:
        flat = (4, width, width)
        outs = list(outs)
        outs = outs[:6] + [w.reshape(flat) for w in outs[6:9]] + outs[9:]
    return outs


def row_mean(v):
    return jnp.mean(v, axis=-1, keepdims=True)


def ffn_kernel(
    n_seq, half, len_ref, hid_ref, cot_ref, u_ref, d_ref, s_ref, v0, v1, v2, v3, v4,
    out_ref, ag_ref, gu_ref, gd_ref, gv_ref, nb_all, fg_all, act_all, pg_all, dg,
):
    b = pl.program_id(0)
    rows = pl.ds(pl.multiple_of(b * half, half), half)
    n_gain, n_shift, b_down, f_gain, f_shift = (v[...].reshape(1, -1) for v in (v0, v1, v2, v3, v4))

    @pl.when(b == 0)
    def _():
        gv_ref[...] = jnp.zeros_like(gv_ref)

    def add(i, v):
        gv_ref[i : i + 1, :] += jnp.sum(v, axis=0, keepdims=True)

    hid = hid_ref[...]
    centred = hid - row_mean(hid)
    inv1 = lax.rsqrt(row_mean(centred * centred) + EPS)
    unit1 = centred * inv1
    normed = unit1 * n_gain + n_shift
    nb = normed.astype(BF16)
    nb_all[rows, :] = nb
    summed = normed + b_down
    for t in range(4):
        pre = dot_nn(nb, u_ref[t]) + s_ref[t, 4:5, 0:768]
        cdf = 0.5 * (1.0 + lax.erf(pre * 0.7071067811865476))
        act = (pre * cdf).astype(BF16)
        dg[t] = cdf + pre * (0.3989422804014327 * jnp.exp(-0.5 * pre * pre))
        act_all[t, rows, :] = act
        summed = summed + dot_nt(act, d_ref[t])
    centred = summed - row_mean(summed)
    inv2 = lax.rsqrt(row_mean(centred * centred) + EPS)
    unit2 = centred * inv2
    valid = (2 * lax.broadcasted_iota(jnp.int32, (half, 1), 0) < len_ref[my_core() * n_seq + b]).astype(F32)
    out_ref[...] = ((unit2 * f_gain + f_shift) * valid).astype(BF16)
    grad = cot_ref[...].astype(F32) * valid
    add(0, grad * unit2)
    add(1, grad)
    scaled = grad * f_gain
    grad_summed = inv2 * (scaled - row_mean(scaled) - unit2 * row_mean(scaled * unit2))
    add(2, grad_summed)
    fg = grad_summed.astype(BF16)
    fg_all[rows, :] = fg
    normed_grad = grad_summed
    for t in range(4):
        pg = (dot_nn(fg, d_ref[t]) * dg[t]).astype(BF16)
        pg_all[t, rows, :] = pg
        normed_grad = normed_grad + dot_nt(pg, u_ref[t])
    add(3, normed_grad * unit1)
    add(4, normed_grad)
    scaled = normed_grad * n_gain
    hidden_grad = inv1 * (scaled - row_mean(scaled) - unit1 * row_mean(scaled * unit1))
    add(5, hidden_grad)
    ag_ref[...] = hidden_grad.astype(BF16)

    @pl.when(b == n_seq - 1)
    def _():
        for i in range(2):
            pg = pg_all[i]
            gu_ref[i] = dot_tn(nb_all[...], pg).astype(BF16)
            gd_ref[i] = dot_tn(fg_all[...], act_all[i]).astype(BF16)
            gv_ref[6 + i : 7 + i, :] = jnp.sum(pg.astype(F32), axis=0, keepdims=True)


def ffn(lengths, hid, cotangent, u4, d4, s4, vectors, n_seq, half):
    width = hid.shape[1]
    once = pl.Buffered(1)
    return pl.pallas_call(
        functools.partial(ffn_kernel, n_seq, half),
        out_shape=(
            jax.ShapeDtypeStruct((n_seq * half, width), BF16),
            jax.ShapeDtypeStruct((n_seq * half, width), BF16),
            jax.ShapeDtypeStruct((2, width, 768), BF16),
            jax.ShapeDtypeStruct((2, width, 768), BF16),
            jax.ShapeDtypeStruct((8, width), F32),
        ),
        grid=(n_seq,),
        in_specs=[
            pl.BlockSpec(memory_space=pltpu.SMEM),
            pl.BlockSpec((half, width), lambda b: (b, 0)),
            pl.BlockSpec((half, width), lambda b: (my_core() * n_seq + b, 0)),
            pl.BlockSpec((4, width, 768), lambda b: (0, 0, 0), pipeline_mode=once),
            pl.BlockSpec((4, width, 768), lambda b: (0, 0, 0), pipeline_mode=once),
            pl.BlockSpec(s4.shape, lambda b: (0, 0, 0), pipeline_mode=once),
        ]
        + [pl.BlockSpec((width,), lambda b: (0,), pipeline_mode=once)] * 5,
        out_specs=[
            pl.BlockSpec((half, width), lambda b: (b, 0)),
            pl.BlockSpec((half, width), lambda b: (b, 0)),
            pl.BlockSpec((2, width, 768), lambda b: (0, 0, 0), pipeline_mode=once),
            pl.BlockSpec((2, width, 768), lambda b: (0, 0, 0), pipeline_mode=once),
            pl.BlockSpec((8, width), lambda b: (0, 0), pipeline_mode=once),
        ],
        scratch_shapes=[
            pltpu.VMEM((n_seq * half, width), BF16),
            pltpu.VMEM((n_seq * half, width), BF16),
            pltpu.VMEM((4, n_seq * half, 768), BF16),
            pltpu.VMEM((4, n_seq * half, 768), BF16),
            pltpu.VMEM((4, half, 768), F32),
        ],
        compiler_params=pltpu.CompilerParams(vmem_limit_bytes=VMEM_LIMIT),
        cost_estimate=pl.CostEstimate(flops=24 * 10**9, bytes_accessed=30 * 10**6, transcendentals=6 * 10**6),
    )(lengths, hid, cotangent, u4, d4, s4, *vectors)


class Net:
    def __init__(self, n_hi):
        self.n_hi = n_hi
        self.dp, self.t = lax.axis_index("dp"), lax.axis_index("tensor")
        self.hi, self.lo = self.dp // 2, lax.rem(self.dp, 2)
        self.core = lax.rem(self.t, 2)
        self.to_x = (self.dp + 1 - 2 * self.lo, self.t)
        self.to_c = (self.dp, self.t + 1 - 2 * self.core)

    def place(self, s):
        return lax.rem(self.hi + s, self.n_hi)

    def z_peer(self, s):
        return (self.place(s) * 2 + self.lo, self.t)

    def greet(self):
        barrier = pltpu.get_barrier_semaphore()
        peers = [self.z_peer(s) for s in range(1, self.n_hi)] + [self.to_x, self.to_c]
        for peer in peers:
            pl.semaphore_signal(barrier, inc=1, device_id=peer, device_id_type=MESH)
        pl.semaphore_wait(barrier, len(peers))

    def remote(self, src, dst, send, recv, peer):
        return pltpu.make_async_remote_copy(src, dst, send, recv, device_id=peer, device_id_type=MESH)


class Scatter:
    PARTS = 2

    def __init__(self, net, mine, other, bufs):
        self.net, self.mine, self.other = net, mine, other
        self.t1, self.t2, self.r3, self.sem, self.xs, self.xr, self.zs, self.zr = bufs
        self.rows = self.t2.shape[1] // self.PARTS

    @staticmethod
    def scratch(n_hi, rows, width):
        dma = pltpu.SemaphoreType.DMA
        both, half = pltpu.VMEM((n_hi, 2, rows, width), BF16), pltpu.VMEM((n_hi, rows, width), BF16)
        parts = Scatter.PARTS
        return [both, half, half, dma((2,)), dma((parts,)), dma((parts,)), dma((parts, n_hi)), dma((parts, n_hi))]

    def part(self, i):
        return pl.ds(i * self.rows, self.rows)

    def over_core(self):
        return self.net.remote(self.other, self.t1, self.sem.at[0], self.sem.at[1], self.net.to_c)

    def over_x(self, i):
        src = self.t1.at[:, 1 - self.net.lo, self.part(i)]
        return self.net.remote(src, self.t2.at[:, self.part(i)], self.xs.at[i], self.xr.at[i], self.net.to_x)

    def over_z(self, i, s):
        src = self.t2.at[self.net.place(s), self.part(i)]
        dst = self.r3.at[s, self.part(i)]
        return self.net.remote(src, dst, self.zs.at[i, s], self.zr.at[i, s], self.net.z_peer(s))

    def core_to_x(self):
        self.over_core().wait_recv()
        self.t1[...] += self.mine[...]
        for i in range(self.PARTS):
            self.over_x(i).start()

    def x_to_z(self, i):
        self.over_x(i).wait_recv()
        rows = self.part(i)
        self.t2[:, rows] += self.t1[:, self.net.lo, rows]
        for s in range(1, self.net.n_hi):
            self.over_z(i, s).start()

    def finish(self, out):
        for i in range(self.PARTS):
            rows = self.part(i)
            total = self.t2[self.net.hi, rows].astype(F32)
            for s in range(1, self.net.n_hi):
                self.over_z(i, s).wait_recv()
                total += self.r3[s, rows].astype(F32)
            out[rows, :] = total

    def sent(self):
        self.over_core().wait_send()
        for i in range(self.PARTS):
            self.over_x(i).wait_send()
            for s in range(1, self.net.n_hi):
                self.over_z(i, s).wait_send()


class SmallSum:
    def __init__(self, net, mine, other, bufs):
        self.net, self.mine, self.other = net, mine, other
        self.rc, self.v1, self.rx, self.v2, self.sem, self.zs, self.zr = bufs

    @staticmethod
    def scratch(n_hi, shape):
        dma = pltpu.SemaphoreType.DMA
        return [
            pltpu.VMEM(shape, F32), pltpu.VMEM(shape, F32), pltpu.VMEM(shape, F32), pltpu.VMEM((n_hi,) + shape, F32),
            dma((4,)), dma((n_hi,)), dma((n_hi,)),
        ]

    def over_core(self):
        return self.net.remote(self.other, self.rc, self.sem.at[0], self.sem.at[1], self.net.to_c)

    def over_x(self):
        return self.net.remote(self.v1, self.rx, self.sem.at[2], self.sem.at[3], self.net.to_x)

    def over_z(self, s):
        here = self.v2.at[self.net.hi]
        return self.net.remote(here, here, self.zs.at[s], self.zr.at[s], self.net.z_peer(s))

    def core_to_x(self):
        self.over_core().wait_recv()
        self.v1[...] = self.mine[...] + self.rc[...]
        self.over_x().start()

    def x_to_z(self):
        self.over_x().wait_recv()
        self.v2[self.net.hi] = self.v1[...] + self.rx[...]
        for s in range(1, self.net.n_hi):
            self.over_z(s).start()

    def finish(self, out):
        for s in range(1, self.net.n_hi):
            self.over_z(s).wait()
        out[...] = jnp.sum(self.v2[...], axis=0)
        self.over_core().wait_send()
        self.over_x().wait_send()

def backward_step(half, own, step_refs):
    kv_ref, q_ref, p_ref, ag, a_of, tacc, kvd, qd_ref = step_refs
    low = lane_low((half, 128))
    cg = dot_nn(ag, a_of(slice(512, 768))).astype(BF16)
    q01 = q_ref[0, :, 0:128]
    cg2, cg01 = cg[:, 0:128], cg[:, 128:256]
    zero = jnp.zeros_like(q01)
    heads = (
        (jnp.where(low, q01, zero), jnp.where(low, cg01, zero), 0, 128),
        (jnp.where(low, zero, q01), jnp.where(low, zero, cg01), 0, 128),
        (q_ref[0, :, 128:256], jnp.where(low, zero, cg2), 256, 256),
    )
    kds, vds, qds = [], [], []
    for h, (q, g, k_at, v_at) in enumerate(heads):
        pb16 = p_ref[0, 0, h]
        p = pb16.astype(F32)
        dp = dot_nt(kv_ref[0, :, v_at : v_at + 128], g)
        row = jnp.sum(p * dp, axis=0, keepdims=True)
        sg = (p * (dp - row)).astype(BF16)
        if own:
            tacc[h] += sg.astype(F32)
        kds.append(dot_nn(sg, q))
        vds.append(dot_nn(pb16, g))
        qds.append(dot_tn(kv_ref[0, :, k_at : k_at + 128], sg))
    kvd[:, 0:128] = (kds[0] + kds[1]).astype(BF16)
    kvd[:, 128:256] = (vds[0] + vds[1]).astype(BF16)
    kvd[:, 256:384] = (kds[2] + vds[2]).astype(BF16)
    qd01 = jnp.concatenate([qds[0][0:64], qds[1][64:128]], axis=0).T
    qd2 = jnp.concatenate([qds[2][0:64], jnp.zeros_like(qds[2][0:64])], axis=0).T
    qd = jnp.concatenate([qd01, qd2], axis=1).astype(BF16)
    qd_ref[...] = qd
    return dot_nt(kvd[...], a_of(slice(0, 384))), dot_nt(qd, a_of(slice(384, 640))) * 0.125


def backward_kernel(n_seq, length, n_dp, comm, *refs):
    half = length // 2
    n_hi = n_dp // 2
    step = pl.program_id(0)
    n_own = 2 * n_seq
    own = step < n_own
    b, g = lax.rem(step, n_own) // 2, 2 * (step // n_own) + lax.rem(step, 2)
    x_any, a_ref, kv_ref, q_ref, p_ref, ctx_any, ag_ref, pb_any = refs[:8]
    refs = refs[8:]
    if comm:
        gu_any, gd_any, gv_ref, half_ref = refs[:4]
        out_any, tok_any, up_out, down_out, a_out, gv_out, sm_out = refs[4:11]
        refs = refs[11:]
    else:
        tok_out, ga_ref, sm_ref = refs[:3]
        refs = refs[3:]
    kvd, qd_all, tacc, tok, pool, x_ref, ctx_ref, pb_ref, fetch = refs[:9]
    refs = refs[9:]
    core = my_core()
    n_tok = n_seq * length
    late = (
        pltpu.make_async_copy(x_any.at[pl.ds(pl.multiple_of(core * n_tok, n_tok), n_tok), :], x_ref, fetch.at[0]),
        pltpu.make_async_copy(ctx_any.at[0:2], ctx_ref, fetch.at[1]),
        pltpu.make_async_copy(pb_any, pb_ref, fetch.at[2]),
    )
    last = step == 2 * n_own - 1

    def at(n, *actions):
        @pl.when(step == n)
        def _():
            for action in actions:
                action()

    if comm:
        ga_ref, sm_ref, gu_mine, gd_mine, stage = refs[:5]
        net = Net(n_hi)
        other = 1 - core
        up = Scatter(net, gu_mine, gu_any.at[other], refs[5:13])
        down = Scatter(net, gd_mine, gd_any.at[other], refs[13:21])
        att = Scatter(net, ga_ref.at[core], ga_ref.at[other], refs[21:29])
        vec = SmallSum(net, gv_ref, gv_ref, refs[29:36])
        small = SmallSum(net, sm_ref.at[core], sm_ref.at[other], refs[36:43])
        o_sem, t_sem = refs[43:45]
        n_rows = n_seq * half
        there = out_any.at[pl.ds(pl.multiple_of(core * n_rows, n_rows), n_rows), :]
        o_copies = (
            pltpu.make_async_copy(half_ref, there, o_sem.at[0]),
            net.remote(half_ref, there, o_sem.at[1], o_sem.at[2], net.to_c),
        )
        mine = (
            pltpu.make_async_copy(gu_any.at[core], gu_mine, fetch.at[3]),
            pltpu.make_async_copy(gd_any.at[core], gd_mine, fetch.at[4]),
        )

        def tok_copies(i):
            row = pl.multiple_of((core * n_seq + i) * length, length)
            where = tok_any.at[pl.ds(row, length), :]
            return (
                pltpu.make_async_copy(stage.at[i], where, t_sem.at[0, i]),
                net.remote(stage.at[i], where, t_sem.at[1, i], t_sem.at[2, i], net.to_c),
            )

        @pl.when(step == 0)
        def _():
            for copy in mine:
                copy.start()
            net.greet()
            vec.over_core().start()
            up.over_core().start()
            down.over_core().start()
            for copy in o_copies:
                copy.start()

        at(1, vec.core_to_x)
        at(2, mine[0].wait, up.core_to_x, mine[1].wait, down.core_to_x)
        at(4, lambda: up.x_to_z(0))
        at(6, lambda: up.x_to_z(1), vec.x_to_z)
        at(7, lambda: down.x_to_z(0))
        at(8, att.over_core().start, small.over_core().start)
        at(9, small.core_to_x, lambda: down.x_to_z(1), att.core_to_x)
        at(13, lambda: att.x_to_z(0))
        at(15, small.x_to_z)
    @pl.when(step == 0)
    def _():
        for copy in late:
            copy.start()

    krows = pl.ds(pl.multiple_of(b * length, length), length)
    qrows = pl.ds(pl.multiple_of(b * half, half), half)

    def run(is_own):
        gg = lax.rem(g, 2) if is_own else 0
        kv_at, q_at = (kvd.at[gg, krows], qd_all.at[gg, qrows]) if is_own else (kvd.at[0, krows], qd_all.at[0, qrows])
        return backward_step(
            half,
            is_own,
            (kv_ref, q_ref, p_ref, ag_ref[qrows, :], lambda lanes: a_ref[g, :, lanes],
             tacc.at[gg] if is_own else None, kv_at, q_at),
        )

    @pl.when(own)
    def _():
        @pl.when(b == 0)
        def _():
            tacc[g] = jnp.zeros_like(tacc[g])

        tok_add, pool_add = run(True)

        @pl.when(g == 0)
        def _():
            tok[krows, :] = tok_add
            pool[qrows, :] = pool_add

        @pl.when(g == 1)
        def _():
            tok[krows, :] += tok_add
            pool[qrows, :] += pool_add

        @pl.when(step == n_own - 2)
        def _():
            for copy in late:
                copy.wait()

        @pl.when(b == n_seq - 1)
        def _():
            def store(lanes, v):
                v = v.astype(BF16)
                ga_ref[g, ..., lanes] = v.reshape(ga_ref.shape[1:-1] + v.shape[-1:])

            store(slice(0, 384), dot_tn(x_ref[...], kvd[g]))
            gq = dot_tn(pb_ref[...], qd_all[g]) * 0.125
            go = dot_tn(ag_ref[...], ctx_ref[g])
            store(slice(384, 512), gq[:, 0:128])
            store(slice(512, 640), gq[:, 128:256] + go[:, 0:128])
            store(slice(640, 768), go[:, 128:256])
            sm_ref[g, 3:8, :] = jnp.zeros((5, 2 * length), F32)
            sm_ref[g, 3:4, 0:384] = jnp.sum(kvd[g].astype(F32), axis=0, keepdims=True)
            i = lax.broadcasted_iota(jnp.int32, (half, half), 0)
            j = lax.broadcasted_iota(jnp.int32, (half, half), 1)
            flip = jnp.where(i + j == half - 1, 1.0, 0.0).astype(BF16)
            for h in range(3):
                high = tacc[g, h].astype(BF16)
                rest = (tacc[g, h] - high.astype(F32)).astype(BF16)
                turned = dot_nt(flip, high) + dot_nt(flip, rest)
                wide = jnp.concatenate([turned, jnp.zeros((half, length), F32)], axis=1)
                rolled = pltpu.roll(wide, 2, 1, stride=2, stride_axis=0)
                sm_ref[g, h : h + 1, :] = jnp.sum(rolled, axis=0, keepdims=True)

    @pl.when(jnp.logical_not(own))
    def _():
        tok_add, pool_add = run(False)

        @pl.when(g == 2)
        def _():
            tok[krows, :] += tok_add
            pool[qrows, :] += pool_add

        @pl.when(g == 3)
        def _():
            total = (pool[qrows, :] + pool_add + ag_ref[qrows, :].astype(F32)).astype(BF16)
            final = (tok[krows, :] + tok_add + dot_tn(pool_matrix(half, length), total)).astype(BF16)
            if comm:
                stage[b] = final
                for copy in tok_copies(b):
                    copy.start()
            else:
                tok_out[...] = final

    if comm:

        @pl.when(last)
        def _():
            vec.finish(gv_out)
            att.x_to_z(1)
            up.finish(up_out)
            down.finish(down_out)
            small.finish(sm_out)
            att.finish(a_out)
            for each in (up, down, att):
                each.sent()
            for copy in o_copies:
                copy.wait()
            for i in range(n_seq):
                for copy in tok_copies(i):
                    copy.wait()


def fixed(shape, first=None):
    def index(*grid):
        head = 0 if first is None else first()
        return (head,) + (0,) * (len(shape) - 1)

    return pl.BlockSpec(shape, index, pipeline_mode=pl.Buffered(1))


ANY = pl.BlockSpec(memory_space=pl.ANY)


def attention_backward(tokens, a4, kv, q, p, ctx, ag, pb, gu, gd, gv, out_half, n_seq, n_dp, comm):
    length = kv.shape[1] // n_seq
    half = length // 2
    width = tokens.shape[1]
    n_tok, n_pool = n_seq * length, n_seq * half
    n_own = 2 * n_seq
    n_hi, rows = n_dp // 2, width // n_dp

    def place(n):
        return 2 * (n // n_own) + lax.rem(n, 2), lax.rem(n, n_own) // 2

    in_specs = [
        ANY,
        fixed((4, width, 768)),
        pl.BlockSpec((1, length, 384), lambda n: place(n) + (0,)),
        pl.BlockSpec((1, half, 256), lambda n: place(n) + (0,)),
        pl.BlockSpec((1, 1, 3, length, half), lambda n: place(n) + (0, 0, 0)),
        ANY,
        fixed((n_pool, width)),
        ANY,
    ]
    args = [tokens, a4, kv, q, p, ctx, ag, pb]
    scratch = [
        pltpu.VMEM((2, n_tok, 384), BF16), pltpu.VMEM((2, n_pool, 256), BF16), pltpu.VMEM((2, 3, length, half), F32),
        pltpu.VMEM((n_tok, width), F32), pltpu.VMEM((n_pool, width), F32),
        pltpu.VMEM((n_tok, width), BF16), pltpu.VMEM((2, n_pool, 256), BF16), pltpu.VMEM((n_pool, width), BF16),
        pltpu.SemaphoreType.DMA((5,)),
    ]
    params = {"vmem_limit_bytes": VMEM_LIMIT}
    small = (8, 2 * length)
    if comm:
        split = (2, n_hi, 2, rows, width)
        in_specs += [ANY, ANY, fixed(gv.shape), fixed(out_half.shape)]
        args += [gu.reshape(split), gd.reshape(split), gv, out_half]
        shares = [jax.ShapeDtypeStruct((rows, width), F32)] * 3
        out_shape = [
            jax.ShapeDtypeStruct((2 * n_pool, width), BF16), jax.ShapeDtypeStruct((2 * n_tok, width), BF16), *shares,
            jax.ShapeDtypeStruct(gv.shape, F32), jax.ShapeDtypeStruct(small, F32),
        ]
        out_specs = [ANY, ANY] + [fixed((rows, width))] * 3 + [fixed(gv.shape), fixed(small)]
        scratch += [
            pltpu.VMEM(split, BF16), pltpu.VMEM((2,) + small, F32), pltpu.VMEM(split[1:], BF16),
            pltpu.VMEM(split[1:], BF16), pltpu.VMEM((n_seq, length, width), BF16),
        ]
        for _ in range(3):
            scratch += Scatter.scratch(n_hi, rows, width)
        scratch += SmallSum.scratch(n_hi, gv.shape) + SmallSum.scratch(n_hi, small)
        scratch += [pltpu.SemaphoreType.DMA((3,)), pltpu.SemaphoreType.DMA((3, n_seq))]
        params.update(collective_id=1, has_side_effects=True)
    else:
        out_shape = [
            jax.ShapeDtypeStruct((n_tok, width), BF16), jax.ShapeDtypeStruct((2, width, 768), BF16),
            jax.ShapeDtypeStruct((2,) + small, F32),
        ]
        out_specs = [
            pl.BlockSpec((length, width), lambda n: (jnp.maximum(n - n_own, 0) // 2, 0)), fixed((2, width, 768)),
            fixed((2,) + small),
        ]
    return pl.pallas_call(
        functools.partial(backward_kernel, n_seq, length, n_dp, comm),
        out_shape=out_shape,
        grid=(2 * n_own,),
        in_specs=in_specs,
        out_specs=out_specs,
        scratch_shapes=scratch,
        compiler_params=pltpu.CompilerParams(**params),
        cost_estimate=pl.CostEstimate(flops=40 * 10**9, bytes_accessed=30 * 10**6, transcendentals=0),
    )(*args)


def finish_kernel(big, a_ref, up_ref, down_ref, gv_ref, sm_ref, *refs):
    n = len(big)
    moves = [
        [
            (
                pltpu.make_async_copy(src.at[pl.ds(i * chunk, chunk)], buf.at[i], sem.at[0, i]),
                pltpu.make_async_copy(buf.at[i], dst.at[pl.ds(i * chunk, chunk)], sem.at[1, i]),
            )
            for i in range(count)
        ]
        for (count, chunk), src, dst, buf, sem in zip(
            big, refs[:n], refs[n : 2 * n], refs[2 * n + 15 :: 2], refs[2 * n + 16 :: 2]
        )
    ]
    moves = sum(moves, [])
    for come, _ in moves:
        come.start()
    query, key, value, out, up, down, table, vbias, ubias, *vectors = refs[2 * n : 2 * n + 15]
    query[...] = a_ref[:, 384:576]
    key[:, 0:128] = a_ref[:, 0:128]
    key[:, 128:192] = a_ref[:, 256:320]
    value[:, 0:128] = a_ref[:, 128:256]
    value[:, 128:192] = a_ref[:, 320:384]
    out[0:128, :] = a_ref[:, 640:768].T
    out[128:192, :] = a_ref[:, 512:640].T[64:128]
    up[...] = up_ref[...]
    down[...] = down_ref[...]
    table[...] = sm_ref[0:3, :]
    vbias[0:128] = sm_ref[3, 128:256]
    vbias[128:192] = sm_ref[3, 320:384]
    ubias[...] = jnp.where(my_core() == 0, gv_ref[6, :], gv_ref[7, :])
    for i, vec in enumerate(vectors):
        vec[...] = gv_ref[i, :]
    for come, go in moves:
        come.wait()
        go.start()
    for _, go in moves:
        go.wait()


def finish(big, a_sum, up_sum, down_sum, gv, sm, length):
    rows, width = a_sum.shape
    shapes = [(rows, 192)] * 3 + [(192, rows), (rows, 768), (rows, 768), (3, 2 * length), (192,), (768,)] + [(width,)] * 6
    cuts, scratch = [], []
    for v in big:
        count = v.shape[0] // 512
        cuts.append((count, 512))
        scratch += [pltpu.VMEM((count, 512, v.shape[1]), v.dtype), pltpu.SemaphoreType.DMA((2, count))]
    whole = pl.BlockSpec(memory_space=pltpu.VMEM)
    return pl.pallas_call(
        functools.partial(finish_kernel, tuple(cuts)),
        out_shape=[jax.ShapeDtypeStruct(v.shape, v.dtype) for v in big]
        + [jax.ShapeDtypeStruct(shape, F32) for shape in shapes],
        in_specs=[whole] * 5 + [ANY] * len(big),
        out_specs=[ANY] * len(big) + [whole] * len(shapes),
        scratch_shapes=scratch,
        compiler_params=pltpu.CompilerParams(vmem_limit_bytes=VMEM_LIMIT),
    )(a_sum, up_sum, down_sum, gv, sm, *big)


def gather_plain(weights, length):
    kw, vw, qw, ow, uw, dw, tab, vbias, hbias = weights
    ot = ow.T
    packed = jnp.concatenate([kw[:, :128], vw[:, :128], kw[:, 128:], vw[:, 128:], qw, ot[:, 128:], ot[:, :128]], axis=1)
    small = jnp.zeros((8, 2 * length), F32).at[0:3].set(tab).at[3, 128:256].set(vbias[:128])
    small = small.at[3, 320:384].set(vbias[128:]).at[4, : hbias.shape[0]].set(hbias)
    first = 2 * (lax.axis_index("tensor") // 2)

    def groups(v):
        every = lax.all_gather(v, "tensor")
        return lax.dynamic_slice_in_dim(jnp.concatenate([every, every]), first, 4)

    wide = jnp.stack([packed, uw, dw], axis=1).astype(BF16)
    wide = groups(lax.all_gather(wide, "dp", axis=0, tiled=True))
    return wide[:, :, 0], wide[:, :, 1], wide[:, :, 2], groups(small)


def sum_plain(grads, n_dp):
    core = my_core()
    mine = lax.dynamic_index_in_dim(grads, core, 0, keepdims=False).astype(F32)
    other = lax.dynamic_index_in_dim(grads, 1 - core, 0, keepdims=False)
    total = mine + lax.ppermute(other, "tensor", [(i, i ^ 1) for i in range(4)]).astype(F32)
    return lax.psum_scatter(total, "dp", scatter_dimension=0, tiled=True)


def shards(
    n_dp, tokens, lengths, cotangent, query_weight, key_weight, value_weight, value_bias, output_weight,
    b_out, rel_table, norm_gain, norm_shift, up_weight, hidden_bias, down_weight, b_down, final_gain, final_shift,
):
    seq_count = lengths.shape[0]
    length = tokens.shape[0] // seq_count
    half = length // 2
    n_seq = seq_count // 2
    core = my_core()
    n_hi, rows = n_dp // 2, tokens.shape[1] // n_dp
    comm = rows % 16 == 0 and n_hi <= 4

    weights = (
        key_weight, value_weight, query_weight, output_weight, up_weight, down_weight.T, rel_table,
        value_bias, hidden_bias,
    )
    if not comm:
        weights = gather_plain(weights, length)
        a4, u4, d4, s4 = weights
        weights = (a4, s4)
    kv, q, p, ctx, hid, pb, *gathered = attention_forward(lengths, tokens, b_out, weights, n_dp, comm)
    if comm:
        a4, u4, d4, s4 = gathered
    vectors = (norm_gain, norm_shift, b_down, final_gain, final_shift)
    out_half, ag, gu, gd, gv = ffn(lengths, hid, cotangent, u4, d4, s4, vectors, n_seq, half)
    sums = attention_backward(tokens, a4, kv, q, p, ctx, ag, pb, gu, gd, gv, out_half, n_seq, n_dp, comm)
    if comm:
        output, tokens_grad, up_sum, down_sum, a_sum, gv, sm = sums
    else:
        tok_half, ga, sm = sums
        up_sum, down_sum, a_sum = (sum_plain(v, n_dp) for v in (gu, gd, ga))
        sm, gv = lax.psum((sm, gv), "dp")

        def over_core(v):
            return lax.ppermute(v, "tensor", [(i, i ^ 1) for i in range(4)])

        gv = gv + over_core(gv)
        mine = lax.dynamic_index_in_dim(sm, core, 0, keepdims=False)
        sm = mine + over_core(lax.dynamic_index_in_dim(sm, 1 - core, 0, keepdims=False))

        def join(part):
            got = over_core(part)
            return jnp.where(core == 0, jnp.concatenate([part, got]), jnp.concatenate([got, part]))

        output, tokens_grad = join(out_half), join(tok_half)
    output, tokens_grad, *cut = finish((output, tokens_grad), a_sum, up_sum, down_sum, gv, sm, length)
    query_sum, key_sum, value_sum, outw_sum, up_sum, down_sum, table_sum, vbias, ubias = cut[:9]
    fgain, fshift, dbias, ngain, nshift, obias = cut[9:]
    return (
        output, tokens_grad, query_sum, key_sum, value_sum, vbias, outw_sum, obias, table_sum,
        ngain, nshift, up_sum, ubias, down_sum.T, dbias, fgain, fshift,
    )


def solution(mesh):
    row, col, both, rep = P("dp", None), P("tensor", "dp"), P("dp", "tensor"), P()
    ten, table = P("tensor"), P("tensor", None)
    in_specs = (
        row, P("dp"), row, both, both, both, ten, col, rep, table, rep, rep, both, ten, col, rep, rep, rep,
    )
    out_specs = (
        row, row, both, both, both, ten, col, rep, table, rep, rep, both, ten, col, rep, rep, rep,
    )
    body = functools.partial(shards, mesh.shape["dp"])
    return jax.shard_map(body, mesh=mesh, in_specs=in_specs, out_specs=out_specs, check_vma=False)
```

```python
import functools

import jax
import jax.numpy as jnp
from jax import lax
from jax.experimental import pallas as pl
from jax.experimental.pallas import tpu as pltpu
from jax.sharding import PartitionSpec as P

MESH = pl.DeviceIdType.MESH
F32 = jnp.float32
BF16 = jnp.bfloat16
EPS = 1e-06
VMEM_LIMIT = 58 * 2**20


def dot_nn(a, b):
    return lax.dot_general(a, b, (((1,), (0,)), ((), ())), preferred_element_type=F32)


def dot_nt(a, b):
    return lax.dot_general(a, b, (((1,), (1,)), ((), ())), preferred_element_type=F32)


def dot_tn(a, b):
    return lax.dot_general(a, b, (((0,), (0,)), ((), ())), preferred_element_type=F32)


class Gather:
    def __init__(self, n_hi, ins, outs, s_in, s_out, sems):
        self.n_hi, self.ins, self.outs, self.s_in, self.s_out = n_hi, ins, outs, s_in, s_out
        self.loc, self.zs, self.zr, self.ls, self.lr, self.fs, self.fr, self.cs, self.cr, self.ss, self.sr = sems
        self.dp, self.t = lax.axis_index("dp"), lax.axis_index("tensor")
        self.hi, self.lo = self.dp // 2, lax.rem(self.dp, 2)
        self.core = lax.rem(self.t, 2)
        t_core = self.t + 1 - 2 * self.core
        self.to_x = (self.dp + 1 - 2 * self.lo, self.t)
        self.to_y = (self.dp, lax.rem(self.t + 2, 4))
        self.to_c = (self.dp, t_core)
        self.to_d = (self.dp, lax.rem(t_core + 2, 4))

    def block(self, s, side):
        return lax.rem(self.hi - s + self.n_hi, self.n_hi) * 2 + side

    def greet(self):
        barrier = pltpu.get_barrier_semaphore()
        for up, exists in ((0, self.hi < self.n_hi - 1), (1, self.hi > 0)):

            @pl.when(exists)
            def _():
                pl.semaphore_signal(barrier, inc=1, device_id=self.z_next(up), device_id_type=MESH)

        for peer in (self.to_x, self.to_y, self.to_c, self.to_d):
            pl.semaphore_signal(barrier, inc=1, device_id=peer, device_id_type=MESH)
        along_z = jnp.where(self.hi < self.n_hi - 1, 1, 0) + jnp.where(self.hi > 0, 1, 0)
        pl.semaphore_wait(barrier, 4 + along_z)

    def z_next(self, down):
        hi = jnp.maximum(self.hi - 1, 0) if down else jnp.minimum(self.hi + 1, self.n_hi - 1)
        return (hi * 2 + self.lo, self.t)

    def remote(self, src, dst, send, recv, peer):
        return pltpu.make_async_remote_copy(src, dst, send, recv, device_id=peer, device_id_type=MESH)

    def small(self):
        core = self.core
        return (
            pltpu.make_async_copy(self.s_in, self.s_out.at[core], self.loc.at[3]),
            self.remote(self.s_in, self.s_out.at[core], self.ss.at[0], self.sr.at[0], self.to_c),
            self.remote(self.s_in, self.s_out.at[2 + core], self.ss.at[1], self.sr.at[1], self.to_y),
            self.remote(self.s_in, self.s_out.at[2 + core], self.ss.at[2], self.sr.at[2], self.to_d),
        )

    def local(self, k):
        return pltpu.make_async_copy(self.ins[k], self.outs[k].at[self.core, self.dp], self.loc.at[k])

    def z_send(self, k, d, down):
        b = self.block(self.n_hi - d if down else d, self.lo)
        dst = self.outs[k].at[self.core, b]
        src = self.ins[k] if d == 0 else dst
        return self.remote(src, dst, self.zs.at[down, k, d], self.zr.at[down, k, d], self.z_next(down))

    def z_more(self, down):
        return self.hi > 0 if down else self.hi < self.n_hi - 1

    def z_came(self, d, down):
        return self.hi + d < self.n_hi if down else self.hi >= d

    def line(self, k, s, way, own=False):
        out, b = self.outs[k], self.block(s, self.lo)
        src = self.ins[k] if own else out.at[self.core, b]
        dst = out.at[self.core if way == 0 else 2 + self.core, b]
        return self.remote(
            src, dst, self.ls.at[way, k, s], self.lr.at[way, k, s], self.to_x if way == 0 else self.to_y
        )

    def onward(self, k, s, way):
        out = self.outs[k]
        if way == 0:
            src = dst = out.at[2 + self.core, self.block(s, self.lo)]
        else:
            b = self.block(s, 1 - self.lo)
            src, dst = out.at[self.core, b], out.at[2 + self.core, b]
        return self.remote(src, dst, self.fs.at[k, s], self.fr.at[k, s], self.to_x if way == 0 else self.to_y)

    def to_core(self, k, s, which, own=False):
        out = self.outs[k]
        side = self.lo if which % 2 == 0 else 1 - self.lo
        where = out.at[self.core if which < 2 else 2 + self.core, self.block(s, side)]
        return self.remote(
            self.ins[k] if own else where, where, self.cs.at[which, k, s], self.cr.at[which, k, s], self.to_c
        )

    def start(self, k):
        for down in range(2):
            pl.when(self.z_more(down))(lambda: self.z_send(k, 0, down).start())
        self.line(k, 0, 0, True).start()
        if k == 0:
            self.line(k, 0, 1, True).start()
        self.to_core(k, 0, 0, True).start()
        self.local(k).start()

    def lines_y(self, k):
        for s in range(self.n_hi):
            self.line(k, s, 1, s == 0).start()

    def near(self, d, action):
        if d == 0:
            action(0)
            return
        pl.when(self.z_came(d, 0))(lambda: action(d))
        pl.when(self.z_came(d, 1))(lambda: action(self.n_hi - d))

    def spread(self, k, d):
        for down in range(2):

            @pl.when(self.z_came(d, down))
            def _():
                self.z_send(k, d - 1, down).wait_recv()
                if d < self.n_hi - 1:
                    pl.when(self.z_more(down))(lambda: self.z_send(k, d, down).start())
                s = self.n_hi - d if down else d
                self.line(k, s, 0).start()
                if k == 0:
                    self.line(k, s, 1).start()
                self.to_core(k, s, 0).start()

    def over_x(self, k, s):
        self.line(k, s, 0).wait_recv()
        self.onward(k, s, 1).start()
        self.to_core(k, s, 1).start()

    def over_y(self, k, s):
        self.line(k, s, 1).wait_recv()
        self.onward(k, s, 0).start()
        self.to_core(k, s, 2).start()

    def late_x(self, k, s):
        self.line(k, s, 0).wait_recv()
        self.to_core(k, s, 1).start()

    def late_y(self, k, s):
        self.line(k, s, 1).wait_recv()
        self.to_core(k, s, 2).start()

    def pass_on(self, k, d, core=None):
        if k == 2:
            way = (self.over_x, self.over_y)[core]
            pl.when(self.core == core)(lambda: self.near(d, lambda s: way(k, s)))
        else:
            way = (self.over_x, self.over_y)[k]
            self.near(d, lambda s: way(k, s))

    def late(self, k):
        for s in range(self.n_hi):
            if k == 2:
                pl.when(self.core == 0)(lambda: self.late_y(k, s))
                pl.when(self.core == 1)(lambda: self.late_x(k, s))
            else:
                (self.late_y, self.late_x)[k](k, s)

    def diagonal(self, k, s):
        self.onward(k, s, 0).wait_recv()
        self.to_core(k, s, 3).start()

    def arrived(self, k, whiches):
        for s in range(self.n_hi):
            for which in whiches:
                self.to_core(k, s, which).wait_recv()

    def sent(self, k):
        for down in range(2):
            for d in range(self.n_hi - 1):
                came = self.z_more(down) if d == 0 else jnp.logical_and(self.z_more(down), self.z_came(d, down))
                pl.when(came)(lambda: self.z_send(k, d, down).wait_send())
        for s in range(self.n_hi):
            self.line(k, s, 0).wait_send()
            self.line(k, s, 1).wait_send()
            self.onward(k, s, 0).wait_send()
            for which in range(4):
                self.to_core(k, s, which).wait_send()


def gather_scratch(n_hi):
    dma = pltpu.SemaphoreType.DMA
    return [
        dma((4,)), dma((2, 3, n_hi)), dma((2, 3, n_hi)), dma((2, 3, n_hi)), dma((2, 3, n_hi)), dma((3, n_hi)),
        dma((3, n_hi)), dma((4, 3, n_hi)), dma((4, 3, n_hi)), dma((3,)), dma((3,)),
    ]


def pool_matrix(pooled, length):
    i = lax.broadcasted_iota(jnp.int32, (pooled, length), 0)
    j = lax.broadcasted_iota(jnp.int32, (pooled, length), 1)
    return jnp.where(j // 2 == i, 0.5, 0.0).astype(BF16)


def lane_low(shape):
    return lax.broadcasted_iota(jnp.int32, shape, 1) < 64


def attention_kernel(n_seq, length, n_dp, comm, *refs):
    half = length // 2
    group, b = pl.program_id(0), pl.program_id(1)
    step = group * n_seq + b
    core = lax.rem(lax.axis_index("tensor"), 2)
    len_ref, x_any, bo_ref = refs[:3]
    refs = refs[3:]
    if comm:
        (kw, vw, qw, ow, uw, dw, tab, vbias, hbias) = refs[:9]
        kv_ref, q_ref, p_ref, ctx_ref, hid_ref, pb_ref, a_out, u_out, d_out, s_out = refs[9:19]
        bias, x_ref, x_sem, a_in, u_in, d_in, s_in, a_all, s_all, a_sem, s_sem = refs[19:30]
        net = Gather(n_dp // 2, (a_in, u_in, d_in), (a_all, u_out, d_out), s_in, s_all, refs[30:])
    else:
        a_ref, s_ref = refs[:2]
        kv_ref, q_ref, p_ref, ctx_ref, hid_ref, pb_ref, bias, x_ref, x_sem = refs[2:]
    n_tok = n_seq * length
    x_copy = pltpu.make_async_copy(x_any.at[pl.ds(pl.multiple_of(core * n_tok, n_tok), n_tok), :], x_ref, x_sem)

    def pool_rows():
        x_copy.wait()
        pool = pool_matrix(half, length)
        for i in range(n_seq):
            pooled = dot_nn(pool, x_ref[i * length : (i + 1) * length, :])
            hid_ref[i * half : (i + 1) * half, :] = pooled + bo_ref[...].reshape(1, -1)
            pb_ref[i * half : (i + 1) * half, :] = pooled.astype(BF16)

    if comm:

        def a_copy(g):
            return pltpu.make_async_copy(a_all.at[g], a_out.at[g], a_sem.at[g])

        s_copy = pltpu.make_async_copy(s_all, s_out, s_sem)

        @pl.when(step == 0)
        def _():
            x_copy.start()
            k, v, o = kw[...], vw[...], ow[...].T
            parts = (k[:, :128], v[:, :128], k[:, 128:], v[:, 128:], qw[...], o[:, 128:], o[:, :128])
            a_in[...] = jnp.concatenate(parts, axis=1).astype(BF16)
            s_in[...] = jnp.zeros_like(s_in)
            s_in[0:3, :] = tab[...]
            vb = vbias[...].reshape(1, -1)
            s_in[3:4, 128:256] = vb[:, 0:128]
            s_in[3:4, 320:384] = vb[:, 128:192]
            s_in[4:5, 0 : hbias.shape[0]] = hbias[...].reshape(1, -1)
            net.greet()
            for copy in net.small():
                copy.start()
            net.start(0)
            u_in[...] = uw[...].astype(BF16)
            d_in[...] = dw[...].astype(BF16)
            for s in range(1, n_dp // 2):
                net.spread(0, s)
                net.pass_on(0, s - 1)
            net.start(1)
            net.pass_on(0, n_dp // 2 - 1)
            pool_rows()
            small = net.small()
            small[0].wait()
            for copy in small[1:]:
                copy.wait()
            s_copy.start()
            net.local(0).wait()
            net.arrived(0, (0, 1))

        n_hi = n_dp // 2
        plan = {}

        def at(n, action, *args):
            plan.setdefault(min(n, 4 * n_seq - 1), []).append(functools.partial(action, *args))

        for d in range(1, n_hi):
            at((1, 2, 3)[d - 1], net.spread, 1, d)
            at((5, 6, 7)[d - 1], net.spread, 2, d)
        at(3, net.start, 2)
        at(4, net.late, 0)
        for d in range(n_hi):
            at(4, net.diagonal, 0, d)
            at((6, 7, 8, 9)[d], net.pass_on, 1, d)
            at((10, 10, 11, 11)[d], net.pass_on, 2, d, 0)
            at((11, 12, 13, 14)[d], net.pass_on, 2, d, 1)
            at((11, 12, 13, 13)[d], lambda i: net.near(i, lambda s: net.diagonal(1, s)), d)
        at(3, net.lines_y, 1)
        at(2 * n_seq, net.arrived, 0, (2, 3))
        for g in range(4):
            at(2 * n_seq, lambda i: a_copy(i).start(), g)
        at(7, net.lines_y, 2)
        at(9, net.late, 1)
        at(14, net.late, 2)
        for n, actions in plan.items():

            @pl.when(step == n)
            def _():
                for action in actions:
                    action()

        def weights(lanes):
            return a_all[group, :, :, lanes].reshape(-1, lanes.stop - lanes.start)

        def small_row(i):
            return s_all[group, i : i + 1, :]
    else:

        @pl.when(step == 0)
        def _():
            x_copy.start()
            pool_rows()

        def weights(lanes):
            return a_ref[0, :, lanes]

        def small_row(i):
            return s_ref[0, i : i + 1, :]

    krows = pl.ds(pl.multiple_of(b * length, length), length)
    qrows = pl.ds(pl.multiple_of(b * half, half), half)

    @pl.when(b == 0)
    def _():
        for h in range(3):
            wide = jnp.broadcast_to(small_row(h), (half, 2 * length))
            bias[h] = pltpu.roll(wide, length, 1, stride=2, stride_axis=0)[:, :length].T

    kv_ref[0] = (dot_nn(x_ref[krows, :], weights(slice(0, 384))) + small_row(3)[:, 0:384]).astype(BF16)
    q = dot_nn(pb_ref[qrows, :], weights(slice(384, 640))) * 0.125
    lanes = lax.broadcasted_iota(jnp.int32, q.shape, 1)
    q = jnp.where(lanes < 192, q, 0.0).astype(BF16)
    q_ref[0] = q
    low = lane_low((half, 128))
    valid = lax.broadcasted_iota(jnp.int32, (length, half), 0) < len_ref[core * n_seq + b]
    q01 = q[:, 0:128]
    zero = jnp.zeros_like(q01)
    heads = (
        (jnp.where(low, q01, zero), 0, 128),
        (jnp.where(low, zero, q01), 0, 128),
        (q[:, 128:256], 256, 256),
    )
    contexts = []
    for h, (qh, k_at, v_at) in enumerate(heads):
        s = dot_nt(kv_ref[0, :, k_at : k_at + 128], qh) + bias[h]
        s = jnp.where(valid, s, -1e30)
        e = jnp.exp(s - jnp.max(s, axis=0, keepdims=True))
        p = (e * (1.0 / jnp.sum(e, axis=0, keepdims=True))).astype(BF16)
        p_ref[0, 0, h] = p
        contexts.append(dot_tn(kv_ref[0, :, v_at : v_at + 128], p))
    c0, c1, c2 = contexts
    ctx01 = jnp.concatenate([c0[0:64], c1[64:128]], axis=0).T
    ctx2 = jnp.concatenate([jnp.zeros_like(c2[0:64]), c2[64:128]], axis=0).T
    ctx = jnp.concatenate([ctx2, ctx01], axis=1).astype(BF16)
    ctx_ref[0] = ctx
    hid_ref[qrows, :] += dot_nt(ctx, weights(slice(512, 768)))

    if comm:

        @pl.when(step == 4 * n_seq - 1)
        def _():
            for s in range(n_hi):
                net.diagonal(2, s)
            for k in range(3):
                net.sent(k)
            for k in (1, 2):
                net.local(k).wait()
                net.arrived(k, (0, 1, 2, 3))
            for g in range(4):
                a_copy(g).wait()
            s_copy.wait()


def my_core():
    return lax.rem(lax.axis_index("tensor"), 2)


def attention_forward(lengths, tokens, b_out, weights, n_dp, comm):
    n_seq = lengths.shape[0] // 2
    length = tokens.shape[0] // lengths.shape[0]
    half = length // 2
    width = tokens.shape[1]
    once = pl.Buffered(1)

    def fixed(shape):
        return pl.BlockSpec(shape, lambda g, b: (0,) * len(shape), pipeline_mode=once)

    in_specs = [
        pl.BlockSpec(memory_space=pltpu.SMEM),
        pl.BlockSpec(memory_space=pl.ANY),
        fixed((width,)),
    ]
    out_shape = [
        jax.ShapeDtypeStruct((4, n_seq * length, 384), BF16),
        jax.ShapeDtypeStruct((4, n_seq * half, 256), BF16),
        jax.ShapeDtypeStruct((4, n_seq, 3, length, half), BF16),
        jax.ShapeDtypeStruct((4, n_seq * half, 256), BF16),
        jax.ShapeDtypeStruct((n_seq * half, width), F32),
        jax.ShapeDtypeStruct((n_seq * half, width), BF16),
    ]
    out_specs = [
        pl.BlockSpec((1, length, 384), lambda g, b: (g, b, 0)),
        pl.BlockSpec((1, half, 256), lambda g, b: (g, b, 0)),
        pl.BlockSpec((1, 1, 3, length, half), lambda g, b: (g, b, 0, 0, 0)),
        pl.BlockSpec((1, half, 256), lambda g, b: (g, b, 0)),
        fixed((n_seq * half, width)),
        fixed((n_seq * half, width)),
    ]
    scratch = [
        pltpu.VMEM((3, length, half), F32), pltpu.VMEM((n_seq * length, width), BF16), pltpu.SemaphoreType.DMA,
    ]
    params = {"vmem_limit_bytes": VMEM_LIMIT}
    if comm:
        rows = width // n_dp
        in_specs += [fixed(w.shape) for w in weights]
        whole = jax.ShapeDtypeStruct((4, n_dp, rows, width), BF16)
        small = jax.ShapeDtypeStruct((4, 8, 2 * length), F32)
        out_shape += [whole, whole, whole, small]
        out_specs += [pl.BlockSpec(memory_space=pl.ANY)] * 4
        scratch += [pltpu.VMEM((rows, width), BF16)] * 3
        scratch += [
            pltpu.VMEM((8, 2 * length), F32),
            pltpu.VMEM((4, n_dp, rows, width), BF16),
            pltpu.VMEM((4, 8, 2 * length), F32),
            pltpu.SemaphoreType.DMA((4,)),
            pltpu.SemaphoreType.DMA,
        ]
        scratch += gather_scratch(n_dp // 2)
        params.update(collective_id=0, has_side_effects=True)
    else:
        in_specs += [
            pl.BlockSpec((1, width, 768), lambda g, b: (g, 0, 0)),
            pl.BlockSpec((1, 8, 2 * length), lambda g, b: (g, 0, 0)),
        ]
    outs = pl.pallas_call(
        functools.partial(attention_kernel, n_seq, length, n_dp, comm),
        out_shape=out_shape,
        grid=(4, n_seq),
        in_specs=in_specs,
        out_specs=out_specs,
        scratch_shapes=scratch,
        compiler_params=pltpu.CompilerParams(**params),
        cost_estimate=pl.CostEstimate(flops=20 * 10**9, bytes_accessed=40 * 10**6, transcendentals=6 * 10**6),
    )(lengths, tokens, b_out, *weights)
    if comm:
        flat = (4, width, width)
        outs = list(outs)
        outs = outs[:6] + [w.reshape(flat) for w in outs[6:9]] + outs[9:]
    return outs


def row_mean(v):
    return jnp.mean(v, axis=-1, keepdims=True)


def ffn_kernel(
    n_seq, half, len_ref, hid_ref, cot_ref, u_ref, d_ref, s_ref, v0, v1, v2, v3, v4,
    out_ref, ag_ref, gu_ref, gd_ref, gv_ref, nb_all, fg_all, act_all, pg_all, dg,
):
    b = pl.program_id(0)
    rows = pl.ds(pl.multiple_of(b * half, half), half)
    n_gain, n_shift, b_down, f_gain, f_shift = (v[...].reshape(1, -1) for v in (v0, v1, v2, v3, v4))

    @pl.when(b == 0)
    def _():
        gv_ref[...] = jnp.zeros_like(gv_ref)

    def add(i, v):
        gv_ref[i : i + 1, :] += jnp.sum(v, axis=0, keepdims=True)

    hid = hid_ref[...]
    centred = hid - row_mean(hid)
    inv1 = lax.rsqrt(row_mean(centred * centred) + EPS)
    unit1 = centred * inv1
    normed = unit1 * n_gain + n_shift
    nb = normed.astype(BF16)
    nb_all[rows, :] = nb
    summed = normed + b_down
    for t in range(4):
        pre = dot_nn(nb, u_ref[t]) + s_ref[t, 4:5, 0:768]
        cdf = 0.5 * (1.0 + lax.erf(pre * 0.7071067811865476))
        act = (pre * cdf).astype(BF16)
        dg[t] = cdf + pre * (0.3989422804014327 * jnp.exp(-0.5 * pre * pre))
        act_all[t, rows, :] = act
        summed = summed + dot_nt(act, d_ref[t])
    centred = summed - row_mean(summed)
    inv2 = lax.rsqrt(row_mean(centred * centred) + EPS)
    unit2 = centred * inv2
    valid = (2 * lax.broadcasted_iota(jnp.int32, (half, 1), 0) < len_ref[my_core() * n_seq + b]).astype(F32)
    out_ref[...] = ((unit2 * f_gain + f_shift) * valid).astype(BF16)
    grad = cot_ref[...].astype(F32) * valid
    add(0, grad * unit2)
    add(1, grad)
    scaled = grad * f_gain
    grad_summed = inv2 * (scaled - row_mean(scaled) - unit2 * row_mean(scaled * unit2))
    add(2, grad_summed)
    fg = grad_summed.astype(BF16)
    fg_all[rows, :] = fg
    normed_grad = grad_summed
    for t in range(4):
        pg = (dot_nn(fg, d_ref[t]) * dg[t]).astype(BF16)
        pg_all[t, rows, :] = pg
        normed_grad = normed_grad + dot_nt(pg, u_ref[t])
    add(3, normed_grad * unit1)
    add(4, normed_grad)
    scaled = normed_grad * n_gain
    hidden_grad = inv1 * (scaled - row_mean(scaled) - unit1 * row_mean(scaled * unit1))
    add(5, hidden_grad)
    ag_ref[...] = hidden_grad.astype(BF16)

    @pl.when(b == n_seq - 1)
    def _():
        for i in range(2):
            pg = pg_all[i]
            gu_ref[i] = dot_tn(nb_all[...], pg).astype(BF16)
            gd_ref[i] = dot_tn(fg_all[...], act_all[i]).astype(BF16)
            gv_ref[6 + i : 7 + i, :] = jnp.sum(pg.astype(F32), axis=0, keepdims=True)


def ffn(lengths, hid, cotangent, u4, d4, s4, vectors, n_seq, half):
    width = hid.shape[1]
    once = pl.Buffered(1)
    return pl.pallas_call(
        functools.partial(ffn_kernel, n_seq, half),
        out_shape=(
            jax.ShapeDtypeStruct((n_seq * half, width), BF16),
            jax.ShapeDtypeStruct((n_seq * half, width), BF16),
            jax.ShapeDtypeStruct((2, width, 768), BF16),
            jax.ShapeDtypeStruct((2, width, 768), BF16),
            jax.ShapeDtypeStruct((8, width), F32),
        ),
        grid=(n_seq,),
        in_specs=[
            pl.BlockSpec(memory_space=pltpu.SMEM),
            pl.BlockSpec((half, width), lambda b: (b, 0)),
            pl.BlockSpec((half, width), lambda b: (my_core() * n_seq + b, 0)),
            pl.BlockSpec((4, width, 768), lambda b: (0, 0, 0), pipeline_mode=once),
            pl.BlockSpec((4, width, 768), lambda b: (0, 0, 0), pipeline_mode=once),
            pl.BlockSpec(s4.shape, lambda b: (0, 0, 0), pipeline_mode=once),
        ]
        + [pl.BlockSpec((width,), lambda b: (0,), pipeline_mode=once)] * 5,
        out_specs=[
            pl.BlockSpec((half, width), lambda b: (b, 0)),
            pl.BlockSpec((half, width), lambda b: (b, 0)),
            pl.BlockSpec((2, width, 768), lambda b: (0, 0, 0), pipeline_mode=once),
            pl.BlockSpec((2, width, 768), lambda b: (0, 0, 0), pipeline_mode=once),
            pl.BlockSpec((8, width), lambda b: (0, 0), pipeline_mode=once),
        ],
        scratch_shapes=[
            pltpu.VMEM((n_seq * half, width), BF16),
            pltpu.VMEM((n_seq * half, width), BF16),
            pltpu.VMEM((4, n_seq * half, 768), BF16),
            pltpu.VMEM((4, n_seq * half, 768), BF16),
            pltpu.VMEM((4, half, 768), F32),
        ],
        compiler_params=pltpu.CompilerParams(vmem_limit_bytes=VMEM_LIMIT),
        cost_estimate=pl.CostEstimate(flops=24 * 10**9, bytes_accessed=30 * 10**6, transcendentals=6 * 10**6),
    )(lengths, hid, cotangent, u4, d4, s4, *vectors)


class Net:
    def __init__(self, n_hi):
        self.n_hi = n_hi
        self.dp, self.t = lax.axis_index("dp"), lax.axis_index("tensor")
        self.hi, self.lo = self.dp // 2, lax.rem(self.dp, 2)
        self.core = lax.rem(self.t, 2)
        self.to_x = (self.dp + 1 - 2 * self.lo, self.t)
        self.to_c = (self.dp, self.t + 1 - 2 * self.core)

    def place(self, s):
        return lax.rem(self.hi + s, self.n_hi)

    def z_peer(self, s):
        return (self.place(s) * 2 + self.lo, self.t)

    def greet(self):
        barrier = pltpu.get_barrier_semaphore()
        peers = [self.z_peer(s) for s in range(1, self.n_hi)] + [self.to_x, self.to_c]
        for peer in peers:
            pl.semaphore_signal(barrier, inc=1, device_id=peer, device_id_type=MESH)
        pl.semaphore_wait(barrier, len(peers))

    def remote(self, src, dst, send, recv, peer):
        return pltpu.make_async_remote_copy(src, dst, send, recv, device_id=peer, device_id_type=MESH)


class Scatter:
    PARTS = 3

    def __init__(self, net, mine, other, bufs):
        self.net, self.mine, self.other = net, mine, other
        self.t1, self.t2, self.r3, self.sem, self.xs, self.xr, self.zs, self.zr = bufs
        self.rows = self.t2.shape[1] // self.PARTS

    @staticmethod
    def scratch(n_hi, rows, width):
        dma = pltpu.SemaphoreType.DMA
        both, half = pltpu.VMEM((n_hi, 2, rows, width), BF16), pltpu.VMEM((n_hi, rows, width), BF16)
        parts = Scatter.PARTS
        return [both, half, half, dma((2,)), dma((parts,)), dma((parts,)), dma((parts, n_hi)), dma((parts, n_hi))]

    def part(self, i):
        return pl.ds(i * self.rows, self.rows)

    def over_core(self):
        return self.net.remote(self.other, self.t1, self.sem.at[0], self.sem.at[1], self.net.to_c)

    def over_x(self, i):
        src = self.t1.at[:, 1 - self.net.lo, self.part(i)]
        return self.net.remote(src, self.t2.at[:, self.part(i)], self.xs.at[i], self.xr.at[i], self.net.to_x)

    def over_z(self, i, s):
        src = self.t2.at[self.net.place(s), self.part(i)]
        dst = self.r3.at[s, self.part(i)]
        return self.net.remote(src, dst, self.zs.at[i, s], self.zr.at[i, s], self.net.z_peer(s))

    def core_to_x(self):
        self.over_core().wait_recv()
        self.t1[...] += self.mine[...]
        for i in range(self.PARTS):
            self.over_x(i).start()

    def x_sum(self, i):
        self.over_x(i).wait_recv()
        rows = self.part(i)
        self.t2[:, rows] += self.t1[:, self.net.lo, rows]

    def start_z(self, i):
        for s in range(1, self.net.n_hi):
            self.over_z(i, s).start()

    def x_to_z(self, i):
        self.x_sum(i)
        self.start_z(i)

    def finish(self, out):
        for i in range(self.PARTS):
            rows = self.part(i)
            total = self.t2[self.net.hi, rows].astype(F32)
            for s in range(1, self.net.n_hi):
                self.over_z(i, s).wait_recv()
                total += self.r3[s, rows].astype(F32)
            out[rows, :] = total

    def sent_x(self):
        self.over_core().wait_send()
        for i in range(self.PARTS):
            self.over_x(i).wait_send()

    def sent_z(self):
        for i in range(self.PARTS):
            for s in range(1, self.net.n_hi):
                self.over_z(i, s).wait_send()


class SmallSum:
    def __init__(self, net, mine, other, bufs):
        self.net, self.mine, self.other = net, mine, other
        self.rc, self.v1, self.rx, self.v2, self.sem, self.zs, self.zr = bufs

    @staticmethod
    def scratch(n_hi, shape):
        dma = pltpu.SemaphoreType.DMA
        return [
            pltpu.VMEM(shape, F32), pltpu.VMEM(shape, F32), pltpu.VMEM(shape, F32), pltpu.VMEM((n_hi,) + shape, F32),
            dma((4,)), dma((n_hi,)), dma((n_hi,)),
        ]

    def over_core(self):
        return self.net.remote(self.other, self.rc, self.sem.at[0], self.sem.at[1], self.net.to_c)

    def over_x(self):
        return self.net.remote(self.v1, self.rx, self.sem.at[2], self.sem.at[3], self.net.to_x)

    def over_z(self, s):
        here = self.v2.at[self.net.hi]
        return self.net.remote(here, here, self.zs.at[s], self.zr.at[s], self.net.z_peer(s))

    def core_to_x(self):
        self.over_core().wait_recv()
        self.v1[...] = self.mine[...] + self.rc[...]
        self.over_x().start()

    def x_to_z(self):
        self.over_x().wait_recv()
        self.v2[self.net.hi] = self.v1[...] + self.rx[...]
        for s in range(1, self.net.n_hi):
            self.over_z(s).start()

    def finish(self, out):
        for s in range(1, self.net.n_hi):
            self.over_z(s).wait()
        out[...] = jnp.sum(self.v2[...], axis=0)
        self.over_core().wait_send()
        self.over_x().wait_send()

def backward_step(half, own, step_refs):
    kv_ref, q_ref, p_ref, ag, a_of, tacc, kvd, qd_ref = step_refs
    low = lane_low((half, 128))
    cg = dot_nn(ag, a_of(slice(512, 768))).astype(BF16)
    q01 = q_ref[0, :, 0:128]
    cg2, cg01 = cg[:, 0:128], cg[:, 128:256]
    zero = jnp.zeros_like(q01)
    heads = (
        (jnp.where(low, q01, zero), jnp.where(low, cg01, zero), 0, 128),
        (jnp.where(low, zero, q01), jnp.where(low, zero, cg01), 0, 128),
        (q_ref[0, :, 128:256], jnp.where(low, zero, cg2), 256, 256),
    )
    kds, vds, qds = [], [], []
    for h, (q, g, k_at, v_at) in enumerate(heads):
        pb16 = p_ref[0, 0, h]
        p = pb16.astype(F32)
        dp = dot_nt(kv_ref[0, :, v_at : v_at + 128], g)
        row = jnp.sum(p * dp, axis=0, keepdims=True)
        sg = (p * (dp - row)).astype(BF16)
        if own:
            tacc[h] += sg.astype(F32)
        kds.append(dot_nn(sg, q))
        vds.append(dot_nn(pb16, g))
        qds.append(dot_tn(kv_ref[0, :, k_at : k_at + 128], sg))
    kvd[:, 0:128] = (kds[0] + kds[1]).astype(BF16)
    kvd[:, 128:256] = (vds[0] + vds[1]).astype(BF16)
    kvd[:, 256:384] = (kds[2] + vds[2]).astype(BF16)
    qd01 = jnp.concatenate([qds[0][0:64], qds[1][64:128]], axis=0).T
    qd2 = jnp.concatenate([qds[2][0:64], jnp.zeros_like(qds[2][0:64])], axis=0).T
    qd = jnp.concatenate([qd01, qd2], axis=1).astype(BF16)
    qd_ref[...] = qd


def backward_place(step, n_seq):
    core = my_core()
    own = jnp.where(step < n_seq, 1 - core, core)
    rest = 2 + lax.rem(step, 2)
    first = step < 2 * n_seq
    return jnp.where(first, own, rest), jnp.where(first, lax.rem(step, n_seq), lax.rem(step, 2 * n_seq) // 2)


def backward_kernel(n_seq, length, n_dp, comm, *refs):
    half = length // 2
    n_hi = n_dp // 2
    step = pl.program_id(0)
    n_own = 2 * n_seq
    own = step < n_own
    g, b = backward_place(step, n_seq)
    x_any, a_ref, kv_ref, q_ref, p_ref, ctx_any, ag_ref, pb_any = refs[:8]
    refs = refs[8:]
    if comm:
        gu_any, gd_any, gv_ref, half_ref = refs[:4]
        out_any, tok_any, up_out, down_out, a_out, gv_out, sm_out = refs[4:11]
        refs = refs[11:]
    else:
        tok_out, ga_ref, sm_ref = refs[:3]
        refs = refs[3:]
    kvd, qd_all, tacc, tok, pool, kvd_rest, qd_rest, x_ref, ctx_ref, pb_ref, fetch = refs[:11]
    refs = refs[11:]
    core = my_core()
    n_tok = n_seq * length
    late = (
        pltpu.make_async_copy(x_any.at[pl.ds(pl.multiple_of(core * n_tok, n_tok), n_tok), :], x_ref, fetch.at[0]),
        pltpu.make_async_copy(ctx_any.at[0:2], ctx_ref, fetch.at[1]),
        pltpu.make_async_copy(pb_any, pb_ref, fetch.at[2]),
    )
    last = step == 2 * n_own - 1

    def at(n, *actions):
        @pl.when(step == n)
        def _():
            for action in actions:
                action()

    if comm:
        ga_ref, sm_ref, gu_mine, gd_mine, stage = refs[:5]
        net = Net(n_hi)
        other = 1 - core
        up = Scatter(net, gu_mine, gu_any.at[other], refs[5:13])
        down = Scatter(net, gd_mine, gd_any.at[other], refs[13:21])
        att = Scatter(net, ga_ref.at[core], ga_ref.at[other], refs[21:29])
        vec = SmallSum(net, gv_ref, gv_ref, refs[29:36])
        small = SmallSum(net, sm_ref.at[core], sm_ref.at[other], refs[36:43])
        o_sem, t_sem = refs[43:45]
        n_rows = n_seq * half
        there = out_any.at[pl.ds(pl.multiple_of(core * n_rows, n_rows), n_rows), :]
        o_copies = (
            pltpu.make_async_copy(half_ref, there, o_sem.at[0]),
            net.remote(half_ref, there, o_sem.at[1], o_sem.at[2], net.to_c),
        )
        mine = (
            pltpu.make_async_copy(gu_any.at[core], gu_mine, fetch.at[3]),
            pltpu.make_async_copy(gd_any.at[core], gd_mine, fetch.at[4]),
        )

        def tok_copies(i):
            row = pl.multiple_of((core * n_seq + i) * length, length)
            where = tok_any.at[pl.ds(row, length), :]
            return (
                pltpu.make_async_copy(stage.at[i], where, t_sem.at[0, i]),
                net.remote(stage.at[i], where, t_sem.at[1, i], t_sem.at[2, i], net.to_c),
            )

        @pl.when(step == 0)
        def _():
            for copy in mine:
                copy.start()
            net.greet()
            vec.over_core().start()
            up.over_core().start()
            down.over_core().start()
            for copy in o_copies:
                copy.start()

        at(1, vec.core_to_x)
        at(2, mine[0].wait, up.core_to_x, mine[1].wait, down.core_to_x)
        at(4, lambda: up.x_to_z(0), vec.x_to_z, att.over_core().start, small.over_core().start)
        at(5, lambda: up.x_to_z(1))
        at(6, lambda: up.x_to_z(2))
        at(8, small.core_to_x, att.core_to_x, lambda: down.x_to_z(0))
        at(9, lambda: down.x_to_z(1))
        at(10, lambda: down.x_to_z(2))
        at(12, lambda: att.x_to_z(0), small.x_to_z)
        at(14, lambda: att.x_to_z(1))
        at(15, lambda: att.x_to_z(2))

    @pl.when(step == 0)
    def _():
        for copy in late:
            copy.start()

    krows = pl.ds(pl.multiple_of(b * length, length), length)
    qrows = pl.ds(pl.multiple_of(b * half, half), half)

    @pl.when(own)
    def _():
        @pl.when(b == 0)
        def _():
            tacc[g] = jnp.zeros_like(tacc[g])

        backward_step(
            half,
            True,
            (kv_ref, q_ref, p_ref, ag_ref[qrows, :], lambda lanes: a_ref[g, :, lanes], tacc.at[g],
             kvd.at[g, krows], qd_all.at[g, qrows]),
        )

        @pl.when(step == n_seq - 1)
        def _():
            for copy in late:
                copy.wait()

        @pl.when(b == n_seq - 1)
        def _():
            def store(lanes, v):
                v = v.astype(BF16)
                ga_ref[g, ..., lanes] = v.reshape(ga_ref.shape[1:-1] + v.shape[-1:])

            store(slice(0, 384), dot_tn(x_ref[...], kvd[g]))
            gq = dot_tn(pb_ref[...], qd_all[g]) * 0.125
            go = dot_tn(ag_ref[...], ctx_ref[g])
            store(slice(384, 512), gq[:, 0:128])
            store(slice(512, 640), gq[:, 128:256] + go[:, 0:128])
            store(slice(640, 768), go[:, 128:256])
            sm_ref[g, 3:8, :] = jnp.zeros((5, 2 * length), F32)
            sm_ref[g, 3:4, 0:384] = jnp.sum(kvd[g].astype(F32), axis=0, keepdims=True)
            i = lax.broadcasted_iota(jnp.int32, (half, half), 0)
            j = lax.broadcasted_iota(jnp.int32, (half, half), 1)
            flip = jnp.where(i + j == half - 1, 1.0, 0.0).astype(BF16)
            for h in range(3):
                high = tacc[g, h].astype(BF16)
                rest = (tacc[g, h] - high.astype(F32)).astype(BF16)
                turned = dot_nt(flip, high) + dot_nt(flip, rest)
                wide = jnp.concatenate([turned, jnp.zeros((half, length), F32)], axis=1)
                rolled = pltpu.roll(wide, 2, 1, stride=2, stride_axis=0)
                sm_ref[g, h : h + 1, :] = jnp.sum(rolled, axis=0, keepdims=True)

    @pl.when(jnp.logical_not(own))
    def _():
        backward_step(
            half,
            False,
            (kv_ref, q_ref, p_ref, ag_ref[qrows, :], lambda lanes: a_ref[g, :, lanes], None, kvd_rest, qd_rest),
        )
        h = g - 2
        tok_add = dot_nt(kvd_rest[...], a_ref[g, :, 0:384]) + dot_nt(kvd[h, krows], a_ref[h, :, 0:384])
        pool_add = dot_nt(qd_rest[...], a_ref[g, :, 384:640]) + dot_nt(qd_all[h, qrows], a_ref[h, :, 384:640])

        @pl.when(g == 2)
        def _():
            tok[...] = tok_add
            pool[...] = pool_add

        @pl.when(g == 3)
        def _():
            total = ((pool[...] + pool_add) * 0.125 + ag_ref[qrows, :].astype(F32)).astype(BF16)
            final = (tok[...] + tok_add + dot_tn(pool_matrix(half, length), total)).astype(BF16)
            if comm:
                stage[b] = final
                for copy in tok_copies(b):
                    copy.start()
            else:
                tok_out[...] = final

    if comm:

        @pl.when(last)
        def _():
            vec.finish(gv_out)
            up.finish(up_out)
            down.finish(down_out)
            small.finish(sm_out)
            att.finish(a_out)
            for each in (up, down, att):
                each.sent_x()
                each.sent_z()
            for copy in o_copies:
                copy.wait()
            for i in range(n_seq):
                for copy in tok_copies(i):
                    copy.wait()


def fixed(shape, first=None):
    def index(*grid):
        head = 0 if first is None else first()
        return (head,) + (0,) * (len(shape) - 1)

    return pl.BlockSpec(shape, index, pipeline_mode=pl.Buffered(1))


ANY = pl.BlockSpec(memory_space=pl.ANY)


def attention_backward(tokens, a4, kv, q, p, ctx, ag, pb, gu, gd, gv, out_half, n_seq, n_dp, comm):
    length = kv.shape[1] // n_seq
    half = length // 2
    width = tokens.shape[1]
    n_tok, n_pool = n_seq * length, n_seq * half
    n_own = 2 * n_seq
    n_hi, rows = n_dp // 2, width // n_dp

    def place(n):
        return backward_place(n, n_seq)

    in_specs = [
        ANY,
        fixed((4, width, 768)),
        pl.BlockSpec((1, length, 384), lambda n: place(n) + (0,)),
        pl.BlockSpec((1, half, 256), lambda n: place(n) + (0,)),
        pl.BlockSpec((1, 1, 3, length, half), lambda n: place(n) + (0, 0, 0)),
        ANY,
        fixed((n_pool, width)),
        ANY,
    ]
    args = [tokens, a4, kv, q, p, ctx, ag, pb]
    scratch = [
        pltpu.VMEM((2, n_tok, 384), BF16), pltpu.VMEM((2, n_pool, 256), BF16), pltpu.VMEM((2, 3, length, half), F32),
        pltpu.VMEM((length, width), F32), pltpu.VMEM((half, width), F32), pltpu.VMEM((length, 384), BF16),
        pltpu.VMEM((half, 256), BF16), pltpu.VMEM((n_tok, width), BF16), pltpu.VMEM((2, n_pool, 256), BF16), pltpu.VMEM((n_pool, width), BF16),
        pltpu.SemaphoreType.DMA((5,)),
    ]
    params = {"vmem_limit_bytes": VMEM_LIMIT}
    small = (8, 2 * length)
    if comm:
        split = (2, n_hi, 2, rows, width)
        in_specs += [ANY, ANY, fixed(gv.shape), fixed(out_half.shape)]
        args += [gu.reshape(split), gd.reshape(split), gv, out_half]
        shares = [jax.ShapeDtypeStruct((rows, width), F32)] * 3
        out_shape = [
            jax.ShapeDtypeStruct((2 * n_pool, width), BF16), jax.ShapeDtypeStruct((2 * n_tok, width), BF16), *shares,
            jax.ShapeDtypeStruct(gv.shape, F32), jax.ShapeDtypeStruct(small, F32),
        ]
        out_specs = [ANY, ANY] + [fixed((rows, width))] * 3 + [fixed(gv.shape), fixed(small)]
        scratch += [
            pltpu.VMEM(split, BF16), pltpu.VMEM((2,) + small, F32), pltpu.VMEM(split[1:], BF16),
            pltpu.VMEM(split[1:], BF16), pltpu.VMEM((n_seq, length, width), BF16),
        ]
        for _ in range(3):
            scratch += Scatter.scratch(n_hi, rows, width)
        scratch += SmallSum.scratch(n_hi, gv.shape) + SmallSum.scratch(n_hi, small)
        scratch += [pltpu.SemaphoreType.DMA((3,)), pltpu.SemaphoreType.DMA((3, n_seq))]
        params.update(collective_id=1, has_side_effects=True)
    else:
        out_shape = [
            jax.ShapeDtypeStruct((n_tok, width), BF16), jax.ShapeDtypeStruct((2, width, 768), BF16),
            jax.ShapeDtypeStruct((2,) + small, F32),
        ]
        out_specs = [
            pl.BlockSpec((length, width), lambda n: (jnp.maximum(n - n_own, 0) // 2, 0)), fixed((2, width, 768)),
            fixed((2,) + small),
        ]
    return pl.pallas_call(
        functools.partial(backward_kernel, n_seq, length, n_dp, comm),
        out_shape=out_shape,
        grid=(2 * n_own,),
        in_specs=in_specs,
        out_specs=out_specs,
        scratch_shapes=scratch,
        compiler_params=pltpu.CompilerParams(**params),
        cost_estimate=pl.CostEstimate(flops=40 * 10**9, bytes_accessed=30 * 10**6, transcendentals=0),
    )(*args)


def finish_kernel(big, a_ref, up_ref, down_ref, gv_ref, sm_ref, *refs):
    n = len(big)
    moves = [
        [
            (
                pltpu.make_async_copy(src.at[pl.ds(i * chunk, chunk)], buf.at[i], sem.at[0, i]),
                pltpu.make_async_copy(buf.at[i], dst.at[pl.ds(i * chunk, chunk)], sem.at[1, i]),
            )
            for i in range(count)
        ]
        for (count, chunk), src, dst, buf, sem in zip(
            big, refs[:n], refs[n : 2 * n], refs[2 * n + 15 :: 2], refs[2 * n + 16 :: 2]
        )
    ]
    moves = sum(moves, [])
    for come, _ in moves:
        come.start()
    query, key, value, out, up, down, table, vbias, ubias, *vectors = refs[2 * n : 2 * n + 15]
    query[...] = a_ref[:, 384:576]
    key[:, 0:128] = a_ref[:, 0:128]
    key[:, 128:192] = a_ref[:, 256:320]
    value[:, 0:128] = a_ref[:, 128:256]
    value[:, 128:192] = a_ref[:, 320:384]
    out[0:128, :] = a_ref[:, 640:768].T
    out[128:192, :] = a_ref[:, 512:640].T[64:128]
    up[...] = up_ref[...]
    down[...] = down_ref[...]
    table[...] = sm_ref[0:3, :]
    vbias[0:128] = sm_ref[3, 128:256]
    vbias[128:192] = sm_ref[3, 320:384]
    ubias[...] = jnp.where(my_core() == 0, gv_ref[6, :], gv_ref[7, :])
    for i, vec in enumerate(vectors):
        vec[...] = gv_ref[i, :]
    for come, go in moves:
        come.wait()
        go.start()
    for _, go in moves:
        go.wait()


def finish(big, a_sum, up_sum, down_sum, gv, sm, length):
    rows, width = a_sum.shape
    shapes = [(rows, 192)] * 3 + [(192, rows), (rows, 768), (rows, 768), (3, 2 * length), (192,), (768,)] + [(width,)] * 6
    cuts, scratch = [], []
    for v in big:
        count = v.shape[0] // 512
        cuts.append((count, 512))
        scratch += [pltpu.VMEM((count, 512, v.shape[1]), v.dtype), pltpu.SemaphoreType.DMA((2, count))]
    whole = pl.BlockSpec(memory_space=pltpu.VMEM)
    return pl.pallas_call(
        functools.partial(finish_kernel, tuple(cuts)),
        out_shape=[jax.ShapeDtypeStruct(v.shape, v.dtype) for v in big]
        + [jax.ShapeDtypeStruct(shape, F32) for shape in shapes],
        in_specs=[whole] * 5 + [ANY] * len(big),
        out_specs=[ANY] * len(big) + [whole] * len(shapes),
        scratch_shapes=scratch,
        compiler_params=pltpu.CompilerParams(vmem_limit_bytes=VMEM_LIMIT),
    )(a_sum, up_sum, down_sum, gv, sm, *big)


def gather_plain(weights, length):
    kw, vw, qw, ow, uw, dw, tab, vbias, hbias = weights
    ot = ow.T
    packed = jnp.concatenate([kw[:, :128], vw[:, :128], kw[:, 128:], vw[:, 128:], qw, ot[:, 128:], ot[:, :128]], axis=1)
    small = jnp.zeros((8, 2 * length), F32).at[0:3].set(tab).at[3, 128:256].set(vbias[:128])
    small = small.at[3, 320:384].set(vbias[128:]).at[4, : hbias.shape[0]].set(hbias)
    first = 2 * (lax.axis_index("tensor") // 2)

    def groups(v):
        every = lax.all_gather(v, "tensor")
        return lax.dynamic_slice_in_dim(jnp.concatenate([every, every]), first, 4)

    wide = jnp.stack([packed, uw, dw], axis=1).astype(BF16)
    wide = groups(lax.all_gather(wide, "dp", axis=0, tiled=True))
    return wide[:, :, 0], wide[:, :, 1], wide[:, :, 2], groups(small)


def sum_plain(grads, n_dp):
    core = my_core()
    mine = lax.dynamic_index_in_dim(grads, core, 0, keepdims=False).astype(F32)
    other = lax.dynamic_index_in_dim(grads, 1 - core, 0, keepdims=False)
    total = mine + lax.ppermute(other, "tensor", [(i, i ^ 1) for i in range(4)]).astype(F32)
    return lax.psum_scatter(total, "dp", scatter_dimension=0, tiled=True)


def shards(
    n_dp, tokens, lengths, cotangent, query_weight, key_weight, value_weight, value_bias, output_weight,
    b_out, rel_table, norm_gain, norm_shift, up_weight, hidden_bias, down_weight, b_down, final_gain, final_shift,
):
    seq_count = lengths.shape[0]
    length = tokens.shape[0] // seq_count
    half = length // 2
    n_seq = seq_count // 2
    core = my_core()
    n_hi, rows = n_dp // 2, tokens.shape[1] // n_dp
    comm = rows % 16 == 0 and n_hi <= 4

    weights = (
        key_weight, value_weight, query_weight, output_weight, up_weight, down_weight.T, rel_table,
        value_bias, hidden_bias,
    )
    if not comm:
        weights = gather_plain(weights, length)
        a4, u4, d4, s4 = weights
        weights = (a4, s4)
    kv, q, p, ctx, hid, pb, *gathered = attention_forward(lengths, tokens, b_out, weights, n_dp, comm)
    if comm:
        a4, u4, d4, s4 = gathered
    vectors = (norm_gain, norm_shift, b_down, final_gain, final_shift)
    out_half, ag, gu, gd, gv = ffn(lengths, hid, cotangent, u4, d4, s4, vectors, n_seq, half)
    sums = attention_backward(tokens, a4, kv, q, p, ctx, ag, pb, gu, gd, gv, out_half, n_seq, n_dp, comm)
    if comm:
        output, tokens_grad, up_sum, down_sum, a_sum, gv, sm = sums
    else:
        tok_half, ga, sm = sums
        up_sum, down_sum, a_sum = (sum_plain(v, n_dp) for v in (gu, gd, ga))
        sm, gv = lax.psum((sm, gv), "dp")

        def over_core(v):
            return lax.ppermute(v, "tensor", [(i, i ^ 1) for i in range(4)])

        gv = gv + over_core(gv)
        mine = lax.dynamic_index_in_dim(sm, core, 0, keepdims=False)
        sm = mine + over_core(lax.dynamic_index_in_dim(sm, 1 - core, 0, keepdims=False))

        def join(part):
            got = over_core(part)
            return jnp.where(core == 0, jnp.concatenate([part, got]), jnp.concatenate([got, part]))

        output, tokens_grad = join(out_half), join(tok_half)
    output, tokens_grad, *cut = finish((output, tokens_grad), a_sum, up_sum, down_sum, gv, sm, length)
    query_sum, key_sum, value_sum, outw_sum, up_sum, down_sum, table_sum, vbias, ubias = cut[:9]
    fgain, fshift, dbias, ngain, nshift, obias = cut[9:]
    return (
        output, tokens_grad, query_sum, key_sum, value_sum, vbias, outw_sum, obias, table_sum,
        ngain, nshift, up_sum, ubias, down_sum.T, dbias, fgain, fshift,
    )


def solution(mesh):
    row, col, both, rep = P("dp", None), P("tensor", "dp"), P("dp", "tensor"), P()
    ten, table = P("tensor"), P("tensor", None)
    in_specs = (
        row, P("dp"), row, both, both, both, ten, col, rep, table, rep, rep, both, ten, col, rep, rep, rep,
    )
    out_specs = (
        row, row, both, both, both, ten, col, rep, table, rep, rep, both, ten, col, rep, rep, rep,
    )
    body = functools.partial(shards, mesh.shape["dp"])
    return jax.shard_map(body, mesh=mesh, in_specs=in_specs, out_specs=out_specs, check_vma=False)
```

```python
import functools

import jax
import jax.numpy as jnp
from jax import lax
from jax.experimental import pallas as pl
from jax.experimental.pallas import tpu as pltpu
from jax.sharding import PartitionSpec as P

MESH = pl.DeviceIdType.MESH
F32 = jnp.float32
BF16 = jnp.bfloat16
EPS = 1e-06
VMEM_LIMIT = 58 * 2**20


def dot_nn(a, b):
    return lax.dot_general(a, b, (((1,), (0,)), ((), ())), preferred_element_type=F32)


def dot_nt(a, b):
    return lax.dot_general(a, b, (((1,), (1,)), ((), ())), preferred_element_type=F32)


def dot_tn(a, b):
    return lax.dot_general(a, b, (((0,), (0,)), ((), ())), preferred_element_type=F32)


class Gather:
    def __init__(self, n_hi, ins, outs, s_in, s_out, sems):
        self.n_hi, self.ins, self.outs, self.s_in, self.s_out = n_hi, ins, outs, s_in, s_out
        self.loc, self.zs, self.zr, self.ls, self.lr, self.fs, self.fr, self.cs, self.cr, self.ss, self.sr = sems
        self.dp, self.t = lax.axis_index("dp"), lax.axis_index("tensor")
        self.hi, self.lo = self.dp // 2, lax.rem(self.dp, 2)
        self.core = lax.rem(self.t, 2)
        t_core = self.t + 1 - 2 * self.core
        self.to_x = (self.dp + 1 - 2 * self.lo, self.t)
        self.to_y = (self.dp, lax.rem(self.t + 2, 4))
        self.to_c = (self.dp, t_core)
        self.to_d = (self.dp, lax.rem(t_core + 2, 4))

    def block(self, s, side):
        return lax.rem(self.hi - s + self.n_hi, self.n_hi) * 2 + side

    def greet(self):
        barrier = pltpu.get_barrier_semaphore()
        for up, exists in ((0, self.hi < self.n_hi - 1), (1, self.hi > 0)):

            @pl.when(exists)
            def _():
                pl.semaphore_signal(barrier, inc=1, device_id=self.z_next(up), device_id_type=MESH)

        for peer in (self.to_x, self.to_y, self.to_c, self.to_d):
            pl.semaphore_signal(barrier, inc=1, device_id=peer, device_id_type=MESH)
        along_z = jnp.where(self.hi < self.n_hi - 1, 1, 0) + jnp.where(self.hi > 0, 1, 0)
        pl.semaphore_wait(barrier, 4 + along_z)

    def z_next(self, down):
        hi = jnp.maximum(self.hi - 1, 0) if down else jnp.minimum(self.hi + 1, self.n_hi - 1)
        return (hi * 2 + self.lo, self.t)

    def remote(self, src, dst, send, recv, peer):
        return pltpu.make_async_remote_copy(src, dst, send, recv, device_id=peer, device_id_type=MESH)

    def small(self):
        core = self.core
        return (
            pltpu.make_async_copy(self.s_in, self.s_out.at[core], self.loc.at[3]),
            self.remote(self.s_in, self.s_out.at[core], self.ss.at[0], self.sr.at[0], self.to_c),
            self.remote(self.s_in, self.s_out.at[2 + core], self.ss.at[1], self.sr.at[1], self.to_y),
            self.remote(self.s_in, self.s_out.at[2 + core], self.ss.at[2], self.sr.at[2], self.to_d),
        )

    def local(self, k):
        return pltpu.make_async_copy(self.ins[k], self.outs[k].at[self.core, self.dp], self.loc.at[k])

    def z_send(self, k, d, down):
        b = self.block(self.n_hi - d if down else d, self.lo)
        dst = self.outs[k].at[self.core, b]
        src = self.ins[k] if d == 0 else dst
        return self.remote(src, dst, self.zs.at[down, k, d], self.zr.at[down, k, d], self.z_next(down))

    def z_more(self, down):
        return self.hi > 0 if down else self.hi < self.n_hi - 1

    def z_came(self, d, down):
        return self.hi + d < self.n_hi if down else self.hi >= d

    def line(self, k, s, way, own=False):
        out, b = self.outs[k], self.block(s, self.lo)
        src = self.ins[k] if own else out.at[self.core, b]
        dst = out.at[self.core if way == 0 else 2 + self.core, b]
        return self.remote(
            src, dst, self.ls.at[way, k, s], self.lr.at[way, k, s], self.to_x if way == 0 else self.to_y
        )

    def onward(self, k, s, way):
        out = self.outs[k]
        if way == 0:
            src = dst = out.at[2 + self.core, self.block(s, self.lo)]
        else:
            b = self.block(s, 1 - self.lo)
            src, dst = out.at[self.core, b], out.at[2 + self.core, b]
        return self.remote(src, dst, self.fs.at[k, s], self.fr.at[k, s], self.to_x if way == 0 else self.to_y)

    def to_core(self, k, s, which, own=False):
        out = self.outs[k]
        side = self.lo if which % 2 == 0 else 1 - self.lo
        where = out.at[self.core if which < 2 else 2 + self.core, self.block(s, side)]
        return self.remote(
            self.ins[k] if own else where, where, self.cs.at[which, k, s], self.cr.at[which, k, s], self.to_c
        )

    def start(self, k):
        for down in range(2):
            pl.when(self.z_more(down))(lambda: self.z_send(k, 0, down).start())
        self.line(k, 0, 0, True).start()
        if k == 0:
            self.line(k, 0, 1, True).start()
        self.to_core(k, 0, 0, True).start()
        self.local(k).start()

    def lines_y(self, k):
        for s in range(self.n_hi):
            self.line(k, s, 1, s == 0).start()

    def near(self, d, action):
        if d == 0:
            action(0)
            return
        pl.when(self.z_came(d, 0))(lambda: action(d))
        pl.when(self.z_came(d, 1))(lambda: action(self.n_hi - d))

    def spread(self, k, d):
        for down in range(2):

            @pl.when(self.z_came(d, down))
            def _():
                self.z_send(k, d - 1, down).wait_recv()
                if d < self.n_hi - 1:
                    pl.when(self.z_more(down))(lambda: self.z_send(k, d, down).start())
                s = self.n_hi - d if down else d
                self.line(k, s, 0).start()
                if k == 0:
                    self.line(k, s, 1).start()
                self.to_core(k, s, 0).start()

    def over_x(self, k, s):
        self.line(k, s, 0).wait_recv()
        self.onward(k, s, 1).start()
        self.to_core(k, s, 1).start()

    def over_y(self, k, s):
        self.line(k, s, 1).wait_recv()
        self.onward(k, s, 0).start()
        self.to_core(k, s, 2).start()

    def late_x(self, k, s):
        self.line(k, s, 0).wait_recv()
        self.to_core(k, s, 1).start()

    def late_y(self, k, s):
        self.line(k, s, 1).wait_recv()
        self.to_core(k, s, 2).start()

    def pass_on(self, k, d, core=None):
        if k == 2:
            way = (self.over_x, self.over_y)[core]
            pl.when(self.core == core)(lambda: self.near(d, lambda s: way(k, s)))
        else:
            way = (self.over_x, self.over_y)[k]
            self.near(d, lambda s: way(k, s))

    def late(self, k):
        for s in range(self.n_hi):
            if k == 2:
                pl.when(self.core == 0)(lambda: self.late_y(k, s))
                pl.when(self.core == 1)(lambda: self.late_x(k, s))
            else:
                (self.late_y, self.late_x)[k](k, s)

    def diagonal(self, k, s):
        self.onward(k, s, 0).wait_recv()
        self.to_core(k, s, 3).start()

    def arrived(self, k, whiches):
        for s in range(self.n_hi):
            for which in whiches:
                self.to_core(k, s, which).wait_recv()

    def sent(self, k):
        for down in range(2):
            for d in range(self.n_hi - 1):
                came = self.z_more(down) if d == 0 else jnp.logical_and(self.z_more(down), self.z_came(d, down))
                pl.when(came)(lambda: self.z_send(k, d, down).wait_send())
        for s in range(self.n_hi):
            self.line(k, s, 0).wait_send()
            self.line(k, s, 1).wait_send()
            self.onward(k, s, 0).wait_send()
            for which in range(4):
                self.to_core(k, s, which).wait_send()


def gather_scratch(n_hi):
    dma = pltpu.SemaphoreType.DMA
    return [
        dma((4,)), dma((2, 3, n_hi)), dma((2, 3, n_hi)), dma((2, 3, n_hi)), dma((2, 3, n_hi)), dma((3, n_hi)),
        dma((3, n_hi)), dma((4, 3, n_hi)), dma((4, 3, n_hi)), dma((3,)), dma((3,)),
    ]


def pool_matrix(pooled, length):
    i = lax.broadcasted_iota(jnp.int32, (pooled, length), 0)
    j = lax.broadcasted_iota(jnp.int32, (pooled, length), 1)
    return jnp.where(j // 2 == i, 0.5, 0.0).astype(BF16)


def lane_low(shape):
    return lax.broadcasted_iota(jnp.int32, shape, 1) < 64


def attention_kernel(n_seq, length, n_dp, comm, *refs):
    half = length // 2
    group, b = pl.program_id(0), pl.program_id(1)
    step = group * n_seq + b
    core = lax.rem(lax.axis_index("tensor"), 2)
    len_ref, x_any, bo_ref = refs[:3]
    refs = refs[3:]
    if comm:
        (kw, vw, qw, ow, uw, dw, tab, vbias, hbias) = refs[:9]
        kv_ref, q_ref, p_ref, ctx_ref, hid_ref, pb_ref, a_out, u_out, d_out, s_out = refs[9:19]
        bias, x_ref, x_sem, a_in, u_in, d_in, s_in, a_all, s_all, a_sem, s_sem = refs[19:30]
        net = Gather(n_dp // 2, (a_in, u_in, d_in), (a_all, u_out, d_out), s_in, s_all, refs[30:])
    else:
        a_ref, s_ref = refs[:2]
        kv_ref, q_ref, p_ref, ctx_ref, hid_ref, pb_ref, bias, x_ref, x_sem = refs[2:]
    n_tok = n_seq * length
    x_copy = pltpu.make_async_copy(x_any.at[pl.ds(pl.multiple_of(core * n_tok, n_tok), n_tok), :], x_ref, x_sem)

    def pool_rows():
        x_copy.wait()
        pool = pool_matrix(half, length)
        for i in range(n_seq):
            pooled = dot_nn(pool, x_ref[i * length : (i + 1) * length, :])
            hid_ref[i * half : (i + 1) * half, :] = pooled + bo_ref[...].reshape(1, -1)
            pb_ref[i * half : (i + 1) * half, :] = pooled.astype(BF16)

    if comm:

        def a_copy(g):
            return pltpu.make_async_copy(a_all.at[g], a_out.at[g], a_sem.at[g])

        s_copy = pltpu.make_async_copy(s_all, s_out, s_sem)

        @pl.when(step == 0)
        def _():
            x_copy.start()
            k, v, o = kw[...], vw[...], ow[...].T
            parts = (k[:, :128], v[:, :128], k[:, 128:], v[:, 128:], qw[...], o[:, 128:], o[:, :128])
            a_in[...] = jnp.concatenate(parts, axis=1).astype(BF16)
            s_in[...] = jnp.zeros_like(s_in)
            s_in[0:3, :] = tab[...]
            vb = vbias[...].reshape(1, -1)
            s_in[3:4, 128:256] = vb[:, 0:128]
            s_in[3:4, 320:384] = vb[:, 128:192]
            s_in[4:5, 0 : hbias.shape[0]] = hbias[...].reshape(1, -1)
            net.greet()
            for copy in net.small():
                copy.start()
            net.start(0)
            u_in[...] = uw[...].astype(BF16)
            d_in[...] = dw[...].astype(BF16)
            for s in range(1, n_dp // 2):
                net.spread(0, s)
                net.pass_on(0, s - 1)
            net.start(1)
            net.pass_on(0, n_dp // 2 - 1)
            pool_rows()
            small = net.small()
            small[0].wait()
            for copy in small[1:]:
                copy.wait()
            s_copy.start()
            net.local(0).wait()
            net.arrived(0, (0, 1))

        n_hi = n_dp // 2
        plan = {}

        def at(n, action, *args):
            plan.setdefault(min(n, 4 * n_seq - 1), []).append(functools.partial(action, *args))

        for d in range(1, n_hi):
            at((1, 2, 3)[d - 1], net.spread, 1, d)
            at((4, 5, 6)[d - 1], net.spread, 2, d)
        at(2, net.start, 2)
        at(4, net.late, 0)
        for d in range(n_hi):
            at(4, net.diagonal, 0, d)
            at((6, 7, 8, 9)[d], net.pass_on, 1, d)
            at((10, 10, 11, 11)[d], net.pass_on, 2, d, 0)
            at((11, 12, 13, 14)[d], net.pass_on, 2, d, 1)
            at((11, 12, 13, 13)[d], lambda i: net.near(i, lambda s: net.diagonal(1, s)), d)
        at(3, net.lines_y, 1)
        at(2 * n_seq, net.arrived, 0, (2, 3))
        for g in range(4):
            at(2 * n_seq, lambda i: a_copy(i).start(), g)
        at(7, net.lines_y, 2)
        at(9, net.late, 1)
        at(14, net.late, 2)
        for n, actions in plan.items():

            @pl.when(step == n)
            def _():
                for action in actions:
                    action()

        def weights(lanes):
            return a_all[group, :, :, lanes].reshape(-1, lanes.stop - lanes.start)

        def small_row(i):
            return s_all[group, i : i + 1, :]
    else:

        @pl.when(step == 0)
        def _():
            x_copy.start()
            pool_rows()

        def weights(lanes):
            return a_ref[0, :, lanes]

        def small_row(i):
            return s_ref[0, i : i + 1, :]

    krows = pl.ds(pl.multiple_of(b * length, length), length)
    qrows = pl.ds(pl.multiple_of(b * half, half), half)

    @pl.when(b == 0)
    def _():
        for h in range(3):
            wide = jnp.broadcast_to(small_row(h), (half, 2 * length))
            bias[h] = pltpu.roll(wide, length, 1, stride=2, stride_axis=0)[:, :length].T

    kv_ref[0] = (dot_nn(x_ref[krows, :], weights(slice(0, 384))) + small_row(3)[:, 0:384]).astype(BF16)
    q = dot_nn(pb_ref[qrows, :], weights(slice(384, 640))) * 0.125
    lanes = lax.broadcasted_iota(jnp.int32, q.shape, 1)
    q = jnp.where(lanes < 192, q, 0.0).astype(BF16)
    q_ref[0] = q
    low = lane_low((half, 128))
    valid = lax.broadcasted_iota(jnp.int32, (length, half), 0) < len_ref[core * n_seq + b]
    q01 = q[:, 0:128]
    zero = jnp.zeros_like(q01)
    heads = (
        (jnp.where(low, q01, zero), 0, 128),
        (jnp.where(low, zero, q01), 0, 128),
        (q[:, 128:256], 256, 256),
    )
    raw = [dot_nt(kv_ref[0, :, k_at : k_at + 128], qh) for qh, k_at, _ in heads]
    probs = []
    for h in range(3):
        s = jnp.where(valid, raw[h] + bias[h], -1e30)
        e = jnp.exp(s - jnp.max(s, axis=0, keepdims=True))
        p = (e * (1.0 / jnp.sum(e, axis=0, keepdims=True))).astype(BF16)
        p_ref[0, 0, h] = p
        probs.append(p)
    contexts = [dot_tn(kv_ref[0, :, v_at : v_at + 128], p) for (_, _, v_at), p in zip(heads, probs)]
    c0, c1, c2 = contexts
    ctx01 = jnp.concatenate([c0[0:64], c1[64:128]], axis=0).T
    ctx2 = jnp.concatenate([jnp.zeros_like(c2[0:64]), c2[64:128]], axis=0).T
    ctx = jnp.concatenate([ctx2, ctx01], axis=1).astype(BF16)
    ctx_ref[0] = ctx
    hid_ref[qrows, :] += dot_nt(ctx, weights(slice(512, 768)))

    if comm:

        @pl.when(step == 4 * n_seq - 1)
        def _():
            for s in range(n_hi):
                net.diagonal(2, s)
            for k in range(3):
                net.sent(k)
            for k in (1, 2):
                net.local(k).wait()
                net.arrived(k, (0, 1, 2, 3))
            for g in range(4):
                a_copy(g).wait()
            s_copy.wait()


def my_core():
    return lax.rem(lax.axis_index("tensor"), 2)


def attention_forward(lengths, tokens, b_out, weights, n_dp, comm):
    n_seq = lengths.shape[0] // 2
    length = tokens.shape[0] // lengths.shape[0]
    half = length // 2
    width = tokens.shape[1]
    once = pl.Buffered(1)

    def fixed(shape):
        return pl.BlockSpec(shape, lambda g, b: (0,) * len(shape), pipeline_mode=once)

    in_specs = [
        pl.BlockSpec(memory_space=pltpu.SMEM),
        pl.BlockSpec(memory_space=pl.ANY),
        fixed((width,)),
    ]
    out_shape = [
        jax.ShapeDtypeStruct((4, n_seq * length, 384), BF16),
        jax.ShapeDtypeStruct((4, n_seq * half, 256), BF16),
        jax.ShapeDtypeStruct((4, n_seq, 3, length, half), BF16),
        jax.ShapeDtypeStruct((4, n_seq * half, 256), BF16),
        jax.ShapeDtypeStruct((n_seq * half, width), F32),
        jax.ShapeDtypeStruct((n_seq * half, width), BF16),
    ]
    out_specs = [
        pl.BlockSpec((1, length, 384), lambda g, b: (g, b, 0)),
        pl.BlockSpec((1, half, 256), lambda g, b: (g, b, 0)),
        pl.BlockSpec((1, 1, 3, length, half), lambda g, b: (g, b, 0, 0, 0)),
        pl.BlockSpec((1, half, 256), lambda g, b: (g, b, 0)),
        fixed((n_seq * half, width)),
        fixed((n_seq * half, width)),
    ]
    scratch = [
        pltpu.VMEM((3, length, half), F32), pltpu.VMEM((n_seq * length, width), BF16), pltpu.SemaphoreType.DMA,
    ]
    params = {"vmem_limit_bytes": VMEM_LIMIT}
    if comm:
        rows = width // n_dp
        in_specs += [fixed(w.shape) for w in weights]
        whole = jax.ShapeDtypeStruct((4, n_dp, rows, width), BF16)
        small = jax.ShapeDtypeStruct((4, 8, 2 * length), F32)
        out_shape += [whole, whole, whole, small]
        out_specs += [pl.BlockSpec(memory_space=pl.ANY)] * 4
        scratch += [pltpu.VMEM((rows, width), BF16)] * 3
        scratch += [
            pltpu.VMEM((8, 2 * length), F32),
            pltpu.VMEM((4, n_dp, rows, width), BF16),
            pltpu.VMEM((4, 8, 2 * length), F32),
            pltpu.SemaphoreType.DMA((4,)),
            pltpu.SemaphoreType.DMA,
        ]
        scratch += gather_scratch(n_dp // 2)
        params.update(collective_id=0, has_side_effects=True)
    else:
        in_specs += [
            pl.BlockSpec((1, width, 768), lambda g, b: (g, 0, 0)),
            pl.BlockSpec((1, 8, 2 * length), lambda g, b: (g, 0, 0)),
        ]
    outs = pl.pallas_call(
        functools.partial(attention_kernel, n_seq, length, n_dp, comm),
        out_shape=out_shape,
        grid=(4, n_seq),
        in_specs=in_specs,
        out_specs=out_specs,
        scratch_shapes=scratch,
        compiler_params=pltpu.CompilerParams(**params),
        cost_estimate=pl.CostEstimate(flops=20 * 10**9, bytes_accessed=40 * 10**6, transcendentals=6 * 10**6),
    )(lengths, tokens, b_out, *weights)
    if comm:
        flat = (4, width, width)
        outs = list(outs)
        outs = outs[:6] + [w.reshape(flat) for w in outs[6:9]] + outs[9:]
    return outs


def row_mean(v):
    return jnp.mean(v, axis=-1, keepdims=True)


def ffn_kernel(
    n_seq, half, len_ref, hid_ref, cot_ref, u_ref, d_ref, s_ref, v0, v1, v2, v3, v4,
    out_ref, ag_ref, gu_ref, gd_ref, gv_ref, nb_all, fg_all, act_all, pg_all, dg,
):
    b = pl.program_id(0)
    rows = pl.ds(pl.multiple_of(b * half, half), half)
    n_gain, n_shift, b_down, f_gain, f_shift = (v[...].reshape(1, -1) for v in (v0, v1, v2, v3, v4))

    @pl.when(b == 0)
    def _():
        gv_ref[...] = jnp.zeros_like(gv_ref)

    def add(i, v):
        gv_ref[i : i + 1, :] += jnp.sum(v, axis=0, keepdims=True)

    hid = hid_ref[...]
    centred = hid - row_mean(hid)
    inv1 = lax.rsqrt(row_mean(centred * centred) + EPS)
    unit1 = centred * inv1
    normed = unit1 * n_gain + n_shift
    nb = normed.astype(BF16)
    nb_all[rows, :] = nb
    summed = normed + b_down
    for t in range(4):
        pre = dot_nn(nb, u_ref[t]) + s_ref[t, 4:5, 0:768]
        cdf = 0.5 * (1.0 + lax.erf(pre * 0.7071067811865476))
        act = (pre * cdf).astype(BF16)
        dg[t] = cdf + pre * (0.3989422804014327 * jnp.exp(-0.5 * pre * pre))
        act_all[t, rows, :] = act
        summed = summed + dot_nt(act, d_ref[t])
    centred = summed - row_mean(summed)
    inv2 = lax.rsqrt(row_mean(centred * centred) + EPS)
    unit2 = centred * inv2
    valid = (2 * lax.broadcasted_iota(jnp.int32, (half, 1), 0) < len_ref[my_core() * n_seq + b]).astype(F32)
    out_ref[...] = ((unit2 * f_gain + f_shift) * valid).astype(BF16)
    grad = cot_ref[...].astype(F32) * valid
    add(0, grad * unit2)
    add(1, grad)
    scaled = grad * f_gain
    grad_summed = inv2 * (scaled - row_mean(scaled) - unit2 * row_mean(scaled * unit2))
    add(2, grad_summed)
    fg = grad_summed.astype(BF16)
    fg_all[rows, :] = fg
    normed_grad = grad_summed
    for t in range(4):
        pg = (dot_nn(fg, d_ref[t]) * dg[t]).astype(BF16)
        pg_all[t, rows, :] = pg
        normed_grad = normed_grad + dot_nt(pg, u_ref[t])
    add(3, normed_grad * unit1)
    add(4, normed_grad)
    scaled = normed_grad * n_gain
    hidden_grad = inv1 * (scaled - row_mean(scaled) - unit1 * row_mean(scaled * unit1))
    add(5, hidden_grad)
    ag_ref[...] = hidden_grad.astype(BF16)

    @pl.when(b == n_seq - 1)
    def _():
        for i in range(2):
            pg = pg_all[i]
            gu_ref[i] = dot_tn(nb_all[...], pg).astype(BF16)
            gd_ref[i] = dot_tn(fg_all[...], act_all[i]).astype(BF16)
            gv_ref[6 + i : 7 + i, :] = jnp.sum(pg.astype(F32), axis=0, keepdims=True)


def ffn(lengths, hid, cotangent, u4, d4, s4, vectors, n_seq, half):
    width = hid.shape[1]
    once = pl.Buffered(1)
    return pl.pallas_call(
        functools.partial(ffn_kernel, n_seq, half),
        out_shape=(
            jax.ShapeDtypeStruct((n_seq * half, width), BF16),
            jax.ShapeDtypeStruct((n_seq * half, width), BF16),
            jax.ShapeDtypeStruct((2, width, 768), BF16),
            jax.ShapeDtypeStruct((2, width, 768), BF16),
            jax.ShapeDtypeStruct((8, width), F32),
        ),
        grid=(n_seq,),
        in_specs=[
            pl.BlockSpec(memory_space=pltpu.SMEM),
            pl.BlockSpec((half, width), lambda b: (b, 0)),
            pl.BlockSpec((half, width), lambda b: (my_core() * n_seq + b, 0)),
            pl.BlockSpec((4, width, 768), lambda b: (0, 0, 0), pipeline_mode=once),
            pl.BlockSpec((4, width, 768), lambda b: (0, 0, 0), pipeline_mode=once),
            pl.BlockSpec(s4.shape, lambda b: (0, 0, 0), pipeline_mode=once),
        ]
        + [pl.BlockSpec((width,), lambda b: (0,), pipeline_mode=once)] * 5,
        out_specs=[
            pl.BlockSpec((half, width), lambda b: (b, 0)),
            pl.BlockSpec((half, width), lambda b: (b, 0)),
            pl.BlockSpec((2, width, 768), lambda b: (0, 0, 0), pipeline_mode=once),
            pl.BlockSpec((2, width, 768), lambda b: (0, 0, 0), pipeline_mode=once),
            pl.BlockSpec((8, width), lambda b: (0, 0), pipeline_mode=once),
        ],
        scratch_shapes=[
            pltpu.VMEM((n_seq * half, width), BF16),
            pltpu.VMEM((n_seq * half, width), BF16),
            pltpu.VMEM((4, n_seq * half, 768), BF16),
            pltpu.VMEM((4, n_seq * half, 768), BF16),
            pltpu.VMEM((4, half, 768), F32),
        ],
        compiler_params=pltpu.CompilerParams(vmem_limit_bytes=VMEM_LIMIT),
        cost_estimate=pl.CostEstimate(flops=24 * 10**9, bytes_accessed=30 * 10**6, transcendentals=6 * 10**6),
    )(lengths, hid, cotangent, u4, d4, s4, *vectors)


class Net:
    def __init__(self, n_hi):
        self.n_hi = n_hi
        self.dp, self.t = lax.axis_index("dp"), lax.axis_index("tensor")
        self.hi, self.lo = self.dp // 2, lax.rem(self.dp, 2)
        self.core = lax.rem(self.t, 2)
        self.to_x = (self.dp + 1 - 2 * self.lo, self.t)
        self.to_c = (self.dp, self.t + 1 - 2 * self.core)

    def place(self, s):
        return lax.rem(self.hi + s, self.n_hi)

    def z_peer(self, s):
        return (self.place(s) * 2 + self.lo, self.t)

    def greet(self):
        barrier = pltpu.get_barrier_semaphore()
        peers = [self.z_peer(s) for s in range(1, self.n_hi)] + [self.to_x, self.to_c]
        for peer in peers:
            pl.semaphore_signal(barrier, inc=1, device_id=peer, device_id_type=MESH)
        pl.semaphore_wait(barrier, len(peers))

    def remote(self, src, dst, send, recv, peer):
        return pltpu.make_async_remote_copy(src, dst, send, recv, device_id=peer, device_id_type=MESH)


class Scatter:
    PARTS = 3

    def __init__(self, net, mine, other, bufs):
        self.net, self.mine, self.other = net, mine, other
        self.t1, self.t2, self.r3, self.sem, self.xs, self.xr, self.zs, self.zr = bufs
        self.rows = self.t2.shape[1] // self.PARTS

    @staticmethod
    def scratch(n_hi, rows, width):
        dma = pltpu.SemaphoreType.DMA
        both, half = pltpu.VMEM((n_hi, 2, rows, width), BF16), pltpu.VMEM((n_hi, rows, width), BF16)
        parts = Scatter.PARTS
        return [both, half, half, dma((2,)), dma((parts,)), dma((parts,)), dma((parts, n_hi)), dma((parts, n_hi))]

    def part(self, i):
        return pl.ds(i * self.rows, self.rows)

    def over_core(self):
        return self.net.remote(self.other, self.t1, self.sem.at[0], self.sem.at[1], self.net.to_c)

    def over_x(self, i):
        src = self.t1.at[:, 1 - self.net.lo, self.part(i)]
        return self.net.remote(src, self.t2.at[:, self.part(i)], self.xs.at[i], self.xr.at[i], self.net.to_x)

    def over_z(self, i, s):
        src = self.t2.at[self.net.place(s), self.part(i)]
        dst = self.r3.at[s, self.part(i)]
        return self.net.remote(src, dst, self.zs.at[i, s], self.zr.at[i, s], self.net.z_peer(s))

    def core_to_x(self):
        self.over_core().wait_recv()
        self.t1[...] += self.mine[...]
        for i in range(self.PARTS):
            self.over_x(i).start()

    def x_sum(self, i):
        self.over_x(i).wait_recv()
        rows = self.part(i)
        self.t2[:, rows] += self.t1[:, self.net.lo, rows]

    def start_z(self, i):
        for s in range(1, self.net.n_hi):
            self.over_z(i, s).start()

    def x_to_z(self, i):
        self.x_sum(i)
        self.start_z(i)

    def finish(self, out):
        for i in range(self.PARTS):
            rows = self.part(i)
            total = self.t2[self.net.hi, rows].astype(F32)
            for s in range(1, self.net.n_hi):
                self.over_z(i, s).wait_recv()
                total += self.r3[s, rows].astype(F32)
            out[rows, :] = total

    def sent_x(self):
        self.over_core().wait_send()
        for i in range(self.PARTS):
            self.over_x(i).wait_send()

    def sent_z(self):
        for i in range(self.PARTS):
            for s in range(1, self.net.n_hi):
                self.over_z(i, s).wait_send()


class SmallSum:
    def __init__(self, net, mine, other, bufs):
        self.net, self.mine, self.other = net, mine, other
        self.rc, self.v1, self.rx, self.v2, self.sem, self.zs, self.zr = bufs

    @staticmethod
    def scratch(n_hi, shape):
        dma = pltpu.SemaphoreType.DMA
        return [
            pltpu.VMEM(shape, F32), pltpu.VMEM(shape, F32), pltpu.VMEM(shape, F32), pltpu.VMEM((n_hi,) + shape, F32),
            dma((4,)), dma((n_hi,)), dma((n_hi,)),
        ]

    def over_core(self):
        return self.net.remote(self.other, self.rc, self.sem.at[0], self.sem.at[1], self.net.to_c)

    def over_x(self):
        return self.net.remote(self.v1, self.rx, self.sem.at[2], self.sem.at[3], self.net.to_x)

    def over_z(self, s):
        here = self.v2.at[self.net.hi]
        return self.net.remote(here, here, self.zs.at[s], self.zr.at[s], self.net.z_peer(s))

    def core_to_x(self):
        self.over_core().wait_recv()
        self.v1[...] = self.mine[...] + self.rc[...]
        self.over_x().start()

    def x_to_z(self):
        self.over_x().wait_recv()
        self.v2[self.net.hi] = self.v1[...] + self.rx[...]
        for s in range(1, self.net.n_hi):
            self.over_z(s).start()

    def finish(self, out):
        for s in range(1, self.net.n_hi):
            self.over_z(s).wait()
        out[...] = jnp.sum(self.v2[...], axis=0)
        self.over_core().wait_send()
        self.over_x().wait_send()

def backward_step(half, own, step_refs):
    kv_ref, q_ref, p_ref, ag, a_of, tacc, kvd, qd_ref = step_refs
    low = lane_low((half, 128))
    cg = dot_nn(ag, a_of(slice(512, 768))).astype(BF16)
    q01 = q_ref[0, :, 0:128]
    cg2, cg01 = cg[:, 0:128], cg[:, 128:256]
    zero = jnp.zeros_like(q01)
    heads = (
        (jnp.where(low, q01, zero), jnp.where(low, cg01, zero), 0, 128),
        (jnp.where(low, zero, q01), jnp.where(low, zero, cg01), 0, 128),
        (q_ref[0, :, 128:256], jnp.where(low, zero, cg2), 256, 256),
    )
    raw = [dot_nt(kv_ref[0, :, v_at : v_at + 128], g) for _, g, _, v_at in heads]
    vds = [dot_nn(p_ref[0, 0, h], head[1]) for h, head in enumerate(heads)]
    grads = []
    for h in range(3):
        p = p_ref[0, 0, h].astype(F32)
        row = jnp.sum(p * raw[h], axis=0, keepdims=True)
        sg = (p * (raw[h] - row)).astype(BF16)
        if own:
            tacc[h] += sg.astype(F32)
        grads.append(sg)
    kds = [dot_nn(sg, head[0]) for sg, head in zip(grads, heads)]
    qds = [dot_tn(kv_ref[0, :, head[2] : head[2] + 128], sg) for sg, head in zip(grads, heads)]
    kvd[:, 0:128] = (kds[0] + kds[1]).astype(BF16)
    kvd[:, 128:256] = (vds[0] + vds[1]).astype(BF16)
    kvd[:, 256:384] = (kds[2] + vds[2]).astype(BF16)
    qd01 = jnp.concatenate([qds[0][0:64], qds[1][64:128]], axis=0).T
    qd2 = jnp.concatenate([qds[2][0:64], jnp.zeros_like(qds[2][0:64])], axis=0).T
    qd = jnp.concatenate([qd01, qd2], axis=1).astype(BF16)
    qd_ref[...] = qd


def backward_place(step, n_seq):
    core = my_core()
    own = jnp.where(step < n_seq, 1 - core, core)
    rest = 2 + lax.rem(step, 2)
    first = step < 2 * n_seq
    return jnp.where(first, own, rest), jnp.where(first, lax.rem(step, n_seq), lax.rem(step, 2 * n_seq) // 2)


def backward_kernel(n_seq, length, n_dp, comm, *refs):
    half = length // 2
    n_hi = n_dp // 2
    step = pl.program_id(0)
    n_own = 2 * n_seq
    own = step < n_own
    g, b = backward_place(step, n_seq)
    x_any, a_any, kv_ref, q_ref, p_ref, ctx_any, ag_ref, pb_any = refs[:8]
    refs = refs[8:]
    if comm:
        gu_any, gd_any, gv_ref, half_any = refs[:4]
        out_any, tok_any, up_out, down_out, a_out, gv_out, sm_out = refs[4:11]
        refs = refs[11:]
    else:
        tok_out, ga_ref, sm_ref = refs[:3]
        refs = refs[3:]
    kvd, qd_all, tacc, tok, pool, kvd_rest, qd_rest, x_ref, ctx_ref, pb_ref, a_ref, fetch = refs[:12]
    refs = refs[12:]
    core = my_core()
    n_tok = n_seq * length
    late = (
        pltpu.make_async_copy(x_any.at[pl.ds(pl.multiple_of(core * n_tok, n_tok), n_tok), :], x_ref, fetch.at[0]),
        pltpu.make_async_copy(ctx_any.at[0:2], ctx_ref, fetch.at[1]),
        pltpu.make_async_copy(pb_any, pb_ref, fetch.at[2]),
    )
    a_copies = [
        pltpu.make_async_copy(a_any.at[pl.ds(i, 2)], a_ref.at[pl.ds(i, 2)], fetch.at[5 + i // 2]) for i in (0, 2)
    ]

    @pl.when(step == 0)
    def _():
        for copy in a_copies:
            copy.start()

    last = step == 2 * n_own - 1

    def at(n, *actions):
        @pl.when(step == n)
        def _():
            for action in actions:
                action()

    if comm:
        ga_ref, sm_ref, gu_mine, gd_mine, stage, half_ref = refs[:6]
        refs = refs[1:]
        net = Net(n_hi)
        other = 1 - core
        up = Scatter(net, gu_mine, gu_any.at[other], refs[5:13])
        down = Scatter(net, gd_mine, gd_any.at[other], refs[13:21])
        att = Scatter(net, ga_ref.at[core], ga_ref.at[other], refs[21:29])
        vec = SmallSum(net, gv_ref, gv_ref, refs[29:36])
        small = SmallSum(net, sm_ref.at[core], sm_ref.at[other], refs[36:43])
        o_sem, t_sem = refs[43:45]
        n_rows = n_seq * half
        there = out_any.at[pl.ds(pl.multiple_of(core * n_rows, n_rows), n_rows), :]
        o_copies = (
            pltpu.make_async_copy(half_ref, there, o_sem.at[0]),
            net.remote(half_ref, there, o_sem.at[1], o_sem.at[2], net.to_c),
        )
        mine = (
            pltpu.make_async_copy(gu_any.at[core], gu_mine, fetch.at[3]),
            pltpu.make_async_copy(gd_any.at[core], gd_mine, fetch.at[4]),
            pltpu.make_async_copy(half_any, half_ref, fetch.at[7]),
        )

        def tok_copies(i):
            row = pl.multiple_of((core * n_seq + i) * length, length)
            where = tok_any.at[pl.ds(row, length), :]
            return (
                pltpu.make_async_copy(stage.at[i], where, t_sem.at[0, i]),
                net.remote(stage.at[i], where, t_sem.at[1, i], t_sem.at[2, i], net.to_c),
            )

        @pl.when(step == 0)
        def _():
            for copy in mine:
                copy.start()
            net.greet()
            vec.over_core().start()
            up.over_core().start()
            down.over_core().start()

        at(1, vec.core_to_x, mine[2].wait, o_copies[0].start, o_copies[1].start)
        at(2, mine[0].wait, up.core_to_x, mine[1].wait, down.core_to_x)
        at(4, att.over_core().start, small.over_core().start, vec.x_to_z, lambda: up.x_to_z(0))
        at(5, lambda: up.x_to_z(1))
        at(6, lambda: up.x_to_z(2))
        at(7, lambda: down.x_to_z(0))
        at(8, small.core_to_x, att.core_to_x, lambda: down.x_to_z(1))
        at(9, lambda: down.x_to_z(2))
        at(11, lambda: att.x_to_z(0), small.x_to_z)
        at(13, lambda: att.x_to_z(1))
        at(15, lambda: att.x_to_z(2))

    @pl.when(step == 0)
    def _():
        for copy in late:
            copy.start()
        a_copies[0].wait()

    pl.when(step == n_own)(a_copies[1].wait)

    krows = pl.ds(pl.multiple_of(b * length, length), length)
    qrows = pl.ds(pl.multiple_of(b * half, half), half)

    @pl.when(own)
    def _():
        @pl.when(b == 0)
        def _():
            tacc[g] = jnp.zeros_like(tacc[g])

        backward_step(
            half,
            True,
            (kv_ref, q_ref, p_ref, ag_ref[qrows, :], lambda lanes: a_ref[g, :, lanes], tacc.at[g],
             kvd.at[g, krows], qd_all.at[g, qrows]),
        )

        @pl.when(step == n_seq - 1)
        def _():
            for copy in late:
                copy.wait()

        @pl.when(b == n_seq - 1)
        def _():
            def store(lanes, v):
                v = v.astype(BF16)
                ga_ref[g, ..., lanes] = v.reshape(ga_ref.shape[1:-1] + v.shape[-1:])

            store(slice(0, 384), dot_tn(x_ref[...], kvd[g]))
            gq = dot_tn(pb_ref[...], qd_all[g]) * 0.125
            go = dot_tn(ag_ref[...], ctx_ref[g])
            store(slice(384, 512), gq[:, 0:128])
            store(slice(512, 640), gq[:, 128:256] + go[:, 0:128])
            store(slice(640, 768), go[:, 128:256])
            sm_ref[g, 3:8, :] = jnp.zeros((5, 2 * length), F32)
            sm_ref[g, 3:4, 0:384] = jnp.sum(kvd[g].astype(F32), axis=0, keepdims=True)
            i = lax.broadcasted_iota(jnp.int32, (half, half), 0)
            j = lax.broadcasted_iota(jnp.int32, (half, half), 1)
            flip = jnp.where(i + j == half - 1, 1.0, 0.0).astype(BF16)
            for h in range(3):
                high = tacc[g, h].astype(BF16)
                rest = (tacc[g, h] - high.astype(F32)).astype(BF16)
                turned = dot_nt(flip, high) + dot_nt(flip, rest)
                wide = jnp.concatenate([turned, jnp.zeros((half, length), F32)], axis=1)
                rolled = pltpu.roll(wide, 2, 1, stride=2, stride_axis=0)
                sm_ref[g, h : h + 1, :] = jnp.sum(rolled, axis=0, keepdims=True)

    @pl.when(jnp.logical_not(own))
    def _():
        backward_step(
            half,
            False,
            (kv_ref, q_ref, p_ref, ag_ref[qrows, :], lambda lanes: a_ref[g, :, lanes], None, kvd_rest, qd_rest),
        )
        h = g - 2
        tok_add = dot_nt(kvd_rest[...], a_ref[g, :, 0:384]) + dot_nt(kvd[h, krows], a_ref[h, :, 0:384])
        pool_add = dot_nt(qd_rest[...], a_ref[g, :, 384:640]) + dot_nt(qd_all[h, qrows], a_ref[h, :, 384:640])

        @pl.when(g == 2)
        def _():
            tok[...] = tok_add
            pool[...] = pool_add

        @pl.when(g == 3)
        def _():
            total = ((pool[...] + pool_add) * 0.125 + ag_ref[qrows, :].astype(F32)).astype(BF16)
            final = (tok[...] + tok_add + dot_tn(pool_matrix(half, length), total)).astype(BF16)
            if comm:
                stage[b] = final
                for copy in tok_copies(b):
                    copy.start()
            else:
                tok_out[...] = final

    if comm:

        @pl.when(last)
        def _():
            vec.finish(gv_out)
            up.finish(up_out)
            down.finish(down_out)
            small.finish(sm_out)
            att.finish(a_out)
            for each in (up, down, att):
                each.sent_x()
                each.sent_z()
            for copy in o_copies:
                copy.wait()
            for i in range(n_seq):
                for copy in tok_copies(i):
                    copy.wait()


def fixed(shape, first=None):
    def index(*grid):
        head = 0 if first is None else first()
        return (head,) + (0,) * (len(shape) - 1)

    return pl.BlockSpec(shape, index, pipeline_mode=pl.Buffered(1))


ANY = pl.BlockSpec(memory_space=pl.ANY)


def attention_backward(tokens, a4, kv, q, p, ctx, ag, pb, gu, gd, gv, out_half, n_seq, n_dp, comm):
    length = kv.shape[1] // n_seq
    half = length // 2
    width = tokens.shape[1]
    n_tok, n_pool = n_seq * length, n_seq * half
    n_own = 2 * n_seq
    n_hi, rows = n_dp // 2, width // n_dp

    def place(n):
        return backward_place(n, n_seq)

    in_specs = [
        ANY,
        ANY,
        pl.BlockSpec((1, length, 384), lambda n: place(n) + (0,)),
        pl.BlockSpec((1, half, 256), lambda n: place(n) + (0,)),
        pl.BlockSpec((1, 1, 3, length, half), lambda n: place(n) + (0, 0, 0)),
        ANY,
        fixed((n_pool, width)),
        ANY,
    ]
    args = [tokens, a4, kv, q, p, ctx, ag, pb]
    scratch = [
        pltpu.VMEM((2, n_tok, 384), BF16), pltpu.VMEM((2, n_pool, 256), BF16), pltpu.VMEM((2, 3, length, half), F32),
        pltpu.VMEM((length, width), F32), pltpu.VMEM((half, width), F32), pltpu.VMEM((length, 384), BF16),
        pltpu.VMEM((half, 256), BF16), pltpu.VMEM((n_tok, width), BF16), pltpu.VMEM((2, n_pool, 256), BF16), pltpu.VMEM((n_pool, width), BF16),
        pltpu.VMEM((4, width, 768), BF16), pltpu.SemaphoreType.DMA((8,)),
    ]
    params = {"vmem_limit_bytes": VMEM_LIMIT}
    small = (8, 2 * length)
    if comm:
        split = (2, n_hi, 2, rows, width)
        in_specs += [ANY, ANY, fixed(gv.shape), ANY]
        args += [gu.reshape(split), gd.reshape(split), gv, out_half]
        shares = [jax.ShapeDtypeStruct((rows, width), F32)] * 3
        out_shape = [
            jax.ShapeDtypeStruct((2 * n_pool, width), BF16), jax.ShapeDtypeStruct((2 * n_tok, width), BF16), *shares,
            jax.ShapeDtypeStruct(gv.shape, F32), jax.ShapeDtypeStruct(small, F32),
        ]
        out_specs = [ANY, ANY] + [fixed((rows, width))] * 3 + [fixed(gv.shape), fixed(small)]
        scratch += [
            pltpu.VMEM(split, BF16), pltpu.VMEM((2,) + small, F32), pltpu.VMEM(split[1:], BF16),
            pltpu.VMEM(split[1:], BF16), pltpu.VMEM((n_seq, length, width), BF16),
            pltpu.VMEM(out_half.shape, BF16),
        ]
        for _ in range(3):
            scratch += Scatter.scratch(n_hi, rows, width)
        scratch += SmallSum.scratch(n_hi, gv.shape) + SmallSum.scratch(n_hi, small)
        scratch += [pltpu.SemaphoreType.DMA((3,)), pltpu.SemaphoreType.DMA((3, n_seq))]
        params.update(collective_id=1, has_side_effects=True)
    else:
        out_shape = [
            jax.ShapeDtypeStruct((n_tok, width), BF16), jax.ShapeDtypeStruct((2, width, 768), BF16),
            jax.ShapeDtypeStruct((2,) + small, F32),
        ]
        out_specs = [
            pl.BlockSpec((length, width), lambda n: (jnp.maximum(n - n_own, 0) // 2, 0)), fixed((2, width, 768)),
            fixed((2,) + small),
        ]
    return pl.pallas_call(
        functools.partial(backward_kernel, n_seq, length, n_dp, comm),
        out_shape=out_shape,
        grid=(2 * n_own,),
        in_specs=in_specs,
        out_specs=out_specs,
        scratch_shapes=scratch,
        compiler_params=pltpu.CompilerParams(**params),
        cost_estimate=pl.CostEstimate(flops=40 * 10**9, bytes_accessed=30 * 10**6, transcendentals=0),
    )(*args)


def finish_kernel(big, a_ref, up_ref, down_ref, gv_ref, sm_ref, *refs):
    n = len(big)
    moves = [
        [
            (
                pltpu.make_async_copy(src.at[pl.ds(i * chunk, chunk)], buf.at[i], sem.at[0, i]),
                pltpu.make_async_copy(buf.at[i], dst.at[pl.ds(i * chunk, chunk)], sem.at[1, i]),
            )
            for i in range(count)
        ]
        for (count, chunk), src, dst, buf, sem in zip(
            big, refs[:n], refs[n : 2 * n], refs[2 * n + 15 :: 2], refs[2 * n + 16 :: 2]
        )
    ]
    moves = sum(moves, [])
    for come, _ in moves:
        come.start()
    query, key, value, out, up, down, table, vbias, ubias, *vectors = refs[2 * n : 2 * n + 15]
    query[...] = a_ref[:, 384:576]
    key[:, 0:128] = a_ref[:, 0:128]
    key[:, 128:192] = a_ref[:, 256:320]
    value[:, 0:128] = a_ref[:, 128:256]
    value[:, 128:192] = a_ref[:, 320:384]
    out[0:128, :] = a_ref[:, 640:768].T
    out[128:192, :] = a_ref[:, 512:640].T[64:128]
    up[...] = up_ref[...]
    down[...] = down_ref[...]
    table[...] = sm_ref[0:3, :]
    vbias[0:128] = sm_ref[3, 128:256]
    vbias[128:192] = sm_ref[3, 320:384]
    ubias[...] = jnp.where(my_core() == 0, gv_ref[6, :], gv_ref[7, :])
    for i, vec in enumerate(vectors):
        vec[...] = gv_ref[i, :]
    for come, go in moves:
        come.wait()
        go.start()
    for _, go in moves:
        go.wait()


def finish(big, a_sum, up_sum, down_sum, gv, sm, length):
    rows, width = a_sum.shape
    shapes = [(rows, 192)] * 3 + [(192, rows), (rows, 768), (rows, 768), (3, 2 * length), (192,), (768,)] + [(width,)] * 6
    cuts, scratch = [], []
    for v in big:
        count = v.shape[0] // 512
        cuts.append((count, 512))
        scratch += [pltpu.VMEM((count, 512, v.shape[1]), v.dtype), pltpu.SemaphoreType.DMA((2, count))]
    whole = pl.BlockSpec(memory_space=pltpu.VMEM)
    return pl.pallas_call(
        functools.partial(finish_kernel, tuple(cuts)),
        out_shape=[jax.ShapeDtypeStruct(v.shape, v.dtype) for v in big]
        + [jax.ShapeDtypeStruct(shape, F32) for shape in shapes],
        in_specs=[whole] * 5 + [ANY] * len(big),
        out_specs=[ANY] * len(big) + [whole] * len(shapes),
        scratch_shapes=scratch,
        compiler_params=pltpu.CompilerParams(vmem_limit_bytes=VMEM_LIMIT),
    )(a_sum, up_sum, down_sum, gv, sm, *big)


def gather_plain(weights, length):
    kw, vw, qw, ow, uw, dw, tab, vbias, hbias = weights
    ot = ow.T
    packed = jnp.concatenate([kw[:, :128], vw[:, :128], kw[:, 128:], vw[:, 128:], qw, ot[:, 128:], ot[:, :128]], axis=1)
    small = jnp.zeros((8, 2 * length), F32).at[0:3].set(tab).at[3, 128:256].set(vbias[:128])
    small = small.at[3, 320:384].set(vbias[128:]).at[4, : hbias.shape[0]].set(hbias)
    first = 2 * (lax.axis_index("tensor") // 2)

    def groups(v):
        every = lax.all_gather(v, "tensor")
        return lax.dynamic_slice_in_dim(jnp.concatenate([every, every]), first, 4)

    wide = jnp.stack([packed, uw, dw], axis=1).astype(BF16)
    wide = groups(lax.all_gather(wide, "dp", axis=0, tiled=True))
    return wide[:, :, 0], wide[:, :, 1], wide[:, :, 2], groups(small)


def sum_plain(grads, n_dp):
    core = my_core()
    mine = lax.dynamic_index_in_dim(grads, core, 0, keepdims=False).astype(F32)
    other = lax.dynamic_index_in_dim(grads, 1 - core, 0, keepdims=False)
    total = mine + lax.ppermute(other, "tensor", [(i, i ^ 1) for i in range(4)]).astype(F32)
    return lax.psum_scatter(total, "dp", scatter_dimension=0, tiled=True)


def shards(
    n_dp, tokens, lengths, cotangent, query_weight, key_weight, value_weight, value_bias, output_weight,
    b_out, rel_table, norm_gain, norm_shift, up_weight, hidden_bias, down_weight, b_down, final_gain, final_shift,
):
    seq_count = lengths.shape[0]
    length = tokens.shape[0] // seq_count
    half = length // 2
    n_seq = seq_count // 2
    core = my_core()
    n_hi, rows = n_dp // 2, tokens.shape[1] // n_dp
    comm = rows % 16 == 0 and n_hi <= 4

    weights = (
        key_weight, value_weight, query_weight, output_weight, up_weight, down_weight.T, rel_table,
        value_bias, hidden_bias,
    )
    if not comm:
        weights = gather_plain(weights, length)
        a4, u4, d4, s4 = weights
        weights = (a4, s4)
    kv, q, p, ctx, hid, pb, *gathered = attention_forward(lengths, tokens, b_out, weights, n_dp, comm)
    if comm:
        a4, u4, d4, s4 = gathered
    vectors = (norm_gain, norm_shift, b_down, final_gain, final_shift)
    out_half, ag, gu, gd, gv = ffn(lengths, hid, cotangent, u4, d4, s4, vectors, n_seq, half)
    sums = attention_backward(tokens, a4, kv, q, p, ctx, ag, pb, gu, gd, gv, out_half, n_seq, n_dp, comm)
    if comm:
        output, tokens_grad, up_sum, down_sum, a_sum, gv, sm = sums
    else:
        tok_half, ga, sm = sums
        up_sum, down_sum, a_sum = (sum_plain(v, n_dp) for v in (gu, gd, ga))
        sm, gv = lax.psum((sm, gv), "dp")

        def over_core(v):
            return lax.ppermute(v, "tensor", [(i, i ^ 1) for i in range(4)])

        gv = gv + over_core(gv)
        mine = lax.dynamic_index_in_dim(sm, core, 0, keepdims=False)
        sm = mine + over_core(lax.dynamic_index_in_dim(sm, 1 - core, 0, keepdims=False))

        def join(part):
            got = over_core(part)
            return jnp.where(core == 0, jnp.concatenate([part, got]), jnp.concatenate([got, part]))

        output, tokens_grad = join(out_half), join(tok_half)
    output, tokens_grad, *cut = finish((output, tokens_grad), a_sum, up_sum, down_sum, gv, sm, length)
    query_sum, key_sum, value_sum, outw_sum, up_sum, down_sum, table_sum, vbias, ubias = cut[:9]
    fgain, fshift, dbias, ngain, nshift, obias = cut[9:]
    return (
        output, tokens_grad, query_sum, key_sum, value_sum, vbias, outw_sum, obias, table_sum,
        ngain, nshift, up_sum, ubias, down_sum.T, dbias, fgain, fshift,
    )


def solution(mesh):
    row, col, both, rep = P("dp", None), P("tensor", "dp"), P("dp", "tensor"), P()
    ten, table = P("tensor"), P("tensor", None)
    in_specs = (
        row, P("dp"), row, both, both, both, ten, col, rep, table, rep, rep, both, ten, col, rep, rep, rep,
    )
    out_specs = (
        row, row, both, both, both, ten, col, rep, table, rep, rep, both, ten, col, rep, rep, rep,
    )
    body = functools.partial(shards, mesh.shape["dp"])
    return jax.shard_map(body, mesh=mesh, in_specs=in_specs, out_specs=out_specs, check_vma=False)
```

```python
import functools

import jax
import jax.numpy as jnp
from jax import lax
from jax.experimental import pallas as pl
from jax.experimental.pallas import tpu as pltpu
from jax.sharding import PartitionSpec as P

MESH = pl.DeviceIdType.MESH
F32 = jnp.float32
BF16 = jnp.bfloat16
EPS = 1e-06
VMEM_LIMIT = 58 * 2**20


def dot_nn(a, b):
    return lax.dot_general(a, b, (((1,), (0,)), ((), ())), preferred_element_type=F32)


def dot_nt(a, b):
    return lax.dot_general(a, b, (((1,), (1,)), ((), ())), preferred_element_type=F32)


def dot_tn(a, b):
    return lax.dot_general(a, b, (((0,), (0,)), ((), ())), preferred_element_type=F32)


class Gather:
    def __init__(self, n_hi, ins, outs, s_in, s_out, sems):
        self.n_hi, self.ins, self.outs, self.s_in, self.s_out = n_hi, ins, outs, s_in, s_out
        self.loc, self.zs, self.zr, self.ls, self.lr, self.fs, self.fr, self.cs, self.cr, self.ss, self.sr = sems
        self.dp, self.t = lax.axis_index("dp"), lax.axis_index("tensor")
        self.hi, self.lo = self.dp // 2, lax.rem(self.dp, 2)
        self.core = lax.rem(self.t, 2)
        t_core = self.t + 1 - 2 * self.core
        self.to_x = (self.dp + 1 - 2 * self.lo, self.t)
        self.to_y = (self.dp, lax.rem(self.t + 2, 4))
        self.to_c = (self.dp, t_core)
        self.to_d = (self.dp, lax.rem(t_core + 2, 4))

    def block(self, s, side):
        return lax.rem(self.hi - s + self.n_hi, self.n_hi) * 2 + side

    def greet(self):
        barrier = pltpu.get_barrier_semaphore()
        for up, exists in ((0, self.hi < self.n_hi - 1), (1, self.hi > 0)):

            @pl.when(exists)
            def _():
                pl.semaphore_signal(barrier, inc=1, device_id=self.z_next(up), device_id_type=MESH)

        for peer in (self.to_x, self.to_y, self.to_c, self.to_d):
            pl.semaphore_signal(barrier, inc=1, device_id=peer, device_id_type=MESH)
        along_z = jnp.where(self.hi < self.n_hi - 1, 1, 0) + jnp.where(self.hi > 0, 1, 0)
        pl.semaphore_wait(barrier, 4 + along_z)

    def z_next(self, down):
        hi = jnp.maximum(self.hi - 1, 0) if down else jnp.minimum(self.hi + 1, self.n_hi - 1)
        return (hi * 2 + self.lo, self.t)

    def remote(self, src, dst, send, recv, peer):
        return pltpu.make_async_remote_copy(src, dst, send, recv, device_id=peer, device_id_type=MESH)

    def small(self):
        core = self.core
        return (
            pltpu.make_async_copy(self.s_in, self.s_out.at[core], self.loc.at[3]),
            self.remote(self.s_in, self.s_out.at[core], self.ss.at[0], self.sr.at[0], self.to_c),
            self.remote(self.s_in, self.s_out.at[2 + core], self.ss.at[1], self.sr.at[1], self.to_y),
            self.remote(self.s_in, self.s_out.at[2 + core], self.ss.at[2], self.sr.at[2], self.to_d),
        )

    def local(self, k):
        return pltpu.make_async_copy(self.ins[k], self.outs[k].at[self.core, self.dp], self.loc.at[k])

    def z_send(self, k, d, down):
        b = self.block(self.n_hi - d if down else d, self.lo)
        dst = self.outs[k].at[self.core, b]
        src = self.ins[k] if d == 0 else dst
        return self.remote(src, dst, self.zs.at[down, k, d], self.zr.at[down, k, d], self.z_next(down))

    def z_more(self, down):
        return self.hi > 0 if down else self.hi < self.n_hi - 1

    def z_came(self, d, down):
        return self.hi + d < self.n_hi if down else self.hi >= d

    def line(self, k, s, way, own=False):
        out, b = self.outs[k], self.block(s, self.lo)
        src = self.ins[k] if own else out.at[self.core, b]
        dst = out.at[self.core if way == 0 else 2 + self.core, b]
        return self.remote(
            src, dst, self.ls.at[way, k, s], self.lr.at[way, k, s], self.to_x if way == 0 else self.to_y
        )

    def onward(self, k, s, way):
        out = self.outs[k]
        if way == 0:
            src = dst = out.at[2 + self.core, self.block(s, self.lo)]
        else:
            b = self.block(s, 1 - self.lo)
            src, dst = out.at[self.core, b], out.at[2 + self.core, b]
        return self.remote(src, dst, self.fs.at[k, s], self.fr.at[k, s], self.to_x if way == 0 else self.to_y)

    def to_core(self, k, s, which, own=False):
        out = self.outs[k]
        side = self.lo if which % 2 == 0 else 1 - self.lo
        where = out.at[self.core if which < 2 else 2 + self.core, self.block(s, side)]
        return self.remote(
            self.ins[k] if own else where, where, self.cs.at[which, k, s], self.cr.at[which, k, s], self.to_c
        )

    def start(self, k):
        for down in range(2):
            pl.when(self.z_more(down))(lambda: self.z_send(k, 0, down).start())
        self.line(k, 0, 0, True).start()
        if k == 0:
            self.line(k, 0, 1, True).start()
        self.to_core(k, 0, 0, True).start()
        self.local(k).start()

    def lines_y(self, k):
        for s in range(self.n_hi):
            self.line(k, s, 1, s == 0).start()

    def near(self, d, action):
        if d == 0:
            action(0)
            return
        pl.when(self.z_came(d, 0))(lambda: action(d))
        pl.when(self.z_came(d, 1))(lambda: action(self.n_hi - d))

    def spread(self, k, d):
        for down in range(2):

            @pl.when(self.z_came(d, down))
            def _():
                self.z_send(k, d - 1, down).wait_recv()
                if d < self.n_hi - 1:
                    pl.when(self.z_more(down))(lambda: self.z_send(k, d, down).start())
                s = self.n_hi - d if down else d
                self.line(k, s, 0).start()
                if k == 0:
                    self.line(k, s, 1).start()
                self.to_core(k, s, 0).start()

    def over_x(self, k, s):
        self.line(k, s, 0).wait_recv()
        self.onward(k, s, 1).start()
        self.to_core(k, s, 1).start()

    def over_y(self, k, s):
        self.line(k, s, 1).wait_recv()
        self.onward(k, s, 0).start()
        self.to_core(k, s, 2).start()

    def late_x(self, k, s):
        self.line(k, s, 0).wait_recv()
        self.to_core(k, s, 1).start()

    def late_y(self, k, s):
        self.line(k, s, 1).wait_recv()
        self.to_core(k, s, 2).start()

    def pass_on(self, k, d, core=None):
        if k == 2:
            way = (self.over_x, self.over_y)[core]
            pl.when(self.core == core)(lambda: self.near(d, lambda s: way(k, s)))
        else:
            way = (self.over_x, self.over_y)[k]
            self.near(d, lambda s: way(k, s))

    def late(self, k):
        for s in range(self.n_hi):
            if k == 2:
                pl.when(self.core == 0)(lambda: self.late_y(k, s))
                pl.when(self.core == 1)(lambda: self.late_x(k, s))
            else:
                (self.late_y, self.late_x)[k](k, s)

    def diagonal(self, k, s):
        self.onward(k, s, 0).wait_recv()
        self.to_core(k, s, 3).start()

    def arrived(self, k, whiches):
        for s in range(self.n_hi):
            for which in whiches:
                self.to_core(k, s, which).wait_recv()

    def sent(self, k):
        for down in range(2):
            for d in range(self.n_hi - 1):
                came = self.z_more(down) if d == 0 else jnp.logical_and(self.z_more(down), self.z_came(d, down))
                pl.when(came)(lambda: self.z_send(k, d, down).wait_send())
        for s in range(self.n_hi):
            self.line(k, s, 0).wait_send()
            self.line(k, s, 1).wait_send()
            self.onward(k, s, 0).wait_send()
            for which in range(4):
                self.to_core(k, s, which).wait_send()


def gather_scratch(n_hi):
    dma = pltpu.SemaphoreType.DMA
    return [
        dma((4,)), dma((2, 3, n_hi)), dma((2, 3, n_hi)), dma((2, 3, n_hi)), dma((2, 3, n_hi)), dma((3, n_hi)),
        dma((3, n_hi)), dma((4, 3, n_hi)), dma((4, 3, n_hi)), dma((3,)), dma((3,)),
    ]


def pool_matrix(pooled, length):
    i = lax.broadcasted_iota(jnp.int32, (pooled, length), 0)
    j = lax.broadcasted_iota(jnp.int32, (pooled, length), 1)
    return jnp.where(j // 2 == i, 0.5, 0.0).astype(BF16)


def lane_low(shape):
    return lax.broadcasted_iota(jnp.int32, shape, 1) < 64


def attention_kernel(n_seq, length, n_dp, comm, *refs):
    half = length // 2
    group, b = pl.program_id(0), pl.program_id(1)
    step = group * n_seq + b
    core = lax.rem(lax.axis_index("tensor"), 2)
    len_ref, x_any, bo_ref = refs[:3]
    refs = refs[3:]
    if comm:
        (kw, vw, qw, ow, uw, dw, tab, vbias, hbias) = refs[:9]
        kv_ref, q_ref, p_ref, ctx_ref, hid_ref, pb_ref, a_out, u_out, d_out, s_out = refs[9:19]
        bias, x_ref, x_sem, a_in, u_in, d_in, s_in, a_all, s_all, a_sem, s_sem = refs[19:30]
        net = Gather(n_dp // 2, (a_in, u_in, d_in), (a_all, u_out, d_out), s_in, s_all, refs[30:])
    else:
        a_ref, s_ref = refs[:2]
        kv_ref, q_ref, p_ref, ctx_ref, hid_ref, pb_ref, bias, x_ref, x_sem = refs[2:]
    n_tok = n_seq * length
    x_copy = pltpu.make_async_copy(x_any.at[pl.ds(pl.multiple_of(core * n_tok, n_tok), n_tok), :], x_ref, x_sem)

    def pool_rows():
        x_copy.wait()
        pool = pool_matrix(half, length)
        for i in range(n_seq):
            pooled = dot_nn(pool, x_ref[i * length : (i + 1) * length, :])
            hid_ref[i * half : (i + 1) * half, :] = pooled + bo_ref[...].reshape(1, -1)
            pb_ref[i * half : (i + 1) * half, :] = pooled.astype(BF16)

    if comm:

        def a_copy(g):
            return pltpu.make_async_copy(a_all.at[g], a_out.at[g], a_sem.at[g])

        s_copy = pltpu.make_async_copy(s_all, s_out, s_sem)

        @pl.when(step == 0)
        def _():
            x_copy.start()
            k, v, o = kw[...], vw[...], ow[...].T
            parts = (k[:, :128], v[:, :128], k[:, 128:], v[:, 128:], qw[...], o[:, 128:], o[:, :128])
            a_in[...] = jnp.concatenate(parts, axis=1).astype(BF16)
            s_in[...] = jnp.zeros_like(s_in)
            s_in[0:3, :] = tab[...]
            vb = vbias[...].reshape(1, -1)
            s_in[3:4, 128:256] = vb[:, 0:128]
            s_in[3:4, 320:384] = vb[:, 128:192]
            s_in[4:5, 0 : hbias.shape[0]] = hbias[...].reshape(1, -1)
            net.greet()
            for copy in net.small():
                copy.start()
            net.start(0)
            u_in[...] = uw[...].astype(BF16)
            d_in[...] = dw[...].astype(BF16)
            for s in range(1, n_dp // 2):
                net.spread(0, s)
                net.pass_on(0, s - 1)
            net.start(1)
            net.pass_on(0, n_dp // 2 - 1)
            pool_rows()
            small = net.small()
            small[0].wait()
            for copy in small[1:]:
                copy.wait()
            s_copy.start()
            net.local(0).wait()
            net.arrived(0, (0, 1))

        n_hi = n_dp // 2
        plan = {}

        def at(n, action, *args):
            plan.setdefault(min(n, 4 * n_seq - 1), []).append(functools.partial(action, *args))

        for d in range(1, n_hi):
            at((1, 2, 3)[d - 1], net.spread, 1, d)
            at((4, 5, 6)[d - 1], net.spread, 2, d)
        at(2, net.start, 2)
        at(4, net.late, 0)
        for d in range(n_hi):
            at(4, net.diagonal, 0, d)
            at((6, 7, 8, 9)[d], net.pass_on, 1, d)
            at((9, 9, 10, 10)[d], net.pass_on, 2, d, 0)
            at((10, 11, 12, 13)[d], net.pass_on, 2, d, 1)
            at((10, 11, 12, 13)[d], lambda i: net.near(i, lambda s: net.diagonal(1, s)), d)
        at(3, net.lines_y, 1)
        at(2 * n_seq, net.arrived, 0, (2, 3))
        for g in range(4):
            at(2 * n_seq, lambda i: a_copy(i).start(), g)
        at(7, net.lines_y, 2)
        at(9, net.late, 1)
        at(14, net.late, 2)
        for n, actions in plan.items():

            @pl.when(step == n)
            def _():
                for action in actions:
                    action()

        def weights(lanes):
            return a_all[group, :, :, lanes].reshape(-1, lanes.stop - lanes.start)

        def small_row(i):
            return s_all[group, i : i + 1, :]
    else:

        @pl.when(step == 0)
        def _():
            x_copy.start()
            pool_rows()

        def weights(lanes):
            return a_ref[0, :, lanes]

        def small_row(i):
            return s_ref[0, i : i + 1, :]

    krows = pl.ds(pl.multiple_of(b * length, length), length)
    qrows = pl.ds(pl.multiple_of(b * half, half), half)

    @pl.when(b == 0)
    def _():
        for h in range(3):
            wide = jnp.broadcast_to(small_row(h), (half, 2 * length))
            bias[h] = pltpu.roll(wide, length, 1, stride=2, stride_axis=0)[:, :length].T

    kv_ref[0] = (dot_nn(x_ref[krows, :], weights(slice(0, 384))) + small_row(3)[:, 0:384]).astype(BF16)
    q = dot_nn(pb_ref[qrows, :], weights(slice(384, 640))) * 0.125
    lanes = lax.broadcasted_iota(jnp.int32, q.shape, 1)
    q = jnp.where(lanes < 192, q, 0.0).astype(BF16)
    q_ref[0] = q
    low = lane_low((half, 128))
    valid = lax.broadcasted_iota(jnp.int32, (length, half), 0) < len_ref[core * n_seq + b]
    q01 = q[:, 0:128]
    zero = jnp.zeros_like(q01)
    heads = (
        (jnp.where(low, q01, zero), 0, 128),
        (jnp.where(low, zero, q01), 0, 128),
        (q[:, 128:256], 256, 256),
    )
    raw = [dot_nt(kv_ref[0, :, k_at : k_at + 128], qh) for qh, k_at, _ in heads]
    probs = []
    for h in range(3):
        s = jnp.where(valid, raw[h] + bias[h], -1e30)
        e = jnp.exp(s - jnp.max(s, axis=0, keepdims=True))
        p = (e * (1.0 / jnp.sum(e, axis=0, keepdims=True))).astype(BF16)
        p_ref[0, 0, h] = p
        probs.append(p)
    contexts = [dot_tn(kv_ref[0, :, v_at : v_at + 128], p) for (_, _, v_at), p in zip(heads, probs)]
    c0, c1, c2 = contexts
    ctx01 = jnp.concatenate([c0[0:64], c1[64:128]], axis=0).T
    ctx2 = jnp.concatenate([jnp.zeros_like(c2[0:64]), c2[64:128]], axis=0).T
    ctx = jnp.concatenate([ctx2, ctx01], axis=1).astype(BF16)
    ctx_ref[0] = ctx
    hid_ref[qrows, :] += dot_nt(ctx, weights(slice(512, 768)))

    if comm:

        @pl.when(step == 4 * n_seq - 1)
        def _():
            for s in range(n_hi):
                net.diagonal(2, s)
            for k in range(3):
                net.sent(k)
            for k in (1, 2):
                net.local(k).wait()
                net.arrived(k, (0, 1, 2, 3))
            for g in range(4):
                a_copy(g).wait()
            s_copy.wait()


def my_core():
    return lax.rem(lax.axis_index("tensor"), 2)


def attention_forward(lengths, tokens, b_out, weights, n_dp, comm):
    n_seq = lengths.shape[0] // 2
    length = tokens.shape[0] // lengths.shape[0]
    half = length // 2
    width = tokens.shape[1]
    once = pl.Buffered(1)

    def fixed(shape):
        return pl.BlockSpec(shape, lambda g, b: (0,) * len(shape), pipeline_mode=once)

    in_specs = [
        pl.BlockSpec(memory_space=pltpu.SMEM),
        pl.BlockSpec(memory_space=pl.ANY),
        fixed((width,)),
    ]
    out_shape = [
        jax.ShapeDtypeStruct((4, n_seq * length, 384), BF16),
        jax.ShapeDtypeStruct((4, n_seq * half, 256), BF16),
        jax.ShapeDtypeStruct((4, n_seq, 3, length, half), BF16),
        jax.ShapeDtypeStruct((4, n_seq * half, 256), BF16),
        jax.ShapeDtypeStruct((n_seq * half, width), F32),
        jax.ShapeDtypeStruct((n_seq * half, width), BF16),
    ]
    out_specs = [
        pl.BlockSpec((1, length, 384), lambda g, b: (g, b, 0)),
        pl.BlockSpec((1, half, 256), lambda g, b: (g, b, 0)),
        pl.BlockSpec((1, 1, 3, length, half), lambda g, b: (g, b, 0, 0, 0)),
        pl.BlockSpec((1, half, 256), lambda g, b: (g, b, 0)),
        fixed((n_seq * half, width)),
        fixed((n_seq * half, width)),
    ]
    scratch = [
        pltpu.VMEM((3, length, half), F32), pltpu.VMEM((n_seq * length, width), BF16), pltpu.SemaphoreType.DMA,
    ]
    params = {"vmem_limit_bytes": VMEM_LIMIT}
    if comm:
        rows = width // n_dp
        in_specs += [fixed(w.shape) for w in weights]
        whole = jax.ShapeDtypeStruct((4, n_dp, rows, width), BF16)
        small = jax.ShapeDtypeStruct((4, 8, 2 * length), F32)
        out_shape += [whole, whole, whole, small]
        out_specs += [pl.BlockSpec(memory_space=pl.ANY)] * 4
        scratch += [pltpu.VMEM((rows, width), BF16)] * 3
        scratch += [
            pltpu.VMEM((8, 2 * length), F32),
            pltpu.VMEM((4, n_dp, rows, width), BF16),
            pltpu.VMEM((4, 8, 2 * length), F32),
            pltpu.SemaphoreType.DMA((4,)),
            pltpu.SemaphoreType.DMA,
        ]
        scratch += gather_scratch(n_dp // 2)
        params.update(collective_id=0, has_side_effects=True)
    else:
        in_specs += [
            pl.BlockSpec((1, width, 768), lambda g, b: (g, 0, 0)),
            pl.BlockSpec((1, 8, 2 * length), lambda g, b: (g, 0, 0)),
        ]
    outs = pl.pallas_call(
        functools.partial(attention_kernel, n_seq, length, n_dp, comm),
        out_shape=out_shape,
        grid=(4, n_seq),
        in_specs=in_specs,
        out_specs=out_specs,
        scratch_shapes=scratch,
        compiler_params=pltpu.CompilerParams(**params),
        cost_estimate=pl.CostEstimate(flops=20 * 10**9, bytes_accessed=40 * 10**6, transcendentals=6 * 10**6),
    )(lengths, tokens, b_out, *weights)
    if comm:
        flat = (4, width, width)
        outs = list(outs)
        outs = outs[:6] + [w.reshape(flat) for w in outs[6:9]] + outs[9:]
    return outs


def row_mean(v):
    return jnp.mean(v, axis=-1, keepdims=True)


def ffn_kernel(
    n_seq, half, len_ref, hid_ref, cot_ref, u_ref, d_ref, s_ref, v0, v1, v2, v3, v4,
    out_ref, ag_ref, gu_ref, gd_ref, gv_ref, nb_all, fg_all, act_all, pg_all, dg,
):
    b = pl.program_id(0)
    rows = pl.ds(pl.multiple_of(b * half, half), half)
    n_gain, n_shift, b_down, f_gain, f_shift = (v[...].reshape(1, -1) for v in (v0, v1, v2, v3, v4))

    @pl.when(b == 0)
    def _():
        gv_ref[...] = jnp.zeros_like(gv_ref)

    def add(i, v):
        gv_ref[i : i + 1, :] += jnp.sum(v, axis=0, keepdims=True)

    hid = hid_ref[...]
    centred = hid - row_mean(hid)
    inv1 = lax.rsqrt(row_mean(centred * centred) + EPS)
    unit1 = centred * inv1
    normed = unit1 * n_gain + n_shift
    nb = normed.astype(BF16)
    nb_all[rows, :] = nb
    summed = normed + b_down
    for t in range(4):
        pre = dot_nn(nb, u_ref[t]) + s_ref[t, 4:5, 0:768]
        cdf = 0.5 * (1.0 + lax.erf(pre * 0.7071067811865476))
        act = (pre * cdf).astype(BF16)
        dg[t] = cdf + pre * (0.3989422804014327 * jnp.exp(-0.5 * pre * pre))
        act_all[t, rows, :] = act
        summed = summed + dot_nt(act, d_ref[t])
    centred = summed - row_mean(summed)
    inv2 = lax.rsqrt(row_mean(centred * centred) + EPS)
    unit2 = centred * inv2
    valid = (2 * lax.broadcasted_iota(jnp.int32, (half, 1), 0) < len_ref[my_core() * n_seq + b]).astype(F32)
    out_ref[...] = ((unit2 * f_gain + f_shift) * valid).astype(BF16)
    grad = cot_ref[...].astype(F32) * valid
    add(0, grad * unit2)
    add(1, grad)
    scaled = grad * f_gain
    grad_summed = inv2 * (scaled - row_mean(scaled) - unit2 * row_mean(scaled * unit2))
    add(2, grad_summed)
    fg = grad_summed.astype(BF16)
    fg_all[rows, :] = fg
    normed_grad = grad_summed
    for t in range(4):
        pg = (dot_nn(fg, d_ref[t]) * dg[t]).astype(BF16)
        pg_all[t, rows, :] = pg
        normed_grad = normed_grad + dot_nt(pg, u_ref[t])
    add(3, normed_grad * unit1)
    add(4, normed_grad)
    scaled = normed_grad * n_gain
    hidden_grad = inv1 * (scaled - row_mean(scaled) - unit1 * row_mean(scaled * unit1))
    add(5, hidden_grad)
    ag_ref[...] = hidden_grad.astype(BF16)

    @pl.when(b == n_seq - 1)
    def _():
        for i in range(2):
            pg = pg_all[i]
            gu_ref[i] = dot_tn(nb_all[...], pg).astype(BF16)
            gd_ref[i] = dot_tn(fg_all[...], act_all[i]).astype(BF16)
            gv_ref[6 + i : 7 + i, :] = jnp.sum(pg.astype(F32), axis=0, keepdims=True)


def ffn(lengths, hid, cotangent, u4, d4, s4, vectors, n_seq, half):
    width = hid.shape[1]
    once = pl.Buffered(1)
    return pl.pallas_call(
        functools.partial(ffn_kernel, n_seq, half),
        out_shape=(
            jax.ShapeDtypeStruct((2 * n_seq * half, width), BF16),
            jax.ShapeDtypeStruct((n_seq * half, width), BF16),
            jax.ShapeDtypeStruct((2, width, 768), BF16),
            jax.ShapeDtypeStruct((2, width, 768), BF16),
            jax.ShapeDtypeStruct((8, width), F32),
        ),
        grid=(n_seq,),
        in_specs=[
            pl.BlockSpec(memory_space=pltpu.SMEM),
            pl.BlockSpec((half, width), lambda b: (b, 0)),
            pl.BlockSpec((half, width), lambda b: (my_core() * n_seq + b, 0)),
            pl.BlockSpec((4, width, 768), lambda b: (0, 0, 0), pipeline_mode=once),
            pl.BlockSpec((4, width, 768), lambda b: (0, 0, 0), pipeline_mode=once),
            pl.BlockSpec(s4.shape, lambda b: (0, 0, 0), pipeline_mode=once),
        ]
        + [pl.BlockSpec((width,), lambda b: (0,), pipeline_mode=once)] * 5,
        out_specs=[
            pl.BlockSpec((half, width), lambda b: (my_core() * n_seq + b, 0)),
            pl.BlockSpec((half, width), lambda b: (b, 0)),
            pl.BlockSpec((2, width, 768), lambda b: (0, 0, 0), pipeline_mode=once),
            pl.BlockSpec((2, width, 768), lambda b: (0, 0, 0), pipeline_mode=once),
            pl.BlockSpec((8, width), lambda b: (0, 0), pipeline_mode=once),
        ],
        scratch_shapes=[
            pltpu.VMEM((n_seq * half, width), BF16),
            pltpu.VMEM((n_seq * half, width), BF16),
            pltpu.VMEM((4, n_seq * half, 768), BF16),
            pltpu.VMEM((4, n_seq * half, 768), BF16),
            pltpu.VMEM((4, half, 768), F32),
        ],
        compiler_params=pltpu.CompilerParams(vmem_limit_bytes=VMEM_LIMIT),
        cost_estimate=pl.CostEstimate(flops=24 * 10**9, bytes_accessed=30 * 10**6, transcendentals=6 * 10**6),
    )(lengths, hid, cotangent, u4, d4, s4, *vectors)


class Net:
    def __init__(self, n_hi):
        self.n_hi = n_hi
        self.dp, self.t = lax.axis_index("dp"), lax.axis_index("tensor")
        self.hi, self.lo = self.dp // 2, lax.rem(self.dp, 2)
        self.core = lax.rem(self.t, 2)
        self.to_x = (self.dp + 1 - 2 * self.lo, self.t)
        self.to_c = (self.dp, self.t + 1 - 2 * self.core)

    def place(self, s):
        return lax.rem(self.hi + s, self.n_hi)

    def z_peer(self, s):
        return (self.place(s) * 2 + self.lo, self.t)

    def greet(self):
        barrier = pltpu.get_barrier_semaphore()
        peers = [self.z_peer(s) for s in range(1, self.n_hi)] + [self.to_x, self.to_c]
        for peer in peers:
            pl.semaphore_signal(barrier, inc=1, device_id=peer, device_id_type=MESH)
        pl.semaphore_wait(barrier, len(peers))

    def remote(self, src, dst, send, recv, peer):
        return pltpu.make_async_remote_copy(src, dst, send, recv, device_id=peer, device_id_type=MESH)


class Scatter:
    PARTS = 3

    def __init__(self, net, mine, other, bufs):
        self.net, self.mine, self.other = net, mine, other
        self.t1, self.t2, self.r3, self.sem, self.xs, self.xr, self.zs, self.zr = bufs
        self.rows = self.t2.shape[1] // self.PARTS

    @staticmethod
    def scratch(n_hi, rows, width):
        dma = pltpu.SemaphoreType.DMA
        both, half = pltpu.VMEM((n_hi, 2, rows, width), BF16), pltpu.VMEM((n_hi, rows, width), BF16)
        parts = Scatter.PARTS
        return [both, half, half, dma((2,)), dma((parts,)), dma((parts,)), dma((parts, n_hi)), dma((parts, n_hi))]

    def part(self, i):
        return pl.ds(i * self.rows, self.rows)

    def over_core(self):
        return self.net.remote(self.other, self.t1, self.sem.at[0], self.sem.at[1], self.net.to_c)

    def over_x(self, i):
        src = self.t1.at[:, 1 - self.net.lo, self.part(i)]
        return self.net.remote(src, self.t2.at[:, self.part(i)], self.xs.at[i], self.xr.at[i], self.net.to_x)

    def over_z(self, i, s):
        src = self.t2.at[self.net.place(s), self.part(i)]
        dst = self.r3.at[s, self.part(i)]
        return self.net.remote(src, dst, self.zs.at[i, s], self.zr.at[i, s], self.net.z_peer(s))

    def core_to_x(self):
        self.over_core().wait_recv()
        self.t1[...] += self.mine[...]
        for i in range(self.PARTS):
            self.over_x(i).start()

    def x_sum(self, i):
        self.over_x(i).wait_recv()
        rows = self.part(i)
        self.t2[:, rows] += self.t1[:, self.net.lo, rows]

    def start_z(self, i):
        for s in range(1, self.net.n_hi):
            self.over_z(i, s).start()

    def x_to_z(self, i):
        self.x_sum(i)
        self.start_z(i)

    def finish(self, out):
        for i in range(self.PARTS):
            rows = self.part(i)
            total = self.t2[self.net.hi, rows].astype(F32)
            for s in range(1, self.net.n_hi):
                self.over_z(i, s).wait_recv()
                total += self.r3[s, rows].astype(F32)
            out[rows, :] = total

    def sent_x(self):
        self.over_core().wait_send()
        for i in range(self.PARTS):
            self.over_x(i).wait_send()

    def sent_z(self):
        for i in range(self.PARTS):
            for s in range(1, self.net.n_hi):
                self.over_z(i, s).wait_send()


class SmallSum:
    def __init__(self, net, mine, other, bufs):
        self.net, self.mine, self.other = net, mine, other
        self.rc, self.v1, self.rx, self.v2, self.sem, self.zs, self.zr = bufs

    @staticmethod
    def scratch(n_hi, shape):
        dma = pltpu.SemaphoreType.DMA
        return [
            pltpu.VMEM(shape, F32), pltpu.VMEM(shape, F32), pltpu.VMEM(shape, F32), pltpu.VMEM((n_hi,) + shape, F32),
            dma((4,)), dma((n_hi,)), dma((n_hi,)),
        ]

    def over_core(self):
        return self.net.remote(self.other, self.rc, self.sem.at[0], self.sem.at[1], self.net.to_c)

    def over_x(self):
        return self.net.remote(self.v1, self.rx, self.sem.at[2], self.sem.at[3], self.net.to_x)

    def over_z(self, s):
        here = self.v2.at[self.net.hi]
        return self.net.remote(here, here, self.zs.at[s], self.zr.at[s], self.net.z_peer(s))

    def core_to_x(self):
        self.over_core().wait_recv()
        self.v1[...] = self.mine[...] + self.rc[...]
        self.over_x().start()

    def x_to_z(self):
        self.over_x().wait_recv()
        self.v2[self.net.hi] = self.v1[...] + self.rx[...]
        for s in range(1, self.net.n_hi):
            self.over_z(s).start()

    def finish(self, out):
        for s in range(1, self.net.n_hi):
            self.over_z(s).wait()
        out[...] = jnp.sum(self.v2[...], axis=0)
        self.over_core().wait_send()
        self.over_x().wait_send()

def backward_step(half, own, step_refs):
    kv_ref, q_ref, p_ref, ag, a_of, tacc, kvd, qd_ref = step_refs
    low = lane_low((half, 128))
    cg = dot_nn(ag, a_of(slice(512, 768))).astype(BF16)
    q01 = q_ref[0, :, 0:128]
    cg2, cg01 = cg[:, 0:128], cg[:, 128:256]
    zero = jnp.zeros_like(q01)
    heads = (
        (jnp.where(low, q01, zero), jnp.where(low, cg01, zero), 0, 128),
        (jnp.where(low, zero, q01), jnp.where(low, zero, cg01), 0, 128),
        (q_ref[0, :, 128:256], jnp.where(low, zero, cg2), 256, 256),
    )
    raw = [dot_nt(kv_ref[0, :, v_at : v_at + 128], g) for _, g, _, v_at in heads]
    vds = [dot_nn(p_ref[0, 0, h], head[1]) for h, head in enumerate(heads)]
    grads = []
    for h in range(3):
        p = p_ref[0, 0, h].astype(F32)
        row = jnp.sum(p * raw[h], axis=0, keepdims=True)
        sg = (p * (raw[h] - row)).astype(BF16)
        if own:
            tacc[h] += sg.astype(F32)
        grads.append(sg)
    kds = [dot_nn(sg, head[0]) for sg, head in zip(grads, heads)]
    qds = [dot_tn(kv_ref[0, :, head[2] : head[2] + 128], sg) for sg, head in zip(grads, heads)]
    kvd[:, 0:128] = (kds[0] + kds[1]).astype(BF16)
    kvd[:, 128:256] = (vds[0] + vds[1]).astype(BF16)
    kvd[:, 256:384] = (kds[2] + vds[2]).astype(BF16)
    qd01 = jnp.concatenate([qds[0][0:64], qds[1][64:128]], axis=0).T
    qd2 = jnp.concatenate([qds[2][0:64], jnp.zeros_like(qds[2][0:64])], axis=0).T
    qd = jnp.concatenate([qd01, qd2], axis=1).astype(BF16)
    qd_ref[...] = qd


def backward_place(step, n_seq):
    core = my_core()
    own = jnp.where(step < n_seq, 1 - core, core)
    rest = 2 + lax.rem(step, 2)
    first = step < 2 * n_seq
    return jnp.where(first, own, rest), jnp.where(first, lax.rem(step, n_seq), lax.rem(step, 2 * n_seq) // 2)


def backward_kernel(n_seq, length, n_dp, comm, *refs):
    half = length // 2
    n_hi = n_dp // 2
    step = pl.program_id(0)
    n_own = 2 * n_seq
    own = step < n_own
    g, b = backward_place(step, n_seq)
    x_any, a_any, kv_ref, q_ref, p_ref, ctx_any, ag_ref, pb_any = refs[:8]
    refs = refs[8:]
    if comm:
        gu_any, gd_any, gv_ref, half_any = refs[:4]
        out_any, tok_any, up_out, down_out, a_out, gv_out, sm_out = refs[4:11]
        refs = refs[11:]
    else:
        tok_out, ga_ref, sm_ref = refs[:3]
        refs = refs[3:]
    kvd, qd_all, tacc, tok, pool, kvd_rest, qd_rest, x_ref, ctx_ref, pb_ref, a_ref, fetch = refs[:12]
    refs = refs[12:]
    core = my_core()
    n_tok = n_seq * length
    late = (
        pltpu.make_async_copy(x_any.at[pl.ds(pl.multiple_of(core * n_tok, n_tok), n_tok), :], x_ref, fetch.at[0]),
        pltpu.make_async_copy(ctx_any.at[0:2], ctx_ref, fetch.at[1]),
        pltpu.make_async_copy(pb_any, pb_ref, fetch.at[2]),
    )
    a_copies = [
        pltpu.make_async_copy(a_any.at[pl.ds(i, 2)], a_ref.at[pl.ds(i, 2)], fetch.at[5 + i // 2]) for i in (0, 2)
    ]

    @pl.when(step == 0)
    def _():
        for copy in a_copies:
            copy.start()

    last = step == 2 * n_own - 1

    def at(n, *actions):
        @pl.when(step == n)
        def _():
            for action in actions:
                action()

    if comm:
        ga_ref, sm_ref, gu_mine, gd_mine, stage = refs[:5]
        net = Net(n_hi)
        other = 1 - core
        up = Scatter(net, gu_mine, gu_any.at[other], refs[5:13])
        down = Scatter(net, gd_mine, gd_any.at[other], refs[13:21])
        att = Scatter(net, ga_ref.at[core], ga_ref.at[other], refs[21:29])
        vec = SmallSum(net, gv_ref, gv_ref, refs[29:36])
        small = SmallSum(net, sm_ref.at[core], sm_ref.at[other], refs[36:43])
        o_sem, t_sem = refs[43:45]
        n_rows = n_seq * half
        o_copy = net.remote(
            half_any.at[pl.ds(pl.multiple_of(core * n_rows, n_rows), n_rows), :], out_any, o_sem.at[0], o_sem.at[1], net.to_c
        )
        mine = (
            pltpu.make_async_copy(gu_any.at[core], gu_mine, fetch.at[3]),
            pltpu.make_async_copy(gd_any.at[core], gd_mine, fetch.at[4]),
        )

        def tok_copies(i):
            row = pl.multiple_of((core * n_seq + i) * length, length)
            where = tok_any.at[pl.ds(row, length), :]
            return (
                pltpu.make_async_copy(stage.at[i], where, t_sem.at[0, i]),
                net.remote(stage.at[i], where, t_sem.at[1, i], t_sem.at[2, i], net.to_c),
            )

        @pl.when(step == 0)
        def _():
            for copy in mine:
                copy.start()
            net.greet()
            vec.over_core().start()
            up.over_core().start()
            down.over_core().start()

        at(3, o_copy.start)
        at(1, vec.core_to_x)
        at(2, mine[0].wait, up.core_to_x, mine[1].wait, down.core_to_x)
        at(4, att.over_core().start, small.over_core().start, vec.x_to_z, lambda: up.x_to_z(0))
        at(5, lambda: up.x_to_z(1))
        at(6, lambda: up.x_to_z(2))
        at(7, lambda: down.x_to_z(0))
        at(8, small.core_to_x, att.core_to_x, lambda: down.x_to_z(1))
        at(9, lambda: down.x_to_z(2))
        at(11, lambda: att.x_to_z(0), small.x_to_z)
        at(13, lambda: att.x_to_z(1))
        at(15, lambda: att.x_to_z(2))

    @pl.when(step == 0)
    def _():
        for copy in late:
            copy.start()
        a_copies[0].wait()

    pl.when(step == n_own)(a_copies[1].wait)

    krows = pl.ds(pl.multiple_of(b * length, length), length)
    qrows = pl.ds(pl.multiple_of(b * half, half), half)

    @pl.when(own)
    def _():
        @pl.when(b == 0)
        def _():
            tacc[g] = jnp.zeros_like(tacc[g])

        backward_step(
            half,
            True,
            (kv_ref, q_ref, p_ref, ag_ref[qrows, :], lambda lanes: a_ref[g, :, lanes], tacc.at[g],
             kvd.at[g, krows], qd_all.at[g, qrows]),
        )

        @pl.when(step == n_seq - 1)
        def _():
            for copy in late:
                copy.wait()

        @pl.when(b == n_seq - 1)
        def _():
            def store(lanes, v):
                v = v.astype(BF16)
                ga_ref[g, ..., lanes] = v.reshape(ga_ref.shape[1:-1] + v.shape[-1:])

            store(slice(0, 384), dot_tn(x_ref[...], kvd[g]))
            gq = dot_tn(pb_ref[...], qd_all[g]) * 0.125
            go = dot_tn(ag_ref[...], ctx_ref[g])
            store(slice(384, 512), gq[:, 0:128])
            store(slice(512, 640), gq[:, 128:256] + go[:, 0:128])
            store(slice(640, 768), go[:, 128:256])
            sm_ref[g, 3:8, :] = jnp.zeros((5, 2 * length), F32)
            sm_ref[g, 3:4, 0:384] = jnp.sum(kvd[g].astype(F32), axis=0, keepdims=True)
            i = lax.broadcasted_iota(jnp.int32, (half, half), 0)
            j = lax.broadcasted_iota(jnp.int32, (half, half), 1)
            flip = jnp.where(i + j == half - 1, 1.0, 0.0).astype(BF16)
            for h in range(3):
                high = tacc[g, h].astype(BF16)
                rest = (tacc[g, h] - high.astype(F32)).astype(BF16)
                turned = dot_nt(flip, high) + dot_nt(flip, rest)
                wide = jnp.concatenate([turned, jnp.zeros((half, length), F32)], axis=1)
                rolled = pltpu.roll(wide, 2, 1, stride=2, stride_axis=0)
                sm_ref[g, h : h + 1, :] = jnp.sum(rolled, axis=0, keepdims=True)

    @pl.when(jnp.logical_not(own))
    def _():
        backward_step(
            half,
            False,
            (kv_ref, q_ref, p_ref, ag_ref[qrows, :], lambda lanes: a_ref[g, :, lanes], None, kvd_rest, qd_rest),
        )
        h = g - 2
        tok_add = dot_nt(kvd_rest[...], a_ref[g, :, 0:384]) + dot_nt(kvd[h, krows], a_ref[h, :, 0:384])
        pool_add = dot_nt(qd_rest[...], a_ref[g, :, 384:640]) + dot_nt(qd_all[h, qrows], a_ref[h, :, 384:640])

        @pl.when(g == 2)
        def _():
            tok[...] = tok_add
            pool[...] = pool_add

        @pl.when(g == 3)
        def _():
            total = ((pool[...] + pool_add) * 0.125 + ag_ref[qrows, :].astype(F32)).astype(BF16)
            final = (tok[...] + tok_add + dot_tn(pool_matrix(half, length), total)).astype(BF16)
            if comm:
                stage[b] = final
                for copy in tok_copies(b):
                    copy.start()
            else:
                tok_out[...] = final

    if comm:

        @pl.when(last)
        def _():
            vec.finish(gv_out)
            up.finish(up_out)
            down.finish(down_out)
            small.finish(sm_out)
            att.finish(a_out)
            for each in (up, down, att):
                each.sent_x()
                each.sent_z()
            o_copy.wait()
            for i in range(n_seq):
                for copy in tok_copies(i):
                    copy.wait()


def fixed(shape, first=None):
    def index(*grid):
        head = 0 if first is None else first()
        return (head,) + (0,) * (len(shape) - 1)

    return pl.BlockSpec(shape, index, pipeline_mode=pl.Buffered(1))


ANY = pl.BlockSpec(memory_space=pl.ANY)


def attention_backward(tokens, a4, kv, q, p, ctx, ag, pb, gu, gd, gv, out_half, n_seq, n_dp, comm):
    length = kv.shape[1] // n_seq
    half = length // 2
    width = tokens.shape[1]
    n_tok, n_pool = n_seq * length, n_seq * half
    n_own = 2 * n_seq
    n_hi, rows = n_dp // 2, width // n_dp

    def place(n):
        return backward_place(n, n_seq)

    in_specs = [
        ANY,
        ANY,
        pl.BlockSpec((1, length, 384), lambda n: place(n) + (0,)),
        pl.BlockSpec((1, half, 256), lambda n: place(n) + (0,)),
        pl.BlockSpec((1, 1, 3, length, half), lambda n: place(n) + (0, 0, 0)),
        ANY,
        fixed((n_pool, width)),
        ANY,
    ]
    args = [tokens, a4, kv, q, p, ctx, ag, pb]
    scratch = [
        pltpu.VMEM((2, n_tok, 384), BF16), pltpu.VMEM((2, n_pool, 256), BF16), pltpu.VMEM((2, 3, length, half), F32),
        pltpu.VMEM((length, width), F32), pltpu.VMEM((half, width), F32), pltpu.VMEM((length, 384), BF16),
        pltpu.VMEM((half, 256), BF16), pltpu.VMEM((n_tok, width), BF16), pltpu.VMEM((2, n_pool, 256), BF16), pltpu.VMEM((n_pool, width), BF16),
        pltpu.VMEM((4, width, 768), BF16), pltpu.SemaphoreType.DMA((7,)),
    ]
    params = {"vmem_limit_bytes": VMEM_LIMIT}
    small = (8, 2 * length)
    if comm:
        split = (2, n_hi, 2, rows, width)
        in_specs += [ANY, ANY, fixed(gv.shape), ANY]
        args += [gu.reshape(split), gd.reshape(split), gv, out_half]
        shares = [jax.ShapeDtypeStruct((rows, width), F32)] * 3
        out_shape = [
            jax.ShapeDtypeStruct((n_pool, width), BF16), jax.ShapeDtypeStruct((2 * n_tok, width), BF16), *shares,
            jax.ShapeDtypeStruct(gv.shape, F32), jax.ShapeDtypeStruct(small, F32),
        ]
        out_specs = [ANY, ANY] + [fixed((rows, width))] * 3 + [fixed(gv.shape), fixed(small)]
        scratch += [
            pltpu.VMEM(split, BF16), pltpu.VMEM((2,) + small, F32), pltpu.VMEM(split[1:], BF16),
            pltpu.VMEM(split[1:], BF16), pltpu.VMEM((n_seq, length, width), BF16),
        ]
        for _ in range(3):
            scratch += Scatter.scratch(n_hi, rows, width)
        scratch += SmallSum.scratch(n_hi, gv.shape) + SmallSum.scratch(n_hi, small)
        scratch += [pltpu.SemaphoreType.DMA((2,)), pltpu.SemaphoreType.DMA((3, n_seq))]
        params.update(collective_id=1, has_side_effects=True)
    else:
        out_shape = [
            jax.ShapeDtypeStruct((n_tok, width), BF16), jax.ShapeDtypeStruct((2, width, 768), BF16),
            jax.ShapeDtypeStruct((2,) + small, F32),
        ]
        out_specs = [
            pl.BlockSpec((length, width), lambda n: (jnp.maximum(n - n_own, 0) // 2, 0)), fixed((2, width, 768)),
            fixed((2,) + small),
        ]
    return pl.pallas_call(
        functools.partial(backward_kernel, n_seq, length, n_dp, comm),
        out_shape=out_shape,
        grid=(2 * n_own,),
        in_specs=in_specs,
        out_specs=out_specs,
        scratch_shapes=scratch,
        compiler_params=pltpu.CompilerParams(**params),
        cost_estimate=pl.CostEstimate(flops=40 * 10**9, bytes_accessed=30 * 10**6, transcendentals=0),
    )(*args)


def finish_kernel(n_out, n_tok, chunk, a_ref, up_ref, down_ref, gv_ref, sm_ref, half_any, other_any, tok_any, *refs):
    out_any, tok_out = refs[:2]
    query, key, value, out, up, down, table, vbias, ubias, *vectors = refs[2:17]
    buf, sem = refs[17:]
    first = (1 - my_core()) * n_out * chunk
    moves = []
    for i in range(n_tok + n_out):
        if i < n_tok:
            src = tok_any.at[pl.ds(i * chunk, chunk)]
            dst = tok_out.at[pl.ds(i * chunk, chunk)]
        else:
            at = (i - n_tok) * chunk
            src = other_any.at[pl.ds(at, chunk)]
            dst = out_any.at[pl.ds(pl.multiple_of(first + at, chunk), chunk)]
        come = pltpu.make_async_copy(src, buf.at[i], sem.at[0, i])
        moves.append((come, pltpu.make_async_copy(buf.at[i], dst, sem.at[1, i])))
    for come, _ in moves:
        come.start()
    query[...] = a_ref[:, 384:576]
    key[:, 0:128] = a_ref[:, 0:128]
    key[:, 128:192] = a_ref[:, 256:320]
    value[:, 0:128] = a_ref[:, 128:256]
    value[:, 128:192] = a_ref[:, 320:384]
    out[0:128, :] = a_ref[:, 640:768].T
    out[128:192, :] = a_ref[:, 512:640].T[64:128]
    up[...] = up_ref[...]
    down[...] = down_ref[...]
    table[...] = sm_ref[0:3, :]
    vbias[0:128] = sm_ref[3, 128:256]
    vbias[128:192] = sm_ref[3, 320:384]
    ubias[...] = jnp.where(my_core() == 0, gv_ref[6, :], gv_ref[7, :])
    for i, vec in enumerate(vectors):
        vec[...] = gv_ref[i, :]
    for come, go in moves:
        come.wait()
        go.start()
    for _, go in moves:
        go.wait()


def finish(half_done, other, tok, a_sum, up_sum, down_sum, gv, sm, length):
    rows, width = a_sum.shape
    shapes = [(rows, 192)] * 3 + [(192, rows), (rows, 768), (rows, 768), (3, 2 * length), (192,), (768,)] + [(width,)] * 6
    n_out, n_tok = other.shape[0] // length, tok.shape[0] // length
    whole = pl.BlockSpec(memory_space=pltpu.VMEM)
    return pl.pallas_call(
        functools.partial(finish_kernel, n_out, n_tok, length),
        out_shape=[jax.ShapeDtypeStruct(half_done.shape, BF16), jax.ShapeDtypeStruct(tok.shape, BF16)]
        + [jax.ShapeDtypeStruct(shape, F32) for shape in shapes],
        in_specs=[whole] * 5 + [ANY] * 3,
        out_specs=[ANY] * 2 + [whole] * len(shapes),
        scratch_shapes=[
            pltpu.VMEM((n_tok + n_out, length, width), BF16), pltpu.SemaphoreType.DMA((2, n_tok + n_out)),
        ],
        input_output_aliases={5: 0},
        compiler_params=pltpu.CompilerParams(vmem_limit_bytes=VMEM_LIMIT),
    )(a_sum, up_sum, down_sum, gv, sm, half_done, other, tok)


def gather_plain(weights, length):
    kw, vw, qw, ow, uw, dw, tab, vbias, hbias = weights
    ot = ow.T
    packed = jnp.concatenate([kw[:, :128], vw[:, :128], kw[:, 128:], vw[:, 128:], qw, ot[:, 128:], ot[:, :128]], axis=1)
    small = jnp.zeros((8, 2 * length), F32).at[0:3].set(tab).at[3, 128:256].set(vbias[:128])
    small = small.at[3, 320:384].set(vbias[128:]).at[4, : hbias.shape[0]].set(hbias)
    first = 2 * (lax.axis_index("tensor") // 2)

    def groups(v):
        every = lax.all_gather(v, "tensor")
        return lax.dynamic_slice_in_dim(jnp.concatenate([every, every]), first, 4)

    wide = jnp.stack([packed, uw, dw], axis=1).astype(BF16)
    wide = groups(lax.all_gather(wide, "dp", axis=0, tiled=True))
    return wide[:, :, 0], wide[:, :, 1], wide[:, :, 2], groups(small)


def sum_plain(grads, n_dp):
    core = my_core()
    mine = lax.dynamic_index_in_dim(grads, core, 0, keepdims=False).astype(F32)
    other = lax.dynamic_index_in_dim(grads, 1 - core, 0, keepdims=False)
    total = mine + lax.ppermute(other, "tensor", [(i, i ^ 1) for i in range(4)]).astype(F32)
    return lax.psum_scatter(total, "dp", scatter_dimension=0, tiled=True)


def shards(
    n_dp, tokens, lengths, cotangent, query_weight, key_weight, value_weight, value_bias, output_weight,
    b_out, rel_table, norm_gain, norm_shift, up_weight, hidden_bias, down_weight, b_down, final_gain, final_shift,
):
    seq_count = lengths.shape[0]
    length = tokens.shape[0] // seq_count
    half = length // 2
    n_seq = seq_count // 2
    core = my_core()
    n_hi, rows = n_dp // 2, tokens.shape[1] // n_dp
    comm = rows % 16 == 0 and n_hi <= 4

    weights = (
        key_weight, value_weight, query_weight, output_weight, up_weight, down_weight.T, rel_table,
        value_bias, hidden_bias,
    )
    if not comm:
        weights = gather_plain(weights, length)
        a4, u4, d4, s4 = weights
        weights = (a4, s4)
    kv, q, p, ctx, hid, pb, *gathered = attention_forward(lengths, tokens, b_out, weights, n_dp, comm)
    if comm:
        a4, u4, d4, s4 = gathered
    vectors = (norm_gain, norm_shift, b_down, final_gain, final_shift)
    out_half, ag, gu, gd, gv = ffn(lengths, hid, cotangent, u4, d4, s4, vectors, n_seq, half)
    sums = attention_backward(tokens, a4, kv, q, p, ctx, ag, pb, gu, gd, gv, out_half, n_seq, n_dp, comm)
    if comm:
        other_half, tokens_grad, up_sum, down_sum, a_sum, gv, sm = sums
    else:
        tok_half, ga, sm = sums
        up_sum, down_sum, a_sum = (sum_plain(v, n_dp) for v in (gu, gd, ga))
        sm, gv = lax.psum((sm, gv), "dp")

        def over_core(v):
            return lax.ppermute(v, "tensor", [(i, i ^ 1) for i in range(4)])

        gv = gv + over_core(gv)
        mine = lax.dynamic_index_in_dim(sm, core, 0, keepdims=False)
        sm = mine + over_core(lax.dynamic_index_in_dim(sm, 1 - core, 0, keepdims=False))

        def join(part):
            got = over_core(part)
            return jnp.where(core == 0, jnp.concatenate([part, got]), jnp.concatenate([got, part]))

        other_half, tokens_grad = over_core(lax.dynamic_slice_in_dim(out_half, core * n_seq * half, n_seq * half)), join(tok_half)
    output, tokens_grad, *cut = finish(out_half, other_half, tokens_grad, a_sum, up_sum, down_sum, gv, sm, length)
    query_sum, key_sum, value_sum, outw_sum, up_sum, down_sum, table_sum, vbias, ubias = cut[:9]
    fgain, fshift, dbias, ngain, nshift, obias = cut[9:]
    return (
        output, tokens_grad, query_sum, key_sum, value_sum, vbias, outw_sum, obias, table_sum,
        ngain, nshift, up_sum, ubias, down_sum.T, dbias, fgain, fshift,
    )


def solution(mesh):
    row, col, both, rep = P("dp", None), P("tensor", "dp"), P("dp", "tensor"), P()
    ten, table = P("tensor"), P("tensor", None)
    in_specs = (
        row, P("dp"), row, both, both, both, ten, col, rep, table, rep, rep, both, ten, col, rep, rep, rep,
    )
    out_specs = (
        row, row, both, both, both, ten, col, rep, table, rep, rep, both, ten, col, rep, rep, rep,
    )
    body = functools.partial(shards, mesh.shape["dp"])
    return jax.shard_map(body, mesh=mesh, in_specs=in_specs, out_specs=out_specs, check_vma=False)
```

```python
import functools

import jax
import jax.numpy as jnp
from jax import lax
from jax.experimental import pallas as pl
from jax.experimental.pallas import tpu as pltpu
from jax.sharding import PartitionSpec as P

MESH = pl.DeviceIdType.MESH
F32 = jnp.float32
BF16 = jnp.bfloat16
EPS = 1e-06
VMEM_LIMIT = 58 * 2**20


def dot_nn(a, b):
    return lax.dot_general(a, b, (((1,), (0,)), ((), ())), preferred_element_type=F32)


def dot_nt(a, b):
    return lax.dot_general(a, b, (((1,), (1,)), ((), ())), preferred_element_type=F32)


def dot_tn(a, b):
    return lax.dot_general(a, b, (((0,), (0,)), ((), ())), preferred_element_type=F32)


class Gather:
    def __init__(self, n_hi, ins, outs, s_in, s_out, sems):
        self.n_hi, self.ins, self.outs, self.s_in, self.s_out = n_hi, ins, outs, s_in, s_out
        self.loc, self.zs, self.zr, self.ls, self.lr, self.fs, self.fr, self.cs, self.cr, self.ss, self.sr = sems
        self.dp, self.t = lax.axis_index("dp"), lax.axis_index("tensor")
        self.hi, self.lo = self.dp // 2, lax.rem(self.dp, 2)
        self.core = lax.rem(self.t, 2)
        t_core = self.t + 1 - 2 * self.core
        self.to_x = (self.dp + 1 - 2 * self.lo, self.t)
        self.to_y = (self.dp, lax.rem(self.t + 2, 4))
        self.to_c = (self.dp, t_core)
        self.to_d = (self.dp, lax.rem(t_core + 2, 4))

    def block(self, s, side):
        return lax.rem(self.hi - s + self.n_hi, self.n_hi) * 2 + side

    def greet(self):
        barrier = pltpu.get_barrier_semaphore()
        for up, exists in ((0, self.hi < self.n_hi - 1), (1, self.hi > 0)):

            @pl.when(exists)
            def _():
                pl.semaphore_signal(barrier, inc=1, device_id=self.z_next(up), device_id_type=MESH)

        for peer in (self.to_x, self.to_y, self.to_c, self.to_d):
            pl.semaphore_signal(barrier, inc=1, device_id=peer, device_id_type=MESH)
        along_z = jnp.where(self.hi < self.n_hi - 1, 1, 0) + jnp.where(self.hi > 0, 1, 0)
        pl.semaphore_wait(barrier, 4 + along_z)

    def z_next(self, down):
        hi = jnp.maximum(self.hi - 1, 0) if down else jnp.minimum(self.hi + 1, self.n_hi - 1)
        return (hi * 2 + self.lo, self.t)

    def remote(self, src, dst, send, recv, peer):
        return pltpu.make_async_remote_copy(src, dst, send, recv, device_id=peer, device_id_type=MESH)

    def small(self):
        core = self.core
        return (
            pltpu.make_async_copy(self.s_in, self.s_out.at[core], self.loc.at[3]),
            self.remote(self.s_in, self.s_out.at[core], self.ss.at[0], self.sr.at[0], self.to_c),
            self.remote(self.s_in, self.s_out.at[2 + core], self.ss.at[1], self.sr.at[1], self.to_y),
            self.remote(self.s_in, self.s_out.at[2 + core], self.ss.at[2], self.sr.at[2], self.to_d),
        )

    def local(self, k):
        return pltpu.make_async_copy(self.ins[k], self.outs[k].at[self.core, self.dp], self.loc.at[k])

    def z_send(self, k, d, down):
        b = self.block(self.n_hi - d if down else d, self.lo)
        dst = self.outs[k].at[self.core, b]
        src = self.ins[k] if d == 0 else dst
        return self.remote(src, dst, self.zs.at[down, k, d], self.zr.at[down, k, d], self.z_next(down))

    def z_more(self, down):
        return self.hi > 0 if down else self.hi < self.n_hi - 1

    def z_came(self, d, down):
        return self.hi + d < self.n_hi if down else self.hi >= d

    def line(self, k, s, way, own=False):
        out, b = self.outs[k], self.block(s, self.lo)
        src = self.ins[k] if own else out.at[self.core, b]
        dst = out.at[self.core if way == 0 else 2 + self.core, b]
        return self.remote(
            src, dst, self.ls.at[way, k, s], self.lr.at[way, k, s], self.to_x if way == 0 else self.to_y
        )

    def onward(self, k, s, way):
        out = self.outs[k]
        if way == 0:
            src = dst = out.at[2 + self.core, self.block(s, self.lo)]
        else:
            b = self.block(s, 1 - self.lo)
            src, dst = out.at[self.core, b], out.at[2 + self.core, b]
        return self.remote(src, dst, self.fs.at[k, s], self.fr.at[k, s], self.to_x if way == 0 else self.to_y)

    def to_core(self, k, s, which, own=False):
        out = self.outs[k]
        side = self.lo if which % 2 == 0 else 1 - self.lo
        where = out.at[self.core if which < 2 else 2 + self.core, self.block(s, side)]
        return self.remote(
            self.ins[k] if own else where, where, self.cs.at[which, k, s], self.cr.at[which, k, s], self.to_c
        )

    def start(self, k):
        for down in range(2):
            pl.when(self.z_more(down))(lambda: self.z_send(k, 0, down).start())
        self.line(k, 0, 0, True).start()
        if k == 0:
            self.line(k, 0, 1, True).start()
        self.to_core(k, 0, 0, True).start()
        self.local(k).start()

    def lines_y(self, k):
        for s in range(self.n_hi):
            self.line(k, s, 1, s == 0).start()

    def near(self, d, action):
        if d == 0:
            action(0)
            return
        pl.when(self.z_came(d, 0))(lambda: action(d))
        pl.when(self.z_came(d, 1))(lambda: action(self.n_hi - d))

    def spread(self, k, d):
        for down in range(2):

            @pl.when(self.z_came(d, down))
            def _():
                self.z_send(k, d - 1, down).wait_recv()
                if d < self.n_hi - 1:
                    pl.when(self.z_more(down))(lambda: self.z_send(k, d, down).start())
                s = self.n_hi - d if down else d
                self.line(k, s, 0).start()
                if k == 0:
                    self.line(k, s, 1).start()
                self.to_core(k, s, 0).start()

    def over_x(self, k, s):
        self.line(k, s, 0).wait_recv()
        self.onward(k, s, 1).start()
        self.to_core(k, s, 1).start()

    def over_y(self, k, s):
        self.line(k, s, 1).wait_recv()
        self.onward(k, s, 0).start()
        self.to_core(k, s, 2).start()

    def late_x(self, k, s):
        self.line(k, s, 0).wait_recv()
        self.to_core(k, s, 1).start()

    def late_y(self, k, s):
        self.line(k, s, 1).wait_recv()
        self.to_core(k, s, 2).start()

    def pass_on(self, k, d, core=None):
        if k == 2:
            way = (self.over_x, self.over_y)[core]
            pl.when(self.core == core)(lambda: self.near(d, lambda s: way(k, s)))
        else:
            way = (self.over_x, self.over_y)[k]
            self.near(d, lambda s: way(k, s))

    def late(self, k):
        for s in range(self.n_hi):
            if k == 2:
                pl.when(self.core == 0)(lambda: self.late_y(k, s))
                pl.when(self.core == 1)(lambda: self.late_x(k, s))
            else:
                (self.late_y, self.late_x)[k](k, s)

    def diagonal(self, k, s):
        self.onward(k, s, 0).wait_recv()
        self.to_core(k, s, 3).start()

    def arrived(self, k, whiches):
        for s in range(self.n_hi):
            for which in whiches:
                self.to_core(k, s, which).wait_recv()

    def sent(self, k):
        for down in range(2):
            for d in range(self.n_hi - 1):
                came = self.z_more(down) if d == 0 else jnp.logical_and(self.z_more(down), self.z_came(d, down))
                pl.when(came)(lambda: self.z_send(k, d, down).wait_send())
        for s in range(self.n_hi):
            self.line(k, s, 0).wait_send()
            self.line(k, s, 1).wait_send()
            self.onward(k, s, 0).wait_send()
            for which in range(4):
                self.to_core(k, s, which).wait_send()


def gather_scratch(n_hi):
    dma = pltpu.SemaphoreType.DMA
    return [
        dma((4,)), dma((2, 3, n_hi)), dma((2, 3, n_hi)), dma((2, 3, n_hi)), dma((2, 3, n_hi)), dma((3, n_hi)),
        dma((3, n_hi)), dma((4, 3, n_hi)), dma((4, 3, n_hi)), dma((3,)), dma((3,)),
    ]


def pool_matrix(pooled, length):
    i = lax.broadcasted_iota(jnp.int32, (pooled, length), 0)
    j = lax.broadcasted_iota(jnp.int32, (pooled, length), 1)
    return jnp.where(j // 2 == i, 0.5, 0.0).astype(BF16)


def lane_low(shape):
    return lax.broadcasted_iota(jnp.int32, shape, 1) < 64


def attention_kernel(n_seq, length, n_dp, comm, *refs):
    half = length // 2
    group, b = pl.program_id(0), pl.program_id(1)
    step = group * n_seq + b
    core = lax.rem(lax.axis_index("tensor"), 2)
    len_ref, x_any, bo_ref = refs[:3]
    refs = refs[3:]
    if comm:
        (kw, vw, qw, ow, uw, dw, tab, vbias, hbias) = refs[:9]
        kv_ref, q_ref, p_ref, ctx_ref, hid_ref, pb_ref, a_out, u_out, d_out, s_out = refs[9:19]
        bias, x_ref, x_sem, a_in, u_in, d_in, s_in, a_all, s_all, a_sem, s_sem = refs[19:30]
        net = Gather(n_dp // 2, (a_in, u_in, d_in), (a_all, u_out, d_out), s_in, s_all, refs[30:])
    else:
        a_ref, s_ref = refs[:2]
        kv_ref, q_ref, p_ref, ctx_ref, hid_ref, pb_ref, bias, x_ref, x_sem = refs[2:]
    n_tok = n_seq * length
    x_copy = pltpu.make_async_copy(x_any.at[pl.ds(pl.multiple_of(core * n_tok, n_tok), n_tok), :], x_ref, x_sem)

    def spread_bias(row_of):
        for h in range(3):
            wide = jnp.broadcast_to(row_of(h), (half, 2 * length))
            bias[h] = pltpu.roll(wide, length, 1, stride=2, stride_axis=0)[:, :length].T

    def pool_rows(first, last):
        if first == 0:
            x_copy.wait()
        pool = pool_matrix(half, length)
        for i in range(first, last):
            pooled = dot_nn(pool, x_ref[i * length : (i + 1) * length, :])
            hid_ref[i * half : (i + 1) * half, :] = pooled + bo_ref[...].reshape(1, -1)
            pb_ref[i * half : (i + 1) * half, :] = pooled.astype(BF16)

    if comm:

        def a_copy(g):
            return pltpu.make_async_copy(a_all.at[g], a_out.at[g], a_sem.at[g])

        s_copy = pltpu.make_async_copy(s_all, s_out, s_sem)

        @pl.when(step == 0)
        def _():
            x_copy.start()
            k, v, o = kw[...], vw[...], ow[...].T
            parts = (k[:, :128], v[:, :128], k[:, 128:], v[:, 128:], qw[...], o[:, 128:], o[:, :128])
            a_in[...] = jnp.concatenate(parts, axis=1).astype(BF16)
            s_in[...] = jnp.zeros_like(s_in)
            s_in[0:3, :] = tab[...]
            vb = vbias[...].reshape(1, -1)
            s_in[3:4, 128:256] = vb[:, 0:128]
            s_in[3:4, 320:384] = vb[:, 128:192]
            s_in[4:5, 0 : hbias.shape[0]] = hbias[...].reshape(1, -1)
            net.greet()
            for copy in net.small():
                copy.start()
            net.start(0)
            u_in[...] = uw[...].astype(BF16)
            d_in[...] = dw[...].astype(BF16)
            cuts = [min(i, n_seq) for i in range(n_dp // 2)]
            for s in range(1, n_dp // 2):
                net.spread(0, s)
                net.pass_on(0, s - 1)
                pool_rows(cuts[s - 1], cuts[s])
            net.start(1)
            small = net.small()
            small[0].wait()
            for copy in small[1:]:
                copy.wait()
            s_copy.start()
            spread_bias(lambda h: s_all[0, h : h + 1, :])
            net.pass_on(0, n_dp // 2 - 1)
            pool_rows(cuts[-1], n_seq)
            net.local(0).wait()
            net.arrived(0, (0, 1))

        n_hi = n_dp // 2
        plan = {}

        def at(n, action, *args):
            plan.setdefault(min(n, 4 * n_seq - 1), []).append(functools.partial(action, *args))

        for d in range(1, n_hi):
            at((1, 2, 3)[d - 1], net.spread, 1, d)
            at((4, 5, 6)[d - 1], net.spread, 2, d)
        at(2, net.start, 2)
        at(4, net.late, 0)
        for d in range(n_hi):
            at(4, net.diagonal, 0, d)
            at((6, 7, 8, 9)[d], net.pass_on, 1, d)
            at((9, 9, 10, 10)[d], net.pass_on, 2, d, 0)
            at((10, 11, 12, 13)[d], net.pass_on, 2, d, 1)
            at((10, 11, 12, 13)[d], lambda i: net.near(i, lambda s: net.diagonal(1, s)), d)
        at(3, net.lines_y, 1)
        at(2 * n_seq, net.arrived, 0, (2, 3))
        for g in range(4):
            at(2 * n_seq, lambda i: a_copy(i).start(), g)
        at(7, net.lines_y, 2)
        at(9, net.late, 1)
        at(14, net.late, 2)
        for n, actions in plan.items():

            @pl.when(step == n)
            def _():
                for action in actions:
                    action()

        def weights(lanes):
            return a_all[group, :, :, lanes].reshape(-1, lanes.stop - lanes.start)

        def small_row(i):
            return s_all[group, i : i + 1, :]
    else:

        @pl.when(step == 0)
        def _():
            x_copy.start()
            pool_rows(0, n_seq)

        def weights(lanes):
            return a_ref[0, :, lanes]

        def small_row(i):
            return s_ref[0, i : i + 1, :]

    krows = pl.ds(pl.multiple_of(b * length, length), length)
    qrows = pl.ds(pl.multiple_of(b * half, half), half)

    @pl.when(jnp.logical_and(b == 0, step > 0) if comm else b == 0)
    def _():
        spread_bias(small_row)

    kv_ref[0] = (dot_nn(x_ref[krows, :], weights(slice(0, 384))) + small_row(3)[:, 0:384]).astype(BF16)
    q = dot_nn(pb_ref[qrows, :], weights(slice(384, 640))) * 0.125
    lanes = lax.broadcasted_iota(jnp.int32, q.shape, 1)
    q = jnp.where(lanes < 192, q, 0.0).astype(BF16)
    q_ref[0] = q
    low = lane_low((half, 128))
    valid = lax.broadcasted_iota(jnp.int32, (length, half), 0) < len_ref[core * n_seq + b]
    q01 = q[:, 0:128]
    zero = jnp.zeros_like(q01)
    heads = (
        (jnp.where(low, q01, zero), 0, 128),
        (jnp.where(low, zero, q01), 0, 128),
        (q[:, 128:256], 256, 256),
    )
    raw = [dot_nt(kv_ref[0, :, k_at : k_at + 128], qh) for qh, k_at, _ in heads]
    probs = []
    for h in range(3):
        s = jnp.where(valid, raw[h] + bias[h], -1e30)
        e = jnp.exp(s - jnp.max(s, axis=0, keepdims=True))
        p = (e * (1.0 / jnp.sum(e, axis=0, keepdims=True))).astype(BF16)
        p_ref[0, 0, h] = p
        probs.append(p)
    contexts = [dot_tn(kv_ref[0, :, v_at : v_at + 128], p) for (_, _, v_at), p in zip(heads, probs)]
    c0, c1, c2 = contexts
    ctx01 = jnp.concatenate([c0[0:64], c1[64:128]], axis=0).T
    ctx2 = jnp.concatenate([jnp.zeros_like(c2[0:64]), c2[64:128]], axis=0).T
    ctx = jnp.concatenate([ctx2, ctx01], axis=1).astype(BF16)
    ctx_ref[0] = ctx
    hid_ref[qrows, :] += dot_nt(ctx, weights(slice(512, 768)))

    if comm:

        @pl.when(step == 4 * n_seq - 1)
        def _():
            for s in range(n_hi):
                net.diagonal(2, s)
            for k in range(3):
                net.sent(k)
            for k in (1, 2):
                net.local(k).wait()
                net.arrived(k, (0, 1, 2, 3))
            for g in range(4):
                a_copy(g).wait()
            s_copy.wait()


def my_core():
    return lax.rem(lax.axis_index("tensor"), 2)


def attention_forward(lengths, tokens, b_out, weights, n_dp, comm):
    n_seq = lengths.shape[0] // 2
    length = tokens.shape[0] // lengths.shape[0]
    half = length // 2
    width = tokens.shape[1]
    once = pl.Buffered(1)

    def fixed(shape):
        return pl.BlockSpec(shape, lambda g, b: (0,) * len(shape), pipeline_mode=once)

    in_specs = [
        pl.BlockSpec(memory_space=pltpu.SMEM),
        pl.BlockSpec(memory_space=pl.ANY),
        fixed((width,)),
    ]
    out_shape = [
        jax.ShapeDtypeStruct((4, n_seq * length, 384), BF16),
        jax.ShapeDtypeStruct((4, n_seq * half, 256), BF16),
        jax.ShapeDtypeStruct((4, n_seq, 3, length, half), BF16),
        jax.ShapeDtypeStruct((4, n_seq * half, 256), BF16),
        jax.ShapeDtypeStruct((n_seq * half, width), F32),
        jax.ShapeDtypeStruct((n_seq * half, width), BF16),
    ]
    out_specs = [
        pl.BlockSpec((1, length, 384), lambda g, b: (g, b, 0)),
        pl.BlockSpec((1, half, 256), lambda g, b: (g, b, 0)),
        pl.BlockSpec((1, 1, 3, length, half), lambda g, b: (g, b, 0, 0, 0)),
        pl.BlockSpec((1, half, 256), lambda g, b: (g, b, 0)),
        fixed((n_seq * half, width)),
        fixed((n_seq * half, width)),
    ]
    scratch = [
        pltpu.VMEM((3, length, half), F32), pltpu.VMEM((n_seq * length, width), BF16), pltpu.SemaphoreType.DMA,
    ]
    params = {"vmem_limit_bytes": VMEM_LIMIT}
    if comm:
        rows = width // n_dp
        in_specs += [fixed(w.shape) for w in weights]
        whole = jax.ShapeDtypeStruct((4, n_dp, rows, width), BF16)
        small = jax.ShapeDtypeStruct((4, 8, 2 * length), F32)
        out_shape += [whole, whole, whole, small]
        out_specs += [pl.BlockSpec(memory_space=pl.ANY)] * 4
        scratch += [pltpu.VMEM((rows, width), BF16)] * 3
        scratch += [
            pltpu.VMEM((8, 2 * length), F32),
            pltpu.VMEM((4, n_dp, rows, width), BF16),
            pltpu.VMEM((4, 8, 2 * length), F32),
            pltpu.SemaphoreType.DMA((4,)),
            pltpu.SemaphoreType.DMA,
        ]
        scratch += gather_scratch(n_dp // 2)
        params.update(collective_id=0, has_side_effects=True)
    else:
        in_specs += [
            pl.BlockSpec((1, width, 768), lambda g, b: (g, 0, 0)),
            pl.BlockSpec((1, 8, 2 * length), lambda g, b: (g, 0, 0)),
        ]
    outs = pl.pallas_call(
        functools.partial(attention_kernel, n_seq, length, n_dp, comm),
        out_shape=out_shape,
        grid=(4, n_seq),
        in_specs=in_specs,
        out_specs=out_specs,
        scratch_shapes=scratch,
        compiler_params=pltpu.CompilerParams(**params),
        cost_estimate=pl.CostEstimate(flops=20 * 10**9, bytes_accessed=40 * 10**6, transcendentals=6 * 10**6),
    )(lengths, tokens, b_out, *weights)
    if comm:
        flat = (4, width, width)
        outs = list(outs)
        outs = outs[:6] + [w.reshape(flat) for w in outs[6:9]] + outs[9:]
    return outs


def row_mean(v):
    return jnp.mean(v, axis=-1, keepdims=True)


def ffn_kernel(
    n_seq, half, len_ref, hid_ref, cot_ref, u_ref, d_ref, s_ref, v0, v1, v2, v3, v4,
    out_ref, ag_ref, gu_ref, gd_ref, gv_ref, nb_all, fg_all, act_all, pg_all, dg,
):
    b = pl.program_id(0)
    rows = pl.ds(pl.multiple_of(b * half, half), half)
    n_gain, n_shift, b_down, f_gain, f_shift = (v[...].reshape(1, -1) for v in (v0, v1, v2, v3, v4))

    @pl.when(b == 0)
    def _():
        gv_ref[...] = jnp.zeros_like(gv_ref)

    def add(i, v):
        gv_ref[i : i + 1, :] += jnp.sum(v, axis=0, keepdims=True)

    hid = hid_ref[...]
    centred = hid - row_mean(hid)
    inv1 = lax.rsqrt(row_mean(centred * centred) + EPS)
    unit1 = centred * inv1
    normed = unit1 * n_gain + n_shift
    nb = normed.astype(BF16)
    nb_all[rows, :] = nb
    summed = normed + b_down
    for t in range(4):
        pre = dot_nn(nb, u_ref[t]) + s_ref[t, 4:5, 0:768]
        cdf = 0.5 * (1.0 + lax.erf(pre * 0.7071067811865476))
        act = (pre * cdf).astype(BF16)
        dg[t] = cdf + pre * (0.3989422804014327 * jnp.exp(-0.5 * pre * pre))
        act_all[t, rows, :] = act
        summed = summed + dot_nt(act, d_ref[t])
    centred = summed - row_mean(summed)
    inv2 = lax.rsqrt(row_mean(centred * centred) + EPS)
    unit2 = centred * inv2
    valid = (2 * lax.broadcasted_iota(jnp.int32, (half, 1), 0) < len_ref[my_core() * n_seq + b]).astype(F32)
    out_ref[...] = ((unit2 * f_gain + f_shift) * valid).astype(BF16)
    grad = cot_ref[...].astype(F32) * valid
    add(0, grad * unit2)
    add(1, grad)
    scaled = grad * f_gain
    grad_summed = inv2 * (scaled - row_mean(scaled) - unit2 * row_mean(scaled * unit2))
    add(2, grad_summed)
    fg = grad_summed.astype(BF16)
    fg_all[rows, :] = fg
    normed_grad = grad_summed
    for t in range(4):
        pg = (dot_nn(fg, d_ref[t]) * dg[t]).astype(BF16)
        pg_all[t, rows, :] = pg
        normed_grad = normed_grad + dot_nt(pg, u_ref[t])
    add(3, normed_grad * unit1)
    add(4, normed_grad)
    scaled = normed_grad * n_gain
    hidden_grad = inv1 * (scaled - row_mean(scaled) - unit1 * row_mean(scaled * unit1))
    add(5, hidden_grad)
    ag_ref[...] = hidden_grad.astype(BF16)

    @pl.when(b == n_seq - 1)
    def _():
        for i in range(2):
            pg = pg_all[i]
            gu_ref[i] = dot_tn(nb_all[...], pg).astype(BF16)
            gd_ref[i] = dot_tn(fg_all[...], act_all[i]).astype(BF16)
            gv_ref[6 + i : 7 + i, :] = jnp.sum(pg.astype(F32), axis=0, keepdims=True)


def ffn(lengths, hid, cotangent, u4, d4, s4, vectors, n_seq, half):
    width = hid.shape[1]
    once = pl.Buffered(1)
    return pl.pallas_call(
        functools.partial(ffn_kernel, n_seq, half),
        out_shape=(
            jax.ShapeDtypeStruct((2 * n_seq * half, width), BF16),
            jax.ShapeDtypeStruct((n_seq * half, width), BF16),
            jax.ShapeDtypeStruct((2, width, 768), BF16),
            jax.ShapeDtypeStruct((2, width, 768), BF16),
            jax.ShapeDtypeStruct((8, width), F32),
        ),
        grid=(n_seq,),
        in_specs=[
            pl.BlockSpec(memory_space=pltpu.SMEM),
            pl.BlockSpec((half, width), lambda b: (b, 0)),
            pl.BlockSpec((half, width), lambda b: (my_core() * n_seq + b, 0)),
            pl.BlockSpec((4, width, 768), lambda b: (0, 0, 0), pipeline_mode=once),
            pl.BlockSpec((4, width, 768), lambda b: (0, 0, 0), pipeline_mode=once),
            pl.BlockSpec(s4.shape, lambda b: (0, 0, 0), pipeline_mode=once),
        ]
        + [pl.BlockSpec((width,), lambda b: (0,), pipeline_mode=once)] * 5,
        out_specs=[
            pl.BlockSpec((half, width), lambda b: (my_core() * n_seq + b, 0)),
            pl.BlockSpec((half, width), lambda b: (b, 0)),
            pl.BlockSpec((2, width, 768), lambda b: (0, 0, 0), pipeline_mode=once),
            pl.BlockSpec((2, width, 768), lambda b: (0, 0, 0), pipeline_mode=once),
            pl.BlockSpec((8, width), lambda b: (0, 0), pipeline_mode=once),
        ],
        scratch_shapes=[
            pltpu.VMEM((n_seq * half, width), BF16),
            pltpu.VMEM((n_seq * half, width), BF16),
            pltpu.VMEM((4, n_seq * half, 768), BF16),
            pltpu.VMEM((4, n_seq * half, 768), BF16),
            pltpu.VMEM((4, half, 768), F32),
        ],
        compiler_params=pltpu.CompilerParams(vmem_limit_bytes=VMEM_LIMIT),
        cost_estimate=pl.CostEstimate(flops=24 * 10**9, bytes_accessed=30 * 10**6, transcendentals=6 * 10**6),
    )(lengths, hid, cotangent, u4, d4, s4, *vectors)


class Net:
    def __init__(self, n_hi):
        self.n_hi = n_hi
        self.dp, self.t = lax.axis_index("dp"), lax.axis_index("tensor")
        self.hi, self.lo = self.dp // 2, lax.rem(self.dp, 2)
        self.core = lax.rem(self.t, 2)
        self.to_x = (self.dp + 1 - 2 * self.lo, self.t)
        self.to_c = (self.dp, self.t + 1 - 2 * self.core)

    def place(self, s):
        return lax.rem(self.hi + s, self.n_hi)

    def z_peer(self, s):
        return (self.place(s) * 2 + self.lo, self.t)

    def greet(self):
        barrier = pltpu.get_barrier_semaphore()
        peers = [self.z_peer(s) for s in range(1, self.n_hi)] + [self.to_x, self.to_c]
        for peer in peers:
            pl.semaphore_signal(barrier, inc=1, device_id=peer, device_id_type=MESH)
        pl.semaphore_wait(barrier, len(peers))

    def remote(self, src, dst, send, recv, peer):
        return pltpu.make_async_remote_copy(src, dst, send, recv, device_id=peer, device_id_type=MESH)


class Scatter:
    PARTS = 3

    def __init__(self, net, mine, other, bufs):
        self.net, self.mine, self.other = net, mine, other
        self.t1, self.t2, self.r3, self.sem, self.xs, self.xr, self.zs, self.zr = bufs
        self.rows = self.t2.shape[1] // self.PARTS

    @staticmethod
    def scratch(n_hi, rows, width):
        dma = pltpu.SemaphoreType.DMA
        both, half = pltpu.VMEM((n_hi, 2, rows, width), BF16), pltpu.VMEM((n_hi, rows, width), BF16)
        parts = Scatter.PARTS
        return [both, half, half, dma((2,)), dma((parts,)), dma((parts,)), dma((parts, n_hi)), dma((parts, n_hi))]

    def part(self, i):
        return pl.ds(i * self.rows, self.rows)

    def over_core(self):
        return self.net.remote(self.other, self.t1, self.sem.at[0], self.sem.at[1], self.net.to_c)

    def over_x(self, i):
        src = self.t1.at[:, 1 - self.net.lo, self.part(i)]
        return self.net.remote(src, self.t2.at[:, self.part(i)], self.xs.at[i], self.xr.at[i], self.net.to_x)

    def over_z(self, i, s):
        src = self.t2.at[self.net.place(s), self.part(i)]
        dst = self.r3.at[s, self.part(i)]
        return self.net.remote(src, dst, self.zs.at[i, s], self.zr.at[i, s], self.net.z_peer(s))

    def core_to_x(self):
        self.over_core().wait_recv()
        self.t1[...] += self.mine[...]
        for i in range(self.PARTS):
            self.over_x(i).start()

    def x_sum(self, i):
        self.over_x(i).wait_recv()
        rows = self.part(i)
        self.t2[:, rows] += self.t1[:, self.net.lo, rows]

    def start_z(self, i):
        for s in range(1, self.net.n_hi):
            self.over_z(i, s).start()

    def x_to_z(self, i):
        self.x_sum(i)
        self.start_z(i)

    def finish(self, out):
        for i in range(self.PARTS):
            rows = self.part(i)
            total = self.t2[self.net.hi, rows].astype(F32)
            for s in range(1, self.net.n_hi):
                self.over_z(i, s).wait_recv()
                total += self.r3[s, rows].astype(F32)
            out[rows, :] = total

    def sent_x(self):
        self.over_core().wait_send()
        for i in range(self.PARTS):
            self.over_x(i).wait_send()

    def sent_z(self):
        for i in range(self.PARTS):
            for s in range(1, self.net.n_hi):
                self.over_z(i, s).wait_send()


class SmallSum:
    def __init__(self, net, mine, other, bufs):
        self.net, self.mine, self.other = net, mine, other
        self.rc, self.v1, self.rx, self.v2, self.sem, self.zs, self.zr = bufs

    @staticmethod
    def scratch(n_hi, shape):
        dma = pltpu.SemaphoreType.DMA
        return [
            pltpu.VMEM(shape, F32), pltpu.VMEM(shape, F32), pltpu.VMEM(shape, F32), pltpu.VMEM((n_hi,) + shape, F32),
            dma((4,)), dma((n_hi,)), dma((n_hi,)),
        ]

    def over_core(self):
        return self.net.remote(self.other, self.rc, self.sem.at[0], self.sem.at[1], self.net.to_c)

    def over_x(self):
        return self.net.remote(self.v1, self.rx, self.sem.at[2], self.sem.at[3], self.net.to_x)

    def over_z(self, s):
        here = self.v2.at[self.net.hi]
        return self.net.remote(here, here, self.zs.at[s], self.zr.at[s], self.net.z_peer(s))

    def core_to_x(self):
        self.over_core().wait_recv()
        self.v1[...] = self.mine[...] + self.rc[...]
        self.over_x().start()

    def x_to_z(self):
        self.over_x().wait_recv()
        self.v2[self.net.hi] = self.v1[...] + self.rx[...]
        for s in range(1, self.net.n_hi):
            self.over_z(s).start()

    def finish(self, out):
        for s in range(1, self.net.n_hi):
            self.over_z(s).wait()
        out[...] = jnp.sum(self.v2[...], axis=0)
        self.over_core().wait_send()
        self.over_x().wait_send()

def backward_step(half, own, step_refs):
    kv_ref, q_ref, p_ref, ag, a_of, tacc, kvd, qd_ref = step_refs
    low = lane_low((half, 128))
    cg = dot_nn(ag, a_of(slice(512, 768))).astype(BF16)
    q01 = q_ref[0, :, 0:128]
    cg2, cg01 = cg[:, 0:128], cg[:, 128:256]
    zero = jnp.zeros_like(q01)
    heads = (
        (jnp.where(low, q01, zero), jnp.where(low, cg01, zero), 0, 128),
        (jnp.where(low, zero, q01), jnp.where(low, zero, cg01), 0, 128),
        (q_ref[0, :, 128:256], jnp.where(low, zero, cg2), 256, 256),
    )
    raw = [dot_nt(kv_ref[0, :, v_at : v_at + 128], g) for _, g, _, v_at in heads]
    vds = [dot_nn(p_ref[0, 0, h], head[1]) for h, head in enumerate(heads)]
    grads = []
    for h in range(3):
        p = p_ref[0, 0, h].astype(F32)
        row = jnp.sum(p * raw[h], axis=0, keepdims=True)
        sg = (p * (raw[h] - row)).astype(BF16)
        if own:
            tacc[h] += sg.astype(F32)
        grads.append(sg)
    kds = [dot_nn(sg, head[0]) for sg, head in zip(grads, heads)]
    qds = [dot_tn(kv_ref[0, :, head[2] : head[2] + 128], sg) for sg, head in zip(grads, heads)]
    kvd[:, 0:128] = (kds[0] + kds[1]).astype(BF16)
    kvd[:, 128:256] = (vds[0] + vds[1]).astype(BF16)
    kvd[:, 256:384] = (kds[2] + vds[2]).astype(BF16)
    qd01 = jnp.concatenate([qds[0][0:64], qds[1][64:128]], axis=0).T
    qd2 = jnp.concatenate([qds[2][0:64], jnp.zeros_like(qds[2][0:64])], axis=0).T
    qd = jnp.concatenate([qd01, qd2], axis=1).astype(BF16)
    qd_ref[...] = qd


def backward_place(step, n_seq):
    core = my_core()
    own = jnp.where(step < n_seq, 1 - core, core)
    rest = 2 + lax.rem(step, 2)
    first = step < 2 * n_seq
    return jnp.where(first, own, rest), jnp.where(first, lax.rem(step, n_seq), lax.rem(step, 2 * n_seq) // 2)


def backward_kernel(n_seq, length, n_dp, comm, *refs):
    half = length // 2
    n_hi = n_dp // 2
    step = pl.program_id(0)
    n_own = 2 * n_seq
    own = step < n_own
    g, b = backward_place(step, n_seq)
    x_any, a_any, kv_ref, q_ref, p_ref, ctx_any, ag_ref, pb_any = refs[:8]
    refs = refs[8:]
    if comm:
        gu_any, gd_any, gv_ref, half_any = refs[:4]
        out_any, tok_any, up_out, down_out, a_out, gv_out, sm_out = refs[4:11]
        refs = refs[11:]
    else:
        tok_out, ga_ref, sm_ref = refs[:3]
        refs = refs[3:]
    kvd, qd_all, tacc, tok, pool, kvd_rest, qd_rest, x_ref, ctx_ref, pb_ref, a_ref, fetch = refs[:12]
    refs = refs[12:]
    core = my_core()
    n_tok = n_seq * length
    late = (
        pltpu.make_async_copy(x_any.at[pl.ds(pl.multiple_of(core * n_tok, n_tok), n_tok), :], x_ref, fetch.at[0]),
        pltpu.make_async_copy(ctx_any.at[0:2], ctx_ref, fetch.at[1]),
        pltpu.make_async_copy(pb_any, pb_ref, fetch.at[2]),
    )
    a_copies = [
        pltpu.make_async_copy(a_any.at[pl.ds(i, 2)], a_ref.at[pl.ds(i, 2)], fetch.at[5 + i // 2]) for i in (0, 2)
    ]

    @pl.when(step == 0)
    def _():
        for copy in a_copies:
            copy.start()

    last = step == 2 * n_own - 1

    def at(n, *actions):
        @pl.when(step == n)
        def _():
            for action in actions:
                action()

    if comm:
        ga_ref, sm_ref, gu_mine, gd_mine, stage = refs[:5]
        net = Net(n_hi)
        other = 1 - core
        up = Scatter(net, gu_mine, gu_any.at[other], refs[5:13])
        down = Scatter(net, gd_mine, gd_any.at[other], refs[13:21])
        att = Scatter(net, ga_ref.at[core], ga_ref.at[other], refs[21:29])
        vec = SmallSum(net, gv_ref, gv_ref, refs[29:36])
        small = SmallSum(net, sm_ref.at[core], sm_ref.at[other], refs[36:43])
        o_sem, t_sem = refs[43:45]
        n_rows = n_seq * half
        o_copy = net.remote(
            half_any.at[pl.ds(pl.multiple_of(core * n_rows, n_rows), n_rows), :], out_any, o_sem.at[0], o_sem.at[1], net.to_c
        )
        mine = (
            pltpu.make_async_copy(gu_any.at[core], gu_mine, fetch.at[3]),
            pltpu.make_async_copy(gd_any.at[core], gd_mine, fetch.at[4]),
        )

        def tok_copies(i):
            row = pl.multiple_of((core * n_seq + i) * length, length)
            where = tok_any.at[pl.ds(row, length), :]
            return (
                pltpu.make_async_copy(stage.at[i], where, t_sem.at[0, i]),
                net.remote(stage.at[i], where, t_sem.at[1, i], t_sem.at[2, i], net.to_c),
            )

        @pl.when(step == 0)
        def _():
            for copy in mine:
                copy.start()
            net.greet()
            vec.over_core().start()
            up.over_core().start()
            down.over_core().start()

        at(3, o_copy.start)
        at(1, vec.core_to_x)
        at(2, mine[0].wait, up.core_to_x, mine[1].wait, down.core_to_x)
        at(4, att.over_core().start, small.over_core().start, vec.x_to_z, lambda: up.x_to_z(0))
        at(5, lambda: up.x_to_z(1))
        at(6, lambda: up.x_to_z(2))
        at(7, lambda: down.x_to_z(0))
        at(8, small.core_to_x, att.core_to_x, lambda: down.x_to_z(1))
        at(9, lambda: down.x_to_z(2))
        at(11, lambda: att.x_to_z(0), small.x_to_z)
        at(13, lambda: att.x_to_z(1))
        at(15, lambda: att.x_to_z(2))

    @pl.when(step == 0)
    def _():
        for copy in late:
            copy.start()
        a_copies[0].wait()

    pl.when(step == n_own)(a_copies[1].wait)

    krows = pl.ds(pl.multiple_of(b * length, length), length)
    qrows = pl.ds(pl.multiple_of(b * half, half), half)

    @pl.when(own)
    def _():
        @pl.when(b == 0)
        def _():
            tacc[g] = jnp.zeros_like(tacc[g])

        backward_step(
            half,
            True,
            (kv_ref, q_ref, p_ref, ag_ref[qrows, :], lambda lanes: a_ref[g, :, lanes], tacc.at[g],
             kvd.at[g, krows], qd_all.at[g, qrows]),
        )

        @pl.when(step == n_seq - 1)
        def _():
            for copy in late:
                copy.wait()

        @pl.when(b == n_seq - 1)
        def _():
            def store(lanes, v):
                v = v.astype(BF16)
                ga_ref[g, ..., lanes] = v.reshape(ga_ref.shape[1:-1] + v.shape[-1:])

            store(slice(0, 384), dot_tn(x_ref[...], kvd[g]))
            gq = dot_tn(pb_ref[...], qd_all[g]) * 0.125
            go = dot_tn(ag_ref[...], ctx_ref[g])
            store(slice(384, 512), gq[:, 0:128])
            store(slice(512, 640), gq[:, 128:256] + go[:, 0:128])
            store(slice(640, 768), go[:, 128:256])
            sm_ref[g, 3:8, :] = jnp.zeros((5, 2 * length), F32)
            sm_ref[g, 3:4, 0:384] = jnp.sum(kvd[g].astype(F32), axis=0, keepdims=True)
            i = lax.broadcasted_iota(jnp.int32, (half, half), 0)
            j = lax.broadcasted_iota(jnp.int32, (half, half), 1)
            flip = jnp.where(i + j == half - 1, 1.0, 0.0).astype(BF16)
            for h in range(3):
                high = tacc[g, h].astype(BF16)
                rest = (tacc[g, h] - high.astype(F32)).astype(BF16)
                turned = dot_nt(flip, high) + dot_nt(flip, rest)
                wide = jnp.concatenate([turned, jnp.zeros((half, length), F32)], axis=1)
                rolled = pltpu.roll(wide, 2, 1, stride=2, stride_axis=0)
                sm_ref[g, h : h + 1, :] = jnp.sum(rolled, axis=0, keepdims=True)

    @pl.when(jnp.logical_not(own))
    def _():
        backward_step(
            half,
            False,
            (kv_ref, q_ref, p_ref, ag_ref[qrows, :], lambda lanes: a_ref[g, :, lanes], None, kvd_rest, qd_rest),
        )
        h = g - 2
        tok_add = dot_nt(kvd_rest[...], a_ref[g, :, 0:384]) + dot_nt(kvd[h, krows], a_ref[h, :, 0:384])
        pool_add = dot_nt(qd_rest[...], a_ref[g, :, 384:640]) + dot_nt(qd_all[h, qrows], a_ref[h, :, 384:640])

        @pl.when(g == 2)
        def _():
            tok[...] = tok_add
            pool[...] = pool_add

        @pl.when(g == 3)
        def _():
            total = ((pool[...] + pool_add) * 0.125 + ag_ref[qrows, :].astype(F32)).astype(BF16)
            final = (tok[...] + tok_add + dot_tn(pool_matrix(half, length), total)).astype(BF16)
            if comm:
                stage[b] = final
                for copy in tok_copies(b):
                    copy.start()
            else:
                tok_out[...] = final

    if comm:

        @pl.when(last)
        def _():
            vec.finish(gv_out)
            up.finish(up_out)
            down.finish(down_out)
            small.finish(sm_out)
            att.finish(a_out)
            for each in (up, down, att):
                each.sent_x()
                each.sent_z()
            o_copy.wait()
            for i in range(n_seq):
                for copy in tok_copies(i):
                    copy.wait()


def fixed(shape, first=None):
    def index(*grid):
        head = 0 if first is None else first()
        return (head,) + (0,) * (len(shape) - 1)

    return pl.BlockSpec(shape, index, pipeline_mode=pl.Buffered(1))


ANY = pl.BlockSpec(memory_space=pl.ANY)


def attention_backward(tokens, a4, kv, q, p, ctx, ag, pb, gu, gd, gv, out_half, n_seq, n_dp, comm):
    length = kv.shape[1] // n_seq
    half = length // 2
    width = tokens.shape[1]
    n_tok, n_pool = n_seq * length, n_seq * half
    n_own = 2 * n_seq
    n_hi, rows = n_dp // 2, width // n_dp

    def place(n):
        return backward_place(n, n_seq)

    in_specs = [
        ANY,
        ANY,
        pl.BlockSpec((1, length, 384), lambda n: place(n) + (0,)),
        pl.BlockSpec((1, half, 256), lambda n: place(n) + (0,)),
        pl.BlockSpec((1, 1, 3, length, half), lambda n: place(n) + (0, 0, 0)),
        ANY,
        fixed((n_pool, width)),
        ANY,
    ]
    args = [tokens, a4, kv, q, p, ctx, ag, pb]
    scratch = [
        pltpu.VMEM((2, n_tok, 384), BF16), pltpu.VMEM((2, n_pool, 256), BF16), pltpu.VMEM((2, 3, length, half), F32),
        pltpu.VMEM((length, width), F32), pltpu.VMEM((half, width), F32), pltpu.VMEM((length, 384), BF16),
        pltpu.VMEM((half, 256), BF16), pltpu.VMEM((n_tok, width), BF16), pltpu.VMEM((2, n_pool, 256), BF16), pltpu.VMEM((n_pool, width), BF16),
        pltpu.VMEM((4, width, 768), BF16), pltpu.SemaphoreType.DMA((7,)),
    ]
    params = {"vmem_limit_bytes": VMEM_LIMIT}
    small = (8, 2 * length)
    if comm:
        split = (2, n_hi, 2, rows, width)
        in_specs += [ANY, ANY, fixed(gv.shape), ANY]
        args += [gu.reshape(split), gd.reshape(split), gv, out_half]
        shares = [jax.ShapeDtypeStruct((rows, width), F32)] * 3
        out_shape = [
            jax.ShapeDtypeStruct((n_pool, width), BF16), jax.ShapeDtypeStruct((2 * n_tok, width), BF16), *shares,
            jax.ShapeDtypeStruct(gv.shape, F32), jax.ShapeDtypeStruct(small, F32),
        ]
        out_specs = [ANY, ANY] + [fixed((rows, width))] * 3 + [fixed(gv.shape), fixed(small)]
        scratch += [
            pltpu.VMEM(split, BF16), pltpu.VMEM((2,) + small, F32), pltpu.VMEM(split[1:], BF16),
            pltpu.VMEM(split[1:], BF16), pltpu.VMEM((n_seq, length, width), BF16),
        ]
        for _ in range(3):
            scratch += Scatter.scratch(n_hi, rows, width)
        scratch += SmallSum.scratch(n_hi, gv.shape) + SmallSum.scratch(n_hi, small)
        scratch += [pltpu.SemaphoreType.DMA((2,)), pltpu.SemaphoreType.DMA((3, n_seq))]
        params.update(collective_id=1, has_side_effects=True)
    else:
        out_shape = [
            jax.ShapeDtypeStruct((n_tok, width), BF16), jax.ShapeDtypeStruct((2, width, 768), BF16),
            jax.ShapeDtypeStruct((2,) + small, F32),
        ]
        out_specs = [
            pl.BlockSpec((length, width), lambda n: (jnp.maximum(n - n_own, 0) // 2, 0)), fixed((2, width, 768)),
            fixed((2,) + small),
        ]
    return pl.pallas_call(
        functools.partial(backward_kernel, n_seq, length, n_dp, comm),
        out_shape=out_shape,
        grid=(2 * n_own,),
        in_specs=in_specs,
        out_specs=out_specs,
        scratch_shapes=scratch,
        compiler_params=pltpu.CompilerParams(**params),
        cost_estimate=pl.CostEstimate(flops=40 * 10**9, bytes_accessed=30 * 10**6, transcendentals=0),
    )(*args)


def finish_kernel(n_out, n_tok, chunk, a_ref, up_ref, down_ref, gv_ref, sm_ref, half_any, other_any, tok_any, *refs):
    out_any, tok_out = refs[:2]
    query, key, value, out, up, down, table, vbias, ubias, *vectors = refs[2:17]
    buf, sem = refs[17:]
    first = (1 - my_core()) * n_out * chunk
    moves = []
    for i in range(n_tok + n_out):
        if i < n_tok:
            src = tok_any.at[pl.ds(i * chunk, chunk)]
            dst = tok_out.at[pl.ds(i * chunk, chunk)]
        else:
            at = (i - n_tok) * chunk
            src = other_any.at[pl.ds(at, chunk)]
            dst = out_any.at[pl.ds(pl.multiple_of(first + at, chunk), chunk)]
        come = pltpu.make_async_copy(src, buf.at[i], sem.at[0, i])
        moves.append((come, pltpu.make_async_copy(buf.at[i], dst, sem.at[1, i])))
    for come, _ in moves:
        come.start()
    query[...] = a_ref[:, 384:576]
    key[:, 0:128] = a_ref[:, 0:128]
    key[:, 128:192] = a_ref[:, 256:320]
    value[:, 0:128] = a_ref[:, 128:256]
    value[:, 128:192] = a_ref[:, 320:384]
    out[0:128, :] = a_ref[:, 640:768].T
    out[128:192, :] = a_ref[:, 512:640].T[64:128]
    up[...] = up_ref[...]
    down[...] = down_ref[...]
    table[...] = sm_ref[0:3, :]
    vbias[0:128] = sm_ref[3, 128:256]
    vbias[128:192] = sm_ref[3, 320:384]
    ubias[...] = jnp.where(my_core() == 0, gv_ref[6, :], gv_ref[7, :])
    for i, vec in enumerate(vectors):
        vec[...] = gv_ref[i, :]
    for come, go in moves:
        come.wait()
        go.start()
    for _, go in moves:
        go.wait()


def finish(half_done, other, tok, a_sum, up_sum, down_sum, gv, sm, length):
    rows, width = a_sum.shape
    shapes = [(rows, 192)] * 3 + [(192, rows), (rows, 768), (rows, 768), (3, 2 * length), (192,), (768,)] + [(width,)] * 6
    n_out, n_tok = other.shape[0] // length, tok.shape[0] // length
    whole = pl.BlockSpec(memory_space=pltpu.VMEM)
    return pl.pallas_call(
        functools.partial(finish_kernel, n_out, n_tok, length),
        out_shape=[jax.ShapeDtypeStruct(half_done.shape, BF16), jax.ShapeDtypeStruct(tok.shape, BF16)]
        + [jax.ShapeDtypeStruct(shape, F32) for shape in shapes],
        in_specs=[whole] * 5 + [ANY] * 3,
        out_specs=[ANY] * 2 + [whole] * len(shapes),
        scratch_shapes=[
            pltpu.VMEM((n_tok + n_out, length, width), BF16), pltpu.SemaphoreType.DMA((2, n_tok + n_out)),
        ],
        input_output_aliases={5: 0},
        compiler_params=pltpu.CompilerParams(vmem_limit_bytes=VMEM_LIMIT),
    )(a_sum, up_sum, down_sum, gv, sm, half_done, other, tok)


def gather_plain(weights, length):
    kw, vw, qw, ow, uw, dw, tab, vbias, hbias = weights
    ot = ow.T
    packed = jnp.concatenate([kw[:, :128], vw[:, :128], kw[:, 128:], vw[:, 128:], qw, ot[:, 128:], ot[:, :128]], axis=1)
    small = jnp.zeros((8, 2 * length), F32).at[0:3].set(tab).at[3, 128:256].set(vbias[:128])
    small = small.at[3, 320:384].set(vbias[128:]).at[4, : hbias.shape[0]].set(hbias)
    first = 2 * (lax.axis_index("tensor") // 2)

    def groups(v):
        every = lax.all_gather(v, "tensor")
        return lax.dynamic_slice_in_dim(jnp.concatenate([every, every]), first, 4)

    wide = jnp.stack([packed, uw, dw], axis=1).astype(BF16)
    wide = groups(lax.all_gather(wide, "dp", axis=0, tiled=True))
    return wide[:, :, 0], wide[:, :, 1], wide[:, :, 2], groups(small)


def sum_plain(grads, n_dp):
    core = my_core()
    mine = lax.dynamic_index_in_dim(grads, core, 0, keepdims=False).astype(F32)
    other = lax.dynamic_index_in_dim(grads, 1 - core, 0, keepdims=False)
    total = mine + lax.ppermute(other, "tensor", [(i, i ^ 1) for i in range(4)]).astype(F32)
    return lax.psum_scatter(total, "dp", scatter_dimension=0, tiled=True)


def shards(
    n_dp, tokens, lengths, cotangent, query_weight, key_weight, value_weight, value_bias, output_weight,
    b_out, rel_table, norm_gain, norm_shift, up_weight, hidden_bias, down_weight, b_down, final_gain, final_shift,
):
    seq_count = lengths.shape[0]
    length = tokens.shape[0] // seq_count
    half = length // 2
    n_seq = seq_count // 2
    core = my_core()
    n_hi, rows = n_dp // 2, tokens.shape[1] // n_dp
    comm = rows % 16 == 0 and n_hi <= 4

    weights = (
        key_weight, value_weight, query_weight, output_weight, up_weight, down_weight.T, rel_table,
        value_bias, hidden_bias,
    )
    if not comm:
        weights = gather_plain(weights, length)
        a4, u4, d4, s4 = weights
        weights = (a4, s4)
    kv, q, p, ctx, hid, pb, *gathered = attention_forward(lengths, tokens, b_out, weights, n_dp, comm)
    if comm:
        a4, u4, d4, s4 = gathered
    vectors = (norm_gain, norm_shift, b_down, final_gain, final_shift)
    out_half, ag, gu, gd, gv = ffn(lengths, hid, cotangent, u4, d4, s4, vectors, n_seq, half)
    sums = attention_backward(tokens, a4, kv, q, p, ctx, ag, pb, gu, gd, gv, out_half, n_seq, n_dp, comm)
    if comm:
        other_half, tokens_grad, up_sum, down_sum, a_sum, gv, sm = sums
    else:
        tok_half, ga, sm = sums
        up_sum, down_sum, a_sum = (sum_plain(v, n_dp) for v in (gu, gd, ga))
        sm, gv = lax.psum((sm, gv), "dp")

        def over_core(v):
            return lax.ppermute(v, "tensor", [(i, i ^ 1) for i in range(4)])

        gv = gv + over_core(gv)
        mine = lax.dynamic_index_in_dim(sm, core, 0, keepdims=False)
        sm = mine + over_core(lax.dynamic_index_in_dim(sm, 1 - core, 0, keepdims=False))

        def join(part):
            got = over_core(part)
            return jnp.where(core == 0, jnp.concatenate([part, got]), jnp.concatenate([got, part]))

        other_half, tokens_grad = over_core(lax.dynamic_slice_in_dim(out_half, core * n_seq * half, n_seq * half)), join(tok_half)
    output, tokens_grad, *cut = finish(out_half, other_half, tokens_grad, a_sum, up_sum, down_sum, gv, sm, length)
    query_sum, key_sum, value_sum, outw_sum, up_sum, down_sum, table_sum, vbias, ubias = cut[:9]
    fgain, fshift, dbias, ngain, nshift, obias = cut[9:]
    return (
        output, tokens_grad, query_sum, key_sum, value_sum, vbias, outw_sum, obias, table_sum,
        ngain, nshift, up_sum, ubias, down_sum.T, dbias, fgain, fshift,
    )


def solution(mesh):
    row, col, both, rep = P("dp", None), P("tensor", "dp"), P("dp", "tensor"), P()
    ten, table = P("tensor"), P("tensor", None)
    in_specs = (
        row, P("dp"), row, both, both, both, ten, col, rep, table, rep, rep, both, ten, col, rep, rep, rep,
    )
    out_specs = (
        row, row, both, both, both, ten, col, rep, table, rep, rep, both, ten, col, rep, rep, rep,
    )
    body = functools.partial(shards, mesh.shape["dp"])
    return jax.shard_map(body, mesh=mesh, in_specs=in_specs, out_specs=out_specs, check_vma=False)
```

```python
import functools

import jax
import jax.numpy as jnp
from jax import lax
from jax.experimental import pallas as pl
from jax.experimental.pallas import tpu as pltpu
from jax.sharding import PartitionSpec as P

MESH = pl.DeviceIdType.MESH
F32 = jnp.float32
BF16 = jnp.bfloat16
EPS = 1e-06
VMEM_LIMIT = 58 * 2**20


def dot_nn(a, b):
    return lax.dot_general(a, b, (((1,), (0,)), ((), ())), preferred_element_type=F32)


def dot_nt(a, b):
    return lax.dot_general(a, b, (((1,), (1,)), ((), ())), preferred_element_type=F32)


def dot_tn(a, b):
    return lax.dot_general(a, b, (((0,), (0,)), ((), ())), preferred_element_type=F32)


class Gather:
    def __init__(self, n_hi, ins, outs, s_in, s_out, sems):
        self.n_hi, self.ins, self.outs, self.s_in, self.s_out = n_hi, ins, outs, s_in, s_out
        self.loc, self.zs, self.zr, self.ls, self.lr, self.fs, self.fr, self.cs, self.cr, self.ss, self.sr = sems
        self.dp, self.t = lax.axis_index("dp"), lax.axis_index("tensor")
        self.hi, self.lo = self.dp // 2, lax.rem(self.dp, 2)
        self.core = lax.rem(self.t, 2)
        t_core = self.t + 1 - 2 * self.core
        self.to_x = (self.dp + 1 - 2 * self.lo, self.t)
        self.to_y = (self.dp, lax.rem(self.t + 2, 4))
        self.to_c = (self.dp, t_core)
        self.to_d = (self.dp, lax.rem(t_core + 2, 4))

    def block(self, s, side):
        return lax.rem(self.hi - s + self.n_hi, self.n_hi) * 2 + side

    def greet(self):
        barrier = pltpu.get_barrier_semaphore()
        for up, exists in ((0, self.hi < self.n_hi - 1), (1, self.hi > 0)):

            @pl.when(exists)
            def _():
                pl.semaphore_signal(barrier, inc=1, device_id=self.z_next(up), device_id_type=MESH)

        for peer in (self.to_x, self.to_y, self.to_c, self.to_d):
            pl.semaphore_signal(barrier, inc=1, device_id=peer, device_id_type=MESH)
        along_z = jnp.where(self.hi < self.n_hi - 1, 1, 0) + jnp.where(self.hi > 0, 1, 0)
        pl.semaphore_wait(barrier, 4 + along_z)

    def z_next(self, down):
        hi = jnp.maximum(self.hi - 1, 0) if down else jnp.minimum(self.hi + 1, self.n_hi - 1)
        return (hi * 2 + self.lo, self.t)

    def remote(self, src, dst, send, recv, peer):
        return pltpu.make_async_remote_copy(src, dst, send, recv, device_id=peer, device_id_type=MESH)

    def small(self):
        core = self.core
        return (
            pltpu.make_async_copy(self.s_in, self.s_out.at[core], self.loc.at[3]),
            self.remote(self.s_in, self.s_out.at[core], self.ss.at[0], self.sr.at[0], self.to_c),
            self.remote(self.s_in, self.s_out.at[2 + core], self.ss.at[1], self.sr.at[1], self.to_y),
            self.remote(self.s_in, self.s_out.at[2 + core], self.ss.at[2], self.sr.at[2], self.to_d),
        )

    def local(self, k):
        return pltpu.make_async_copy(self.ins[k], self.outs[k].at[self.core, self.dp], self.loc.at[k])

    def z_send(self, k, d, down):
        b = self.block(self.n_hi - d if down else d, self.lo)
        dst = self.outs[k].at[self.core, b]
        src = self.ins[k] if d == 0 else dst
        return self.remote(src, dst, self.zs.at[down, k, d], self.zr.at[down, k, d], self.z_next(down))

    def z_more(self, down):
        return self.hi > 0 if down else self.hi < self.n_hi - 1

    def z_came(self, d, down):
        return self.hi + d < self.n_hi if down else self.hi >= d

    def line(self, k, s, way, own=False):
        out, b = self.outs[k], self.block(s, self.lo)
        src = self.ins[k] if own else out.at[self.core, b]
        dst = out.at[self.core if way == 0 else 2 + self.core, b]
        return self.remote(
            src, dst, self.ls.at[way, k, s], self.lr.at[way, k, s], self.to_x if way == 0 else self.to_y
        )

    def onward(self, k, s, way):
        out = self.outs[k]
        if way == 0:
            src = dst = out.at[2 + self.core, self.block(s, self.lo)]
        else:
            b = self.block(s, 1 - self.lo)
            src, dst = out.at[self.core, b], out.at[2 + self.core, b]
        return self.remote(src, dst, self.fs.at[k, s], self.fr.at[k, s], self.to_x if way == 0 else self.to_y)

    def to_core(self, k, s, which, own=False):
        out = self.outs[k]
        side = self.lo if which % 2 == 0 else 1 - self.lo
        where = out.at[self.core if which < 2 else 2 + self.core, self.block(s, side)]
        return self.remote(
            self.ins[k] if own else where, where, self.cs.at[which, k, s], self.cr.at[which, k, s], self.to_c
        )

    def start(self, k):
        for down in range(2):
            pl.when(self.z_more(down))(lambda: self.z_send(k, 0, down).start())
        self.line(k, 0, 0, True).start()
        if k == 0:
            self.line(k, 0, 1, True).start()
        self.to_core(k, 0, 0, True).start()
        self.local(k).start()

    def lines_y(self, k):
        for s in range(self.n_hi):
            self.line(k, s, 1, s == 0).start()

    def near(self, d, action):
        if d == 0:
            action(0)
            return
        pl.when(self.z_came(d, 0))(lambda: action(d))
        pl.when(self.z_came(d, 1))(lambda: action(self.n_hi - d))

    def spread(self, k, d):
        for down in range(2):

            @pl.when(self.z_came(d, down))
            def _():
                self.z_send(k, d - 1, down).wait_recv()
                if d < self.n_hi - 1:
                    pl.when(self.z_more(down))(lambda: self.z_send(k, d, down).start())
                s = self.n_hi - d if down else d
                self.line(k, s, 0).start()
                if k == 0:
                    self.line(k, s, 1).start()
                self.to_core(k, s, 0).start()

    def over_x(self, k, s):
        self.line(k, s, 0).wait_recv()
        self.onward(k, s, 1).start()
        self.to_core(k, s, 1).start()

    def over_y(self, k, s):
        self.line(k, s, 1).wait_recv()
        self.onward(k, s, 0).start()
        self.to_core(k, s, 2).start()

    def late_x(self, k, s):
        self.line(k, s, 0).wait_recv()
        self.to_core(k, s, 1).start()

    def late_y(self, k, s):
        self.line(k, s, 1).wait_recv()
        self.to_core(k, s, 2).start()

    def pass_on(self, k, d, core=None):
        if k == 2:
            way = (self.over_x, self.over_y)[core]
            pl.when(self.core == core)(lambda: self.near(d, lambda s: way(k, s)))
        else:
            way = (self.over_x, self.over_y)[k]
            self.near(d, lambda s: way(k, s))

    def late(self, k):
        for s in range(self.n_hi):
            if k == 2:
                pl.when(self.core == 0)(lambda: self.late_y(k, s))
                pl.when(self.core == 1)(lambda: self.late_x(k, s))
            else:
                (self.late_y, self.late_x)[k](k, s)

    def diagonal(self, k, s):
        self.onward(k, s, 0).wait_recv()
        self.to_core(k, s, 3).start()

    def arrived(self, k, whiches):
        for s in range(self.n_hi):
            for which in whiches:
                self.to_core(k, s, which).wait_recv()

    def sent(self, k):
        for down in range(2):
            for d in range(self.n_hi - 1):
                came = self.z_more(down) if d == 0 else jnp.logical_and(self.z_more(down), self.z_came(d, down))
                pl.when(came)(lambda: self.z_send(k, d, down).wait_send())
        for s in range(self.n_hi):
            self.line(k, s, 0).wait_send()
            self.line(k, s, 1).wait_send()
            self.onward(k, s, 0).wait_send()
            for which in range(4):
                self.to_core(k, s, which).wait_send()


def gather_scratch(n_hi):
    dma = pltpu.SemaphoreType.DMA
    return [
        dma((4,)), dma((2, 3, n_hi)), dma((2, 3, n_hi)), dma((2, 3, n_hi)), dma((2, 3, n_hi)), dma((3, n_hi)),
        dma((3, n_hi)), dma((4, 3, n_hi)), dma((4, 3, n_hi)), dma((3,)), dma((3,)),
    ]


def pool_matrix(pooled, length):
    i = lax.broadcasted_iota(jnp.int32, (pooled, length), 0)
    j = lax.broadcasted_iota(jnp.int32, (pooled, length), 1)
    return jnp.where(j // 2 == i, 0.5, 0.0).astype(BF16)


def lane_low(shape):
    return lax.broadcasted_iota(jnp.int32, shape, 1) < 64


def attention_kernel(n_seq, length, n_dp, comm, *refs):
    half = length // 2
    group, b = pl.program_id(0), pl.program_id(1)
    step = group * n_seq + b
    core = lax.rem(lax.axis_index("tensor"), 2)
    len_ref, x_any, bo_ref = refs[:3]
    refs = refs[3:]
    if comm:
        (kw, vw, qw, ow, uw, dw, tab, vbias, hbias) = refs[:9]
        kv_ref, q_ref, p_ref, ctx_ref, hid_ref, pb_ref, a_out, u_out, d_out, s_out = refs[9:19]
        bias, x_ref, x_sem, a_in, u_in, d_in, s_in, a_all, s_all, a_sem, s_sem = refs[19:30]
        net = Gather(n_dp // 2, (a_in, u_in, d_in), (a_all, u_out, d_out), s_in, s_all, refs[30:])
    else:
        a_ref, s_ref = refs[:2]
        kv_ref, q_ref, p_ref, ctx_ref, hid_ref, pb_ref, bias, x_ref, x_sem = refs[2:]
    n_tok = n_seq * length
    x_copy = pltpu.make_async_copy(x_any.at[pl.ds(pl.multiple_of(core * n_tok, n_tok), n_tok), :], x_ref, x_sem)

    def spread_bias(row_of):
        for h in range(3):
            wide = jnp.broadcast_to(row_of(h), (half, 2 * length))
            bias[h] = pltpu.roll(wide, length, 1, stride=2, stride_axis=0)[:, :length].T

    def pool_rows(first, last):
        if first == 0:
            x_copy.wait()
        pool = pool_matrix(half, length)
        for i in range(first, last):
            pooled = dot_nn(pool, x_ref[i * length : (i + 1) * length, :])
            hid_ref[i * half : (i + 1) * half, :] = pooled + bo_ref[...].reshape(1, -1)
            pb_ref[i * half : (i + 1) * half, :] = pooled.astype(BF16)

    if comm:

        def a_copy(g):
            return pltpu.make_async_copy(a_all.at[g], a_out.at[g], a_sem.at[g])

        s_copy = pltpu.make_async_copy(s_all, s_out, s_sem)

        @pl.when(step == 0)
        def _():
            x_copy.start()
            k, v, o = kw[...], vw[...], ow[...].T
            parts = (k[:, :128], v[:, :128], k[:, 128:], v[:, 128:], qw[...], o[:, 128:], o[:, :128])
            a_in[...] = jnp.concatenate(parts, axis=1).astype(BF16)
            s_in[...] = jnp.zeros_like(s_in)
            s_in[0:3, :] = tab[...]
            vb = vbias[...].reshape(1, -1)
            s_in[3:4, 128:256] = vb[:, 0:128]
            s_in[3:4, 320:384] = vb[:, 128:192]
            s_in[4:5, 0 : hbias.shape[0]] = hbias[...].reshape(1, -1)
            net.greet()
            for copy in net.small():
                copy.start()
            net.start(0)
            u_in[...] = uw[...].astype(BF16)
            d_in[...] = dw[...].astype(BF16)
            cuts = [min(i, n_seq) for i in range(n_dp // 2)]
            for s in range(1, n_dp // 2):
                net.spread(0, s)
                net.pass_on(0, s - 1)
                pool_rows(cuts[s - 1], cuts[s])
            net.start(1)
            small = net.small()
            small[0].wait()
            for copy in small[1:]:
                copy.wait()
            s_copy.start()
            spread_bias(lambda h: s_all[0, h : h + 1, :])
            net.pass_on(0, n_dp // 2 - 1)
            pool_rows(cuts[-1], n_seq)
            net.local(0).wait()
            net.arrived(0, (0, 1))

        n_hi = n_dp // 2
        plan = {}

        def at(n, action, *args):
            plan.setdefault(min(n, 4 * n_seq - 1), []).append(functools.partial(action, *args))

        for d in range(1, n_hi):
            at((1, 2, 3)[d - 1], net.spread, 1, d)
            at((4, 5, 6)[d - 1], net.spread, 2, d)
        at(2, net.start, 2)
        at(4, net.late, 0)
        for d in range(n_hi):
            at(4, net.diagonal, 0, d)
            at((6, 7, 8, 9)[d], net.pass_on, 1, d)
            at((9, 9, 10, 10)[d], net.pass_on, 2, d, 0)
            at((10, 11, 12, 13)[d], net.pass_on, 2, d, 1)
            at((10, 11, 12, 13)[d], lambda i: net.near(i, lambda s: net.diagonal(1, s)), d)
        at(3, net.lines_y, 1)
        at(2 * n_seq, net.arrived, 0, (2, 3))
        for g in range(4):
            at(2 * n_seq, lambda i: a_copy(i).start(), g)
        at(7, net.lines_y, 2)
        at(9, net.late, 1)
        at(14, net.late, 2)
        for n, actions in plan.items():

            @pl.when(step == n)
            def _():
                for action in actions:
                    action()

        def weights(lanes):
            return a_all[group, :, :, lanes].reshape(-1, lanes.stop - lanes.start)

        def small_row(i):
            return s_all[group, i : i + 1, :]
    else:

        @pl.when(step == 0)
        def _():
            x_copy.start()
            pool_rows(0, n_seq)

        def weights(lanes):
            return a_ref[0, :, lanes]

        def small_row(i):
            return s_ref[0, i : i + 1, :]

    krows = pl.ds(pl.multiple_of(b * length, length), length)
    qrows = pl.ds(pl.multiple_of(b * half, half), half)

    @pl.when(jnp.logical_and(b == 0, step > 0) if comm else b == 0)
    def _():
        spread_bias(small_row)

    kv_ref[0] = (dot_nn(x_ref[krows, :], weights(slice(0, 384))) + small_row(3)[:, 0:384]).astype(BF16)
    q = dot_nn(pb_ref[qrows, :], weights(slice(384, 640))) * 0.125
    lanes = lax.broadcasted_iota(jnp.int32, q.shape, 1)
    q = jnp.where(lanes < 192, q, 0.0).astype(BF16)
    q_ref[0] = q
    low = lane_low((half, 128))
    valid = lax.broadcasted_iota(jnp.int32, (length, half), 0) < len_ref[core * n_seq + b]
    q01 = q[:, 0:128]
    zero = jnp.zeros_like(q01)
    heads = (
        (jnp.where(low, q01, zero), 0, 128),
        (jnp.where(low, zero, q01), 0, 128),
        (q[:, 128:256], 256, 256),
    )
    raw = [dot_nt(kv_ref[0, :, k_at : k_at + 128], qh) for qh, k_at, _ in heads]
    probs = []
    for h in range(3):
        s = jnp.where(valid, raw[h] + bias[h], -1e30)
        e = jnp.exp(s - jnp.max(s, axis=0, keepdims=True))
        p = (e * (1.0 / jnp.sum(e, axis=0, keepdims=True))).astype(BF16)
        p_ref[0, 0, h] = p
        probs.append(p)
    contexts = [dot_tn(kv_ref[0, :, v_at : v_at + 128], p) for (_, _, v_at), p in zip(heads, probs)]
    c0, c1, c2 = contexts
    ctx01 = jnp.concatenate([c0[0:64], c1[64:128]], axis=0).T
    ctx2 = jnp.concatenate([jnp.zeros_like(c2[0:64]), c2[64:128]], axis=0).T
    ctx = jnp.concatenate([ctx2, ctx01], axis=1).astype(BF16)
    ctx_ref[0] = ctx
    hid_ref[qrows, :] += dot_nt(ctx, weights(slice(512, 768)))

    if comm:

        @pl.when(step == 4 * n_seq - 1)
        def _():
            for s in range(n_hi):
                net.diagonal(2, s)
            for k in range(3):
                net.sent(k)
            for k in (1, 2):
                net.local(k).wait()
                net.arrived(k, (0, 1, 2, 3))
            for g in range(4):
                a_copy(g).wait()
            s_copy.wait()


def my_core():
    return lax.rem(lax.axis_index("tensor"), 2)


def attention_forward(lengths, tokens, b_out, weights, n_dp, comm):
    n_seq = lengths.shape[0] // 2
    length = tokens.shape[0] // lengths.shape[0]
    half = length // 2
    width = tokens.shape[1]
    once = pl.Buffered(1)

    def fixed(shape):
        return pl.BlockSpec(shape, lambda g, b: (0,) * len(shape), pipeline_mode=once)

    in_specs = [
        pl.BlockSpec(memory_space=pltpu.SMEM),
        pl.BlockSpec(memory_space=pl.ANY),
        fixed((width,)),
    ]
    out_shape = [
        jax.ShapeDtypeStruct((4, n_seq * length, 384), BF16),
        jax.ShapeDtypeStruct((4, n_seq * half, 256), BF16),
        jax.ShapeDtypeStruct((4, n_seq, 3, length, half), BF16),
        jax.ShapeDtypeStruct((4, n_seq * half, 256), BF16),
        jax.ShapeDtypeStruct((n_seq * half, width), F32),
        jax.ShapeDtypeStruct((n_seq * half, width), BF16),
    ]
    out_specs = [
        pl.BlockSpec((1, length, 384), lambda g, b: (g, b, 0)),
        pl.BlockSpec((1, half, 256), lambda g, b: (g, b, 0)),
        pl.BlockSpec((1, 1, 3, length, half), lambda g, b: (g, b, 0, 0, 0)),
        pl.BlockSpec((1, half, 256), lambda g, b: (g, b, 0)),
        fixed((n_seq * half, width)),
        fixed((n_seq * half, width)),
    ]
    scratch = [
        pltpu.VMEM((3, length, half), F32), pltpu.VMEM((n_seq * length, width), BF16), pltpu.SemaphoreType.DMA,
    ]
    params = {"vmem_limit_bytes": VMEM_LIMIT}
    if comm:
        rows = width // n_dp
        in_specs += [fixed(w.shape) for w in weights]
        whole = jax.ShapeDtypeStruct((4, n_dp, rows, width), BF16)
        small = jax.ShapeDtypeStruct((4, 8, 2 * length), F32)
        out_shape += [whole, whole, whole, small]
        out_specs += [pl.BlockSpec(memory_space=pl.ANY)] * 4
        scratch += [pltpu.VMEM((rows, width), BF16)] * 3
        scratch += [
            pltpu.VMEM((8, 2 * length), F32),
            pltpu.VMEM((4, n_dp, rows, width), BF16),
            pltpu.VMEM((4, 8, 2 * length), F32),
            pltpu.SemaphoreType.DMA((4,)),
            pltpu.SemaphoreType.DMA,
        ]
        scratch += gather_scratch(n_dp // 2)
        params.update(collective_id=0, has_side_effects=True)
    else:
        in_specs += [
            pl.BlockSpec((1, width, 768), lambda g, b: (g, 0, 0)),
            pl.BlockSpec((1, 8, 2 * length), lambda g, b: (g, 0, 0)),
        ]
    outs = pl.pallas_call(
        functools.partial(attention_kernel, n_seq, length, n_dp, comm),
        out_shape=out_shape,
        grid=(4, n_seq),
        in_specs=in_specs,
        out_specs=out_specs,
        scratch_shapes=scratch,
        compiler_params=pltpu.CompilerParams(**params),
        cost_estimate=pl.CostEstimate(flops=20 * 10**9, bytes_accessed=40 * 10**6, transcendentals=6 * 10**6),
    )(lengths, tokens, b_out, *weights)
    if comm:
        flat = (4, width, width)
        outs = list(outs)
        outs = outs[:6] + [w.reshape(flat) for w in outs[6:9]] + outs[9:]
    return outs


def row_mean(v):
    return jnp.mean(v, axis=-1, keepdims=True)


def ffn_kernel(
    n_seq, half, len_ref, hid_ref, cot_ref, u_ref, d_ref, s_ref, v0, v1, v2, v3, v4,
    out_ref, ag_ref, gu_ref, gd_ref, gv_ref, nb_all, fg_all, act_all, pg_all, dg,
):
    b = pl.program_id(0)
    rows = pl.ds(pl.multiple_of(b * half, half), half)
    n_gain, n_shift, b_down, f_gain, f_shift = (v[...].reshape(1, -1) for v in (v0, v1, v2, v3, v4))

    @pl.when(b == 0)
    def _():
        gv_ref[...] = jnp.zeros_like(gv_ref)

    def add(i, v):
        gv_ref[i : i + 1, :] += jnp.sum(v, axis=0, keepdims=True)

    hid = hid_ref[...]
    centred = hid - row_mean(hid)
    inv1 = lax.rsqrt(row_mean(centred * centred) + EPS)
    unit1 = centred * inv1
    normed = unit1 * n_gain + n_shift
    nb = normed.astype(BF16)
    nb_all[rows, :] = nb
    summed = normed + b_down
    for t in range(4):
        pre = dot_nn(nb, u_ref[t]) + s_ref[t, 4:5, 0:768]
        cdf = 0.5 * (1.0 + lax.erf(pre * 0.7071067811865476))
        act = (pre * cdf).astype(BF16)
        dg[t] = cdf + pre * (0.3989422804014327 * jnp.exp(-0.5 * pre * pre))
        act_all[t, rows, :] = act
        summed = summed + dot_nt(act, d_ref[t])
    centred = summed - row_mean(summed)
    inv2 = lax.rsqrt(row_mean(centred * centred) + EPS)
    unit2 = centred * inv2
    valid = (2 * lax.broadcasted_iota(jnp.int32, (half, 1), 0) < len_ref[my_core() * n_seq + b]).astype(F32)
    out_ref[...] = ((unit2 * f_gain + f_shift) * valid).astype(BF16)
    grad = cot_ref[...].astype(F32) * valid
    add(0, grad * unit2)
    add(1, grad)
    scaled = grad * f_gain
    grad_summed = inv2 * (scaled - row_mean(scaled) - unit2 * row_mean(scaled * unit2))
    add(2, grad_summed)
    fg = grad_summed.astype(BF16)
    fg_all[rows, :] = fg
    normed_grad = grad_summed
    for t in range(4):
        pg = (dot_nn(fg, d_ref[t]) * dg[t]).astype(BF16)
        pg_all[t, rows, :] = pg
        normed_grad = normed_grad + dot_nt(pg, u_ref[t])
    add(3, normed_grad * unit1)
    add(4, normed_grad)
    scaled = normed_grad * n_gain
    hidden_grad = inv1 * (scaled - row_mean(scaled) - unit1 * row_mean(scaled * unit1))
    add(5, hidden_grad)
    ag_ref[...] = hidden_grad.astype(BF16)

    @pl.when(b == n_seq - 1)
    def _():
        for i in range(2):
            pg = pg_all[i]
            gu_ref[i] = dot_tn(nb_all[...], pg).astype(BF16)
            gd_ref[i] = dot_tn(fg_all[...], act_all[i]).astype(BF16)
            gv_ref[6 + i : 7 + i, :] = jnp.sum(pg.astype(F32), axis=0, keepdims=True)


def ffn(lengths, hid, cotangent, u4, d4, s4, vectors, n_seq, half):
    width = hid.shape[1]
    once = pl.Buffered(1)
    return pl.pallas_call(
        functools.partial(ffn_kernel, n_seq, half),
        out_shape=(
            jax.ShapeDtypeStruct((2 * n_seq * half, width), BF16),
            jax.ShapeDtypeStruct((n_seq * half, width), BF16),
            jax.ShapeDtypeStruct((2, width, 768), BF16),
            jax.ShapeDtypeStruct((2, width, 768), BF16),
            jax.ShapeDtypeStruct((8, width), F32),
        ),
        grid=(n_seq,),
        in_specs=[
            pl.BlockSpec(memory_space=pltpu.SMEM),
            pl.BlockSpec((half, width), lambda b: (b, 0)),
            pl.BlockSpec((half, width), lambda b: (my_core() * n_seq + b, 0)),
            pl.BlockSpec((4, width, 768), lambda b: (0, 0, 0), pipeline_mode=once),
            pl.BlockSpec((4, width, 768), lambda b: (0, 0, 0), pipeline_mode=once),
            pl.BlockSpec(s4.shape, lambda b: (0, 0, 0), pipeline_mode=once),
        ]
        + [pl.BlockSpec((width,), lambda b: (0,), pipeline_mode=once)] * 5,
        out_specs=[
            pl.BlockSpec((half, width), lambda b: (my_core() * n_seq + b, 0)),
            pl.BlockSpec((half, width), lambda b: (b, 0)),
            pl.BlockSpec((2, width, 768), lambda b: (0, 0, 0), pipeline_mode=once),
            pl.BlockSpec((2, width, 768), lambda b: (0, 0, 0), pipeline_mode=once),
            pl.BlockSpec((8, width), lambda b: (0, 0), pipeline_mode=once),
        ],
        scratch_shapes=[
            pltpu.VMEM((n_seq * half, width), BF16),
            pltpu.VMEM((n_seq * half, width), BF16),
            pltpu.VMEM((4, n_seq * half, 768), BF16),
            pltpu.VMEM((4, n_seq * half, 768), BF16),
            pltpu.VMEM((4, half, 768), F32),
        ],
        compiler_params=pltpu.CompilerParams(vmem_limit_bytes=VMEM_LIMIT),
        cost_estimate=pl.CostEstimate(flops=24 * 10**9, bytes_accessed=30 * 10**6, transcendentals=6 * 10**6),
    )(lengths, hid, cotangent, u4, d4, s4, *vectors)


class Net:
    def __init__(self, n_hi):
        self.n_hi = n_hi
        self.dp, self.t = lax.axis_index("dp"), lax.axis_index("tensor")
        self.hi, self.lo = self.dp // 2, lax.rem(self.dp, 2)
        self.core = lax.rem(self.t, 2)
        self.to_x = (self.dp + 1 - 2 * self.lo, self.t)
        self.to_c = (self.dp, self.t + 1 - 2 * self.core)

    def place(self, s):
        return lax.rem(self.hi + s, self.n_hi)

    def z_peer(self, s):
        return (self.place(s) * 2 + self.lo, self.t)

    def greet(self):
        barrier = pltpu.get_barrier_semaphore()
        peers = [self.z_peer(s) for s in range(1, self.n_hi)] + [self.to_x, self.to_c]
        for peer in peers:
            pl.semaphore_signal(barrier, inc=1, device_id=peer, device_id_type=MESH)
        pl.semaphore_wait(barrier, len(peers))

    def remote(self, src, dst, send, recv, peer):
        return pltpu.make_async_remote_copy(src, dst, send, recv, device_id=peer, device_id_type=MESH)


class Scatter:
    PARTS = 3

    def __init__(self, net, mine, other, bufs):
        self.net, self.mine, self.other = net, mine, other
        self.t1, self.t2, self.r3, self.sem, self.xs, self.xr, self.zs, self.zr = bufs
        self.rows = self.t2.shape[1] // self.PARTS

    @staticmethod
    def scratch(n_hi, rows, width):
        dma = pltpu.SemaphoreType.DMA
        both, half = pltpu.VMEM((n_hi, 2, rows, width), BF16), pltpu.VMEM((n_hi, rows, width), BF16)
        parts = Scatter.PARTS
        return [both, half, half, dma((2,)), dma((parts,)), dma((parts,)), dma((parts, n_hi)), dma((parts, n_hi))]

    def part(self, i):
        return pl.ds(i * self.rows, self.rows)

    def over_core(self):
        return self.net.remote(self.other, self.t1, self.sem.at[0], self.sem.at[1], self.net.to_c)

    def over_x(self, i):
        src = self.t1.at[:, 1 - self.net.lo, self.part(i)]
        return self.net.remote(src, self.t2.at[:, self.part(i)], self.xs.at[i], self.xr.at[i], self.net.to_x)

    def over_z(self, i, s):
        src = self.t2.at[self.net.place(s), self.part(i)]
        dst = self.r3.at[s, self.part(i)]
        return self.net.remote(src, dst, self.zs.at[i, s], self.zr.at[i, s], self.net.z_peer(s))

    def core_to_x(self):
        self.over_core().wait_recv()
        self.t1[...] += self.mine[...]
        for i in range(self.PARTS):
            self.over_x(i).start()

    def x_sum(self, i):
        self.over_x(i).wait_recv()
        rows = self.part(i)
        self.t2[:, rows] += self.t1[:, self.net.lo, rows]

    def start_z(self, i):
        for s in range(1, self.net.n_hi):
            self.over_z(i, s).start()

    def x_to_z(self, i):
        self.x_sum(i)
        self.start_z(i)

    def finish(self, out):
        for i in range(self.PARTS):
            rows = self.part(i)
            total = self.t2[self.net.hi, rows].astype(F32)
            for s in range(1, self.net.n_hi):
                self.over_z(i, s).wait_recv()
                total += self.r3[s, rows].astype(F32)
            out[rows, :] = total

    def sent_x(self):
        self.over_core().wait_send()
        for i in range(self.PARTS):
            self.over_x(i).wait_send()

    def sent_z(self):
        for i in range(self.PARTS):
            for s in range(1, self.net.n_hi):
                self.over_z(i, s).wait_send()


class SmallSum:
    def __init__(self, net, mine, other, bufs):
        self.net, self.mine, self.other = net, mine, other
        self.rc, self.v1, self.rx, self.v2, self.sem, self.zs, self.zr = bufs

    @staticmethod
    def scratch(n_hi, shape):
        dma = pltpu.SemaphoreType.DMA
        return [
            pltpu.VMEM(shape, F32), pltpu.VMEM(shape, F32), pltpu.VMEM(shape, F32), pltpu.VMEM((n_hi,) + shape, F32),
            dma((4,)), dma((n_hi,)), dma((n_hi,)),
        ]

    def over_core(self):
        return self.net.remote(self.other, self.rc, self.sem.at[0], self.sem.at[1], self.net.to_c)

    def over_x(self):
        return self.net.remote(self.v1, self.rx, self.sem.at[2], self.sem.at[3], self.net.to_x)

    def over_z(self, s):
        here = self.v2.at[self.net.hi]
        return self.net.remote(here, here, self.zs.at[s], self.zr.at[s], self.net.z_peer(s))

    def core_to_x(self):
        self.over_core().wait_recv()
        self.v1[...] = self.mine[...] + self.rc[...]
        self.over_x().start()

    def x_to_z(self):
        self.over_x().wait_recv()
        self.v2[self.net.hi] = self.v1[...] + self.rx[...]
        for s in range(1, self.net.n_hi):
            self.over_z(s).start()

    def finish(self, out):
        for s in range(1, self.net.n_hi):
            self.over_z(s).wait()
        out[...] = jnp.sum(self.v2[...], axis=0)
        self.over_core().wait_send()
        self.over_x().wait_send()

def backward_step(half, own, step_refs):
    kv_ref, q_ref, p_ref, ag, a_of, tacc, kvd, qd_ref = step_refs
    low = lane_low((half, 128))
    cg = dot_nn(ag, a_of(slice(512, 768))).astype(BF16)
    q01 = q_ref[0, :, 0:128]
    cg2, cg01 = cg[:, 0:128], cg[:, 128:256]
    zero = jnp.zeros_like(q01)
    heads = (
        (jnp.where(low, q01, zero), jnp.where(low, cg01, zero), 0, 128),
        (jnp.where(low, zero, q01), jnp.where(low, zero, cg01), 0, 128),
        (q_ref[0, :, 128:256], jnp.where(low, zero, cg2), 256, 256),
    )
    raw = [dot_nt(kv_ref[0, :, v_at : v_at + 128], g) for _, g, _, v_at in heads]
    vds = [dot_nn(p_ref[0, 0, h], head[1]) for h, head in enumerate(heads)]
    grads = []
    for h in range(3):
        p = p_ref[0, 0, h].astype(F32)
        row = jnp.sum(p * raw[h], axis=0, keepdims=True)
        sg = (p * (raw[h] - row)).astype(BF16)
        if own:
            tacc[h] += sg.astype(F32)
        grads.append(sg)
    kds = [dot_nn(sg, head[0]) for sg, head in zip(grads, heads)]
    qds = [dot_tn(kv_ref[0, :, head[2] : head[2] + 128], sg) for sg, head in zip(grads, heads)]
    kvd[:, 0:128] = (kds[0] + kds[1]).astype(BF16)
    kvd[:, 128:256] = (vds[0] + vds[1]).astype(BF16)
    kvd[:, 256:384] = (kds[2] + vds[2]).astype(BF16)
    qd01 = jnp.concatenate([qds[0][0:64], qds[1][64:128]], axis=0).T
    qd2 = jnp.concatenate([qds[2][0:64], jnp.zeros_like(qds[2][0:64])], axis=0).T
    qd = jnp.concatenate([qd01, qd2], axis=1).astype(BF16)
    qd_ref[...] = qd


def backward_place(step, n_seq):
    core = my_core()
    own = jnp.where(step < n_seq, 1 - core, core)
    rest = 2 + lax.rem(step, 2)
    first = step < 2 * n_seq
    return jnp.where(first, own, rest), jnp.where(first, lax.rem(step, n_seq), lax.rem(step, 2 * n_seq) // 2)


def backward_kernel(n_seq, length, n_dp, comm, *refs):
    half = length // 2
    n_hi = n_dp // 2
    step = pl.program_id(0)
    n_own = 2 * n_seq
    own = step < n_own
    g, b = backward_place(step, n_seq)
    x_any, a_any, kv_ref, q_ref, p_ref, ctx_any, ag_ref, pb_any = refs[:8]
    refs = refs[8:]
    if comm:
        gu_any, gd_any, gv_ref, half_any = refs[:4]
        out_any, tok_any, up_out, down_out, a_out, gv_out, sm_out = refs[4:11]
        refs = refs[11:]
    else:
        tok_out, ga_ref, sm_ref = refs[:3]
        refs = refs[3:]
    kvd, qd_all, tacc, tok, pool, kvd_rest, qd_rest, x_ref, ctx_ref, pb_ref, a_ref, fetch = refs[:12]
    refs = refs[12:]
    core = my_core()
    n_tok = n_seq * length
    late = (
        pltpu.make_async_copy(x_any.at[pl.ds(pl.multiple_of(core * n_tok, n_tok), n_tok), :], x_ref, fetch.at[0]),
        pltpu.make_async_copy(ctx_any.at[0:2], ctx_ref, fetch.at[1]),
        pltpu.make_async_copy(pb_any, pb_ref, fetch.at[2]),
    )
    a_copies = [
        pltpu.make_async_copy(a_any.at[pl.ds(i, 2)], a_ref.at[pl.ds(i, 2)], fetch.at[5 + i // 2]) for i in (0, 2)
    ]

    @pl.when(step == 0)
    def _():
        for copy in a_copies:
            copy.start()

    last = step == 2 * n_own - 1

    def at(n, *actions):
        @pl.when(step == n)
        def _():
            for action in actions:
                action()

    if comm:
        ga_ref, sm_ref, gu_mine, gd_mine, stage = refs[:5]
        net = Net(n_hi)
        other = 1 - core
        up = Scatter(net, gu_mine, gu_any.at[other], refs[5:13])
        down = Scatter(net, gd_mine, gd_any.at[other], refs[13:21])
        att = Scatter(net, ga_ref.at[core], ga_ref.at[other], refs[21:29])
        vec = SmallSum(net, gv_ref, gv_ref, refs[29:36])
        small = SmallSum(net, sm_ref.at[core], sm_ref.at[other], refs[36:43])
        o_sem, t_sem = refs[43:45]
        n_rows = n_seq * half
        o_copy = net.remote(
            half_any.at[pl.ds(pl.multiple_of(core * n_rows, n_rows), n_rows), :], out_any, o_sem.at[0], o_sem.at[1], net.to_c
        )
        mine = (
            pltpu.make_async_copy(gu_any.at[core], gu_mine, fetch.at[3]),
            pltpu.make_async_copy(gd_any.at[core], gd_mine, fetch.at[4]),
        )

        def tok_copies(i):
            row = pl.multiple_of((core * n_seq + i) * length, length)
            where = tok_any.at[pl.ds(row, length), :]
            return (
                pltpu.make_async_copy(stage.at[i], where, t_sem.at[0, i]),
                net.remote(stage.at[i], where, t_sem.at[1, i], t_sem.at[2, i], net.to_c),
            )

        @pl.when(step == 0)
        def _():
            for copy in mine:
                copy.start()
            net.greet()
            vec.over_core().start()
            up.over_core().start()
            down.over_core().start()

        at(3, o_copy.start)
        at(1, vec.core_to_x)
        at(2, mine[0].wait, up.core_to_x, mine[1].wait, down.core_to_x)
        at(4, att.over_core().start, small.over_core().start, vec.x_to_z, lambda: up.x_to_z(0))
        at(5, lambda: up.x_to_z(1))
        at(6, lambda: up.x_to_z(2))
        at(7, lambda: down.x_to_z(0))
        at(8, small.core_to_x, att.core_to_x, lambda: down.x_to_z(1))
        at(9, lambda: down.x_to_z(2))
        at(11, lambda: att.x_to_z(0), small.x_to_z)
        at(13, lambda: att.x_to_z(1))
        at(15, lambda: att.x_to_z(2))

    @pl.when(step == 0)
    def _():
        for copy in late:
            copy.start()
        a_copies[0].wait()

    pl.when(step == n_own)(a_copies[1].wait)

    krows = pl.ds(pl.multiple_of(b * length, length), length)
    qrows = pl.ds(pl.multiple_of(b * half, half), half)

    @pl.when(own)
    def _():
        @pl.when(b == 0)
        def _():
            tacc[g] = jnp.zeros_like(tacc[g])

        backward_step(
            half,
            True,
            (kv_ref, q_ref, p_ref, ag_ref[qrows, :], lambda lanes: a_ref[g, :, lanes], tacc.at[g],
             kvd.at[g, krows], qd_all.at[g, qrows]),
        )

        @pl.when(step == n_seq - 1)
        def _():
            for copy in late:
                copy.wait()

        @pl.when(b == n_seq - 1)
        def _():
            def store(lanes, v):
                v = v.astype(BF16)
                ga_ref[g, ..., lanes] = v.reshape(ga_ref.shape[1:-1] + v.shape[-1:])

            store(slice(0, 384), dot_tn(x_ref[...], kvd[g]))
            gq = dot_tn(pb_ref[...], qd_all[g]) * 0.125
            go = dot_tn(ag_ref[...], ctx_ref[g])
            store(slice(384, 512), gq[:, 0:128])
            store(slice(512, 640), gq[:, 128:256] + go[:, 0:128])
            store(slice(640, 768), go[:, 128:256])
            sm_ref[g, 3:8, :] = jnp.zeros((5, 2 * length), F32)
            sm_ref[g, 3:4, 0:384] = jnp.sum(kvd[g].astype(F32), axis=0, keepdims=True)
            i = lax.broadcasted_iota(jnp.int32, (half, half), 0)
            j = lax.broadcasted_iota(jnp.int32, (half, half), 1)
            flip = jnp.where(i + j == half - 1, 1.0, 0.0).astype(BF16)
            for h in range(3):
                high = tacc[g, h].astype(BF16)
                rest = (tacc[g, h] - high.astype(F32)).astype(BF16)
                turned = dot_nt(flip, high) + dot_nt(flip, rest)
                wide = jnp.concatenate([turned, jnp.zeros((half, length), F32)], axis=1)
                rolled = pltpu.roll(wide, 2, 1, stride=2, stride_axis=0)
                sm_ref[g, h : h + 1, :] = jnp.sum(rolled, axis=0, keepdims=True)

    @pl.when(jnp.logical_not(own))
    def _():
        backward_step(
            half,
            False,
            (kv_ref, q_ref, p_ref, ag_ref[qrows, :], lambda lanes: a_ref[g, :, lanes], None, kvd_rest, qd_rest),
        )
        h = g - 2
        tok_add = dot_nt(kvd_rest[...], a_ref[g, :, 0:384]) + dot_nt(kvd[h, krows], a_ref[h, :, 0:384])
        pool_add = dot_nt(qd_rest[...], a_ref[g, :, 384:640]) + dot_nt(qd_all[h, qrows], a_ref[h, :, 384:640])

        @pl.when(g == 2)
        def _():
            tok[...] = tok_add
            pool[...] = pool_add

        @pl.when(g == 3)
        def _():
            total = ((pool[...] + pool_add) * 0.125 + ag_ref[qrows, :].astype(F32)).astype(BF16)
            final = (tok[...] + tok_add + dot_tn(pool_matrix(half, length), total)).astype(BF16)
            if comm:
                stage[b] = final
                for copy in tok_copies(b):
                    copy.start()
            else:
                tok_out[...] = final

    if comm:

        @pl.when(last)
        def _():
            vec.finish(gv_out)
            up.finish(up_out)
            down.finish(down_out)
            small.finish(sm_out)
            att.finish(a_out)
            for each in (up, down, att):
                each.sent_x()
                each.sent_z()
            o_copy.wait()
            for i in range(n_seq):
                for copy in tok_copies(i):
                    copy.wait()


def fixed(shape, first=None):
    def index(*grid):
        head = 0 if first is None else first()
        return (head,) + (0,) * (len(shape) - 1)

    return pl.BlockSpec(shape, index, pipeline_mode=pl.Buffered(1))


ANY = pl.BlockSpec(memory_space=pl.ANY)


def attention_backward(tokens, a4, kv, q, p, ctx, ag, pb, gu, gd, gv, out_half, n_seq, n_dp, comm):
    length = kv.shape[1] // n_seq
    half = length // 2
    width = tokens.shape[1]
    n_tok, n_pool = n_seq * length, n_seq * half
    n_own = 2 * n_seq
    n_hi, rows = n_dp // 2, width // n_dp

    def place(n):
        return backward_place(n, n_seq)

    in_specs = [
        ANY,
        ANY,
        pl.BlockSpec((1, length, 384), lambda n: place(n) + (0,)),
        pl.BlockSpec((1, half, 256), lambda n: place(n) + (0,)),
        pl.BlockSpec((1, 1, 3, length, half), lambda n: place(n) + (0, 0, 0)),
        ANY,
        fixed((n_pool, width)),
        ANY,
    ]
    args = [tokens, a4, kv, q, p, ctx, ag, pb]
    scratch = [
        pltpu.VMEM((2, n_tok, 384), BF16), pltpu.VMEM((2, n_pool, 256), BF16), pltpu.VMEM((2, 3, length, half), F32),
        pltpu.VMEM((length, width), F32), pltpu.VMEM((half, width), F32), pltpu.VMEM((length, 384), BF16),
        pltpu.VMEM((half, 256), BF16), pltpu.VMEM((n_tok, width), BF16), pltpu.VMEM((2, n_pool, 256), BF16), pltpu.VMEM((n_pool, width), BF16),
        pltpu.VMEM((4, width, 768), BF16), pltpu.SemaphoreType.DMA((7,)),
    ]
    params = {"vmem_limit_bytes": VMEM_LIMIT}
    small = (8, 2 * length)
    if comm:
        split = (2, n_hi, 2, rows, width)
        in_specs += [ANY, ANY, fixed(gv.shape), ANY]
        args += [gu.reshape(split), gd.reshape(split), gv, out_half]
        shares = [jax.ShapeDtypeStruct((rows, width), F32)] * 3
        out_shape = [
            jax.ShapeDtypeStruct((n_pool, width), BF16), jax.ShapeDtypeStruct((2 * n_tok, width), BF16), *shares,
            jax.ShapeDtypeStruct(gv.shape, F32), jax.ShapeDtypeStruct(small, F32),
        ]
        out_specs = [ANY, ANY] + [fixed((rows, width))] * 3 + [fixed(gv.shape), fixed(small)]
        scratch += [
            pltpu.VMEM(split, BF16), pltpu.VMEM((2,) + small, F32), pltpu.VMEM(split[1:], BF16),
            pltpu.VMEM(split[1:], BF16), pltpu.VMEM((n_seq, length, width), BF16),
        ]
        for _ in range(3):
            scratch += Scatter.scratch(n_hi, rows, width)
        scratch += SmallSum.scratch(n_hi, gv.shape) + SmallSum.scratch(n_hi, small)
        scratch += [pltpu.SemaphoreType.DMA((2,)), pltpu.SemaphoreType.DMA((3, n_seq))]
        params.update(collective_id=1, has_side_effects=True)
    else:
        out_shape = [
            jax.ShapeDtypeStruct((n_tok, width), BF16), jax.ShapeDtypeStruct((2, width, 768), BF16),
            jax.ShapeDtypeStruct((2,) + small, F32),
        ]
        out_specs = [
            pl.BlockSpec((length, width), lambda n: (jnp.maximum(n - n_own, 0) // 2, 0)), fixed((2, width, 768)),
            fixed((2,) + small),
        ]
    return pl.pallas_call(
        functools.partial(backward_kernel, n_seq, length, n_dp, comm),
        out_shape=out_shape,
        grid=(2 * n_own,),
        in_specs=in_specs,
        out_specs=out_specs,
        scratch_shapes=scratch,
        compiler_params=pltpu.CompilerParams(**params),
        cost_estimate=pl.CostEstimate(flops=40 * 10**9, bytes_accessed=30 * 10**6, transcendentals=0),
    )(*args)


def finish_kernel(n_out, n_tok, chunk, a_ref, up_ref, down_ref, gv_ref, sm_ref, half_any, other_any, tok_any, *refs):
    out_any, tok_out = refs[:2]
    query, key, value, out, up, down, table, vbias, ubias, *vectors = refs[2:17]
    buf, sem = refs[17:]
    first = (1 - my_core()) * n_out * chunk
    moves = []
    for i in range(n_tok + n_out):
        if i < n_tok:
            src = tok_any.at[pl.ds(i * chunk, chunk)]
            dst = tok_out.at[pl.ds(i * chunk, chunk)]
        else:
            at = (i - n_tok) * chunk
            src = other_any.at[pl.ds(at, chunk)]
            dst = out_any.at[pl.ds(pl.multiple_of(first + at, chunk), chunk)]
        come = pltpu.make_async_copy(src, buf.at[i], sem.at[0, i])
        moves.append((come, pltpu.make_async_copy(buf.at[i], dst, sem.at[1, i])))
    for come, _ in moves:
        come.start()
    query[...] = a_ref[:, 384:576]
    key[:, 0:128] = a_ref[:, 0:128]
    key[:, 128:192] = a_ref[:, 256:320]
    value[:, 0:128] = a_ref[:, 128:256]
    value[:, 128:192] = a_ref[:, 320:384]
    out[0:128, :] = a_ref[:, 640:768].T
    out[128:192, :] = a_ref[:, 512:640].T[64:128]
    up[...] = up_ref[...]
    down[...] = down_ref[...]
    table[...] = sm_ref[0:3, :]
    vbias[0:128] = sm_ref[3, 128:256]
    vbias[128:192] = sm_ref[3, 320:384]
    ubias[...] = jnp.where(my_core() == 0, gv_ref[6, :], gv_ref[7, :])
    for i, vec in enumerate(vectors):
        vec[...] = gv_ref[i, :]
    for come, go in moves:
        come.wait()
        go.start()
    for _, go in moves:
        go.wait()


def finish(half_done, other, tok, a_sum, up_sum, down_sum, gv, sm, length):
    rows, width = a_sum.shape
    shapes = [(rows, 192)] * 3 + [(192, rows), (rows, 768), (rows, 768), (3, 2 * length), (192,), (768,)] + [(width,)] * 6
    chunk = length // 2
    n_out, n_tok = other.shape[0] // chunk, tok.shape[0] // chunk
    whole = pl.BlockSpec(memory_space=pltpu.VMEM)
    return pl.pallas_call(
        functools.partial(finish_kernel, n_out, n_tok, chunk),
        out_shape=[jax.ShapeDtypeStruct(half_done.shape, BF16), jax.ShapeDtypeStruct(tok.shape, BF16)]
        + [jax.ShapeDtypeStruct(shape, F32) for shape in shapes],
        in_specs=[whole] * 5 + [ANY] * 3,
        out_specs=[ANY] * 2 + [whole] * len(shapes),
        scratch_shapes=[
            pltpu.VMEM((n_tok + n_out, chunk, width), BF16), pltpu.SemaphoreType.DMA((2, n_tok + n_out)),
        ],
        input_output_aliases={5: 0},
        compiler_params=pltpu.CompilerParams(vmem_limit_bytes=VMEM_LIMIT),
    )(a_sum, up_sum, down_sum, gv, sm, half_done, other, tok)


def gather_plain(weights, length):
    kw, vw, qw, ow, uw, dw, tab, vbias, hbias = weights
    ot = ow.T
    packed = jnp.concatenate([kw[:, :128], vw[:, :128], kw[:, 128:], vw[:, 128:], qw, ot[:, 128:], ot[:, :128]], axis=1)
    small = jnp.zeros((8, 2 * length), F32).at[0:3].set(tab).at[3, 128:256].set(vbias[:128])
    small = small.at[3, 320:384].set(vbias[128:]).at[4, : hbias.shape[0]].set(hbias)
    first = 2 * (lax.axis_index("tensor") // 2)

    def groups(v):
        every = lax.all_gather(v, "tensor")
        return lax.dynamic_slice_in_dim(jnp.concatenate([every, every]), first, 4)

    wide = jnp.stack([packed, uw, dw], axis=1).astype(BF16)
    wide = groups(lax.all_gather(wide, "dp", axis=0, tiled=True))
    return wide[:, :, 0], wide[:, :, 1], wide[:, :, 2], groups(small)


def sum_plain(grads, n_dp):
    core = my_core()
    mine = lax.dynamic_index_in_dim(grads, core, 0, keepdims=False).astype(F32)
    other = lax.dynamic_index_in_dim(grads, 1 - core, 0, keepdims=False)
    total = mine + lax.ppermute(other, "tensor", [(i, i ^ 1) for i in range(4)]).astype(F32)
    return lax.psum_scatter(total, "dp", scatter_dimension=0, tiled=True)


def shards(
    n_dp, tokens, lengths, cotangent, query_weight, key_weight, value_weight, value_bias, output_weight,
    b_out, rel_table, norm_gain, norm_shift, up_weight, hidden_bias, down_weight, b_down, final_gain, final_shift,
):
    seq_count = lengths.shape[0]
    length = tokens.shape[0] // seq_count
    half = length // 2
    n_seq = seq_count // 2
    core = my_core()
    n_hi, rows = n_dp // 2, tokens.shape[1] // n_dp
    comm = rows % 16 == 0 and n_hi <= 4

    weights = (
        key_weight, value_weight, query_weight, output_weight, up_weight, down_weight.T, rel_table,
        value_bias, hidden_bias,
    )
    if not comm:
        weights = gather_plain(weights, length)
        a4, u4, d4, s4 = weights
        weights = (a4, s4)
    kv, q, p, ctx, hid, pb, *gathered = attention_forward(lengths, tokens, b_out, weights, n_dp, comm)
    if comm:
        a4, u4, d4, s4 = gathered
    vectors = (norm_gain, norm_shift, b_down, final_gain, final_shift)
    out_half, ag, gu, gd, gv = ffn(lengths, hid, cotangent, u4, d4, s4, vectors, n_seq, half)
    sums = attention_backward(tokens, a4, kv, q, p, ctx, ag, pb, gu, gd, gv, out_half, n_seq, n_dp, comm)
    if comm:
        other_half, tokens_grad, up_sum, down_sum, a_sum, gv, sm = sums
    else:
        tok_half, ga, sm = sums
        up_sum, down_sum, a_sum = (sum_plain(v, n_dp) for v in (gu, gd, ga))
        sm, gv = lax.psum((sm, gv), "dp")

        def over_core(v):
            return lax.ppermute(v, "tensor", [(i, i ^ 1) for i in range(4)])

        gv = gv + over_core(gv)
        mine = lax.dynamic_index_in_dim(sm, core, 0, keepdims=False)
        sm = mine + over_core(lax.dynamic_index_in_dim(sm, 1 - core, 0, keepdims=False))

        def join(part):
            got = over_core(part)
            return jnp.where(core == 0, jnp.concatenate([part, got]), jnp.concatenate([got, part]))

        other_half, tokens_grad = over_core(lax.dynamic_slice_in_dim(out_half, core * n_seq * half, n_seq * half)), join(tok_half)
    output, tokens_grad, *cut = finish(out_half, other_half, tokens_grad, a_sum, up_sum, down_sum, gv, sm, length)
    query_sum, key_sum, value_sum, outw_sum, up_sum, down_sum, table_sum, vbias, ubias = cut[:9]
    fgain, fshift, dbias, ngain, nshift, obias = cut[9:]
    return (
        output, tokens_grad, query_sum, key_sum, value_sum, vbias, outw_sum, obias, table_sum,
        ngain, nshift, up_sum, ubias, down_sum.T, dbias, fgain, fshift,
    )


def solution(mesh):
    row, col, both, rep = P("dp", None), P("tensor", "dp"), P("dp", "tensor"), P()
    ten, table = P("tensor"), P("tensor", None)
    in_specs = (
        row, P("dp"), row, both, both, both, ten, col, rep, table, rep, rep, both, ten, col, rep, rep, rep,
    )
    out_specs = (
        row, row, both, both, both, ten, col, rep, table, rep, rep, both, ten, col, rep, rep, rep,
    )
    body = functools.partial(shards, mesh.shape["dp"])
    return jax.shard_map(body, mesh=mesh, in_specs=in_specs, out_specs=out_specs, check_vma=False)
```
